32 devices in a mesh: section: 4 (over x, core), batch: 8 (over z, y).
Axes of the slice: x: 2, y: 2, z: 4, core: 2. Of those that a mesh axis runs over, the one named last changes fastest.
Arguments:
- activations: bfloat16 [16, 1024, 512], P('batch', 'section'), may hold values from -6 to 6
- cotangent: bfloat16 [16, 1024, 512], P('batch', 'section'), may hold values from -6 to 6
- lengths: int32 [16, 8], replicated, may hold values from 0 to 1024, as said below
- gate_weight: bfloat16 [2, 512, 3072], replicated, may hold values from -0.25 to 0.25
- gate_bias: float32 [2, 3072], replicated, may hold values from -12 to 5
- out_weight: bfloat16 [2, 1024, 512], replicated, may hold values from -0.1875 to 0.1875
- up_weight: bfloat16 [2, 512, 2048], replicated, may hold values from -0.25 to 0.25
- down_weight: bfloat16 [2, 2048, 512], replicated, may hold values from -0.125 to 0.125
- mix_gain: float32 [2, 512], replicated, may hold values from 0.25 to 1.75
- mlp_gain: float32 [2, 512], replicated, may hold values from 0.25 to 1.75
Outputs:
- layer_out: float32 [16, 1024, 512], P('batch', 'section')
- input_grad: float32 [16, 1024, 512], P('batch', 'section')
- gate_weight_grad: float32 [2, 512, 3072], P(None, 'section', 'batch')
- gate_bias_grad: float32 [2, 3072], replicated
- out_weight_grad: float32 [2, 1024, 512], P(None, 'section', 'batch')
- up_weight_grad: float32 [2, 512, 2048], P(None, 'section', 'batch')
- down_weight_grad: float32 [2, 2048, 512], P(None, 'section', 'batch')
- mix_gain_grad: float32 [2, 512], replicated
- mlp_gain_grad: float32 [2, 512], replicated
- forget_mean: float32 [2], replicated
The draws below stay inside these ranges and needn't reach their ends.
Inputs may be any that keep to these rules, and one draw needn't show every extreme that they name: In each sequence the nonzero lengths come first; each is between 128 and 512 and their sum is at most 1024, except that in each aligned block of 2 sequences one sequence holds a single document of 1024 positions.
All inputs are finite; a program needn't handle non-finite values.
Results may differ from the reference program's by a relative error of at most 0.007.
Values sent between devices are 32-bit elements; how exact they have to be, the bound alone decides.
A program may use at most 192 MiB of HBM per device.

```python
import math
import jax
import jax.numpy as jnp
from jax import lax

D = 512
HID = 1024
FF = 2048
LAYERS = 2
MICRO = 2
ROW = 1024
DOC_MIN = 128
SEQS = 16
DOCS = 8


def draw_lengths(key, part):
    key = jax.random.fold_in(key, 5)
    subkeys = jax.random.split(key, 3)
    raw_lens = jax.random.randint(subkeys[0], (SEQS, DOCS), DOC_MIN, ROW // 2 + 1, dtype=jnp.int32)
    padding = jax.random.randint(subkeys[1], (SEQS, 1), 0, DOC_MIN, dtype=jnp.int32)
    doc_ends = jnp.cumsum(raw_lens, axis=1).astype(jnp.int32)
    packed = jnp.where(doc_ends <= ROW - padding, raw_lens, 0).astype(jnp.int32)
    chosen = jax.random.randint(subkeys[2], (SEQS // MICRO, 1), 0, MICRO, dtype=jnp.int32)
    member = (jnp.arange(SEQS, dtype=jnp.int32) % MICRO).reshape(SEQS // MICRO, MICRO)
    whole_row = (member == chosen).reshape(SEQS, 1)
    first_slot = (jnp.arange(DOCS, dtype=jnp.int32) == 0)[None, :]
    whole_lens = jnp.where(first_slot, ROW, 0).astype(jnp.int32)
    return jnp.where(whole_row, whole_lens, packed).astype(jnp.int32)


def draw_gate_bias(key, part):
    key = jax.random.fold_in(key, 7)
    subkeys = jax.random.split(key, 3)
    shape_part = (LAYERS, HID)
    forget_part = jax.random.uniform(subkeys[0], shape_part, jnp.float32, 0.0, 4.0)
    input_part = jax.random.uniform(subkeys[1], shape_part, jnp.float32, -11.0, -1.0)
    cand_part = jnp.clip(jax.random.normal(subkeys[2], shape_part, jnp.float32), -3.0, 3.0)
    return jnp.concatenate([forget_part, input_part, cand_part], axis=1)


def shard_levels(stream_key, dims, cuts, least, largest):
    def one(axis_at, shards_of):
        draws = jax.random.uniform(jax.random.fold_in(jax.random.fold_in(stream_key, 6), axis_at), (shards_of,), jnp.float32, least / len(cuts), largest / len(cuts))
        return jnp.repeat(jnp.exp(draws), dims[axis_at] // shards_of).reshape((-1,) + (1,) * (len(dims) - axis_at - 1))

    factor_of = one(*cuts[0])
    for cut in cuts[1:]:
        factor_of = factor_of * one(*cut)
    return factor_of


def normal_values(own_key, dims, width, bound, cuts=(), kind=jnp.bfloat16):
    values = width * jax.random.normal(own_key, dims, jnp.float32)
    if cuts:
        values = values * shard_levels(own_key, dims, cuts, -0.22, 0.18)
    return jnp.clip(values, -bound, bound).astype(kind)


def setup_inputs(seed: int = 0) -> dict:
    keys = jax.random.split(jax.random.key(seed), 11)
    return {
        "activations": normal_values(keys[0], (SEQS, ROW, D), 1.0, 6.0, ((0, 8), (1, 4))),
        "cotangent": normal_values(keys[1], (SEQS, ROW, D), 1.0, 6.0, ((0, 8), (1, 4))),
        "lengths": draw_lengths(jax.random.fold_in(keys[10], 71), 0),
        "gate_weight": normal_values(keys[3], (LAYERS, D, 3 * HID), D ** -0.5, 0.25),
        "gate_bias": draw_gate_bias(jax.random.fold_in(keys[10], 71), 0),
        "out_weight": normal_values(keys[5], (LAYERS, HID, D), HID ** -0.5, 0.1875),
        "up_weight": normal_values(keys[6], (LAYERS, D, FF), D ** -0.5, 0.25),
        "down_weight": normal_values(keys[7], (LAYERS, FF, D), FF ** -0.5, 0.125),
        "mix_gain": jnp.clip(1.0 + 0.15 * jax.random.normal(keys[8], (LAYERS, D), jnp.float32), 0.25, 1.75),
        "mlp_gain": jnp.clip(1.0 + 0.15 * jax.random.normal(keys[9], (LAYERS, D), jnp.float32), 0.25, 1.75),
    }


epsilon = 1e-06

@jax.custom_vjp
def low(v):
    return lax.optimization_barrier(v.astype(jnp.bfloat16)).astype(jnp.float32)

@jax.custom_vjp
def low_back(v):
    return v

def low_keep(v):
    return (low(v), None)

def low_pass(kept, grad):
    return (grad,)

def back_keep(v):
    return (v, None)

def back_low(kept, grad):
    return (low(grad),)
low.defvjp(low_keep, low_pass)
low_back.defvjp(back_keep, back_low)

def compose(earlier_pair, later_pair):
    return (earlier_pair[0] * later_pair[0], later_pair[0] * earlier_pair[1] + later_pair[1])

def normed(values, gain_row):
    return values * lax.rsqrt(lax.optimization_barrier(jnp.mean(values * values, axis=-1, keepdims=True)) + epsilon) * gain_row

def project(left, right):
    return jnp.einsum('rtk,kn->rtn', left, right, precision=lax.Precision.HIGHEST)

def row_masks(lens_rows):
    doc_starts = (jnp.cumsum(lens_rows, axis=1) - lens_rows).astype(jnp.int32)
    row_totals = lax.optimization_barrier(jnp.sum(lens_rows, axis=1)).astype(jnp.int32)
    places = jnp.arange(ROW, dtype=jnp.int32)
    valid_mask = places[None, :] < row_totals[:, None]
    begins = jnp.any((places[None, :, None] == doc_starts[:, None, :]) & (lens_rows[:, None, :] > 0), axis=2)
    keep_mask = valid_mask & jnp.logical_not(begins)
    return (valid_mask.astype(jnp.float32), keep_mask.astype(jnp.float32))

def layer_pass(stream, layer_params, valid_mask, keep_mask):
    gate_w, gate_b, out_w, up_w, down_w, mix_g, mlp_g = layer_params
    hidden_width = out_w.shape[0]
    normed_in = low(normed(stream, mix_g))
    pre_gates = low_back(project(normed_in, gate_w) + gate_b)
    sig_forget = jax.nn.sigmoid(pre_gates[..., :hidden_width])
    sig_input = jax.nn.sigmoid(pre_gates[..., hidden_width:2 * hidden_width])
    candidate = pre_gates[..., 2 * hidden_width:]
    denom_sum = sig_forget + sig_input
    fprime = sig_forget / denom_sum
    decay = fprime * keep_mask[..., None]
    drive = sig_input / denom_sum * candidate * valid_mask[..., None]
    state = lax.associative_scan(compose, (decay, drive), axis=1)[1]
    mixed = stream + low_back(project(low(state), out_w))
    mlp_in = low(normed(mixed, mlp_g))
    pre_up = low_back(project(mlp_in, up_w))
    result = mixed + low_back(project(low(jax.nn.gelu(pre_up, approximate=False)), down_w))
    return (result, jnp.sum(fprime * valid_mask[..., None]))

def forward(params, stream, valid_mask, keep_mask):
    sums = []
    for layer in range(LAYERS):
        layer_params = tuple((weight[layer] for weight in params))
        stream, forget_sum = layer_pass(stream, layer_params, valid_mask, keep_mask)
        sums.append(forget_sum)
    return (stream, jnp.stack(sums))

def reference(activations, cotangent, lengths, gate_weight, gate_bias, out_weight, up_weight, down_weight, mix_gain, mlp_gain):
    params = tuple((weight.astype(jnp.float32) for weight in (gate_weight, gate_bias, out_weight, up_weight, down_weight, mix_gain, mlp_gain)))
    rows_block = math.gcd(SEQS, max(1, 4096 // ROW))
    blocks = SEQS // rows_block
    inputs_blocks = activations.reshape(blocks, rows_block, ROW, D)
    cot_blocks = cotangent.reshape(blocks, rows_block, ROW, D)
    len_blocks = lengths.reshape(blocks, rows_block, DOCS)

    def block_step(carry, item):
        grad_acc, forget_acc = carry
        input_block, cot_block, len_block = item
        valid_mask, keep_mask = row_masks(len_block)

        def run_layers(weights, stream):
            return forward(weights, stream, valid_mask, keep_mask)
        output_block, pull_back, forget_sums = jax.vjp(run_layers, params, input_block.astype(jnp.float32), has_aux=True)
        param_grads, input_block_grad = pull_back(cot_block.astype(jnp.float32))
        grad_acc = jax.tree.map(lambda total, extra: total + extra, grad_acc, param_grads)
        return ((grad_acc, forget_acc + forget_sums), (output_block, input_block_grad))
    start_grads = tuple((jnp.zeros_like(weight) for weight in params))
    start_forget = jnp.zeros((LAYERS,), jnp.float32)
    (grads, forget_sums), (output_rows, input_grads) = lax.scan(block_step, (start_grads, start_forget), (inputs_blocks, cot_blocks, len_blocks))
    true_count = jnp.sum(lengths).astype(jnp.float32)
    forget_mean = forget_sums / (true_count * HID)
    return (output_rows.reshape(SEQS, ROW, D), input_grads.reshape(SEQS, ROW, D), grads[0], grads[1], grads[2], grads[3], grads[4], grads[5], grads[6], forget_mean)
```

```python
import functools
import types

import jax
import jax.numpy as jnp
from jax import lax
from jax.experimental import pallas as pl
from jax.experimental.pallas import tpu as pltpu
from jax.sharding import PartitionSpec as P

epsilon = 1e-06
MESH = pl.DeviceIdType.MESH
F32, BF16 = jnp.float32, jnp.bfloat16
CHUNKS = 8
LANES = 128
ROOT_HALF = 0.7071067811865476
ROOT_TAU = 0.3989422804014327


def tile(index, size):
    return pl.ds(pl.multiple_of(index * size, size), size)


def inverse(value):
    r = pltpu.reciprocal(value, approx=True)
    return r * (2.0 - value * r)


def normal_below(p):
    return 0.5 + 0.5 * lax.erf(p * ROOT_HALF)


def steps_of(count, unroll, one, start, reverse=False):
    def turn(i, carry):
        for k in range(unroll):
            at = i * unroll + k
            carry = one(count - 1 - at if reverse else at, carry)
        return carry

    return lax.fori_loop(0, count // unroll, turn, start)


def gate_weights(a, b):
    inv = inverse(2.0 + a + b)
    return (1.0 + b) * inv, (1.0 + a) * inv, inv


def greet_section(sections):
    me = lax.axis_index("section")
    barrier = pltpu.get_barrier_semaphore()
    for hop in range(1, sections):
        pl.semaphore_signal(
            barrier, inc=1, device_id={"section": lax.rem(me + hop, sections)}, device_id_type=MESH
        )
    pl.semaphore_wait(barrier, sections - 1)


def exchange(mine, slots, send_sems, recv_sems, sections):
    me = lax.axis_index("section")
    copies = []
    for hop in range(1, sections):
        copies.append(
            pltpu.make_async_remote_copy(
                src_ref=mine,
                dst_ref=slots.at[me],
                send_sem=send_sems.at[hop - 1],
                recv_sem=recv_sems.at[hop - 1],
                device_id={"section": lax.rem(me + hop, sections)},
                device_id_type=MESH,
            )
        )
    for copy in copies:
        copy.start()
    slots[me] = mine[...]
    for copy in copies:
        copy.wait()


def norm_rows(stream, gain, low, rows, step):
    def one(i, carry):
        at = tile(i, step)
        x = stream[at, :]
        r = lax.rsqrt(jnp.mean(x * x, axis=-1, keepdims=True) + epsilon)
        low[at, :] = (x * r * gain[...]).astype(BF16)
        return carry

    lax.fori_loop(0, rows // step, one, 0)


def norm_back(stream, gain, grad, through, out, gain_sum, rows, step):
    width = stream.shape[1]

    def one(i, total):
        at = tile(i, step)
        x = stream[at, :]
        r = lax.rsqrt(jnp.mean(x * x, axis=-1, keepdims=True) + epsilon)
        n = x * r
        g = grad[at, :]
        a = g * gain[...]
        out[at, :] = through[at, :] + r * (a - n * jnp.mean(a * n, axis=-1, keepdims=True))
        return total + jnp.sum((g * n).reshape(step // 8, 8, width), axis=0)

    gain_sum[...] = lax.fori_loop(0, rows // step, one, jnp.zeros((8, width), F32))


def fill_masks(lens, valid, keep, sizes, turned=False):
    section = lax.axis_index("section")
    group = lax.axis_index("batch")
    starts, totals = [], []
    for s in range(sizes.micro):
        total, begin = 0, []
        for d in range(lens.shape[0 if turned else 1]):
            row = group * sizes.micro + s
            length = lens[d, row] if turned else lens[row, d]
            begin.append(jnp.where(length > 0, total, -1))
            total = total + length
        starts.append(begin)
        totals.append(total)
    chunk_place = lax.broadcasted_iota(jnp.int32, (8, LANES), 0) * sizes.steps

    def one(j, carry):
        for s in range(sizes.micro):
            place = section * sizes.span + j + chunk_place
            true = place < totals[s]
            first = place == starts[s][0]
            for begin in starts[s][1:]:
                first = first | (place == begin)
            at = pl.ds(pl.multiple_of(j * sizes.group + s * 8, 8), 8)
            valid[at, :] = jnp.where(true, 1.0, 0.0)
            keep[at, :] = jnp.where(true & jnp.logical_not(first), 1.0, 0.0)
        return carry

    lax.fori_loop(0, sizes.steps, one, 0)


def scan_totals(first, second, sizes, reverse, prefix, chunk, mine):
    for s in range(sizes.micro):
        p = jnp.ones((1, sizes.hidden), F32)
        t = jnp.zeros((1, sizes.hidden), F32)
        for c in reversed(range(CHUNKS)) if reverse else range(CHUNKS):
            at = s * 8 + c
            prefix[0, at : at + 1, :] = p
            prefix[1, at : at + 1, :] = t
            pc = first[at : at + 1, :]
            t = pc * t + second[at : at + 1, :]
            p = p * pc
        mine[s : s + 1, :] = p
        mine[sizes.micro + s : sizes.micro + s + 1, :] = t


def scan_enter(slots, prefix, enter, sizes, reverse):
    me = lax.axis_index("section")
    for s in range(sizes.micro):
        a = jnp.zeros((1, sizes.hidden), F32)
        order = range(sizes.sections - 1, 0, -1) if reverse else range(sizes.sections - 1)
        for k in order:
            reached = k > me if reverse else k < me
            pk = slots[k, s : s + 1, :]
            tk = slots[k, sizes.micro + s : sizes.micro + s + 1, :]
            a = jnp.where(reached, pk * a + tk, a)
        at = slice(s * 8, s * 8 + 8)
        enter[at, :] = prefix[0, at, :] * a + prefix[1, at, :]


class Sizes:
    def __init__(self, micro, span, width, hidden, inner, sections):
        self.micro, self.span, self.width = micro, span, width
        self.hidden, self.inner, self.sections = hidden, inner, sections
        self.rows = micro * span
        self.steps = span // CHUNKS
        self.group = micro * CHUNKS


def forward_kernel(
    sizes,
    layer,
    stream,
    valid,
    keep,
    bias,
    mix_gain,
    mlp_gain,
    gate_hbm,
    out_hbm,
    up_hbm,
    down_hbm,
    next_stream,
    u,
    sf_out,
    si_out,
    zc_out,
    states,
    y1,
    v,
    p_out,
    gb,
    forget,
    pair_slots,
    gate_w,
    out_w,
    up_w,
    down_w,
    z,
    decay,
    drive,
    hb,
    chunk_p,
    chunk_t,
    prefix,
    enter,
    mine,
    weight_sems,
    send_sems,
    recv_sems,
):
    sz = sizes
    loads = [
        pltpu.make_async_copy(src.at[layer], dst, weight_sems.at[i])
        for i, (src, dst) in enumerate(
            ((gate_hbm, gate_w), (out_hbm, out_w), (up_hbm, up_w), (down_hbm, down_w))
        )
    ]
    for load in loads:
        load.start()
    greet_section(sz.sections)
    mine[...] = jnp.zeros_like(mine)
    norm_rows(stream, mix_gain, u, sz.rows, 64)
    loads[0].wait()
    forget[...] = jnp.zeros_like(forget)
    hw = 256

    def gate_tile(n, carry):
        for part in range(3):
            cols = pl.ds(pl.multiple_of(part * sz.hidden + n * hw, hw), hw)
            z[:, part * hw : (part + 1) * hw] = (
                jnp.dot(u[...], gate_w[:, cols], preferred_element_type=F32) + bias[:, cols]
            )

        def one(i, inner):
            at = tile(i, 64)
            for lane in range(hw // LANES):
                src = lambda part: z[
                    at, part * hw + lane * LANES : part * hw + (lane + 1) * LANES
                ]
                dst = pl.ds(pl.multiple_of(n * hw + lane * LANES, LANES), LANES)
                a = jnp.exp(jnp.minimum(-src(0), 86.0))
                b = jnp.exp(jnp.minimum(-src(1), 86.0))
                zc = src(2)
                fp, ip, _ = gate_weights(a, b)
                vm = valid[at, :]
                decay[at, dst] = fp * keep[at, :]
                drive[at, dst] = ip * zc * vm
                sf_out[at, dst] = a
                si_out[at, dst] = b
                zc_out[at, dst] = zc
                forget[...] += jnp.sum((fp * vm).reshape(8, 8, LANES), axis=0)
            return inner

        lax.fori_loop(0, sz.rows // 64, one, 0)
        return carry

    lax.fori_loop(0, sz.hidden // hw, gate_tile, 0)
    half = sz.hidden // 2
    for part in range(2):
        lanes = slice(part * half, (part + 1) * half)

        def totals(j, pair):
            at = tile(j, sz.group)
            d = decay[at, lanes]
            return pair[0] * d, pair[1] * d + drive[at, lanes]

        one = jnp.ones((sz.group, half), F32)
        pair = steps_of(sz.steps, 4, totals, (one, jnp.zeros_like(one)))
        chunk_p[:, lanes] = pair[0]
        chunk_t[:, lanes] = pair[1]
    scan_totals(chunk_p, chunk_t, sz, False, prefix, None, mine)
    exchange(mine, pair_slots, send_sems, recv_sems, sz.sections)
    scan_enter(pair_slots, prefix, enter, sz, False)
    states[0 : sz.group, :] = enter[...]
    for part in range(2):
        lanes = slice(part * half, (part + 1) * half)

        def walk(j, h):
            at = tile(j, sz.group)
            h = decay[at, lanes] * h + drive[at, lanes]
            states[tile(j + 1, sz.group), lanes] = h
            hb[at, lanes] = h.astype(BF16)
            return h

        steps_of(sz.steps, 4, walk, enter[:, lanes])
    loads[1].wait()

    def out_tile(n, carry):
        cols = tile(n, 256)
        y1[:, cols] = stream[:, cols] + jnp.dot(
            hb[...], out_w[:, cols], preferred_element_type=F32
        )
        return carry

    lax.fori_loop(0, sz.width // 256, out_tile, 0)
    norm_rows(y1, mlp_gain, v, sz.rows, 64)
    loads[2].wait()

    def up_tile(n, carry):
        cols = tile(n, 256)
        p_out[:, cols] = jnp.dot(v[...], up_w[:, cols], preferred_element_type=F32)

        def one(i, inner):
            at = tile(i, 64)
            p = p_out[at, cols]
            gb[at, cols] = (p * normal_below(p)).astype(BF16)
            return inner

        lax.fori_loop(0, sz.rows // 64, one, 0)
        return carry

    lax.fori_loop(0, sz.inner // 256, up_tile, 0)
    loads[3].wait()

    def down_tile(n, carry):
        cols = tile(n, 256)
        next_stream[:, cols] = y1[:, cols] + jnp.dot(
            gb[...], down_w[:, cols], preferred_element_type=F32
        )
        return carry

    lax.fori_loop(0, sz.width // 256, down_tile, 0)


def backward_kernel(
    sizes,
    layer,
    gx,
    stream,
    valid,
    keep,
    mix_gain,
    mlp_gain,
    u,
    sf_in,
    si_in,
    zc_in,
    states,
    y1,
    v,
    p_in,
    gb,
    pair_slots,
    gate_hbm,
    out_hbm,
    up_hbm,
    down_hbm,
    next_gx,
    gate_grad,
    out_grad,
    up_grad,
    down_grad,
    bias_sum,
    mix_sum,
    mlp_sum,
    gate_w,
    out_w,
    up_w,
    down_w,
    low,
    low_t,
    wide_t,
    hb,
    ga,
    gp,
    gz,
    grad,
    gy1,
    decay,
    chunk_p,
    chunk_t,
    prefix,
    enter,
    mine,
    slots,
    weight_sems,
    send_sems,
    recv_sems,
):
    sz = sizes
    loads = [
        pltpu.make_async_copy(src.at[layer], dst, weight_sems.at[i])
        for i, (src, dst) in enumerate(
            ((gate_hbm, gate_w), (out_hbm, out_w), (up_hbm, up_w), (down_hbm, down_w))
        )
    ]
    for load in reversed(loads):
        load.start()
    greet_section(sz.sections)
    mine[...] = jnp.zeros_like(mine)

    def cast(i, carry):
        at = tile(i, 64)
        low[at, :] = gx[at, :].astype(BF16)
        return carry

    lax.fori_loop(0, sz.rows // 64, cast, 0)
    low_t[...] = low[...].T

    def weight_grad(left_t, right, dst, step):
        def one(n, carry):
            cols = tile(n, step)
            dst[:, cols] = jnp.dot(left_t[...], right[:, cols], preferred_element_type=F32)
            return carry

        lax.fori_loop(0, right.shape[1] // step, one, 0)

    weight_grad(low_t, gb, down_grad, 256)
    loads[3].wait()

    def act_tile(n, carry):
        cols = tile(n, 256)
        ga[:, :256] = lax.dot_general(
            low[...], down_w[cols, :], (((1,), (1,)), ((), ())), preferred_element_type=F32
        )

        def one(i, inner):
            at = tile(i, 64)
            p = p_in[at, cols]
            slope = normal_below(p) + ROOT_TAU * p * jnp.exp(-0.5 * p * p)
            gp[at, cols] = (ga[at, :256] * slope).astype(BF16)
            return inner

        lax.fori_loop(0, sz.rows // 64, one, 0)
        return carry

    lax.fori_loop(0, sz.inner // 256, act_tile, 0)
    wide_t[...] = v[...].T
    weight_grad(wide_t, gp, up_grad, 256)
    loads[2].wait()

    def contract(left, weight, dst, step):
        def one(n, carry):
            cols = tile(n, step)
            dst[:, cols] = lax.dot_general(
                left[...], weight[cols, :], (((1,), (1,)), ((), ())), preferred_element_type=F32
            )
            return carry

        lax.fori_loop(0, weight.shape[0] // step, one, 0)

    contract(gp, up_w, grad, 256)
    norm_back(y1, mlp_gain, grad, gx, gy1, mlp_sum, sz.rows, 64)

    def cast_more(i, carry):
        at = tile(i, 64)
        low[at, :] = gy1[at, :].astype(BF16)
        return carry

    lax.fori_loop(0, sz.rows // 64, cast_more, 0)

    def cast_state(i, carry):
        hb[tile(i, sz.group), :] = states[tile(i + 1, sz.group), :].astype(BF16)
        return carry

    lax.fori_loop(0, sz.steps, cast_state, 0)
    low_t[...] = low[...].T
    weight_grad(low_t, hb, out_grad, 256)
    loads[1].wait()
    contract(low, out_w, ga, 256)
    half = sz.hidden // 2
    for part in range(2):
        lanes = slice(part * half, (part + 1) * half)

        def totals(i, pair):
            at = tile(sz.steps - 1 - i, sz.group)
            mask = jnp.concatenate([keep[at, :]] * (half // LANES), axis=1)
            d = gate_weights(sf_in[at, lanes], si_in[at, lanes])[0] * mask
            decay[at, lanes] = d
            return pair[0] * d, d * (ga[at, lanes] + pair[1])

        pair = lax.fori_loop(
            0,
            sz.steps,
            totals,
            (jnp.ones((sz.group, half), F32), jnp.zeros((sz.group, half), F32)),
        )
        chunk_p[:, lanes] = pair[0]
        chunk_t[:, lanes] = pair[1]
    scan_totals(chunk_p, chunk_t, sz, True, prefix, None, mine)
    exchange(mine, slots, send_sems, recv_sems, sz.sections)
    scan_enter(slots, prefix, enter, sz, True)

    def gate_lane(n, carry):
        lanes = tile(n, LANES)

        def walk(i, kept):
            m, bf, bi, bc = kept
            j = sz.steps - 1 - i
            at = tile(j, sz.group)
            d = decay[at, lanes]
            q = ga[at, lanes] + m
            a = sf_in[at, lanes]
            b = si_in[at, lanes]
            zc = zc_in[at, lanes]
            vm = valid[at, :]
            fp, ip, inv = gate_weights(a, b)
            gf = q * (states[at, lanes] * keep[at, :] - zc * vm)
            gzf = (gf * (a * inv) * fp).astype(BF16)
            gzi = (-gf * (b * inv) * ip).astype(BF16)
            gzc = (q * vm * ip).astype(BF16)
            gz[at, lanes] = gzf
            gz[at, pl.ds(pl.multiple_of(sz.hidden + n * LANES, LANES), LANES)] = gzi
            gz[at, pl.ds(pl.multiple_of(2 * sz.hidden + n * LANES, LANES), LANES)] = gzc
            return (
                d * q,
                bf + gzf.astype(F32),
                bi + gzi.astype(F32),
                bc + gzc.astype(F32),
            )

        zero = jnp.zeros((sz.group, LANES), F32)
        _, bf, bi, bc = lax.fori_loop(0, sz.steps, walk, (enter[:, lanes], zero, zero, zero))
        for part, total in enumerate((bf, bi, bc)):
            where = pl.ds(pl.multiple_of(part * sz.hidden + n * LANES, LANES), LANES)
            bias_sum[:, where] = jnp.sum(total.reshape(sz.group // 8, 8, LANES), axis=0)
        return carry

    lax.fori_loop(0, sz.hidden // LANES, gate_lane, 0)
    wide_t[...] = u[...].T
    weight_grad(wide_t, gz, gate_grad, 256)
    loads[0].wait()
    contract(gz, gate_w, grad, 256)
    norm_back(stream, mix_gain, grad, gy1, next_gx, mix_sum, sz.rows, 64)


VMEM = pl.BlockSpec(memory_space=pltpu.VMEM)
ANY = pl.BlockSpec(memory_space=pl.ANY)
LIMIT = 62 * 2**20


def shape(*dims, kind=F32):
    return jax.ShapeDtypeStruct(dims, kind)


def exchange_scratch(sz):
    return [
        pltpu.SemaphoreType.DMA((4,)),
        pltpu.SemaphoreType.DMA((sz.sections - 1,)),
        pltpu.SemaphoreType.DMA((sz.sections - 1,)),
    ]


def weight_scratch(sz):
    return [
        pltpu.VMEM((sz.width, 3 * sz.hidden), BF16),
        pltpu.VMEM((sz.hidden, sz.width), BF16),
        pltpu.VMEM((sz.width, sz.inner), BF16),
        pltpu.VMEM((sz.inner, sz.width), BF16),
    ]


def scan_scratch(sz):
    return [
        pltpu.VMEM((sz.group, sz.hidden), F32),
        pltpu.VMEM((sz.group, sz.hidden), F32),
        pltpu.VMEM((2, sz.group, sz.hidden), F32),
        pltpu.VMEM((sz.group, sz.hidden), F32),
        pltpu.VMEM((8, sz.hidden), F32),
    ]


def run_forward(sz, layer, stream, masks, bias, mix_gain, mlp_gain, weights):
    r, d, h, f = sz.rows, sz.width, sz.hidden, sz.inner
    return pl.pallas_call(
        functools.partial(forward_kernel, sz, layer),
        out_shape=(
            shape(r, d),
            shape(r, d, kind=BF16),
            shape(r, h),
            shape(r, h),
            shape(r, h),
            shape(r + sz.group, h),
            shape(r, d),
            shape(r, d, kind=BF16),
            shape(r, f),
            shape(r, f, kind=BF16),
            shape(8, LANES),
            shape(sz.sections, 8, h),
        ),
        in_specs=[VMEM] * 6 + [ANY] * 4,
        out_specs=[VMEM] * 12,
        scratch_shapes=weight_scratch(sz)
        + [
            pltpu.VMEM((r, 3 * 256), F32),
            pltpu.VMEM((r, h), F32),
            pltpu.VMEM((r, h), F32),
            pltpu.VMEM((r, h), BF16),
        ]
        + scan_scratch(sz)
        + exchange_scratch(sz),
        compiler_params=pltpu.CompilerParams(
            collective_id=layer, has_side_effects=True, vmem_limit_bytes=LIMIT
        ),
        name=f"forward_{layer}",
    )(stream, *masks, bias, mix_gain, mlp_gain, *weights)


def run_backward(sz, layer, gx, stream, masks, mix_gain, mlp_gain, saved, weights):
    r, d, h, f = sz.rows, sz.width, sz.hidden, sz.inner
    return pl.pallas_call(
        functools.partial(backward_kernel, sz, layer),
        out_shape=(
            shape(r, d),
            shape(d, 3 * h),
            shape(d, h),
            shape(d, f),
            shape(d, f),
            shape(8, 3 * h),
            shape(8, d),
            shape(8, d),
        ),
        in_specs=[VMEM] * 16 + [ANY] * 4,
        out_specs=[VMEM] * 8,
        scratch_shapes=weight_scratch(sz)
        + [
            pltpu.VMEM((r, d), BF16),
            pltpu.VMEM((d, r), BF16),
            pltpu.VMEM((d, r), BF16),
            pltpu.VMEM((r, h), BF16),
            pltpu.VMEM((r, h), F32),
            pltpu.VMEM((r, f), BF16),
            pltpu.VMEM((r, 3 * h), BF16),
            pltpu.VMEM((r, d), F32),
            pltpu.VMEM((r, d), F32),
            pltpu.VMEM((r, h), F32),
        ]
        + scan_scratch(sz)
        + [pltpu.VMEM((sz.sections, 8, h), F32)]
        + exchange_scratch(sz),
        compiler_params=pltpu.CompilerParams(
            collective_id=2 + layer, has_side_effects=True, vmem_limit_bytes=LIMIT
        ),
        name=f"backward_{layer}",
    )(gx, stream, *masks, mix_gain, mlp_gain, *saved, *weights)


BLOCK = 64
HELD = 3
RINGS = (4, 5, 5, 5, 5)
SENDS = 8
STAGES = 5
WINDOW = 4
SMALL = 1280


class Units:
    def __init__(self, count, refs):
        self.count = count
        self.__dict__.update(vars(refs))
        self.arrived = [getattr(refs, f"arrived{stage}") for stage in range(STAGES)]
        section, batch = lax.axis_index("section"), lax.axis_index("batch")
        core, x = section % 2, section // 2
        y, za, zb = batch % 2, (batch // 2) % 2, batch // 4
        self.core = core
        self.bits = ((x, za, y, zb), (y, za, x, zb))
        self.names = (("x", "za", "y", "zb"), ("y", "za", "x", "zb"))
        self.partner = {
            "core": {"section": section + 1 - 2 * core},
            "x": {"section": section + 2 - 4 * x},
            "y": {"batch": batch + 1 - 2 * y},
            "za": {"batch": batch + 2 - 4 * za},
            "zb": {"batch": batch + 4 - 8 * zb},
        }
        self.now = 0.0
        self.links = ("core", "x", "y", "z")
        self.free_at = dict.fromkeys(self.links, 0.0)
        self.flying = dict.fromkeys(self.links, 0)
        self.queues = {link: [] for link in self.links}
        self.ready = {}
        self.summed = set()
        self.copies = {}
        self.small_left = None

    def greet(self):
        barrier = pltpu.get_barrier_semaphore()
        section = lax.axis_index("section")
        others = [self.partner["y"], self.partner["za"], self.partner["zb"]]
        others += [{"section": lax.rem(section + hop, 4)} for hop in range(1, 4)]
        for other in others:
            pl.semaphore_signal(barrier, inc=1, device_id=other, device_id_type=MESH)
        pl.semaphore_wait(barrier, len(others))

    def name(self, stage, half):
        return "core" if stage == 0 else self.names[half][stage - 1]

    def link(self, stage, half):
        name = self.name(stage, half)
        return "z" if name[0] == "z" else name

    def arrival(self, unit, stage, half):
        ref = self.arrived[stage].at[unit % RINGS[stage]]
        return ref if stage == 0 else ref.at[half]

    def copy(self, unit, stage, half):
        at = 0 if stage == 0 else 2 * stage - 1 + half
        if stage == 0:
            src = self.held.at[unit % HELD, 1 - self.core]
        else:
            count = 16 >> stage
            src = self.arrived[stage - 1].at[unit % RINGS[stage - 1], half]
            src = src.at[pl.ds((1 - self.bits[half][stage - 1]) * count, count)]
        return pltpu.make_async_remote_copy(
            src_ref=src,
            dst_ref=self.arrival(unit, stage, half),
            send_sem=self.send_sems.at[unit % SENDS, at],
            recv_sem=self.recv_sems.at[unit % RINGS[stage], at],
            device_id=self.partner[self.name(stage, half)],
            device_id_type=MESH,
        )

    def has_place(self, unit, stage, half):
        before = unit - RINGS[stage]
        if before < 0:
            return True
        if stage == 0:
            return (before, 1, 0) in self.summed and (before, 1, 1) in self.summed
        return (before, min(stage + 1, STAGES - 1), half) in self.summed

    def credit(self, unit, stage, half):
        if unit + RINGS[stage] < self.count:
            pl.semaphore_signal(
                self.credits.at[0 if stage == 0 else 2 * stage - 1 + half],
                inc=1,
                device_id=self.partner[self.name(stage, half)],
                device_id_type=MESH,
            )

    def pump(self):
        for link, queue in self.queues.items():
            while self.flying[link] < WINDOW:
                key = next((key for key in queue if self.has_place(*key)), None)
                if key is None:
                    break
                queue.remove(key)
                self.flying[link] += 1
                unit, stage, half = key
                if unit >= RINGS[stage]:
                    at = 0 if stage == 0 else 2 * stage - 1 + half
                    pl.semaphore_wait(self.credits.at[at], 1)
                self.copies[key] = self.copy(*key)
                self.copies[key].start()
                size = (32 if stage == 0 else 16 >> stage) * BLOCK * LANES * 4
                rate = 250e3 if link == "core" else 45e3
                self.free_at[link] = max(self.now, self.free_at[link]) + size / rate
                self.ready[key] = self.free_at[link] + 1.5

    def push(self, unit, stage, half):
        self.queues[self.link(stage, half)].append((unit, stage, half))
        self.pump()

    def produced(self, *which):
        for unit in which:
            self.push(unit, 0, 0)

    def add(self, dst, src, count):
        turn = min(count, 4)

        def one(i, carry):
            for k in range(turn):
                dst[i * turn + k] += src[i * turn + k]
            return carry

        if count == turn:
            one(0, 0)
        else:
            lax.fori_loop(0, count // turn, one, 0)

    def step(self, unit, stage, half):
        key = (unit, stage, half)
        del self.ready[key]
        assert unit == 0 or (unit - 1, stage, half) in self.summed
        self.copies[key].wait_recv()
        here = self.arrival(unit, stage, half)
        if stage == 0:
            for h in range(2):
                self.add(here.at[h], self.held.at[unit % HELD, self.core, h], 16)
        else:
            count = 16 >> stage
            before = self.arrived[stage - 1].at[unit % RINGS[stage - 1], half]
            self.add(here, before.at[pl.ds(self.bits[half][stage - 1] * count, count)], count)
            self.copies.pop(key).wait_send()
        self.summed.add(key)
        self.flying[self.link(stage, half)] -= 1
        self.now += 0.25
        if stage > 1 or (unit, 1, 1 - half) in self.summed:
            if stage > 0:
                self.credit(unit, stage - 1, half if stage > 1 else 0)
        if stage == 0:
            for h in range(2):
                self.push(unit, 1, h)
        elif stage < STAGES - 1:
            self.push(unit, stage + 1, half)
        else:
            self.finish(unit, half, here[0])
            self.credit(unit, stage, half)
        self.pump()

    def finish(self, unit, half, block):
        layer, k = self.count // 8 - 1 - unit // 8, unit % 8
        if k < 2 or k == 4:
            ref, at = (self.down_weight_grad, k) if k < 2 else (self.out_weight_grad, 0)
            ref[layer, :, at * 256 + half * 128 : at * 256 + half * 128 + 128] = block
        else:
            ref, at = (self.up_weight_grad, k - 2) if k < 4 else (self.gate_weight_grad, k - 5)
            rows = slice(half * BLOCK, half * BLOCK + BLOCK)
            ref[layer, rows, at * LANES : at * LANES + LANES] = block

    def small_copy(self, stage):
        name = ("core", "x", "y", "za", "zb")[stage]
        return pltpu.make_async_remote_copy(
            src_ref=self.small.at[stage],
            dst_ref=self.small_arrived.at[stage],
            send_sem=self.small_send.at[stage],
            recv_sem=self.small_recv.at[stage],
            device_id=self.partner[name],
            device_id_type=MESH,
        )

    def small_start(self):
        self.small_left = 0
        self.small_copies = [self.small_copy(0)]
        self.small_copies[0].start()
        self.small_ready = self.now + 3.0

    def small_step(self):
        stage = self.small_left
        self.small_copies[stage].wait_recv()
        self.small[stage + 1] = self.small[stage] + self.small_arrived[stage]
        self.small_left += 1
        if self.small_left < STAGES:
            self.small_copies.append(self.small_copy(self.small_left))
            self.small_copies[-1].start()
            self.small_ready = self.now + 3.0
        else:
            for copy in self.small_copies:
                copy.wait_send()

    def open(self, unit, stage, half):
        halves = range(2) if stage == 0 else (half,)
        before = unit - RING
        return (
            before < 0
            or stage == STAGES - 1
            or all((before, stage + 1, h) in self.consumed for h in halves)
        )

    def next(self):
        best = min(self.ready.items(), key=lambda item: (item[1], item[0]), default=None)
        small = self.small_left is not None and self.small_left < STAGES
        if small and (best is None or self.small_ready <= best[1]):
            return self.small_ready, None
        return (best[1], best[0]) if best else None

    def take(self, item):
        self.now = max(self.now, item[0])
        if item[1] is None:
            self.small_step()
        else:
            self.step(*item[1])

    def passed(self, us):
        self.now += us
        while (item := self.next()) and item[0] <= self.now:
            self.take(item)

    def room(self, unit):
        before = (unit - HELD, 0, 0)
        while unit >= HELD and before not in self.summed:
            self.take(self.next())
        if before in self.copies:
            self.copies.pop(before).wait_send()

    def drain(self):
        while item := self.next():
            self.take(item)
        for key in list(self.copies):
            self.copies.pop(key).wait_send()


def place(half, x, y, za, zb):
    return (x * 8 + za * 4 + y * 2 + zb) if half == 0 else (y * 8 + za * 4 + x * 2 + zb)


def strided(start, steps):
    return pl.ds(start, CHUNKS, stride=steps)


def whole_step(sz, layers, names, *args):
    r = types.SimpleNamespace(**dict(zip(names, args)))
    units = Units(8 * layers, r)
    valid, keep, low, low_t, wide_t = r.valid, r.keep, r.low, r.low_t, r.wide_t
    hb, ga, gz, grad, gy1, gx = r.hb, r.ga, r.gz, r.grad, r.gy1, r.gx
    gp = gz.at[:, : sz.inner]
    decay, enter, prefix, mine = r.decay, r.enter, r.prefix, r.mine
    small, held = r.small, r.held
    natural = r.natural
    last = layers - 1
    half = sz.hidden // 2
    drive = r.p.at[:, : sz.hidden]
    homes = dict(gate_w=r.gate_hbm, out_w=r.out_hbm, up_w=r.up_hbm, down_w=r.down_hbm)
    homes.update(u=r.u_save, a=r.a_save, b=r.b_save, zc=r.zc_save, states=r.states_save)
    homes.update(y1=r.y1_save, v=r.v_save, p=r.p_save, gb=r.gb_save, stream=r.stream_save)
    keys = types.SimpleNamespace(**{name: name for name in homes})
    index_of = {name: i for i, name in enumerate(homes)}
    loads, saves = {}, {}

    def load(layer, name):
        copy = pltpu.make_async_copy(
            homes[name].at[layer], getattr(r, name), r.load_sems.at[index_of[name]]
        )
        copy.start()
        loads[name] = copy

    def need(*wanted):
        for name in wanted:
            if name in loads:
                loads.pop(name).wait()

    def save(layer, name, ref=None):
        if layer < last:
            src = getattr(r, name) if ref is None else ref
            copy = pltpu.make_async_copy(
                src, homes[name].at[layer], r.save_sems.at[index_of[name]]
            )
            copy.start()
            saves[name] = copy

    def settled(*which):
        for name in which:
            if name in saves:
                saves.pop(name).wait()

    def over(count, one):
        def each(i, carry):
            one(i)
            return carry

        lax.fori_loop(0, count, each, 0)

    act_load = pltpu.make_async_copy(r.activations, hb.at[:, : sz.width], r.in_sems.at[0])
    cot_load = pltpu.make_async_copy(r.cotangent, wide_t, r.in_sems.at[1])
    len_load = pltpu.make_async_copy(r.lengths, r.lens, r.in_sems.at[2])
    len_load.start()
    act_load.start()
    for name in (keys.gate_w, keys.out_w, keys.up_w, keys.down_w):
        load(0, name)
    cot_load.start()
    units.greet()
    mine[...] = jnp.zeros_like(mine)
    small[0] = jnp.zeros((8, SMALL), F32)
    len_load.wait()
    fill_masks(r.lens, valid, keep, sz, True)

    def to_steps(src, put):
        def cast(i):
            at = tile(i, 64)
            for k in range(sz.width // LANES):
                natural[k, at, :] = src[at, k * LANES : (k + 1) * LANES].astype(F32)

        over(sz.rows // 64, cast)

        def gather(j):
            for k in range(sz.width // LANES):
                parts = [
                    natural[k, strided(s * sz.span + j, sz.steps), :] for s in range(sz.micro)
                ]
                put(tile(j, sz.group), slice(k * LANES, (k + 1) * LANES), jnp.concatenate(parts, axis=0))

        over(sz.steps, gather)

    def from_steps(src, dst, sem):
        def scatter(j):
            for k in range(sz.width // LANES):
                value = src[tile(j, sz.group), k * LANES : (k + 1) * LANES]
                for s in range(sz.micro):
                    natural[k, strided(s * sz.span + j, sz.steps), :] = value[s * 8 : s * 8 + 8]

        over(sz.steps, scatter)
        copies = []
        for k in range(sz.width // LANES):
            lanes = slice(k * LANES, (k + 1) * LANES)
            copies.append(pltpu.make_async_copy(natural.at[k], dst.at[:, lanes], sem.at[k]))
            copies[-1].start()
        return copies

    act_load.wait()

    def put_gx(at, lanes, value):
        gx[at, lanes] = value

    to_steps(hb.at[:, : sz.width], put_gx)

    def exchange_start(way, layer):
        slots = r.slots.at[way, layer]
        me = lax.axis_index("section")
        copies = []
        for hop in range(1, sz.sections):
            copies.append(
                pltpu.make_async_remote_copy(
                    src_ref=mine,
                    dst_ref=slots.at[me],
                    send_sem=r.pair_send.at[way, layer, hop - 1],
                    recv_sem=r.pair_recv.at[way, layer, hop - 1],
                    device_id={"section": lax.rem(me + hop, sz.sections)},
                    device_id_type=MESH,
                )
            )
        for copy in copies:
            copy.start()
        slots[me] = mine[...]
        return slots, copies

    def exchange_end(slots, copies, reverse):
        for copy in copies:
            copy.wait()
        scan_enter(slots, prefix, enter, sz, reverse)

    def keep_cotangent():
        cot_load.wait()

        def put_low(at, lanes, value):
            low[at, lanes] = value.astype(BF16)

        to_steps(wide_t, put_low)
        low_t[...] = low[...].T

    def forward(layer):
        stream = r.stream if layer > 0 else gx
        settled(keys.u)
        norm_rows(stream, r.mix_gain.at[layer : layer + 1], r.u, sz.rows, 64)
        save(layer, keys.u)
        if layer == 0:
            save(layer, keys.stream, gx)
        need(keys.gate_w)
        settled(keys.a, keys.b, keys.zc, keys.p)
        hw = 256
        bias = r.gate_bias

        def gate_tile(n, forget):
            for part in range(3):
                cols = pl.ds(pl.multiple_of(part * sz.hidden + n * hw, hw), hw)
                ga[:, part * hw : (part + 1) * hw] = (
                    jnp.dot(r.u[...], r.gate_w[:, cols], preferred_element_type=F32)
                    + bias[layer : layer + 1, cols]
                )
            return lax.fori_loop(0, sz.rows // 64, functools.partial(gate_rows, n), forget)

        def gate_rows(n, i, forget):
            at = tile(i, 64)
            vm, km = valid[at, :], keep[at, :]
            for lane in range(hw // LANES):
                zf, zi, zc = (
                    ga[at, part * hw + lane * LANES : part * hw + (lane + 1) * LANES]
                    for part in range(3)
                )
                dst = pl.ds(pl.multiple_of(n * hw + lane * LANES, LANES), LANES)
                a = jnp.exp(jnp.minimum(-zf, 86.0))
                b = jnp.exp(jnp.minimum(-zi, 86.0))
                fp, ip, _ = gate_weights(a, b)
                decay[at, dst] = fp * km
                drive[at, dst] = ip * zc * vm
                r.a[at, dst] = a
                r.b[at, dst] = b
                r.zc[at, dst] = zc
                forget = forget + jnp.sum((fp * vm).reshape(8, 8, LANES), axis=0)
            return forget

        forget = lax.fori_loop(0, sz.hidden // hw, gate_tile, jnp.zeros((8, LANES), F32))
        small[0, layer * 4 : layer * 4 + 1, sz.hidden : sz.hidden + LANES] = jnp.sum(
            forget, axis=0, keepdims=True
        )
        for name in (keys.a, keys.b, keys.zc):
            save(layer, name)
        if layer < last:
            load(layer + 1, keys.gate_w)
        for part in range(2):
            lanes = slice(part * half, (part + 1) * half)

            def totals(j, pair):
                at = tile(j, sz.group)
                d = decay[at, lanes]
                return pair[0] * d, pair[1] * d + drive[at, lanes]

            one = jnp.ones((sz.group, half), F32)
            pair = steps_of(sz.steps, 2, totals, (one, jnp.zeros_like(one)))
            r.chunk_p[:, lanes] = pair[0]
            r.chunk_t[:, lanes] = pair[1]
        scan_totals(r.chunk_p, r.chunk_t, sz, False, prefix, None, mine)
        flight = exchange_start(0, layer)
        settled(keys.states, keys.y1, keys.v, keys.gb, keys.stream)
        exchange_end(*flight, False)
        states = r.states
        states[0 : sz.group, :] = enter[...]
        for part in range(2):
            lanes = slice(part * half, (part + 1) * half)

            def walk(j, h):
                at = tile(j, sz.group)
                h = decay[at, lanes] * h + drive[at, lanes]
                states[tile(j + 1, sz.group), lanes] = h
                hb[at, lanes] = h.astype(BF16)
                return h

            steps_of(sz.steps, 4, walk, enter[:, lanes])
        save(layer, keys.states)
        need(keys.out_w)

        def out_tile(n):
            cols = tile(n, 256)
            r.y1[:, cols] = stream[:, cols] + jnp.dot(
                hb[...], r.out_w[:, cols], preferred_element_type=F32
            )

        over(sz.width // 256, out_tile)
        save(layer, keys.y1)
        if layer < last:
            load(layer + 1, keys.out_w)
        norm_rows(r.y1, r.mlp_gain.at[layer : layer + 1], r.v, sz.rows, 64)
        save(layer, keys.v)
        need(keys.up_w)

        def up_tile(n):
            cols = tile(n, 256)
            r.p[:, cols] = jnp.dot(r.v[...], r.up_w[:, cols], preferred_element_type=F32)

            def one(i):
                at = tile(i, 64)
                p = r.p[at, cols]
                r.gb[at, cols] = (p * normal_below(p)).astype(BF16)

            over(sz.rows // 64, one)

        over(sz.inner // 256, up_tile)
        save(layer, keys.p)
        save(layer, keys.gb)
        if layer < last:
            load(layer + 1, keys.up_w)
        else:
            down_grad(layer, 0)
        need(keys.down_w)
        out = r.stream if layer < last else gy1

        def down_tile(n):
            cols = tile(n, 256)
            out[:, cols] = r.y1[:, cols] + jnp.dot(
                r.gb[...], r.down_w[:, cols], preferred_element_type=F32
            )

        over(sz.width // 256, down_tile)
        if layer < last:
            load(layer + 1, keys.down_w)

    def down_grad(layer, unit):
        for k in range(2):
            units.room(unit + k)

        def one(n):
            s, t = n // 2, n % 2
            value = jnp.dot(low_t[...], r.gb[:, tile(n, 256)], preferred_element_type=F32)
            for b in range(8):
                for h in range(2):
                    at = place(h, s // 2, b % 2, (b // 2) % 2, b // 4)
                    held[(unit + t) % HELD, s % 2, h, at] = value[
                        b * 64 : b * 64 + 64, h * 128 : h * 128 + 128
                    ]

        over(8, one)
        units.produced(unit, unit + 1)
        units.passed(3)

    def cast(src, dst):
        def one(i):
            at = tile(i, 64)
            dst[at, :] = src[at, :].astype(dst.dtype)

        over(sz.rows // 64, one)

    def contract(left, weight, dst, count):
        def one(n):
            cols = tile(n, 256)
            dst[:, cols] = lax.dot_general(
                left[...], weight[cols, :], (((1,), (1,)), ((), ())), preferred_element_type=F32
            )

        over(count // 256, one)

    def backward(layer, unit):
        def freed(*which):
            if layer > 0:
                for name in which:
                    load(layer - 1, name)

        if layer < last:
            cast(gx, low)
            low_t[...] = low[...].T
            need(keys.gb)
            down_grad(layer, unit)
        freed(keys.gb)
        unit += 2
        need(keys.down_w, keys.p)

        def act_tile(n):
            cols = tile(n, 256)
            ga[:, :256] = lax.dot_general(
                low[...], r.down_w[cols, :], (((1,), (1,)), ((), ())), preferred_element_type=F32
            )

            def one(i):
                at = tile(i, 64)
                p = r.p[at, cols]
                slope = normal_below(p) + ROOT_TAU * p * jnp.exp(-0.5 * p * p)
                gp[at, cols] = (ga[at, :256] * slope).astype(BF16)

            over(sz.rows // 64, one)

        for quarter in range(4):
            over(sz.inner // 1024, lambda n: act_tile(n + quarter * (sz.inner // 1024)))
            units.passed(1.5)
        freed(keys.down_w, keys.p)
        need(keys.v)
        wide_t[...] = r.v[...].T
        freed(keys.v)
        for k in range(2):
            units.room(unit + k)

        def up_grad(b):
            value = jnp.dot(wide_t[...], gp[:, tile(b, 256)], preferred_element_type=F32)
            for s in range(4):
                for h in range(2):
                    at = place(h, s // 2, b % 2, (b // 2) % 2, b // 4)
                    for t in range(2):
                        held[(unit + t) % HELD, s % 2, h, at] = value[
                            s * 128 + h * 64 : s * 128 + h * 64 + 64, t * 128 : t * 128 + 128
                        ]

        over(8, up_grad)
        units.produced(unit, unit + 1)
        unit += 2
        units.passed(3)
        need(keys.up_w, keys.y1)
        contract(gp, r.up_w, grad, sz.width)
        freed(keys.up_w)
        units.passed(2)
        norm_back(r.y1, r.mlp_gain.at[layer : layer + 1], grad, gx, gy1, r.mlp_sum, sz.rows, 64)
        freed(keys.y1)
        cast(gy1, low)
        need(keys.states)

        def cast_state(i):
            hb[tile(i, sz.group), :] = r.states[tile(i + 1, sz.group), :].astype(BF16)

        if layer < last:
            over(sz.steps, cast_state)
        low_t[...] = low[...].T
        units.room(unit)
        units.passed(2)

        def out_grad(s):
            value = jnp.dot(low_t[...], hb[:, tile(s, 256)], preferred_element_type=F32)
            for b in range(8):
                for h in range(2):
                    at = place(h, s // 2, b % 2, (b // 2) % 2, b // 4)
                    held[unit % HELD, s % 2, h, at] = value[
                        b * 64 : b * 64 + 64, h * 128 : h * 128 + 128
                    ]

        over(4, out_grad)
        units.produced(unit)
        unit += 1
        units.passed(1.5)
        need(keys.out_w, keys.a, keys.b)
        contract(low, r.out_w, ga, sz.hidden)
        freed(keys.out_w)
        units.passed(1.5)
        for part in range(2):
            lanes = slice(part * half, (part + 1) * half)

            def totals(j, pair):
                at = tile(j, sz.group)
                mask = jnp.concatenate([keep[at, :]] * (half // LANES), axis=1)
                d = gate_weights(r.a[at, lanes], r.b[at, lanes])[0] * mask
                decay[at, lanes] = d
                return pair[0] * d, d * (ga[at, lanes] + pair[1])

            one = jnp.ones((sz.group, half), F32)
            pair = steps_of(sz.steps, 2, totals, (one, jnp.zeros_like(one)), reverse=True)
            r.chunk_p[:, lanes] = pair[0]
            r.chunk_t[:, lanes] = pair[1]
        scan_totals(r.chunk_p, r.chunk_t, sz, True, prefix, None, mine)
        flight = exchange_start(1, layer)
        units.passed(3)
        exchange_end(*flight, True)
        need(keys.zc)

        def gate_lanes(n):
            wide = 2 * LANES
            lanes = tile(n, wide)

            def walk(j, kept):
                m, bf, bi, bc = kept
                at = tile(j, sz.group)
                d = decay[at, lanes]
                q = ga[at, lanes] + m
                a, b, zc = r.a[at, lanes], r.b[at, lanes], r.zc[at, lanes]
                vm = jnp.concatenate([valid[at, :]] * 2, axis=1)
                km = jnp.concatenate([keep[at, :]] * 2, axis=1)
                fp, ip, inv = gate_weights(a, b)
                gf = q * (r.states[at, lanes] * km - zc * vm)
                parts = (
                    (gf * (a * inv) * fp).astype(BF16),
                    (-gf * (b * inv) * ip).astype(BF16),
                    (q * vm * ip).astype(BF16),
                )
                for part, value in enumerate(parts):
                    gz[at, pl.ds(pl.multiple_of(part * sz.hidden + n * wide, wide), wide)] = value
                return (d * q,) + tuple(
                    a + value.astype(F32) for a, value in zip((bf, bi, bc), parts)
                )

            zero = jnp.zeros((sz.group, wide), F32)
            _, *sums = steps_of(
                sz.steps, 4, walk, (enter[:, lanes], zero, zero, zero), reverse=True
            )
            for part, total in enumerate(sums):
                small[0, layer * 4 + part : layer * 4 + part + 1, lanes] = jnp.sum(
                    total, axis=0, keepdims=True
                )

        turns = sz.hidden // LANES // 4
        over(turns, gate_lanes)
        units.passed(2)
        over(turns, lambda n: gate_lanes(n + turns))
        freed(keys.a, keys.b, keys.zc, keys.states)
        units.passed(2)
        need(keys.u)
        wide_t[...] = r.u[...].T
        freed(keys.u)
        for k in range(2):
            units.room(unit + k)

        def gate_grad(b):
            cols = pl.ds(pl.multiple_of(b * 384, 128), 256)
            value = jnp.dot(wide_t[...], gz[:, cols], preferred_element_type=F32)
            for s in range(4):
                for h in range(2):
                    at = place(h, s // 2, b % 2, (b // 2) % 2, b // 4)
                    for t in range(2):
                        held[(unit + t) % HELD, s % 2, h, at] = value[
                            s * 128 + h * 64 : s * 128 + h * 64 + 64, t * 128 : t * 128 + 128
                        ]

        over(8, gate_grad)
        units.produced(unit, unit + 1)
        unit += 2
        units.passed(3)
        units.room(unit)

        def gate_rest(z):
            right = jnp.concatenate(
                [
                    gz[:, pl.ds(pl.multiple_of((2 * z + y) * 384 + 256, 128), 128)]
                    for y in range(2)
                ],
                axis=1,
            )
            value = jnp.dot(wide_t[...], right, preferred_element_type=F32)
            for s in range(4):
                for h in range(2):
                    for y in range(2):
                        at = place(h, s // 2, y, z % 2, z // 2)
                        held[unit % HELD, s % 2, h, at] = value[
                            s * 128 + h * 64 : s * 128 + h * 64 + 64, y * 128 : y * 128 + 128
                        ]

        over(4, gate_rest)
        units.produced(unit)
        unit += 1
        units.passed(1.5)
        need(keys.gate_w, keys.stream)
        contract(gz, r.gate_w, grad, sz.width)
        freed(keys.gate_w)
        units.passed(2.5)
        norm_back(r.stream, r.mix_gain.at[layer : layer + 1], grad, gy1, gx, r.mix_sum, sz.rows, 64)
        freed(keys.stream)
        row = slice(layer * 4 + 3, layer * 4 + 4)
        small[0, row, : sz.width] = jnp.sum(r.mix_sum[...], axis=0, keepdims=True)
        small[0, row, sz.width : 2 * sz.width] = jnp.sum(r.mlp_sum[...], axis=0, keepdims=True)
        units.passed(1.5)

    forward(0)
    keep_cotangent()
    for layer in range(1, layers):
        forward(layer)
    out_copies = from_steps(gy1, r.layer_out, r.out_sems)
    cast(low, gx)
    units.passed(2)
    for index, layer in enumerate(reversed(range(layers))):
        backward(layer, 8 * index)
    units.small_start()
    for copy in out_copies:
        copy.wait()
    out_copies = from_steps(gx, r.input_grad, r.out_sems)
    units.passed(1)
    units.drain()
    for copy in out_copies:
        copy.wait()
    total = small[STAGES]
    count = jnp.int32(0)
    for s in range(r.lens.shape[0]):
        for d in range(r.lens.shape[1]):
            count = count + r.lens[s, d]
    scale = 1.0 / (count.astype(F32) * sz.hidden)
    for layer in range(layers):
        for part in range(3):
            r.gate_bias_grad[layer : layer + 1, part * sz.hidden : (part + 1) * sz.hidden] = total[
                layer * 4 + part : layer * 4 + part + 1, : sz.hidden
            ]
        row = slice(layer * 4 + 3, layer * 4 + 4)
        r.mix_gain_grad[layer : layer + 1, :] = total[row, : sz.width]
        r.mlp_gain_grad[layer : layer + 1, :] = total[row, sz.width : 2 * sz.width]
        lanes = total[layer * 4 : layer * 4 + 1, sz.hidden : sz.hidden + LANES]
        r.forget_mean[layer : layer + 1, :] = (
            jnp.sum(lanes, axis=1, keepdims=True) * scale + jnp.zeros((1, LANES), F32)
        )


def run_whole_step(sz, layers, named):
    lengths = named["lengths"]
    rows, d, h, f = sz.rows, sz.width, sz.hidden, sz.inner
    vm = lambda *dims, kind=F32: pltpu.VMEM(dims, kind)
    sems = pltpu.SemaphoreType
    spec = dict(gate_bias=VMEM, mix_gain=VMEM, mlp_gain=VMEM)
    outputs = dict(
        layer_out=(shape(rows, d), ANY),
        input_grad=(shape(rows, d), ANY),
        gate_weight_grad=(shape(layers, 128, 384), VMEM),
        gate_bias_grad=(shape(layers, 3 * h), VMEM),
        out_weight_grad=(shape(layers, 64, 256), VMEM),
        up_weight_grad=(shape(layers, 128, 256), VMEM),
        down_weight_grad=(shape(layers, 64, 512), VMEM),
        mix_gain_grad=(shape(layers, d), VMEM),
        mlp_gain_grad=(shape(layers, d), VMEM),
        forget_mean=(shape(layers, LANES), VMEM),
    )
    results = len(outputs)
    kept = dict(
        u=((rows, d), BF16),
        a=((rows, h), F32),
        b=((rows, h), F32),
        zc=((rows, h), F32),
        states=((rows + sz.group, h), F32),
        y1=((rows, d), F32),
        v=((rows, d), BF16),
        p=((rows, f), F32),
        gb=((rows, f), BF16),
        stream=((rows, d), F32),
    )
    scratch = {}
    for name, (dims, kind) in kept.items():
        outputs[name + "_save"] = (shape(layers - 1, *dims, kind=kind), ANY)
        scratch[name] = vm(*dims, kind=kind)
    scratch.update(
        gate_w=vm(d, 3 * h, kind=BF16),
        out_w=vm(h, d, kind=BF16),
        up_w=vm(d, f, kind=BF16),
        down_w=vm(f, d, kind=BF16),
        valid=vm(rows, LANES),
        keep=vm(rows, LANES),
        gx=vm(rows, d),
        low=vm(rows, d, kind=BF16),
        low_t=vm(d, rows, kind=BF16),
        wide_t=vm(d, rows, kind=BF16),
        hb=vm(rows, h, kind=BF16),
        ga=vm(rows, h),
        gz=vm(rows, 3 * h, kind=BF16),
        grad=vm(rows, d),
        gy1=vm(rows, d),
        decay=vm(rows, h),
        chunk_p=vm(sz.group, h),
        chunk_t=vm(sz.group, h),
        prefix=vm(2, sz.group, h),
        enter=vm(sz.group, h),
        mine=vm(8, h),
        slots=vm(2, layers, sz.sections, 8, h),
        mlp_sum=vm(8, d),
        mix_sum=vm(8, d),
        held=vm(HELD, 2, 2, 16, BLOCK, LANES),
        small=vm(STAGES + 1, 8, SMALL),
        small_arrived=vm(STAGES, 8, SMALL),
        in_sems=sems.DMA((3,)),
        lens=pltpu.SMEM(lengths.shape, jnp.int32),
        out_sems=sems.DMA((d // LANES,)),
        natural=vm(d // LANES, rows, LANES),
        load_sems=sems.DMA((len(kept) + 4,)),
        save_sems=sems.DMA((len(kept) + 4,)),
        pair_send=sems.DMA((2, layers, sz.sections - 1)),
        pair_recv=sems.DMA((2, layers, sz.sections - 1)),
        send_sems=sems.DMA((SENDS, 2 * STAGES - 1)),
        recv_sems=sems.DMA((max(RINGS), 2 * STAGES - 1)),
        credits=sems.REGULAR((2 * STAGES - 1,)),
        small_send=sems.DMA((STAGES,)),
        small_recv=sems.DMA((STAGES,)),
    )
    for stage in range(STAGES):
        scratch[f"arrived{stage}"] = vm(RINGS[stage], 2, 16 >> stage, BLOCK, LANES)
    names = list(named) + list(outputs) + list(scratch)
    out = pl.pallas_call(
        functools.partial(whole_step, sz, layers, names),
        out_shape=tuple(value for value, _ in outputs.values()),
        in_specs=[spec.get(name, ANY) for name in named],
        out_specs=[place_of for _, place_of in outputs.values()],
        scratch_shapes=list(scratch.values()),
        compiler_params=pltpu.CompilerParams(
            collective_id=4, has_side_effects=True, vmem_limit_bytes=LIMIT
        ),
        name="whole_step",
    )(*named.values())
    return out[:results]


def deliver_kernel(count, *refs):
    sources, targets, held = refs[:count], refs[count : 2 * count], refs[2 * count : 3 * count - 1]
    sems = refs[3 * count - 1]
    arrivals = [
        pltpu.make_async_copy(sources[i], held[i], sems.at[0, i]) for i in range(count - 1)
    ]
    departures = [
        pltpu.make_async_copy(held[i], targets[i], sems.at[1, i]) for i in range(count - 1)
    ]
    for copy in arrivals:
        copy.start()
    for layer in range(targets[-1].shape[0]):
        targets[-1][layer] = sources[-1][layer, 0]
    for arrival, departure in zip(arrivals, departures):
        arrival.wait()
        departure.start()
    for copy in departures:
        copy.wait()


def deliver(values):
    count = len(values)
    scalars = pl.BlockSpec(memory_space=pltpu.SMEM)
    shapes = [shape(*value.shape) for value in values[:-1]] + [shape(values[-1].shape[0])]
    return pl.pallas_call(
        functools.partial(deliver_kernel, count),
        out_shape=tuple(shapes),
        in_specs=[ANY] * (count - 1) + [scalars],
        out_specs=[ANY] * (count - 1) + [scalars],
        scratch_shapes=[pltpu.VMEM(value.shape, F32) for value in values[:-1]]
        + [pltpu.SemaphoreType.DMA((2, count - 1))],
        compiler_params=pltpu.CompilerParams(vmem_limit_bytes=LIMIT),
        name="deliver",
    )(*values)


def mask_kernel(sizes, lens, valid, keep):
    fill_masks(lens, valid, keep, sizes)


def body(
    activations,
    cotangent,
    lengths,
    gate_weight,
    gate_bias,
    out_weight,
    up_weight,
    down_weight,
    mix_gain,
    mlp_gain,
):
    micro, span, width = activations.shape
    layers = gate_weight.shape[0]
    sz = Sizes(
        micro, span, width, out_weight.shape[1], up_weight.shape[2], lax.axis_size("section")
    )

    blocks = (width // 4, 3 * sz.hidden // 8, width // 8, sz.inner // 4, sz.hidden // 4)
    axes = (lax.axis_size("section"), lax.axis_size("batch"))
    if axes == (4, 8) and blocks == (128, 384, 64, 512, 256):
        out = run_whole_step(
            sz,
            layers,
            dict(
                activations=activations.reshape(sz.rows, width),
                cotangent=cotangent.reshape(sz.rows, width),
                lengths=lengths.T,
                gate_bias=gate_bias,
                mix_gain=mix_gain,
                mlp_gain=mlp_gain,
                gate_hbm=gate_weight,
                out_hbm=out_weight,
                up_hbm=up_weight,
                down_hbm=down_weight,
            ),
        )
        stream_out, input_grad, gate_g, bias_g, out_g, up_g, down_g, *rest = deliver(out)
        return (
            stream_out.reshape(activations.shape),
            input_grad.reshape(activations.shape),
            gate_g,
            bias_g,
            out_g.transpose(0, 2, 1),
            up_g,
            down_g.transpose(0, 2, 1),
            *rest,
        )

    def arranged(value):
        value = value.astype(F32).reshape(micro, CHUNKS, sz.steps, width)
        return value.transpose(2, 0, 1, 3).reshape(sz.rows, width)

    def restored(value):
        value = value.reshape(sz.steps, micro, CHUNKS, width).transpose(1, 2, 0, 3)
        return value.reshape(micro, span, width)

    masks = pl.pallas_call(
        functools.partial(mask_kernel, sz),
        out_shape=(shape(sz.rows, LANES), shape(sz.rows, LANES)),
        in_specs=[pl.BlockSpec(memory_space=pltpu.SMEM)],
        out_specs=[VMEM] * 2,
        name="masks",
    )(lengths)
    weights = (gate_weight, out_weight, up_weight, down_weight)
    stream = arranged(activations)
    streams, saved, forgets = [], [], []
    for layer in range(layers):
        streams.append(stream)
        stream, *kept, forget, pairs = run_forward(
            sz,
            layer,
            stream,
            masks,
            gate_bias[layer : layer + 1],
            mix_gain[layer : layer + 1],
            mlp_gain[layer : layer + 1],
            weights,
        )
        saved.append((*kept, pairs))
        forgets.append(forget)
    layer_out = restored(stream)
    gx = arranged(cotangent)
    true_count = jnp.sum(lengths).astype(F32)
    forgets = [jnp.sum(forget) for forget in forgets]
    sums, small = [None] * layers, [None] * layers
    for layer in reversed(range(layers)):
        gx, gate_g, out_g, up_g, down_g, bias_g, mix_g, mlp_g = run_backward(
            sz,
            layer,
            gx,
            streams[layer],
            masks,
            mix_gain[layer : layer + 1],
            mlp_gain[layer : layer + 1],
            saved[layer],
            weights,
        )
        sums[layer] = (gate_g, out_g.T, up_g, down_g.T)
        small[layer] = tuple(jnp.sum(part, axis=0) for part in (bias_g, mix_g, mlp_g))
    input_grad = restored(gx)
    stacked = tuple(jnp.stack(parts) for parts in zip(*sums))
    partial_sums = lax.psum_scatter(stacked, "section", scatter_dimension=1, tiled=True)
    large = lax.psum_scatter(partial_sums, "batch", scatter_dimension=2, tiled=True)
    bias_grad, mix_grad, mlp_grad = (jnp.stack(parts) for parts in zip(*small))
    bias_grad, mix_grad, mlp_grad, forget = lax.psum(
        (bias_grad, mix_grad, mlp_grad, jnp.stack(forgets)), ("section", "batch")
    )
    forget_mean = forget / (true_count * sz.hidden)
    return (
        layer_out,
        input_grad,
        large[0],
        bias_grad,
        large[1],
        large[2],
        large[3],
        mix_grad,
        mlp_grad,
        forget_mean,
    )


def solution(mesh):
    stream = P("batch", "section", None)
    block = P(None, "section", "batch")
    return jax.shard_map(
        body,
        mesh=mesh,
        in_specs=(stream, stream) + (P(),) * 8,
        out_specs=(stream, stream, block, P(), block, block, block, P(), P(), P()),
        check_vma=False,
    )
```

```python
import functools
import types

import jax
import jax.numpy as jnp
from jax import lax
from jax.experimental import pallas as pl
from jax.experimental.pallas import tpu as pltpu
from jax.sharding import PartitionSpec as P

epsilon = 1e-06
MESH = pl.DeviceIdType.MESH
F32, BF16 = jnp.float32, jnp.bfloat16
CHUNKS = 8
LANES = 128
ROOT_HALF = 0.7071067811865476
ROOT_TAU = 0.3989422804014327


def tile(index, size):
    return pl.ds(pl.multiple_of(index * size, size), size)


def inverse(value):
    r = pltpu.reciprocal(value, approx=True)
    return r * (2.0 - value * r)


def normal_below(p):
    return 0.5 + 0.5 * lax.erf(p * ROOT_HALF)


def steps_of(count, unroll, one, start, reverse=False):
    def turn(i, carry):
        for k in range(unroll):
            at = i * unroll + k
            carry = one(count - 1 - at if reverse else at, carry)
        return carry

    return lax.fori_loop(0, count // unroll, turn, start)


def gate_weights(a, b):
    inv = inverse(2.0 + a + b)
    return (1.0 + b) * inv, (1.0 + a) * inv, inv


def greet_section(sections):
    me = lax.axis_index("section")
    barrier = pltpu.get_barrier_semaphore()
    for hop in range(1, sections):
        pl.semaphore_signal(
            barrier, inc=1, device_id={"section": lax.rem(me + hop, sections)}, device_id_type=MESH
        )
    pl.semaphore_wait(barrier, sections - 1)


def exchange(mine, slots, send_sems, recv_sems, sections):
    me = lax.axis_index("section")
    copies = []
    for hop in range(1, sections):
        copies.append(
            pltpu.make_async_remote_copy(
                src_ref=mine,
                dst_ref=slots.at[me],
                send_sem=send_sems.at[hop - 1],
                recv_sem=recv_sems.at[hop - 1],
                device_id={"section": lax.rem(me + hop, sections)},
                device_id_type=MESH,
            )
        )
    for copy in copies:
        copy.start()
    slots[me] = mine[...]
    for copy in copies:
        copy.wait()


def norm_rows(stream, gain, low, rows, step):
    def one(i, carry):
        at = tile(i, step)
        x = stream[at, :]
        r = lax.rsqrt(jnp.mean(x * x, axis=-1, keepdims=True) + epsilon)
        low[at, :] = (x * r * gain[...]).astype(BF16)
        return carry

    lax.fori_loop(0, rows // step, one, 0)


def norm_back(stream, gain, grad, through, out, gain_sum, rows, step):
    width = stream.shape[1]

    def one(i, total):
        at = tile(i, step)
        x = stream[at, :]
        r = lax.rsqrt(jnp.mean(x * x, axis=-1, keepdims=True) + epsilon)
        n = x * r
        g = grad[at, :]
        a = g * gain[...]
        out[at, :] = through[at, :] + r * (a - n * jnp.mean(a * n, axis=-1, keepdims=True))
        return total + jnp.sum((g * n).reshape(step // 8, 8, width), axis=0)

    gain_sum[...] = lax.fori_loop(0, rows // step, one, jnp.zeros((8, width), F32))


def fill_masks(lens, valid, keep, sizes, turned=False):
    section = lax.axis_index("section")
    group = lax.axis_index("batch")
    starts, totals = [], []
    for s in range(sizes.micro):
        total, begin = 0, []
        for d in range(lens.shape[0 if turned else 1]):
            row = group * sizes.micro + s
            length = lens[d, row] if turned else lens[row, d]
            begin.append(jnp.where(length > 0, total, -1))
            total = total + length
        starts.append(begin)
        totals.append(total)
    chunk_place = lax.broadcasted_iota(jnp.int32, (8, LANES), 0) * sizes.steps

    def one(j, carry):
        for s in range(sizes.micro):
            place = section * sizes.span + j + chunk_place
            true = place < totals[s]
            first = place == starts[s][0]
            for begin in starts[s][1:]:
                first = first | (place == begin)
            at = pl.ds(pl.multiple_of(j * sizes.group + s * 8, 8), 8)
            valid[at, :] = jnp.where(true, 1.0, 0.0)
            keep[at, :] = jnp.where(true & jnp.logical_not(first), 1.0, 0.0)
        return carry

    lax.fori_loop(0, sizes.steps, one, 0)


def scan_totals(first, second, sizes, reverse, prefix, chunk, mine):
    for s in range(sizes.micro):
        p = jnp.ones((1, sizes.hidden), F32)
        t = jnp.zeros((1, sizes.hidden), F32)
        for c in reversed(range(CHUNKS)) if reverse else range(CHUNKS):
            at = s * 8 + c
            prefix[0, at : at + 1, :] = p
            prefix[1, at : at + 1, :] = t
            pc = first[at : at + 1, :]
            t = pc * t + second[at : at + 1, :]
            p = p * pc
        mine[s : s + 1, :] = p
        mine[sizes.micro + s : sizes.micro + s + 1, :] = t


def scan_enter(slots, prefix, enter, sizes, reverse):
    me = lax.axis_index("section")
    for s in range(sizes.micro):
        a = jnp.zeros((1, sizes.hidden), F32)
        order = range(sizes.sections - 1, 0, -1) if reverse else range(sizes.sections - 1)
        for k in order:
            reached = k > me if reverse else k < me
            pk = slots[k, s : s + 1, :]
            tk = slots[k, sizes.micro + s : sizes.micro + s + 1, :]
            a = jnp.where(reached, pk * a + tk, a)
        at = slice(s * 8, s * 8 + 8)
        enter[at, :] = prefix[0, at, :] * a + prefix[1, at, :]


def part_totals(first, second, sizes, reverse, prefix, mine, lanes):
    for s in range(sizes.micro):
        p = jnp.ones((1, lanes.stop - lanes.start), F32)
        t = jnp.zeros_like(p)
        for c in reversed(range(CHUNKS)) if reverse else range(CHUNKS):
            at = s * 8 + c
            prefix[0, at : at + 1, lanes] = p
            prefix[1, at : at + 1, lanes] = t
            pc = first[at : at + 1, lanes]
            t = pc * t + second[at : at + 1, lanes]
            p = p * pc
        mine[s : s + 1, lanes] = p
        mine[sizes.micro + s : sizes.micro + s + 1, lanes] = t


def part_enter(slots, prefix, enter, sizes, reverse, lanes):
    me = lax.axis_index("section")
    for s in range(sizes.micro):
        a = jnp.zeros((1, lanes.stop - lanes.start), F32)
        order = range(sizes.sections - 1, 0, -1) if reverse else range(sizes.sections - 1)
        for k in order:
            reached = k > me if reverse else k < me
            pk = slots[k, s : s + 1, lanes]
            tk = slots[k, sizes.micro + s : sizes.micro + s + 1, lanes]
            a = jnp.where(reached, pk * a + tk, a)
        at = slice(s * 8, s * 8 + 8)
        enter[at, lanes] = prefix[0, at, lanes] * a + prefix[1, at, lanes]


class Sizes:
    def __init__(self, micro, span, width, hidden, inner, sections):
        self.micro, self.span, self.width = micro, span, width
        self.hidden, self.inner, self.sections = hidden, inner, sections
        self.rows = micro * span
        self.steps = span // CHUNKS
        self.group = micro * CHUNKS


def forward_kernel(
    sizes,
    layer,
    stream,
    valid,
    keep,
    bias,
    mix_gain,
    mlp_gain,
    gate_hbm,
    out_hbm,
    up_hbm,
    down_hbm,
    next_stream,
    u,
    sf_out,
    si_out,
    zc_out,
    states,
    y1,
    v,
    p_out,
    gb,
    forget,
    pair_slots,
    gate_w,
    out_w,
    up_w,
    down_w,
    z,
    decay,
    drive,
    hb,
    chunk_p,
    chunk_t,
    prefix,
    enter,
    mine,
    weight_sems,
    send_sems,
    recv_sems,
):
    sz = sizes
    loads = [
        pltpu.make_async_copy(src.at[layer], dst, weight_sems.at[i])
        for i, (src, dst) in enumerate(
            ((gate_hbm, gate_w), (out_hbm, out_w), (up_hbm, up_w), (down_hbm, down_w))
        )
    ]
    for load in loads:
        load.start()
    greet_section(sz.sections)
    mine[...] = jnp.zeros_like(mine)
    norm_rows(stream, mix_gain, u, sz.rows, 64)
    loads[0].wait()
    forget[...] = jnp.zeros_like(forget)
    hw = 256

    def gate_tile(n, carry):
        for part in range(3):
            cols = pl.ds(pl.multiple_of(part * sz.hidden + n * hw, hw), hw)
            z[:, part * hw : (part + 1) * hw] = (
                jnp.dot(u[...], gate_w[:, cols], preferred_element_type=F32) + bias[:, cols]
            )

        def one(i, inner):
            at = tile(i, 64)
            for lane in range(hw // LANES):
                src = lambda part: z[
                    at, part * hw + lane * LANES : part * hw + (lane + 1) * LANES
                ]
                dst = pl.ds(pl.multiple_of(n * hw + lane * LANES, LANES), LANES)
                a = jnp.exp(jnp.minimum(-src(0), 86.0))
                b = jnp.exp(jnp.minimum(-src(1), 86.0))
                zc = src(2)
                fp, ip, _ = gate_weights(a, b)
                vm = valid[at, :]
                decay[at, dst] = fp * keep[at, :]
                drive[at, dst] = ip * zc * vm
                sf_out[at, dst] = a
                si_out[at, dst] = b
                zc_out[at, dst] = zc
                forget[...] += jnp.sum((fp * vm).reshape(8, 8, LANES), axis=0)
            return inner

        lax.fori_loop(0, sz.rows // 64, one, 0)
        return carry

    lax.fori_loop(0, sz.hidden // hw, gate_tile, 0)
    half = sz.hidden // 2
    for part in range(2):
        lanes = slice(part * half, (part + 1) * half)

        def totals(j, pair):
            at = tile(j, sz.group)
            d = decay[at, lanes]
            return pair[0] * d, pair[1] * d + drive[at, lanes]

        one = jnp.ones((sz.group, half), F32)
        pair = steps_of(sz.steps, 4, totals, (one, jnp.zeros_like(one)))
        chunk_p[:, lanes] = pair[0]
        chunk_t[:, lanes] = pair[1]
    scan_totals(chunk_p, chunk_t, sz, False, prefix, None, mine)
    exchange(mine, pair_slots, send_sems, recv_sems, sz.sections)
    scan_enter(pair_slots, prefix, enter, sz, False)
    states[0 : sz.group, :] = enter[...]
    for part in range(2):
        lanes = slice(part * half, (part + 1) * half)

        def walk(j, h):
            at = tile(j, sz.group)
            h = decay[at, lanes] * h + drive[at, lanes]
            states[tile(j + 1, sz.group), lanes] = h
            hb[at, lanes] = h.astype(BF16)
            return h

        steps_of(sz.steps, 4, walk, enter[:, lanes])
    loads[1].wait()

    def out_tile(n, carry):
        cols = tile(n, 256)
        y1[:, cols] = stream[:, cols] + jnp.dot(
            hb[...], out_w[:, cols], preferred_element_type=F32
        )
        return carry

    lax.fori_loop(0, sz.width // 256, out_tile, 0)
    norm_rows(y1, mlp_gain, v, sz.rows, 64)
    loads[2].wait()

    def up_tile(n, carry):
        cols = tile(n, 256)
        p_out[:, cols] = jnp.dot(v[...], up_w[:, cols], preferred_element_type=F32)

        def one(i, inner):
            at = tile(i, 64)
            p = p_out[at, cols]
            gb[at, cols] = (p * normal_below(p)).astype(BF16)
            return inner

        lax.fori_loop(0, sz.rows // 64, one, 0)
        return carry

    lax.fori_loop(0, sz.inner // 256, up_tile, 0)
    loads[3].wait()

    def down_tile(n, carry):
        cols = tile(n, 256)
        next_stream[:, cols] = y1[:, cols] + jnp.dot(
            gb[...], down_w[:, cols], preferred_element_type=F32
        )
        return carry

    lax.fori_loop(0, sz.width // 256, down_tile, 0)


def backward_kernel(
    sizes,
    layer,
    gx,
    stream,
    valid,
    keep,
    mix_gain,
    mlp_gain,
    u,
    sf_in,
    si_in,
    zc_in,
    states,
    y1,
    v,
    p_in,
    gb,
    pair_slots,
    gate_hbm,
    out_hbm,
    up_hbm,
    down_hbm,
    next_gx,
    gate_grad,
    out_grad,
    up_grad,
    down_grad,
    bias_sum,
    mix_sum,
    mlp_sum,
    gate_w,
    out_w,
    up_w,
    down_w,
    low,
    low_t,
    wide_t,
    hb,
    ga,
    gp,
    gz,
    grad,
    gy1,
    decay,
    chunk_p,
    chunk_t,
    prefix,
    enter,
    mine,
    slots,
    weight_sems,
    send_sems,
    recv_sems,
):
    sz = sizes
    loads = [
        pltpu.make_async_copy(src.at[layer], dst, weight_sems.at[i])
        for i, (src, dst) in enumerate(
            ((gate_hbm, gate_w), (out_hbm, out_w), (up_hbm, up_w), (down_hbm, down_w))
        )
    ]
    for load in reversed(loads):
        load.start()
    greet_section(sz.sections)
    mine[...] = jnp.zeros_like(mine)

    def cast(i, carry):
        at = tile(i, 64)
        low[at, :] = gx[at, :].astype(BF16)
        return carry

    lax.fori_loop(0, sz.rows // 64, cast, 0)
    low_t[...] = low[...].T

    def weight_grad(left_t, right, dst, step):
        def one(n, carry):
            cols = tile(n, step)
            dst[:, cols] = jnp.dot(left_t[...], right[:, cols], preferred_element_type=F32)
            return carry

        lax.fori_loop(0, right.shape[1] // step, one, 0)

    weight_grad(low_t, gb, down_grad, 256)
    loads[3].wait()

    def act_tile(n, carry):
        cols = tile(n, 256)
        ga[:, :256] = lax.dot_general(
            low[...], down_w[cols, :], (((1,), (1,)), ((), ())), preferred_element_type=F32
        )

        def one(i, inner):
            at = tile(i, 64)
            p = p_in[at, cols]
            slope = normal_below(p) + ROOT_TAU * p * jnp.exp(-0.5 * p * p)
            gp[at, cols] = (ga[at, :256] * slope).astype(BF16)
            return inner

        lax.fori_loop(0, sz.rows // 64, one, 0)
        return carry

    lax.fori_loop(0, sz.inner // 256, act_tile, 0)
    wide_t[...] = v[...].T
    weight_grad(wide_t, gp, up_grad, 256)
    loads[2].wait()

    def contract(left, weight, dst, step):
        def one(n, carry):
            cols = tile(n, step)
            dst[:, cols] = lax.dot_general(
                left[...], weight[cols, :], (((1,), (1,)), ((), ())), preferred_element_type=F32
            )
            return carry

        lax.fori_loop(0, weight.shape[0] // step, one, 0)

    contract(gp, up_w, grad, 256)
    norm_back(y1, mlp_gain, grad, gx, gy1, mlp_sum, sz.rows, 64)

    def cast_more(i, carry):
        at = tile(i, 64)
        low[at, :] = gy1[at, :].astype(BF16)
        return carry

    lax.fori_loop(0, sz.rows // 64, cast_more, 0)

    def cast_state(i, carry):
        hb[tile(i, sz.group), :] = states[tile(i + 1, sz.group), :].astype(BF16)
        return carry

    lax.fori_loop(0, sz.steps, cast_state, 0)
    low_t[...] = low[...].T
    weight_grad(low_t, hb, out_grad, 256)
    loads[1].wait()
    contract(low, out_w, ga, 256)
    half = sz.hidden // 2
    for part in range(2):
        lanes = slice(part * half, (part + 1) * half)

        def totals(i, pair):
            at = tile(sz.steps - 1 - i, sz.group)
            mask = jnp.concatenate([keep[at, :]] * (half // LANES), axis=1)
            d = gate_weights(sf_in[at, lanes], si_in[at, lanes])[0] * mask
            decay[at, lanes] = d
            return pair[0] * d, d * (ga[at, lanes] + pair[1])

        pair = lax.fori_loop(
            0,
            sz.steps,
            totals,
            (jnp.ones((sz.group, half), F32), jnp.zeros((sz.group, half), F32)),
        )
        chunk_p[:, lanes] = pair[0]
        chunk_t[:, lanes] = pair[1]
    scan_totals(chunk_p, chunk_t, sz, True, prefix, None, mine)
    exchange(mine, slots, send_sems, recv_sems, sz.sections)
    scan_enter(slots, prefix, enter, sz, True)

    def gate_lane(n, carry):
        lanes = tile(n, LANES)

        def walk(i, kept):
            m, bf, bi, bc = kept
            j = sz.steps - 1 - i
            at = tile(j, sz.group)
            d = decay[at, lanes]
            q = ga[at, lanes] + m
            a = sf_in[at, lanes]
            b = si_in[at, lanes]
            zc = zc_in[at, lanes]
            vm = valid[at, :]
            fp, ip, inv = gate_weights(a, b)
            gf = q * (states[at, lanes] * keep[at, :] - zc * vm)
            gzf = (gf * (a * inv) * fp).astype(BF16)
            gzi = (-gf * (b * inv) * ip).astype(BF16)
            gzc = (q * vm * ip).astype(BF16)
            gz[at, lanes] = gzf
            gz[at, pl.ds(pl.multiple_of(sz.hidden + n * LANES, LANES), LANES)] = gzi
            gz[at, pl.ds(pl.multiple_of(2 * sz.hidden + n * LANES, LANES), LANES)] = gzc
            return (
                d * q,
                bf + gzf.astype(F32),
                bi + gzi.astype(F32),
                bc + gzc.astype(F32),
            )

        zero = jnp.zeros((sz.group, LANES), F32)
        _, bf, bi, bc = lax.fori_loop(0, sz.steps, walk, (enter[:, lanes], zero, zero, zero))
        for part, total in enumerate((bf, bi, bc)):
            where = pl.ds(pl.multiple_of(part * sz.hidden + n * LANES, LANES), LANES)
            bias_sum[:, where] = jnp.sum(total.reshape(sz.group // 8, 8, LANES), axis=0)
        return carry

    lax.fori_loop(0, sz.hidden // LANES, gate_lane, 0)
    wide_t[...] = u[...].T
    weight_grad(wide_t, gz, gate_grad, 256)
    loads[0].wait()
    contract(gz, gate_w, grad, 256)
    norm_back(stream, mix_gain, grad, gy1, next_gx, mix_sum, sz.rows, 64)


VMEM = pl.BlockSpec(memory_space=pltpu.VMEM)
ANY = pl.BlockSpec(memory_space=pl.ANY)
LIMIT = 62 * 2**20


def shape(*dims, kind=F32):
    return jax.ShapeDtypeStruct(dims, kind)


def exchange_scratch(sz):
    return [
        pltpu.SemaphoreType.DMA((4,)),
        pltpu.SemaphoreType.DMA((sz.sections - 1,)),
        pltpu.SemaphoreType.DMA((sz.sections - 1,)),
    ]


def weight_scratch(sz):
    return [
        pltpu.VMEM((sz.width, 3 * sz.hidden), BF16),
        pltpu.VMEM((sz.hidden, sz.width), BF16),
        pltpu.VMEM((sz.width, sz.inner), BF16),
        pltpu.VMEM((sz.inner, sz.width), BF16),
    ]


def scan_scratch(sz):
    return [
        pltpu.VMEM((sz.group, sz.hidden), F32),
        pltpu.VMEM((sz.group, sz.hidden), F32),
        pltpu.VMEM((2, sz.group, sz.hidden), F32),
        pltpu.VMEM((sz.group, sz.hidden), F32),
        pltpu.VMEM((8, sz.hidden), F32),
    ]


def run_forward(sz, layer, stream, masks, bias, mix_gain, mlp_gain, weights):
    r, d, h, f = sz.rows, sz.width, sz.hidden, sz.inner
    return pl.pallas_call(
        functools.partial(forward_kernel, sz, layer),
        out_shape=(
            shape(r, d),
            shape(r, d, kind=BF16),
            shape(r, h),
            shape(r, h),
            shape(r, h),
            shape(r + sz.group, h),
            shape(r, d),
            shape(r, d, kind=BF16),
            shape(r, f),
            shape(r, f, kind=BF16),
            shape(8, LANES),
            shape(sz.sections, 8, h),
        ),
        in_specs=[VMEM] * 6 + [ANY] * 4,
        out_specs=[VMEM] * 12,
        scratch_shapes=weight_scratch(sz)
        + [
            pltpu.VMEM((r, 3 * 256), F32),
            pltpu.VMEM((r, h), F32),
            pltpu.VMEM((r, h), F32),
            pltpu.VMEM((r, h), BF16),
        ]
        + scan_scratch(sz)
        + exchange_scratch(sz),
        compiler_params=pltpu.CompilerParams(
            collective_id=layer, has_side_effects=True, vmem_limit_bytes=LIMIT
        ),
        name=f"forward_{layer}",
    )(stream, *masks, bias, mix_gain, mlp_gain, *weights)


def run_backward(sz, layer, gx, stream, masks, mix_gain, mlp_gain, saved, weights):
    r, d, h, f = sz.rows, sz.width, sz.hidden, sz.inner
    return pl.pallas_call(
        functools.partial(backward_kernel, sz, layer),
        out_shape=(
            shape(r, d),
            shape(d, 3 * h),
            shape(d, h),
            shape(d, f),
            shape(d, f),
            shape(8, 3 * h),
            shape(8, d),
            shape(8, d),
        ),
        in_specs=[VMEM] * 16 + [ANY] * 4,
        out_specs=[VMEM] * 8,
        scratch_shapes=weight_scratch(sz)
        + [
            pltpu.VMEM((r, d), BF16),
            pltpu.VMEM((d, r), BF16),
            pltpu.VMEM((d, r), BF16),
            pltpu.VMEM((r, h), BF16),
            pltpu.VMEM((r, h), F32),
            pltpu.VMEM((r, f), BF16),
            pltpu.VMEM((r, 3 * h), BF16),
            pltpu.VMEM((r, d), F32),
            pltpu.VMEM((r, d), F32),
            pltpu.VMEM((r, h), F32),
        ]
        + scan_scratch(sz)
        + [pltpu.VMEM((sz.sections, 8, h), F32)]
        + exchange_scratch(sz),
        compiler_params=pltpu.CompilerParams(
            collective_id=2 + layer, has_side_effects=True, vmem_limit_bytes=LIMIT
        ),
        name=f"backward_{layer}",
    )(gx, stream, *masks, mix_gain, mlp_gain, *saved, *weights)


BLOCK = 64
HELD = 3
RINGS = (4, 5, 6, 16, 16)
SENDS = 16
STAGES = 5
WINDOW = 4
SMALL = 1280


class Units:
    def __init__(self, count, refs):
        self.count = count
        self.__dict__.update(vars(refs))
        self.arrived = [getattr(refs, f"arrived{stage}") for stage in range(STAGES)]
        section, batch = lax.axis_index("section"), lax.axis_index("batch")
        core, x = section % 2, section // 2
        y, za, zb = batch % 2, (batch // 2) % 2, batch // 4
        self.core = core
        self.bits = ((x, za, y, zb), (y, za, x, zb))
        self.names = (("x", "za", "y", "zb"), ("y", "za", "x", "zb"))
        self.partner = {
            "core": {"section": section + 1 - 2 * core},
            "x": {"section": section + 2 - 4 * x},
            "y": {"batch": batch + 1 - 2 * y},
            "za": {"batch": batch + 2 - 4 * za},
            "zb": {"batch": batch + 4 - 8 * zb},
        }
        self.now = 0.0
        self.links = ("core", "x", "y", "z")
        self.free_at = dict.fromkeys(self.links, 0.0)
        self.flying = dict.fromkeys(self.links, 0)
        self.queues = {link: [] for link in self.links}
        self.ready = {}
        self.summed = set()
        self.copies = {}
        self.small_left = None

    def greet(self):
        barrier = pltpu.get_barrier_semaphore()
        section = lax.axis_index("section")
        others = [self.partner["y"], self.partner["za"], self.partner["zb"]]
        others += [{"section": lax.rem(section + hop, 4)} for hop in range(1, 4)]
        for other in others:
            pl.semaphore_signal(barrier, inc=1, device_id=other, device_id_type=MESH)
        pl.semaphore_wait(barrier, len(others))

    def name(self, stage, half):
        return "core" if stage == 0 else self.names[half][stage - 1]

    def link(self, stage, half):
        name = self.name(stage, half)
        return "z" if name[0] == "z" else name

    def arrival(self, unit, stage, half):
        ref = self.arrived[stage].at[unit % RINGS[stage]]
        return ref if stage == 0 else ref.at[half]

    def copy(self, unit, stage, half):
        at = 0 if stage == 0 else 2 * stage - 1 + half
        if stage == 0:
            src = self.held.at[unit % HELD, 1 - self.core]
        else:
            count = 16 >> stage
            src = self.arrived[stage - 1].at[unit % RINGS[stage - 1], half]
            src = src.at[pl.ds((1 - self.bits[half][stage - 1]) * count, count)]
        return pltpu.make_async_remote_copy(
            src_ref=src,
            dst_ref=self.arrival(unit, stage, half),
            send_sem=self.send_sems.at[unit % SENDS, at],
            recv_sem=self.recv_sems.at[unit % RINGS[stage], at],
            device_id=self.partner[self.name(stage, half)],
            device_id_type=MESH,
        )

    def has_place(self, unit, stage, half):
        before = unit - RINGS[stage]
        if before < 0:
            return True
        if stage == 0:
            return (before, 1, 0) in self.summed and (before, 1, 1) in self.summed
        return (before, min(stage + 1, STAGES - 1), half) in self.summed

    def credit(self, unit, stage, half):
        if unit + RINGS[stage] < self.count:
            pl.semaphore_signal(
                self.credits.at[0 if stage == 0 else 2 * stage - 1 + half],
                inc=1,
                device_id=self.partner[self.name(stage, half)],
                device_id_type=MESH,
            )

    def pump(self):
        for link, queue in self.queues.items():
            while self.flying[link] < WINDOW:
                key = next((key for key in queue if self.has_place(*key)), None)
                if key is None:
                    break
                queue.remove(key)
                self.flying[link] += 1
                unit, stage, half = key
                if unit >= RINGS[stage]:
                    at = 0 if stage == 0 else 2 * stage - 1 + half
                    pl.semaphore_wait(self.credits.at[at], 1)
                self.copies[key] = self.copy(*key)
                self.copies[key].start()
                size = (32 if stage == 0 else 16 >> stage) * BLOCK * LANES * 4
                rate = 250e3 if link == "core" else 45e3
                self.free_at[link] = max(self.now, self.free_at[link]) + size / rate
                self.ready[key] = self.free_at[link] + 1.5

    def push(self, unit, stage, half):
        self.queues[self.link(stage, half)].append((unit, stage, half))
        self.pump()

    def produced(self, *which):
        for unit in which:
            self.push(unit, 0, 0)

    def add(self, dst, src, count):
        turn = min(count, 4)

        def one(i, carry):
            for k in range(turn):
                dst[i * turn + k] += src[i * turn + k]
            return carry

        if count == turn:
            one(0, 0)
        else:
            lax.fori_loop(0, count // turn, one, 0)

    def step(self, unit, stage, half):
        key = (unit, stage, half)
        del self.ready[key]
        assert unit == 0 or (unit - 1, stage, half) in self.summed
        self.copies[key].wait_recv()
        here = self.arrival(unit, stage, half)
        if stage == 0:
            for h in range(2):
                self.add(here.at[h], self.held.at[unit % HELD, self.core, h], 16)
        else:
            count = 16 >> stage
            before = self.arrived[stage - 1].at[unit % RINGS[stage - 1], half]
            self.add(here, before.at[pl.ds(self.bits[half][stage - 1] * count, count)], count)
            self.copies.pop(key).wait_send()
        self.summed.add(key)
        self.flying[self.link(stage, half)] -= 1
        self.now += 0.25
        if stage > 1 or (unit, 1, 1 - half) in self.summed:
            if stage > 0:
                self.credit(unit, stage - 1, half if stage > 1 else 0)
        if stage == 0:
            for h in range(2):
                self.push(unit, 1, h)
        elif stage < STAGES - 1:
            self.push(unit, stage + 1, half)
        else:
            self.finish(unit, half, here[0])
            self.credit(unit, stage, half)
        self.pump()

    def finish(self, unit, half, block):
        layer, k = self.count // 8 - 1 - unit // 8, unit % 8
        if k < 2 or k == 4:
            ref, at = (self.down_weight_grad, k) if k < 2 else (self.out_weight_grad, 0)
            ref[layer, :, at * 256 + half * 128 : at * 256 + half * 128 + 128] = block
        else:
            ref, at = (self.up_weight_grad, k - 2) if k < 4 else (self.gate_weight_grad, k - 5)
            rows = slice(half * BLOCK, half * BLOCK + BLOCK)
            ref[layer, rows, at * LANES : at * LANES + LANES] = block

    def small_copy(self, stage):
        name = ("core", "x", "y", "za", "zb")[stage]
        return pltpu.make_async_remote_copy(
            src_ref=self.small.at[stage],
            dst_ref=self.small_arrived.at[stage],
            send_sem=self.small_send.at[stage],
            recv_sem=self.small_recv.at[stage],
            device_id=self.partner[name],
            device_id_type=MESH,
        )

    def small_start(self):
        self.small_left = 0
        self.small_copies = [self.small_copy(0)]
        self.small_copies[0].start()
        self.small_ready = self.now + 3.0

    def small_step(self):
        stage = self.small_left
        self.small_copies[stage].wait_recv()
        self.small[stage + 1] = self.small[stage] + self.small_arrived[stage]
        self.small_left += 1
        if self.small_left < STAGES:
            self.small_copies.append(self.small_copy(self.small_left))
            self.small_copies[-1].start()
            self.small_ready = self.now + 3.0
        else:
            for copy in self.small_copies:
                copy.wait_send()

    def open(self, unit, stage, half):
        halves = range(2) if stage == 0 else (half,)
        before = unit - RING
        return (
            before < 0
            or stage == STAGES - 1
            or all((before, stage + 1, h) in self.consumed for h in halves)
        )

    def next(self):
        best = min(self.ready.items(), key=lambda item: (item[1], item[0]), default=None)
        small = self.small_left is not None and self.small_left < STAGES
        if small and (best is None or self.small_ready <= best[1]):
            return self.small_ready, None
        return (best[1], best[0]) if best else None

    def take(self, item):
        self.now = max(self.now, item[0])
        if item[1] is None:
            self.small_step()
        else:
            self.step(*item[1])

    def passed(self, us):
        self.now += us
        while (item := self.next()) and item[0] <= self.now:
            self.take(item)

    def room(self, unit):
        before = (unit - HELD, 0, 0)
        while unit >= HELD and before not in self.summed:
            self.take(self.next())
        if before in self.copies:
            self.copies.pop(before).wait_send()

    def drain(self):
        while item := self.next():
            self.take(item)
        for key in list(self.copies):
            self.copies.pop(key).wait_send()


def place(half, x, y, za, zb):
    return (x * 8 + za * 4 + y * 2 + zb) if half == 0 else (y * 8 + za * 4 + x * 2 + zb)


def strided(start, steps):
    return pl.ds(start, CHUNKS, stride=steps)


def whole_step(sz, layers, names, *args):
    r = types.SimpleNamespace(**dict(zip(names, args)))
    units = Units(8 * layers, r)
    valid, keep, low, low_t, wide_t = r.valid, r.keep, r.low, r.low_t, r.wide_t
    hb, ga, gz, grad, gy1, gx = r.hb, r.ga, r.gz, r.grad, r.gy1, r.gx
    gp = gz.at[:, : sz.inner]
    decay, enter, prefix, mine = r.decay, r.enter, r.prefix, r.mine
    small, held = r.small, r.held
    natural = r.natural
    last = layers - 1
    half = sz.hidden // 2
    z0, z1 = ga.at[:, :768], r.z1
    drive = r.p.at[:, : sz.hidden]
    homes = dict(gate_w=r.gate_hbm, out_w=r.out_hbm, up_w=r.up_hbm, down_w=r.down_hbm)
    homes.update(u=r.u_save, a=r.a_save, b=r.b_save, zc=r.zc_save, states=r.states_save)
    homes.update(y1=r.y1_save, v=r.v_save, p=r.p_save, gb=r.gb_save, stream=r.stream_save)
    keys = types.SimpleNamespace(**{name: name for name in homes})
    index_of = {name: i for i, name in enumerate(homes)}
    loads, saves = {}, {}

    def load(layer, name):
        copy = pltpu.make_async_copy(
            homes[name].at[layer], getattr(r, name), r.load_sems.at[index_of[name]]
        )
        copy.start()
        loads[name] = copy

    def need(*wanted):
        for name in wanted:
            if name in loads:
                loads.pop(name).wait()

    def save(layer, name, ref=None):
        if layer < last:
            src = getattr(r, name) if ref is None else ref
            copy = pltpu.make_async_copy(
                src, homes[name].at[layer], r.save_sems.at[index_of[name]]
            )
            copy.start()
            saves[name] = copy

    def settled(*which):
        for name in which:
            if name in saves:
                saves.pop(name).wait()

    def over(count, one):
        def each(i, carry):
            one(i)
            return carry

        lax.fori_loop(0, count, each, 0)

    act_load = pltpu.make_async_copy(r.activations, hb.at[:, : sz.width], r.in_sems.at[0])
    cot_load = pltpu.make_async_copy(r.cotangent, wide_t, r.in_sems.at[1])
    len_load = pltpu.make_async_copy(r.lengths, r.lens, r.in_sems.at[2])
    len_load.start()
    act_load.start()
    for name in (keys.gate_w, keys.out_w, keys.up_w, keys.down_w):
        load(0, name)
    cot_load.start()
    units.greet()
    mine[...] = jnp.zeros_like(mine)
    small[0] = jnp.zeros((8, SMALL), F32)
    len_load.wait()
    fill_masks(r.lens, valid, keep, sz, True)

    def to_steps(src, put):
        def cast(i):
            at = tile(i, 64)
            for k in range(sz.width // LANES):
                natural[k, at, :] = src[at, k * LANES : (k + 1) * LANES].astype(F32)

        over(sz.rows // 64, cast)

        def gather(j):
            for k in range(sz.width // LANES):
                parts = [
                    natural[k, strided(s * sz.span + j, sz.steps), :] for s in range(sz.micro)
                ]
                put(tile(j, sz.group), slice(k * LANES, (k + 1) * LANES), jnp.concatenate(parts, axis=0))

        over(sz.steps, gather)

    def from_steps(src, dst, sem):
        def scatter(j):
            for k in range(sz.width // LANES):
                value = src[tile(j, sz.group), k * LANES : (k + 1) * LANES]
                for s in range(sz.micro):
                    natural[k, strided(s * sz.span + j, sz.steps), :] = value[s * 8 : s * 8 + 8]

        over(sz.steps, scatter)
        copies = []
        for k in range(sz.width // LANES):
            lanes = slice(k * LANES, (k + 1) * LANES)
            copies.append(pltpu.make_async_copy(natural.at[k], dst.at[:, lanes], sem.at[k]))
            copies[-1].start()
        return copies

    act_load.wait()

    def put_gx(at, lanes, value):
        gx[at, lanes] = value

    to_steps(hb.at[:, : sz.width], put_gx)

    parts = [slice(part * half, (part + 1) * half) for part in range(2)]

    def exchange_start(way, layer, part):
        lanes = parts[part]
        slots = r.slots.at[way, layer]
        me = lax.axis_index("section")
        copies = []
        for hop in range(1, sz.sections):
            copies.append(
                pltpu.make_async_remote_copy(
                    src_ref=mine.at[:, lanes],
                    dst_ref=slots.at[me, :, lanes],
                    send_sem=r.pair_send.at[way, layer, part, hop - 1],
                    recv_sem=r.pair_recv.at[way, layer, part, hop - 1],
                    device_id={"section": lax.rem(me + hop, sz.sections)},
                    device_id_type=MESH,
                )
            )
        for copy in copies:
            copy.start()
        slots[me, :, lanes] = mine[:, lanes]
        return slots, copies

    def exchange_end(slots, copies, reverse, part):
        for copy in copies:
            copy.wait()
        part_enter(slots, prefix, enter, sz, reverse, parts[part])

    def in_turn(count, dots, rest, after=None):
        zs = (z0, z1)
        over(sz.rows // 256, lambda i: dots(0, zs[0], i))
        for n in range(count):

            def both(i):
                if n + 1 < count:
                    dots(n + 1, zs[(n + 1) % 2], i)
                rest(n, zs[n % 2], i)

            over(sz.rows // 256, both)
            if after is not None:
                after(n)

    def keep_cotangent():
        cot_load.wait()

        def put_low(at, lanes, value):
            low[at, lanes] = value.astype(BF16)

        to_steps(wide_t, put_low)
        low_t[...] = low[...].T

    def forward(layer):
        stream = r.stream if layer > 0 else gx
        settled(keys.u)
        norm_rows(stream, r.mix_gain.at[layer : layer + 1], r.u, sz.rows, 128)
        save(layer, keys.u)
        if layer == 0:
            save(layer, keys.stream, gx)
        need(keys.gate_w)
        settled(keys.a, keys.b, keys.zc, keys.p)
        hw = 256
        bias = r.gate_bias

        def gate_dots(n, z, i):
            rows = tile(i, 256)
            for part in range(3):
                cols = slice(part * sz.hidden + n * hw, part * sz.hidden + (n + 1) * hw)
                z[rows, part * hw : (part + 1) * hw] = (
                    jnp.dot(r.u[rows, :], r.gate_w[:, cols], preferred_element_type=F32)
                    + bias[layer : layer + 1, cols]
                )

        def gate_rest(n, z, i):
            for chunk in range(4):
                at = pl.ds(pl.multiple_of(i * 256 + chunk * 64, 64), 64)
                vm, km = valid[at, :], keep[at, :]
                for lane in range(hw // LANES):
                    zf, zi, zc = (
                        z[at, part * hw + lane * LANES : part * hw + (lane + 1) * LANES]
                        for part in range(3)
                    )
                    dst = slice(n * hw + lane * LANES, n * hw + (lane + 1) * LANES)
                    a = jnp.exp(jnp.minimum(-zf, 86.0))
                    b = jnp.exp(jnp.minimum(-zi, 86.0))
                    fp, ip, _ = gate_weights(a, b)
                    decay[at, dst] = fp * km
                    drive[at, dst] = ip * zc * vm
                    r.a[at, dst] = a
                    r.b[at, dst] = b
                    r.zc[at, dst] = zc
                    r.forget[...] += jnp.sum((fp * vm).reshape(8, 8, LANES), axis=0)

        flights = []

        def gate_after(n):
            if n % 2 == 0:
                return
            lanes = parts[n // 2]

            def totals(j, pair):
                at = tile(j, sz.group)
                d = decay[at, lanes]
                return pair[0] * d, pair[1] * d + drive[at, lanes]

            one = jnp.ones((sz.group, half), F32)
            pair = steps_of(sz.steps, 2, totals, (one, jnp.zeros_like(one)))
            r.chunk_p[:, lanes] = pair[0]
            r.chunk_t[:, lanes] = pair[1]
            part_totals(r.chunk_p, r.chunk_t, sz, False, prefix, mine, lanes)
            flights.append(exchange_start(0, layer, n // 2))

        r.forget[...] = jnp.zeros_like(r.forget)
        in_turn(sz.hidden // hw, gate_dots, gate_rest, gate_after)
        small[0, layer * 4 : layer * 4 + 1, sz.hidden : sz.hidden + LANES] = jnp.sum(
            r.forget[...], axis=0, keepdims=True
        )
        for name in (keys.a, keys.b, keys.zc):
            save(layer, name)
        if layer < last:
            load(layer + 1, keys.gate_w)
        settled(keys.states, keys.y1, keys.v, keys.gb, keys.stream)
        states = r.states
        for part, lanes in enumerate(parts):
            exchange_end(*flights[part], False, part)
            states[0 : sz.group, lanes] = enter[:, lanes]

            def walk(j, h):
                at = tile(j, sz.group)
                h = decay[at, lanes] * h + drive[at, lanes]
                states[tile(j + 1, sz.group), lanes] = h
                hb[at, lanes] = h.astype(BF16)
                return h

            steps_of(sz.steps, 4, walk, enter[:, lanes])
        save(layer, keys.states)
        need(keys.out_w)

        def out_tile(n):
            cols = tile(n, 256)
            r.y1[:, cols] = stream[:, cols] + jnp.dot(
                hb[...], r.out_w[:, cols], preferred_element_type=F32
            )

        over(sz.width // 256, out_tile)
        save(layer, keys.y1)
        if layer < last:
            load(layer + 1, keys.out_w)
        norm_rows(r.y1, r.mlp_gain.at[layer : layer + 1], r.v, sz.rows, 128)
        save(layer, keys.v)
        need(keys.up_w)

        def up_dots(n, z, i):
            rows = tile(i, 256)
            z[rows, :256] = jnp.dot(
                r.v[rows, :], r.up_w[:, n * 256 : (n + 1) * 256], preferred_element_type=F32
            )

        def up_rest(n, z, i):
            cols = slice(n * 256, (n + 1) * 256)
            for chunk in range(4):
                at = pl.ds(pl.multiple_of(i * 256 + chunk * 64, 64), 64)
                p = z[at, :256]
                r.p[at, cols] = p
                r.gb[at, cols] = (p * normal_below(p)).astype(BF16)

        in_turn(sz.inner // 256, up_dots, up_rest)
        save(layer, keys.p)
        save(layer, keys.gb)
        if layer < last:
            load(layer + 1, keys.up_w)
        else:
            down_grad(layer, 0)
        need(keys.down_w)
        out = r.stream if layer < last else gy1

        def down_tile(n):
            cols = tile(n, 256)
            out[:, cols] = r.y1[:, cols] + jnp.dot(
                r.gb[...], r.down_w[:, cols], preferred_element_type=F32
            )

        over(sz.width // 256, down_tile)
        if layer < last:
            load(layer + 1, keys.down_w)

    def down_grad(layer, unit):
        for k in range(2):
            units.room(unit + k)

        def one(n):
            s, t = n // 2, n % 2
            value = jnp.dot(low_t[...], r.gb[:, tile(n, 256)], preferred_element_type=F32)
            for b in range(8):
                for h in range(2):
                    at = place(h, s // 2, b % 2, (b // 2) % 2, b // 4)
                    held[(unit + t) % HELD, s % 2, h, at] = value[
                        b * 64 : b * 64 + 64, h * 128 : h * 128 + 128
                    ]

        over(8, one)
        units.produced(unit, unit + 1)
        units.passed(3)

    def cast(src, dst):
        def one(i):
            at = tile(i, 64)
            dst[at, :] = src[at, :].astype(dst.dtype)

        over(sz.rows // 64, one)

    def contract(left, weight, dst, count):
        def one(n):
            cols = tile(n, 256)
            dst[:, cols] = lax.dot_general(
                left[...], weight[cols, :], (((1,), (1,)), ((), ())), preferred_element_type=F32
            )

        over(count // 256, one)

    def backward(layer, unit):
        def freed(*which):
            if layer > 0:
                for name in which:
                    load(layer - 1, name)

        if layer < last:
            cast(gx, low)
            low_t[...] = low[...].T
            need(keys.gb)
            down_grad(layer, unit)
        freed(keys.gb)
        unit += 2
        need(keys.down_w, keys.p)

        def act_dots(n, z, i):
            rows = tile(i, 256)
            z[rows, :256] = lax.dot_general(
                low[rows, :],
                r.down_w[n * 256 : (n + 1) * 256, :],
                (((1,), (1,)), ((), ())),
                preferred_element_type=F32,
            )

        def act_rest(n, z, i):
            cols = slice(n * 256, (n + 1) * 256)
            for chunk in range(4):
                at = pl.ds(pl.multiple_of(i * 256 + chunk * 64, 64), 64)
                p = r.p[at, cols]
                slope = normal_below(p) + ROOT_TAU * p * jnp.exp(-0.5 * p * p)
                gp[at, cols] = (z[at, :256] * slope).astype(BF16)

        in_turn(sz.inner // 256, act_dots, act_rest, lambda n: units.passed(0.6))
        freed(keys.down_w, keys.p)
        need(keys.v)
        wide_t[...] = r.v[...].T
        freed(keys.v)
        for k in range(2):
            units.room(unit + k)

        def up_grad(b):
            value = jnp.dot(wide_t[...], gp[:, tile(b, 256)], preferred_element_type=F32)
            for s in range(4):
                for h in range(2):
                    at = place(h, s // 2, b % 2, (b // 2) % 2, b // 4)
                    for t in range(2):
                        held[(unit + t) % HELD, s % 2, h, at] = value[
                            s * 128 + h * 64 : s * 128 + h * 64 + 64, t * 128 : t * 128 + 128
                        ]

        over(8, up_grad)
        units.produced(unit, unit + 1)
        unit += 2
        units.passed(3)
        need(keys.up_w, keys.y1)
        contract(gp, r.up_w, grad, sz.width)
        freed(keys.up_w)
        units.passed(2)
        norm_back(r.y1, r.mlp_gain.at[layer : layer + 1], grad, gx, gy1, r.mlp_sum, sz.rows, 64)
        freed(keys.y1)
        cast(gy1, low)
        need(keys.states)

        def cast_state(i):
            hb[tile(i, sz.group), :] = r.states[tile(i + 1, sz.group), :].astype(BF16)

        if layer < last:
            over(sz.steps, cast_state)
        low_t[...] = low[...].T
        units.room(unit)
        units.passed(2)

        def out_grad(s):
            value = jnp.dot(low_t[...], hb[:, tile(s, 256)], preferred_element_type=F32)
            for b in range(8):
                for h in range(2):
                    at = place(h, s // 2, b % 2, (b // 2) % 2, b // 4)
                    held[unit % HELD, s % 2, h, at] = value[
                        b * 64 : b * 64 + 64, h * 128 : h * 128 + 128
                    ]

        over(4, out_grad)
        units.produced(unit)
        unit += 1
        units.passed(1.5)
        need(keys.out_w, keys.a, keys.b)
        contract(low, r.out_w, ga, sz.hidden)
        freed(keys.out_w)
        units.passed(1.5)
        flights = []
        for part, lanes in enumerate(parts):

            def totals(j, pair):
                at = tile(j, sz.group)
                if layer < last:
                    mask = jnp.concatenate([keep[at, :]] * (half // LANES), axis=1)
                    d = gate_weights(r.a[at, lanes], r.b[at, lanes])[0] * mask
                    decay[at, lanes] = d
                else:
                    d = decay[at, lanes]
                return pair[0] * d, d * (ga[at, lanes] + pair[1])

            one = jnp.ones((sz.group, half), F32)
            pair = steps_of(sz.steps, 2, totals, (one, jnp.zeros_like(one)), reverse=True)
            r.chunk_p[:, lanes] = pair[0]
            r.chunk_t[:, lanes] = pair[1]
            part_totals(r.chunk_p, r.chunk_t, sz, True, prefix, mine, lanes)
            flights.append(exchange_start(1, layer, part))
            units.passed(1.5)
        need(keys.zc)

        def gate_lanes(n):
            wide = 2 * LANES
            lanes = tile(n, wide)

            def walk(j, kept):
                m, bf, bi, bc = kept
                at = tile(j, sz.group)
                d = decay[at, lanes]
                q = ga[at, lanes] + m
                a, b, zc = r.a[at, lanes], r.b[at, lanes], r.zc[at, lanes]
                vm = jnp.concatenate([valid[at, :]] * 2, axis=1)
                km = jnp.concatenate([keep[at, :]] * 2, axis=1)
                fp, ip, inv = gate_weights(a, b)
                gf = q * (r.states[at, lanes] * km - zc * vm)
                parts = (
                    (gf * (a * inv) * fp).astype(BF16),
                    (-gf * (b * inv) * ip).astype(BF16),
                    (q * vm * ip).astype(BF16),
                )
                for part, value in enumerate(parts):
                    gz[at, pl.ds(pl.multiple_of(part * sz.hidden + n * wide, wide), wide)] = value
                return (d * q,) + tuple(
                    a + value.astype(F32) for a, value in zip((bf, bi, bc), parts)
                )

            zero = jnp.zeros((sz.group, wide), F32)
            _, *sums = steps_of(
                sz.steps, 4, walk, (enter[:, lanes], zero, zero, zero), reverse=True
            )
            for part, total in enumerate(sums):
                small[0, layer * 4 + part : layer * 4 + part + 1, lanes] = jnp.sum(
                    total, axis=0, keepdims=True
                )

        turns = sz.hidden // LANES // 4
        for part in range(2):
            exchange_end(*flights[part], True, part)
            over(turns, lambda n: gate_lanes(n + part * turns))
            units.passed(2)
        freed(keys.a, keys.b, keys.zc, keys.states)
        need(keys.u)
        wide_t[...] = r.u[...].T
        freed(keys.u)
        for k in range(2):
            units.room(unit + k)

        def gate_grad(b):
            cols = pl.ds(pl.multiple_of(b * 384, 128), 256)
            value = jnp.dot(wide_t[...], gz[:, cols], preferred_element_type=F32)
            for s in range(4):
                for h in range(2):
                    at = place(h, s // 2, b % 2, (b // 2) % 2, b // 4)
                    for t in range(2):
                        held[(unit + t) % HELD, s % 2, h, at] = value[
                            s * 128 + h * 64 : s * 128 + h * 64 + 64, t * 128 : t * 128 + 128
                        ]

        over(8, gate_grad)
        units.produced(unit, unit + 1)
        unit += 2
        units.passed(3)
        units.room(unit)

        def gate_rest(z):
            right = jnp.concatenate(
                [
                    gz[:, pl.ds(pl.multiple_of((2 * z + y) * 384 + 256, 128), 128)]
                    for y in range(2)
                ],
                axis=1,
            )
            value = jnp.dot(wide_t[...], right, preferred_element_type=F32)
            for s in range(4):
                for h in range(2):
                    for y in range(2):
                        at = place(h, s // 2, y, z % 2, z // 2)
                        held[unit % HELD, s % 2, h, at] = value[
                            s * 128 + h * 64 : s * 128 + h * 64 + 64, y * 128 : y * 128 + 128
                        ]

        over(4, gate_rest)
        units.produced(unit)
        unit += 1
        units.passed(1.5)
        need(keys.gate_w, keys.stream)
        contract(gz, r.gate_w, grad, sz.width)
        freed(keys.gate_w)
        units.passed(2.5)
        norm_back(r.stream, r.mix_gain.at[layer : layer + 1], grad, gy1, gx, r.mix_sum, sz.rows, 64)
        freed(keys.stream)
        row = slice(layer * 4 + 3, layer * 4 + 4)
        small[0, row, : sz.width] = jnp.sum(r.mix_sum[...], axis=0, keepdims=True)
        small[0, row, sz.width : 2 * sz.width] = jnp.sum(r.mlp_sum[...], axis=0, keepdims=True)
        units.passed(1.5)

    forward(0)
    keep_cotangent()
    for layer in range(1, layers):
        forward(layer)
    out_copies = from_steps(gy1, r.layer_out, r.out_sems)
    cast(low, gx)
    units.passed(2)
    for index, layer in enumerate(reversed(range(layers))):
        backward(layer, 8 * index)
    units.small_start()
    for copy in out_copies:
        copy.wait()
    out_copies = from_steps(gx, r.input_grad, r.out_sems)
    units.passed(1)
    units.drain()
    for copy in out_copies:
        copy.wait()
    total = small[STAGES]
    count = jnp.int32(0)
    for s in range(r.lens.shape[0]):
        for d in range(r.lens.shape[1]):
            count = count + r.lens[s, d]
    scale = 1.0 / (count.astype(F32) * sz.hidden)
    for layer in range(layers):
        for part in range(3):
            r.gate_bias_grad[layer : layer + 1, part * sz.hidden : (part + 1) * sz.hidden] = total[
                layer * 4 + part : layer * 4 + part + 1, : sz.hidden
            ]
        row = slice(layer * 4 + 3, layer * 4 + 4)
        r.mix_gain_grad[layer : layer + 1, :] = total[row, : sz.width]
        r.mlp_gain_grad[layer : layer + 1, :] = total[row, sz.width : 2 * sz.width]
        lanes = total[layer * 4 : layer * 4 + 1, sz.hidden : sz.hidden + LANES]
        r.forget_mean[layer : layer + 1, :] = (
            jnp.sum(lanes, axis=1, keepdims=True) * scale + jnp.zeros((1, LANES), F32)
        )


def run_whole_step(sz, layers, named):
    lengths = named["lengths"]
    rows, d, h, f = sz.rows, sz.width, sz.hidden, sz.inner
    vm = lambda *dims, kind=F32: pltpu.VMEM(dims, kind)
    sems = pltpu.SemaphoreType
    spec = dict(gate_bias=VMEM, mix_gain=VMEM, mlp_gain=VMEM)
    outputs = dict(
        layer_out=(shape(rows, d), ANY),
        input_grad=(shape(rows, d), ANY),
        gate_weight_grad=(shape(layers, 128, 384), VMEM),
        gate_bias_grad=(shape(layers, 3 * h), VMEM),
        out_weight_grad=(shape(layers, 64, 256), VMEM),
        up_weight_grad=(shape(layers, 128, 256), VMEM),
        down_weight_grad=(shape(layers, 64, 512), VMEM),
        mix_gain_grad=(shape(layers, d), VMEM),
        mlp_gain_grad=(shape(layers, d), VMEM),
        forget_mean=(shape(layers, LANES), VMEM),
    )
    results = len(outputs)
    kept = dict(
        u=((rows, d), BF16),
        a=((rows, h), F32),
        b=((rows, h), F32),
        zc=((rows, h), F32),
        states=((rows + sz.group, h), F32),
        y1=((rows, d), F32),
        v=((rows, d), BF16),
        p=((rows, f), F32),
        gb=((rows, f), BF16),
        stream=((rows, d), F32),
    )
    scratch = {}
    for name, (dims, kind) in kept.items():
        outputs[name + "_save"] = (shape(layers - 1, *dims, kind=kind), ANY)
        scratch[name] = vm(*dims, kind=kind)
    scratch.update(
        gate_w=vm(d, 3 * h, kind=BF16),
        out_w=vm(h, d, kind=BF16),
        up_w=vm(d, f, kind=BF16),
        down_w=vm(f, d, kind=BF16),
        valid=vm(rows, LANES),
        keep=vm(rows, LANES),
        gx=vm(rows, d),
        low=vm(rows, d, kind=BF16),
        low_t=vm(d, rows, kind=BF16),
        wide_t=vm(d, rows, kind=BF16),
        hb=vm(rows, h, kind=BF16),
        z1=vm(rows, 768),
        forget=vm(8, LANES),
        ga=vm(rows, h),
        gz=vm(rows, 3 * h, kind=BF16),
        grad=vm(rows, d),
        gy1=vm(rows, d),
        decay=vm(rows, h),
        chunk_p=vm(sz.group, h),
        chunk_t=vm(sz.group, h),
        prefix=vm(2, sz.group, h),
        enter=vm(sz.group, h),
        mine=vm(8, h),
        slots=vm(2, layers, sz.sections, 8, h),
        mlp_sum=vm(8, d),
        mix_sum=vm(8, d),
        held=vm(HELD, 2, 2, 16, BLOCK, LANES),
        small=vm(STAGES + 1, 8, SMALL),
        small_arrived=vm(STAGES, 8, SMALL),
        in_sems=sems.DMA((3,)),
        lens=pltpu.SMEM(lengths.shape, jnp.int32),
        out_sems=sems.DMA((d // LANES,)),
        natural=vm(d // LANES, rows, LANES),
        load_sems=sems.DMA((len(kept) + 4,)),
        save_sems=sems.DMA((len(kept) + 4,)),
        pair_send=sems.DMA((2, layers, 2, sz.sections - 1)),
        pair_recv=sems.DMA((2, layers, 2, sz.sections - 1)),
        send_sems=sems.DMA((SENDS, 2 * STAGES - 1)),
        recv_sems=sems.DMA((max(RINGS), 2 * STAGES - 1)),
        credits=sems.REGULAR((2 * STAGES - 1,)),
        small_send=sems.DMA((STAGES,)),
        small_recv=sems.DMA((STAGES,)),
    )
    for stage in range(STAGES):
        scratch[f"arrived{stage}"] = vm(RINGS[stage], 2, 16 >> stage, BLOCK, LANES)
    names = list(named) + list(outputs) + list(scratch)
    out = pl.pallas_call(
        functools.partial(whole_step, sz, layers, names),
        out_shape=tuple(value for value, _ in outputs.values()),
        in_specs=[spec.get(name, ANY) for name in named],
        out_specs=[place_of for _, place_of in outputs.values()],
        scratch_shapes=list(scratch.values()),
        compiler_params=pltpu.CompilerParams(
            collective_id=4, has_side_effects=True, vmem_limit_bytes=LIMIT
        ),
        name="whole_step",
    )(*named.values())
    return out[:results]


def deliver_kernel(count, *refs):
    sources, targets, held = refs[:count], refs[count : 2 * count], refs[2 * count : 3 * count - 1]
    sems = refs[3 * count - 1]
    arrivals = [
        pltpu.make_async_copy(sources[i], held[i], sems.at[0, i]) for i in range(count - 1)
    ]
    departures = [
        pltpu.make_async_copy(held[i], targets[i], sems.at[1, i]) for i in range(count - 1)
    ]
    for copy in arrivals:
        copy.start()
    for layer in range(targets[-1].shape[0]):
        targets[-1][layer] = sources[-1][layer, 0]
    for arrival, departure in zip(arrivals, departures):
        arrival.wait()
        departure.start()
    for copy in departures:
        copy.wait()


def deliver(values):
    count = len(values)
    scalars = pl.BlockSpec(memory_space=pltpu.SMEM)
    shapes = [shape(*value.shape) for value in values[:-1]] + [shape(values[-1].shape[0])]
    return pl.pallas_call(
        functools.partial(deliver_kernel, count),
        out_shape=tuple(shapes),
        in_specs=[ANY] * (count - 1) + [scalars],
        out_specs=[ANY] * (count - 1) + [scalars],
        scratch_shapes=[pltpu.VMEM(value.shape, F32) for value in values[:-1]]
        + [pltpu.SemaphoreType.DMA((2, count - 1))],
        compiler_params=pltpu.CompilerParams(vmem_limit_bytes=LIMIT),
        name="deliver",
    )(*values)


def mask_kernel(sizes, lens, valid, keep):
    fill_masks(lens, valid, keep, sizes)


def body(
    activations,
    cotangent,
    lengths,
    gate_weight,
    gate_bias,
    out_weight,
    up_weight,
    down_weight,
    mix_gain,
    mlp_gain,
):
    micro, span, width = activations.shape
    layers = gate_weight.shape[0]
    sz = Sizes(
        micro, span, width, out_weight.shape[1], up_weight.shape[2], lax.axis_size("section")
    )

    blocks = (width // 4, 3 * sz.hidden // 8, width // 8, sz.inner // 4, sz.hidden // 4)
    axes = (lax.axis_size("section"), lax.axis_size("batch"))
    if axes == (4, 8) and blocks == (128, 384, 64, 512, 256):
        out = run_whole_step(
            sz,
            layers,
            dict(
                activations=activations.reshape(sz.rows, width),
                cotangent=cotangent.reshape(sz.rows, width),
                lengths=lengths.T,
                gate_bias=gate_bias,
                mix_gain=mix_gain,
                mlp_gain=mlp_gain,
                gate_hbm=gate_weight,
                out_hbm=out_weight,
                up_hbm=up_weight,
                down_hbm=down_weight,
            ),
        )
        stream_out, input_grad, gate_g, bias_g, out_g, up_g, down_g, *rest = deliver(out)
        return (
            stream_out.reshape(activations.shape),
            input_grad.reshape(activations.shape),
            gate_g,
            bias_g,
            out_g.transpose(0, 2, 1),
            up_g,
            down_g.transpose(0, 2, 1),
            *rest,
        )

    def arranged(value):
        value = value.astype(F32).reshape(micro, CHUNKS, sz.steps, width)
        return value.transpose(2, 0, 1, 3).reshape(sz.rows, width)

    def restored(value):
        value = value.reshape(sz.steps, micro, CHUNKS, width).transpose(1, 2, 0, 3)
        return value.reshape(micro, span, width)

    masks = pl.pallas_call(
        functools.partial(mask_kernel, sz),
        out_shape=(shape(sz.rows, LANES), shape(sz.rows, LANES)),
        in_specs=[pl.BlockSpec(memory_space=pltpu.SMEM)],
        out_specs=[VMEM] * 2,
        name="masks",
    )(lengths)
    weights = (gate_weight, out_weight, up_weight, down_weight)
    stream = arranged(activations)
    streams, saved, forgets = [], [], []
    for layer in range(layers):
        streams.append(stream)
        stream, *kept, forget, pairs = run_forward(
            sz,
            layer,
            stream,
            masks,
            gate_bias[layer : layer + 1],
            mix_gain[layer : layer + 1],
            mlp_gain[layer : layer + 1],
            weights,
        )
        saved.append((*kept, pairs))
        forgets.append(forget)
    layer_out = restored(stream)
    gx = arranged(cotangent)
    true_count = jnp.sum(lengths).astype(F32)
    forgets = [jnp.sum(forget) for forget in forgets]
    sums, small = [None] * layers, [None] * layers
    for layer in reversed(range(layers)):
        gx, gate_g, out_g, up_g, down_g, bias_g, mix_g, mlp_g = run_backward(
            sz,
            layer,
            gx,
            streams[layer],
            masks,
            mix_gain[layer : layer + 1],
            mlp_gain[layer : layer + 1],
            saved[layer],
            weights,
        )
        sums[layer] = (gate_g, out_g.T, up_g, down_g.T)
        small[layer] = tuple(jnp.sum(part, axis=0) for part in (bias_g, mix_g, mlp_g))
    input_grad = restored(gx)
    stacked = tuple(jnp.stack(parts) for parts in zip(*sums))
    partial_sums = lax.psum_scatter(stacked, "section", scatter_dimension=1, tiled=True)
    large = lax.psum_scatter(partial_sums, "batch", scatter_dimension=2, tiled=True)
    bias_grad, mix_grad, mlp_grad = (jnp.stack(parts) for parts in zip(*small))
    bias_grad, mix_grad, mlp_grad, forget = lax.psum(
        (bias_grad, mix_grad, mlp_grad, jnp.stack(forgets)), ("section", "batch")
    )
    forget_mean = forget / (true_count * sz.hidden)
    return (
        layer_out,
        input_grad,
        large[0],
        bias_grad,
        large[1],
        large[2],
        large[3],
        mix_grad,
        mlp_grad,
        forget_mean,
    )


def solution(mesh):
    stream = P("batch", "section", None)
    block = P(None, "section", "batch")
    return jax.shard_map(
        body,
        mesh=mesh,
        in_specs=(stream, stream) + (P(),) * 8,
        out_specs=(stream, stream, block, P(), block, block, block, P(), P(), P()),
        check_vma=False,
    )
```

```python
import functools
import types

import jax
import jax.numpy as jnp
from jax import lax
from jax.experimental import pallas as pl
from jax.experimental.pallas import tpu as pltpu
from jax.sharding import PartitionSpec as P

epsilon = 1e-06
MESH = pl.DeviceIdType.MESH
F32, BF16 = jnp.float32, jnp.bfloat16
CHUNKS = 8
LANES = 128
ROOT_HALF = 0.7071067811865476
ROOT_TAU = 0.3989422804014327


def tile(index, size):
    return pl.ds(pl.multiple_of(index * size, size), size)


def inverse(value):
    r = pltpu.reciprocal(value, approx=True)
    return r * (2.0 - value * r)


def normal_below(p):
    return 0.5 + 0.5 * lax.erf(p * ROOT_HALF)


def steps_of(count, unroll, one, start, reverse=False):
    def turn(i, carry):
        for k in range(unroll):
            at = i * unroll + k
            carry = one(count - 1 - at if reverse else at, carry)
        return carry

    return lax.fori_loop(0, count // unroll, turn, start)


def gate_weights(a, b):
    inv = inverse(2.0 + a + b)
    return (1.0 + b) * inv, (1.0 + a) * inv, inv


def greet_section(sections):
    me = lax.axis_index("section")
    barrier = pltpu.get_barrier_semaphore()
    for hop in range(1, sections):
        pl.semaphore_signal(
            barrier, inc=1, device_id={"section": lax.rem(me + hop, sections)}, device_id_type=MESH
        )
    pl.semaphore_wait(barrier, sections - 1)


def exchange(mine, slots, send_sems, recv_sems, sections):
    me = lax.axis_index("section")
    copies = []
    for hop in range(1, sections):
        copies.append(
            pltpu.make_async_remote_copy(
                src_ref=mine,
                dst_ref=slots.at[me],
                send_sem=send_sems.at[hop - 1],
                recv_sem=recv_sems.at[hop - 1],
                device_id={"section": lax.rem(me + hop, sections)},
                device_id_type=MESH,
            )
        )
    for copy in copies:
        copy.start()
    slots[me] = mine[...]
    for copy in copies:
        copy.wait()


def norm_rows(stream, gain, low, rows, step):
    def one(i, carry):
        at = tile(i, step)
        x = stream[at, :]
        r = lax.rsqrt(jnp.mean(x * x, axis=-1, keepdims=True) + epsilon)
        low[at, :] = (x * r * gain[...]).astype(BF16)
        return carry

    lax.fori_loop(0, rows // step, one, 0)


def norm_back(stream, gain, grad, through, out, gain_sum, rows, step):
    width = stream.shape[1]

    def one(i, total):
        at = tile(i, step)
        x = stream[at, :]
        r = lax.rsqrt(jnp.mean(x * x, axis=-1, keepdims=True) + epsilon)
        n = x * r
        g = grad[at, :]
        a = g * gain[...]
        out[at, :] = through[at, :] + r * (a - n * jnp.mean(a * n, axis=-1, keepdims=True))
        return total + jnp.sum((g * n).reshape(step // 8, 8, width), axis=0)

    gain_sum[...] = lax.fori_loop(0, rows // step, one, jnp.zeros((8, width), F32))


def fill_masks(lens, valid, keep, sizes, turned=False):
    section = lax.axis_index("section")
    group = lax.axis_index("batch")
    starts, totals = [], []
    for s in range(sizes.micro):
        total, begin = 0, []
        for d in range(lens.shape[0 if turned else 1]):
            row = group * sizes.micro + s
            length = lens[d, row] if turned else lens[row, d]
            begin.append(jnp.where(length > 0, total, -1))
            total = total + length
        starts.append(begin)
        totals.append(total)
    chunk_place = lax.broadcasted_iota(jnp.int32, (8, LANES), 0) * sizes.steps

    def one(j, carry):
        for s in range(sizes.micro):
            place = section * sizes.span + j + chunk_place
            true = place < totals[s]
            first = place == starts[s][0]
            for begin in starts[s][1:]:
                first = first | (place == begin)
            at = pl.ds(pl.multiple_of(j * sizes.group + s * 8, 8), 8)
            valid[at, :] = jnp.where(true, 1.0, 0.0)
            keep[at, :] = jnp.where(true & jnp.logical_not(first), 1.0, 0.0)
        return carry

    lax.fori_loop(0, sizes.steps, one, 0)


def scan_totals(first, second, sizes, reverse, prefix, chunk, mine):
    for s in range(sizes.micro):
        p = jnp.ones((1, sizes.hidden), F32)
        t = jnp.zeros((1, sizes.hidden), F32)
        for c in reversed(range(CHUNKS)) if reverse else range(CHUNKS):
            at = s * 8 + c
            prefix[0, at : at + 1, :] = p
            prefix[1, at : at + 1, :] = t
            pc = first[at : at + 1, :]
            t = pc * t + second[at : at + 1, :]
            p = p * pc
        mine[s : s + 1, :] = p
        mine[sizes.micro + s : sizes.micro + s + 1, :] = t


def scan_enter(slots, prefix, enter, sizes, reverse):
    me = lax.axis_index("section")
    for s in range(sizes.micro):
        a = jnp.zeros((1, sizes.hidden), F32)
        order = range(sizes.sections - 1, 0, -1) if reverse else range(sizes.sections - 1)
        for k in order:
            reached = k > me if reverse else k < me
            pk = slots[k, s : s + 1, :]
            tk = slots[k, sizes.micro + s : sizes.micro + s + 1, :]
            a = jnp.where(reached, pk * a + tk, a)
        at = slice(s * 8, s * 8 + 8)
        enter[at, :] = prefix[0, at, :] * a + prefix[1, at, :]


def part_totals(first, second, sizes, reverse, prefix, mine, lanes):
    for s in range(sizes.micro):
        p = jnp.ones((1, lanes.stop - lanes.start), F32)
        t = jnp.zeros_like(p)
        for c in reversed(range(CHUNKS)) if reverse else range(CHUNKS):
            at = s * 8 + c
            prefix[0, at : at + 1, lanes] = p
            prefix[1, at : at + 1, lanes] = t
            pc = first[at : at + 1, lanes]
            t = pc * t + second[at : at + 1, lanes]
            p = p * pc
        mine[s : s + 1, lanes] = p
        mine[sizes.micro + s : sizes.micro + s + 1, lanes] = t


def part_enter(slots, prefix, enter, sizes, reverse, lanes):
    me = lax.axis_index("section")
    for s in range(sizes.micro):
        a = jnp.zeros((1, lanes.stop - lanes.start), F32)
        order = range(sizes.sections - 1, 0, -1) if reverse else range(sizes.sections - 1)
        for k in order:
            reached = k > me if reverse else k < me
            pk = slots[k, s : s + 1, lanes]
            tk = slots[k, sizes.micro + s : sizes.micro + s + 1, lanes]
            a = jnp.where(reached, pk * a + tk, a)
        at = slice(s * 8, s * 8 + 8)
        enter[at, lanes] = prefix[0, at, lanes] * a + prefix[1, at, lanes]


class Sizes:
    def __init__(self, micro, span, width, hidden, inner, sections):
        self.micro, self.span, self.width = micro, span, width
        self.hidden, self.inner, self.sections = hidden, inner, sections
        self.rows = micro * span
        self.steps = span // CHUNKS
        self.group = micro * CHUNKS


def forward_kernel(
    sizes,
    layer,
    stream,
    valid,
    keep,
    bias,
    mix_gain,
    mlp_gain,
    gate_hbm,
    out_hbm,
    up_hbm,
    down_hbm,
    next_stream,
    u,
    sf_out,
    si_out,
    zc_out,
    states,
    y1,
    v,
    p_out,
    gb,
    forget,
    pair_slots,
    gate_w,
    out_w,
    up_w,
    down_w,
    z,
    decay,
    drive,
    hb,
    chunk_p,
    chunk_t,
    prefix,
    enter,
    mine,
    weight_sems,
    send_sems,
    recv_sems,
):
    sz = sizes
    loads = [
        pltpu.make_async_copy(src.at[layer], dst, weight_sems.at[i])
        for i, (src, dst) in enumerate(
            ((gate_hbm, gate_w), (out_hbm, out_w), (up_hbm, up_w), (down_hbm, down_w))
        )
    ]
    for load in loads:
        load.start()
    greet_section(sz.sections)
    mine[...] = jnp.zeros_like(mine)
    norm_rows(stream, mix_gain, u, sz.rows, 64)
    loads[0].wait()
    forget[...] = jnp.zeros_like(forget)
    hw = 256

    def gate_tile(n, carry):
        for part in range(3):
            cols = pl.ds(pl.multiple_of(part * sz.hidden + n * hw, hw), hw)
            z[:, part * hw : (part + 1) * hw] = (
                jnp.dot(u[...], gate_w[:, cols], preferred_element_type=F32) + bias[:, cols]
            )

        def one(i, inner):
            at = tile(i, 64)
            for lane in range(hw // LANES):
                src = lambda part: z[
                    at, part * hw + lane * LANES : part * hw + (lane + 1) * LANES
                ]
                dst = pl.ds(pl.multiple_of(n * hw + lane * LANES, LANES), LANES)
                a = jnp.exp(jnp.minimum(-src(0), 86.0))
                b = jnp.exp(jnp.minimum(-src(1), 86.0))
                zc = src(2)
                fp, ip, _ = gate_weights(a, b)
                vm = valid[at, :]
                decay[at, dst] = fp * keep[at, :]
                drive[at, dst] = ip * zc * vm
                sf_out[at, dst] = a
                si_out[at, dst] = b
                zc_out[at, dst] = zc
                forget[...] += jnp.sum((fp * vm).reshape(8, 8, LANES), axis=0)
            return inner

        lax.fori_loop(0, sz.rows // 64, one, 0)
        return carry

    lax.fori_loop(0, sz.hidden // hw, gate_tile, 0)
    half = sz.hidden // 2
    for part in range(2):
        lanes = slice(part * half, (part + 1) * half)

        def totals(j, pair):
            at = tile(j, sz.group)
            d = decay[at, lanes]
            return pair[0] * d, pair[1] * d + drive[at, lanes]

        one = jnp.ones((sz.group, half), F32)
        pair = steps_of(sz.steps, 4, totals, (one, jnp.zeros_like(one)))
        chunk_p[:, lanes] = pair[0]
        chunk_t[:, lanes] = pair[1]
    scan_totals(chunk_p, chunk_t, sz, False, prefix, None, mine)
    exchange(mine, pair_slots, send_sems, recv_sems, sz.sections)
    scan_enter(pair_slots, prefix, enter, sz, False)
    states[0 : sz.group, :] = enter[...]
    for part in range(2):
        lanes = slice(part * half, (part + 1) * half)

        def walk(j, h):
            at = tile(j, sz.group)
            h = decay[at, lanes] * h + drive[at, lanes]
            states[tile(j + 1, sz.group), lanes] = h
            hb[at, lanes] = h.astype(BF16)
            return h

        steps_of(sz.steps, 4, walk, enter[:, lanes])
    loads[1].wait()

    def out_tile(n, carry):
        cols = tile(n, 256)
        y1[:, cols] = stream[:, cols] + jnp.dot(
            hb[...], out_w[:, cols], preferred_element_type=F32
        )
        return carry

    lax.fori_loop(0, sz.width // 256, out_tile, 0)
    norm_rows(y1, mlp_gain, v, sz.rows, 64)
    loads[2].wait()

    def up_tile(n, carry):
        cols = tile(n, 256)
        p_out[:, cols] = jnp.dot(v[...], up_w[:, cols], preferred_element_type=F32)

        def one(i, inner):
            at = tile(i, 64)
            p = p_out[at, cols]
            gb[at, cols] = (p * normal_below(p)).astype(BF16)
            return inner

        lax.fori_loop(0, sz.rows // 64, one, 0)
        return carry

    lax.fori_loop(0, sz.inner // 256, up_tile, 0)
    loads[3].wait()

    def down_tile(n, carry):
        cols = tile(n, 256)
        next_stream[:, cols] = y1[:, cols] + jnp.dot(
            gb[...], down_w[:, cols], preferred_element_type=F32
        )
        return carry

    lax.fori_loop(0, sz.width // 256, down_tile, 0)


def backward_kernel(
    sizes,
    layer,
    gx,
    stream,
    valid,
    keep,
    mix_gain,
    mlp_gain,
    u,
    sf_in,
    si_in,
    zc_in,
    states,
    y1,
    v,
    p_in,
    gb,
    pair_slots,
    gate_hbm,
    out_hbm,
    up_hbm,
    down_hbm,
    next_gx,
    gate_grad,
    out_grad,
    up_grad,
    down_grad,
    bias_sum,
    mix_sum,
    mlp_sum,
    gate_w,
    out_w,
    up_w,
    down_w,
    low,
    low_t,
    wide_t,
    hb,
    ga,
    gp,
    gz,
    grad,
    gy1,
    decay,
    chunk_p,
    chunk_t,
    prefix,
    enter,
    mine,
    slots,
    weight_sems,
    send_sems,
    recv_sems,
):
    sz = sizes
    loads = [
        pltpu.make_async_copy(src.at[layer], dst, weight_sems.at[i])
        for i, (src, dst) in enumerate(
            ((gate_hbm, gate_w), (out_hbm, out_w), (up_hbm, up_w), (down_hbm, down_w))
        )
    ]
    for load in reversed(loads):
        load.start()
    greet_section(sz.sections)
    mine[...] = jnp.zeros_like(mine)

    def cast(i, carry):
        at = tile(i, 64)
        low[at, :] = gx[at, :].astype(BF16)
        return carry

    lax.fori_loop(0, sz.rows // 64, cast, 0)
    low_t[...] = low[...].T

    def weight_grad(left_t, right, dst, step):
        def one(n, carry):
            cols = tile(n, step)
            dst[:, cols] = jnp.dot(left_t[...], right[:, cols], preferred_element_type=F32)
            return carry

        lax.fori_loop(0, right.shape[1] // step, one, 0)

    weight_grad(low_t, gb, down_grad, 256)
    loads[3].wait()

    def act_tile(n, carry):
        cols = tile(n, 256)
        ga[:, :256] = lax.dot_general(
            low[...], down_w[cols, :], (((1,), (1,)), ((), ())), preferred_element_type=F32
        )

        def one(i, inner):
            at = tile(i, 64)
            p = p_in[at, cols]
            slope = normal_below(p) + ROOT_TAU * p * jnp.exp(-0.5 * p * p)
            gp[at, cols] = (ga[at, :256] * slope).astype(BF16)
            return inner

        lax.fori_loop(0, sz.rows // 64, one, 0)
        return carry

    lax.fori_loop(0, sz.inner // 256, act_tile, 0)
    wide_t[...] = v[...].T
    weight_grad(wide_t, gp, up_grad, 256)
    loads[2].wait()

    def contract(left, weight, dst, step):
        def one(n, carry):
            cols = tile(n, step)
            dst[:, cols] = lax.dot_general(
                left[...], weight[cols, :], (((1,), (1,)), ((), ())), preferred_element_type=F32
            )
            return carry

        lax.fori_loop(0, weight.shape[0] // step, one, 0)

    contract(gp, up_w, grad, 256)
    norm_back(y1, mlp_gain, grad, gx, gy1, mlp_sum, sz.rows, 64)

    def cast_more(i, carry):
        at = tile(i, 64)
        low[at, :] = gy1[at, :].astype(BF16)
        return carry

    lax.fori_loop(0, sz.rows // 64, cast_more, 0)

    def cast_state(i, carry):
        hb[tile(i, sz.group), :] = states[tile(i + 1, sz.group), :].astype(BF16)
        return carry

    lax.fori_loop(0, sz.steps, cast_state, 0)
    low_t[...] = low[...].T
    weight_grad(low_t, hb, out_grad, 256)
    loads[1].wait()
    contract(low, out_w, ga, 256)
    half = sz.hidden // 2
    for part in range(2):
        lanes = slice(part * half, (part + 1) * half)

        def totals(i, pair):
            at = tile(sz.steps - 1 - i, sz.group)
            mask = jnp.concatenate([keep[at, :]] * (half // LANES), axis=1)
            d = gate_weights(sf_in[at, lanes], si_in[at, lanes])[0] * mask
            decay[at, lanes] = d
            return pair[0] * d, d * (ga[at, lanes] + pair[1])

        pair = lax.fori_loop(
            0,
            sz.steps,
            totals,
            (jnp.ones((sz.group, half), F32), jnp.zeros((sz.group, half), F32)),
        )
        chunk_p[:, lanes] = pair[0]
        chunk_t[:, lanes] = pair[1]
    scan_totals(chunk_p, chunk_t, sz, True, prefix, None, mine)
    exchange(mine, slots, send_sems, recv_sems, sz.sections)
    scan_enter(slots, prefix, enter, sz, True)

    def gate_lane(n, carry):
        lanes = tile(n, LANES)

        def walk(i, kept):
            m, bf, bi, bc = kept
            j = sz.steps - 1 - i
            at = tile(j, sz.group)
            d = decay[at, lanes]
            q = ga[at, lanes] + m
            a = sf_in[at, lanes]
            b = si_in[at, lanes]
            zc = zc_in[at, lanes]
            vm = valid[at, :]
            fp, ip, inv = gate_weights(a, b)
            gf = q * (states[at, lanes] * keep[at, :] - zc * vm)
            gzf = (gf * (a * inv) * fp).astype(BF16)
            gzi = (-gf * (b * inv) * ip).astype(BF16)
            gzc = (q * vm * ip).astype(BF16)
            gz[at, lanes] = gzf
            gz[at, pl.ds(pl.multiple_of(sz.hidden + n * LANES, LANES), LANES)] = gzi
            gz[at, pl.ds(pl.multiple_of(2 * sz.hidden + n * LANES, LANES), LANES)] = gzc
            return (
                d * q,
                bf + gzf.astype(F32),
                bi + gzi.astype(F32),
                bc + gzc.astype(F32),
            )

        zero = jnp.zeros((sz.group, LANES), F32)
        _, bf, bi, bc = lax.fori_loop(0, sz.steps, walk, (enter[:, lanes], zero, zero, zero))
        for part, total in enumerate((bf, bi, bc)):
            where = pl.ds(pl.multiple_of(part * sz.hidden + n * LANES, LANES), LANES)
            bias_sum[:, where] = jnp.sum(total.reshape(sz.group // 8, 8, LANES), axis=0)
        return carry

    lax.fori_loop(0, sz.hidden // LANES, gate_lane, 0)
    wide_t[...] = u[...].T
    weight_grad(wide_t, gz, gate_grad, 256)
    loads[0].wait()
    contract(gz, gate_w, grad, 256)
    norm_back(stream, mix_gain, grad, gy1, next_gx, mix_sum, sz.rows, 64)


VMEM = pl.BlockSpec(memory_space=pltpu.VMEM)
ANY = pl.BlockSpec(memory_space=pl.ANY)
LIMIT = 62 * 2**20


def shape(*dims, kind=F32):
    return jax.ShapeDtypeStruct(dims, kind)


def exchange_scratch(sz):
    return [
        pltpu.SemaphoreType.DMA((4,)),
        pltpu.SemaphoreType.DMA((sz.sections - 1,)),
        pltpu.SemaphoreType.DMA((sz.sections - 1,)),
    ]


def weight_scratch(sz):
    return [
        pltpu.VMEM((sz.width, 3 * sz.hidden), BF16),
        pltpu.VMEM((sz.hidden, sz.width), BF16),
        pltpu.VMEM((sz.width, sz.inner), BF16),
        pltpu.VMEM((sz.inner, sz.width), BF16),
    ]


def scan_scratch(sz):
    return [
        pltpu.VMEM((sz.group, sz.hidden), F32),
        pltpu.VMEM((sz.group, sz.hidden), F32),
        pltpu.VMEM((2, sz.group, sz.hidden), F32),
        pltpu.VMEM((sz.group, sz.hidden), F32),
        pltpu.VMEM((8, sz.hidden), F32),
    ]


def run_forward(sz, layer, stream, masks, bias, mix_gain, mlp_gain, weights):
    r, d, h, f = sz.rows, sz.width, sz.hidden, sz.inner
    return pl.pallas_call(
        functools.partial(forward_kernel, sz, layer),
        out_shape=(
            shape(r, d),
            shape(r, d, kind=BF16),
            shape(r, h),
            shape(r, h),
            shape(r, h),
            shape(r + sz.group, h),
            shape(r, d),
            shape(r, d, kind=BF16),
            shape(r, f),
            shape(r, f, kind=BF16),
            shape(8, LANES),
            shape(sz.sections, 8, h),
        ),
        in_specs=[VMEM] * 6 + [ANY] * 4,
        out_specs=[VMEM] * 12,
        scratch_shapes=weight_scratch(sz)
        + [
            pltpu.VMEM((r, 3 * 256), F32),
            pltpu.VMEM((r, h), F32),
            pltpu.VMEM((r, h), F32),
            pltpu.VMEM((r, h), BF16),
        ]
        + scan_scratch(sz)
        + exchange_scratch(sz),
        compiler_params=pltpu.CompilerParams(
            collective_id=layer, has_side_effects=True, vmem_limit_bytes=LIMIT
        ),
        name=f"forward_{layer}",
    )(stream, *masks, bias, mix_gain, mlp_gain, *weights)


def run_backward(sz, layer, gx, stream, masks, mix_gain, mlp_gain, saved, weights):
    r, d, h, f = sz.rows, sz.width, sz.hidden, sz.inner
    return pl.pallas_call(
        functools.partial(backward_kernel, sz, layer),
        out_shape=(
            shape(r, d),
            shape(d, 3 * h),
            shape(d, h),
            shape(d, f),
            shape(d, f),
            shape(8, 3 * h),
            shape(8, d),
            shape(8, d),
        ),
        in_specs=[VMEM] * 16 + [ANY] * 4,
        out_specs=[VMEM] * 8,
        scratch_shapes=weight_scratch(sz)
        + [
            pltpu.VMEM((r, d), BF16),
            pltpu.VMEM((d, r), BF16),
            pltpu.VMEM((d, r), BF16),
            pltpu.VMEM((r, h), BF16),
            pltpu.VMEM((r, h), F32),
            pltpu.VMEM((r, f), BF16),
            pltpu.VMEM((r, 3 * h), BF16),
            pltpu.VMEM((r, d), F32),
            pltpu.VMEM((r, d), F32),
            pltpu.VMEM((r, h), F32),
        ]
        + scan_scratch(sz)
        + [pltpu.VMEM((sz.sections, 8, h), F32)]
        + exchange_scratch(sz),
        compiler_params=pltpu.CompilerParams(
            collective_id=2 + layer, has_side_effects=True, vmem_limit_bytes=LIMIT
        ),
        name=f"backward_{layer}",
    )(gx, stream, *masks, mix_gain, mlp_gain, *saved, *weights)


BLOCK = 64
HELD = 3
RINGS = (4, 5, 6, 16, 16)
SENDS = 16
STAGES = 5
WINDOW = 4
SMALL = 1280


class Units:
    def __init__(self, count, refs):
        self.count = count
        self.__dict__.update(vars(refs))
        self.arrived = [getattr(refs, f"arrived{stage}") for stage in range(STAGES)]
        section, batch = lax.axis_index("section"), lax.axis_index("batch")
        core, x = section % 2, section // 2
        y, za, zb = batch % 2, (batch // 2) % 2, batch // 4
        self.core = core
        self.bits = ((x, za, y, zb), (y, za, x, zb))
        self.names = (("x", "za", "y", "zb"), ("y", "za", "x", "zb"))
        self.partner = {
            "core": {"section": section + 1 - 2 * core},
            "x": {"section": section + 2 - 4 * x},
            "y": {"batch": batch + 1 - 2 * y},
            "za": {"batch": batch + 2 - 4 * za},
            "zb": {"batch": batch + 4 - 8 * zb},
        }
        self.now = 0.0
        self.links = ("core", "x", "y", "z")
        self.free_at = dict.fromkeys(self.links, 0.0)
        self.flying = dict.fromkeys(self.links, 0)
        self.window = dict.fromkeys(self.links, WINDOW)
        self.queues = {link: [] for link in self.links}
        self.ready = {}
        self.summed = set()
        self.copies = {}
        self.small_left = None

    def greet(self):
        barrier = pltpu.get_barrier_semaphore()
        section = lax.axis_index("section")
        others = [self.partner["y"], self.partner["za"], self.partner["zb"]]
        others += [{"section": lax.rem(section + hop, 4)} for hop in range(1, 4)]
        for other in others:
            pl.semaphore_signal(barrier, inc=1, device_id=other, device_id_type=MESH)
        pl.semaphore_wait(barrier, len(others))

    def name(self, stage, half):
        return "core" if stage == 0 else self.names[half][stage - 1]

    def link(self, stage, half):
        name = self.name(stage, half)
        return "z" if name[0] == "z" else name

    def arrival(self, unit, stage, half):
        ref = self.arrived[stage].at[unit % RINGS[stage]]
        return ref if stage == 0 else ref.at[half]

    def copy(self, unit, stage, half):
        at = 0 if stage == 0 else 2 * stage - 1 + half
        if stage == 0:
            src = self.held.at[unit % HELD, 1 - self.core]
        else:
            count = 16 >> stage
            src = self.arrived[stage - 1].at[unit % RINGS[stage - 1], half]
            src = src.at[pl.ds((1 - self.bits[half][stage - 1]) * count, count)]
        return pltpu.make_async_remote_copy(
            src_ref=src,
            dst_ref=self.arrival(unit, stage, half),
            send_sem=self.send_sems.at[unit % SENDS, at],
            recv_sem=self.recv_sems.at[unit % RINGS[stage], at],
            device_id=self.partner[self.name(stage, half)],
            device_id_type=MESH,
        )

    def has_place(self, unit, stage, half):
        before = unit - RINGS[stage]
        if before < 0:
            return True
        if stage == 0:
            return (before, 1, 0) in self.summed and (before, 1, 1) in self.summed
        return (before, min(stage + 1, STAGES - 1), half) in self.summed

    def credit(self, unit, stage, half):
        if unit + RINGS[stage] < self.count:
            pl.semaphore_signal(
                self.credits.at[0 if stage == 0 else 2 * stage - 1 + half],
                inc=1,
                device_id=self.partner[self.name(stage, half)],
                device_id_type=MESH,
            )

    def pump(self):
        for link, queue in self.queues.items():
            while self.flying[link] < self.window[link]:
                key = next((key for key in queue if self.has_place(*key)), None)
                if key is None:
                    break
                queue.remove(key)
                self.flying[link] += 1
                unit, stage, half = key
                if unit >= RINGS[stage]:
                    at = 0 if stage == 0 else 2 * stage - 1 + half
                    pl.semaphore_wait(self.credits.at[at], 1)
                self.copies[key] = self.copy(*key)
                self.copies[key].start()
                blocks = 32 if stage == 0 else 16 >> stage
                self.ready[key] = self.expect(link, blocks * BLOCK * LANES * 4)

    def expect(self, link, size):
        rate = 250e3 if link == "core" else 45e3
        self.free_at[link] = max(self.now, self.free_at[link]) + size / rate
        return self.free_at[link] + 1.5

    def hold(self, link, window):
        self.window[link] = window
        self.pump()

    def push(self, unit, stage, half):
        self.queues[self.link(stage, half)].append((unit, stage, half))
        self.pump()

    def produced(self, us, *which):
        self.now += us
        for unit in which:
            self.push(unit, 0, 0)
        self.passed(0)

    def add(self, dst, src, count):
        turn = min(count, 4)

        def one(i, carry):
            for k in range(turn):
                dst[i * turn + k] += src[i * turn + k]
            return carry

        if count == turn:
            one(0, 0)
        else:
            lax.fori_loop(0, count // turn, one, 0)

    def step(self, unit, stage, half):
        key = (unit, stage, half)
        del self.ready[key]
        assert unit == 0 or (unit - 1, stage, half) in self.summed
        self.copies[key].wait_recv()
        here = self.arrival(unit, stage, half)
        if stage == 0:
            for h in range(2):
                self.add(here.at[h], self.held.at[unit % HELD, self.core, h], 16)
        else:
            count = 16 >> stage
            before = self.arrived[stage - 1].at[unit % RINGS[stage - 1], half]
            self.add(here, before.at[pl.ds(self.bits[half][stage - 1] * count, count)], count)
            self.copies.pop(key).wait_send()
        self.summed.add(key)
        self.flying[self.link(stage, half)] -= 1
        self.now += 0.25
        if stage > 1 or (unit, 1, 1 - half) in self.summed:
            if stage > 0:
                self.credit(unit, stage - 1, half if stage > 1 else 0)
        if stage == 0:
            for h in range(2):
                self.push(unit, 1, h)
        elif stage < STAGES - 1:
            self.push(unit, stage + 1, half)
        else:
            self.finish(unit, half, here[0])
            self.credit(unit, stage, half)
        self.pump()

    def finish(self, unit, half, block):
        layer, k = self.count // 8 - 1 - unit // 8, unit % 8
        if k < 2 or k == 4:
            ref, at = (self.down_weight_grad, k) if k < 2 else (self.out_weight_grad, 0)
            ref[layer, :, at * 256 + half * 128 : at * 256 + half * 128 + 128] = block
        else:
            ref, at = (self.up_weight_grad, k - 2) if k < 4 else (self.gate_weight_grad, k - 5)
            rows = slice(half * BLOCK, half * BLOCK + BLOCK)
            ref[layer, rows, at * LANES : at * LANES + LANES] = block

    def small_copy(self, stage):
        name = ("core", "x", "y", "za", "zb")[stage]
        return pltpu.make_async_remote_copy(
            src_ref=self.small.at[stage],
            dst_ref=self.small_arrived.at[stage],
            send_sem=self.small_send.at[stage],
            recv_sem=self.small_recv.at[stage],
            device_id=self.partner[name],
            device_id_type=MESH,
        )

    def small_start(self):
        self.small_left = 0
        self.small_copies = [self.small_copy(0)]
        self.small_copies[0].start()
        self.small_ready = self.now + 3.0

    def small_step(self):
        stage = self.small_left
        self.small_copies[stage].wait_recv()
        self.small[stage + 1] = self.small[stage] + self.small_arrived[stage]
        self.small_left += 1
        if self.small_left < STAGES:
            self.small_copies.append(self.small_copy(self.small_left))
            self.small_copies[-1].start()
            self.small_ready = self.now + 3.0
        else:
            for copy in self.small_copies:
                copy.wait_send()

    def open(self, unit, stage, half):
        halves = range(2) if stage == 0 else (half,)
        before = unit - RING
        return (
            before < 0
            or stage == STAGES - 1
            or all((before, stage + 1, h) in self.consumed for h in halves)
        )

    def next(self):
        best = min(self.ready.items(), key=lambda item: (item[1], item[0]), default=None)
        small = self.small_left is not None and self.small_left < STAGES
        if small and (best is None or self.small_ready <= best[1]):
            return self.small_ready, None
        return (best[1], best[0]) if best else None

    def take(self, item):
        self.now = max(self.now, item[0])
        if item[1] is None:
            self.small_step()
        else:
            self.step(*item[1])

    def passed(self, us):
        self.now += us
        while (item := self.next()) and item[0] <= self.now:
            self.take(item)

    def room(self, unit):
        before = (unit - HELD, 0, 0)
        while unit >= HELD and before not in self.summed:
            self.take(self.next())
        if before in self.copies:
            self.copies.pop(before).wait_send()

    def drain(self):
        while item := self.next():
            self.take(item)
        for key in list(self.copies):
            self.copies.pop(key).wait_send()


def place(half, x, y, za, zb):
    return (x * 8 + za * 4 + y * 2 + zb) if half == 0 else (y * 8 + za * 4 + x * 2 + zb)


def strided(start, steps):
    return pl.ds(start, CHUNKS, stride=steps)


def whole_step(sz, layers, names, *args):
    r = types.SimpleNamespace(**dict(zip(names, args)))
    units = Units(8 * layers, r)
    valid, keep, low, low_t, wide_t = r.valid, r.keep, r.low, r.low_t, r.wide_t
    hb, ga, gz, grad, gy1, gx = r.hb, r.ga, r.gz, r.grad, r.gy1, r.gx
    gp = gz.at[:, : sz.inner]
    decay, enter, prefix, mine = r.decay, r.enter, r.prefix, r.mine
    small, held = r.small, r.held
    natural = r.natural
    last = layers - 1
    half = sz.hidden // 2
    z0, z1 = ga.at[:, :768], r.z1
    drive = r.p.at[:, : sz.hidden]
    homes = dict(gate_w=r.gate_hbm, out_w=r.out_hbm, up_w=r.up_hbm, down_w=r.down_hbm)
    homes.update(u=r.u_save, a=r.a_save, b=r.b_save, zc=r.zc_save, states=r.states_save)
    homes.update(y1=r.y1_save, v=r.v_save, p=r.p_save, gb=r.gb_save, stream=r.stream_save)
    keys = types.SimpleNamespace(**{name: name for name in homes})
    index_of = {name: i for i, name in enumerate(homes)}
    loads, saves = {}, {}

    def load(layer, name):
        copy = pltpu.make_async_copy(
            homes[name].at[layer], getattr(r, name), r.load_sems.at[index_of[name]]
        )
        copy.start()
        loads[name] = copy

    def need(*wanted):
        for name in wanted:
            if name in loads:
                loads.pop(name).wait()

    def save(layer, name, ref=None):
        if layer < last:
            src = getattr(r, name) if ref is None else ref
            copy = pltpu.make_async_copy(
                src, homes[name].at[layer], r.save_sems.at[index_of[name]]
            )
            copy.start()
            saves[name] = copy

    def settled(*which):
        for name in which:
            if name in saves:
                saves.pop(name).wait()

    def over(count, one):
        def each(i, carry):
            one(i)
            return carry

        lax.fori_loop(0, count, each, 0)

    act_load = pltpu.make_async_copy(r.activations, hb.at[:, : sz.width], r.in_sems.at[0])
    cot_load = pltpu.make_async_copy(r.cotangent, wide_t, r.in_sems.at[1])
    len_load = pltpu.make_async_copy(r.lengths, r.lens, r.in_sems.at[2])
    len_load.start()
    act_load.start()
    for name in (keys.gate_w, keys.out_w, keys.up_w, keys.down_w):
        load(0, name)
    cot_load.start()
    units.greet()
    mine[...] = jnp.zeros_like(mine)
    small[0] = jnp.zeros((8, SMALL), F32)
    len_load.wait()
    fill_masks(r.lens, valid, keep, sz, True)

    def to_steps(src, put):
        def cast(i):
            at = tile(i, 64)
            for k in range(sz.width // LANES):
                natural[k, at, :] = src[at, k * LANES : (k + 1) * LANES].astype(F32)

        over(sz.rows // 64, cast)

        def gather(j):
            for k in range(sz.width // LANES):
                parts = [
                    natural[k, strided(s * sz.span + j, sz.steps), :] for s in range(sz.micro)
                ]
                put(tile(j, sz.group), slice(k * LANES, (k + 1) * LANES), jnp.concatenate(parts, axis=0))

        over(sz.steps, gather)

    def from_steps(src, dst, sem):
        def scatter(j):
            for k in range(sz.width // LANES):
                value = src[tile(j, sz.group), k * LANES : (k + 1) * LANES]
                for s in range(sz.micro):
                    natural[k, strided(s * sz.span + j, sz.steps), :] = value[s * 8 : s * 8 + 8]

        over(sz.steps, scatter)
        copies = []
        for k in range(sz.width // LANES):
            lanes = slice(k * LANES, (k + 1) * LANES)
            copies.append(pltpu.make_async_copy(natural.at[k], dst.at[:, lanes], sem.at[k]))
            copies[-1].start()
        return copies

    act_load.wait()

    def put_gx(at, lanes, value):
        gx[at, lanes] = value

    to_steps(hb.at[:, : sz.width], put_gx)

    parts = [slice(part * half, (part + 1) * half) for part in range(2)]

    def exchange_start(way, layer, part):
        lanes = parts[part]
        slots = r.slots.at[way, layer]
        me = lax.axis_index("section")
        copies = []
        for hop in range(1, sz.sections):
            copies.append(
                pltpu.make_async_remote_copy(
                    src_ref=mine.at[:, lanes],
                    dst_ref=slots.at[me, :, lanes],
                    send_sem=r.pair_send.at[way, layer, part, hop - 1],
                    recv_sem=r.pair_recv.at[way, layer, part, hop - 1],
                    device_id={"section": lax.rem(me + hop, sz.sections)},
                    device_id_type=MESH,
                )
            )
        for copy in copies:
            copy.start()
        slots[me, :, lanes] = mine[:, lanes]
        return slots, copies

    def exchange_end(slots, copies, reverse, part):
        for copy in copies:
            copy.wait()
        part_enter(slots, prefix, enter, sz, reverse, parts[part])

    def in_turn(count, dots, rest, after=None):
        zs = (z0, z1)
        over(sz.rows // 256, lambda i: dots(0, zs[0], i))
        for n in range(count):

            def both(i):
                if n + 1 < count:
                    dots(n + 1, zs[(n + 1) % 2], i)
                rest(n, zs[n % 2], i)

            over(sz.rows // 256, both)
            if after is not None:
                after(n)

    def keep_cotangent():
        cot_load.wait()

        def put_low(at, lanes, value):
            low[at, lanes] = value.astype(BF16)

        to_steps(wide_t, put_low)
        low_t[...] = low[...].T

    def forward(layer):
        stream = r.stream if layer > 0 else gx
        settled(keys.u)
        norm_rows(stream, r.mix_gain.at[layer : layer + 1], r.u, sz.rows, 128)
        save(layer, keys.u)
        if layer == 0:
            save(layer, keys.stream, gx)
        need(keys.gate_w)
        settled(keys.a, keys.b, keys.zc, keys.p)
        hw = 256
        bias = r.gate_bias

        def gate_dots(n, z, i):
            rows = tile(i, 256)
            for part in range(3):
                cols = slice(part * sz.hidden + n * hw, part * sz.hidden + (n + 1) * hw)
                z[rows, part * hw : (part + 1) * hw] = (
                    jnp.dot(r.u[rows, :], r.gate_w[:, cols], preferred_element_type=F32)
                    + bias[layer : layer + 1, cols]
                )

        def gate_rest(n, z, i):
            for chunk in range(4):
                at = pl.ds(pl.multiple_of(i * 256 + chunk * 64, 64), 64)
                vm, km = valid[at, :], keep[at, :]
                for lane in range(hw // LANES):
                    zf, zi, zc = (
                        z[at, part * hw + lane * LANES : part * hw + (lane + 1) * LANES]
                        for part in range(3)
                    )
                    dst = slice(n * hw + lane * LANES, n * hw + (lane + 1) * LANES)
                    a = jnp.exp(jnp.minimum(-zf, 86.0))
                    b = jnp.exp(jnp.minimum(-zi, 86.0))
                    fp, ip, _ = gate_weights(a, b)
                    decay[at, dst] = fp * km
                    drive[at, dst] = ip * zc * vm
                    r.a[at, dst] = a
                    r.b[at, dst] = b
                    r.zc[at, dst] = zc
                    r.forget[...] += jnp.sum((fp * vm).reshape(8, 8, LANES), axis=0)

        flights = []

        def gate_after(n):
            if n % 2 == 0:
                return
            lanes = parts[n // 2]

            def totals(j, pair):
                at = tile(j, sz.group)
                d = decay[at, lanes]
                return pair[0] * d, pair[1] * d + drive[at, lanes]

            one = jnp.ones((sz.group, half), F32)
            pair = steps_of(sz.steps, 2, totals, (one, jnp.zeros_like(one)))
            r.chunk_p[:, lanes] = pair[0]
            r.chunk_t[:, lanes] = pair[1]
            part_totals(r.chunk_p, r.chunk_t, sz, False, prefix, mine, lanes)
            flights.append(exchange_start(0, layer, n // 2))

        r.forget[...] = jnp.zeros_like(r.forget)
        in_turn(sz.hidden // hw, gate_dots, gate_rest, gate_after)
        small[0, layer * 4 : layer * 4 + 1, sz.hidden : sz.hidden + LANES] = jnp.sum(
            r.forget[...], axis=0, keepdims=True
        )
        for name in (keys.a, keys.b, keys.zc):
            save(layer, name)
        if layer < last:
            load(layer + 1, keys.gate_w)
        settled(keys.states, keys.y1, keys.v, keys.gb, keys.stream)
        states = r.states
        for part, lanes in enumerate(parts):
            exchange_end(*flights[part], False, part)
            states[0 : sz.group, lanes] = enter[:, lanes]

            def walk(j, h):
                at = tile(j, sz.group)
                h = decay[at, lanes] * h + drive[at, lanes]
                states[tile(j + 1, sz.group), lanes] = h
                hb[at, lanes] = h.astype(BF16)
                return h

            steps_of(sz.steps, 4, walk, enter[:, lanes])
        save(layer, keys.states)
        need(keys.out_w)

        def out_tile(n):
            cols = tile(n, 256)
            r.y1[:, cols] = stream[:, cols] + jnp.dot(
                hb[...], r.out_w[:, cols], preferred_element_type=F32
            )

        over(sz.width // 256, out_tile)
        save(layer, keys.y1)
        if layer < last:
            load(layer + 1, keys.out_w)
        norm_rows(r.y1, r.mlp_gain.at[layer : layer + 1], r.v, sz.rows, 128)
        save(layer, keys.v)
        need(keys.up_w)

        def up_dots(n, z, i):
            rows = tile(i, 256)
            z[rows, :256] = jnp.dot(
                r.v[rows, :], r.up_w[:, n * 256 : (n + 1) * 256], preferred_element_type=F32
            )

        def up_rest(n, z, i):
            cols = slice(n * 256, (n + 1) * 256)
            for chunk in range(4):
                at = pl.ds(pl.multiple_of(i * 256 + chunk * 64, 64), 64)
                p = z[at, :256]
                r.p[at, cols] = p
                r.gb[at, cols] = (p * normal_below(p)).astype(BF16)

        in_turn(sz.inner // 256, up_dots, up_rest)
        save(layer, keys.p)
        save(layer, keys.gb)
        if layer < last:
            load(layer + 1, keys.up_w)
        else:
            down_grad(layer, 0)
        need(keys.down_w)
        out = r.stream if layer < last else gy1

        def down_tile(n):
            cols = tile(n, 256)
            out[:, cols] = r.y1[:, cols] + jnp.dot(
                r.gb[...], r.down_w[:, cols], preferred_element_type=F32
            )

        over(sz.width // 256, down_tile)
        if layer < last:
            load(layer + 1, keys.down_w)

    def down_grad(layer, unit):
        for k in range(2):
            units.room(unit + k)

        def one(n):
            s, t = n // 2, n % 2
            value = jnp.dot(low_t[...], r.gb[:, tile(n, 256)], preferred_element_type=F32)
            for b in range(8):
                for h in range(2):
                    at = place(h, s // 2, b % 2, (b // 2) % 2, b // 4)
                    held[(unit + t) % HELD, s % 2, h, at] = value[
                        b * 64 : b * 64 + 64, h * 128 : h * 128 + 128
                    ]

        over(8, one)
        units.produced(2, unit, unit + 1)

    def cast(src, dst):
        def one(i):
            at = tile(i, 64)
            dst[at, :] = src[at, :].astype(dst.dtype)

        over(sz.rows // 64, one)

    def contract(left, weight, dst, count):
        def one(n):
            cols = tile(n, 256)
            dst[:, cols] = lax.dot_general(
                left[...], weight[cols, :], (((1,), (1,)), ((), ())), preferred_element_type=F32
            )

        over(count // 256, one)

    def up_grad(layer, unit):
        need(keys.v)
        wide_t[...] = r.v[...].T
        for k in range(2):
            units.room(unit + k)

        def one(b):
            value = jnp.dot(wide_t[...], gp[:, tile(b, 256)], preferred_element_type=F32)
            for s in range(4):
                for h in range(2):
                    at = place(h, s // 2, b % 2, (b // 2) % 2, b // 4)
                    for t in range(2):
                        held[(unit + t) % HELD, s % 2, h, at] = value[
                            s * 128 + h * 64 : s * 128 + h * 64 + 64, t * 128 : t * 128 + 128
                        ]

        over(8, one)
        units.produced(2.5, unit, unit + 1)

    def out_grad(layer, unit):
        def cast_state(i):
            hb[tile(i, sz.group), :] = r.states[tile(i + 1, sz.group), :].astype(BF16)

        if layer < last:
            over(sz.steps, cast_state)
        low_t[...] = low[...].T
        units.room(unit)

        def one(s):
            value = jnp.dot(low_t[...], hb[:, tile(s, 256)], preferred_element_type=F32)
            for b in range(8):
                for h in range(2):
                    at = place(h, s // 2, b % 2, (b // 2) % 2, b // 4)
                    held[unit % HELD, s % 2, h, at] = value[
                        b * 64 : b * 64 + 64, h * 128 : h * 128 + 128
                    ]

        over(4, one)
        units.produced(1.2, unit)

    def backward(layer, unit):
        late = layer < last

        def freed(*which):
            if layer > 0:
                for name in which:
                    load(layer - 1, name)

        if late:
            cast(gx, low)
            low_t[...] = low[...].T
            units.passed(1)
        else:
            freed(keys.gb)
        need(keys.down_w, keys.p)

        def act_dots(n, z, i):
            rows = tile(i, 256)
            z[rows, :256] = lax.dot_general(
                low[rows, :],
                r.down_w[n * 256 : (n + 1) * 256, :],
                (((1,), (1,)), ((), ())),
                preferred_element_type=F32,
            )

        def act_rest(n, z, i):
            cols = slice(n * 256, (n + 1) * 256)
            for chunk in range(4):
                at = pl.ds(pl.multiple_of(i * 256 + chunk * 64, 64), 64)
                p = r.p[at, cols]
                slope = normal_below(p) + ROOT_TAU * p * jnp.exp(-0.5 * p * p)
                gp[at, cols] = (z[at, :256] * slope).astype(BF16)

        in_turn(sz.inner // 256, act_dots, act_rest, lambda n: units.passed(0.6))
        freed(keys.down_w, keys.p)
        if not late:
            up_grad(layer, unit + 2)
            freed(keys.v)
        need(keys.up_w, keys.y1)
        contract(gp, r.up_w, grad, sz.width)
        freed(keys.up_w)
        units.passed(1.5)
        norm_back(r.y1, r.mlp_gain.at[layer : layer + 1], grad, gx, gy1, r.mlp_sum, sz.rows, 64)
        freed(keys.y1)
        cast(gy1, low)
        need(keys.states)
        units.passed(2)
        units.hold("x", 1)
        if not late:
            out_grad(layer, unit + 4)
        need(keys.out_w, keys.a, keys.b)
        contract(low, r.out_w, ga, sz.hidden)
        freed(keys.out_w)
        units.passed(1)
        flights = []
        for part, lanes in enumerate(parts):

            def totals(j, pair):
                at = tile(j, sz.group)
                if layer < last:
                    mask = jnp.concatenate([keep[at, :]] * (half // LANES), axis=1)
                    d = gate_weights(r.a[at, lanes], r.b[at, lanes])[0] * mask
                    decay[at, lanes] = d
                else:
                    d = decay[at, lanes]
                return pair[0] * d, d * (ga[at, lanes] + pair[1])

            one = jnp.ones((sz.group, half), F32)
            pair = steps_of(sz.steps, 2, totals, (one, jnp.zeros_like(one)), reverse=True)
            r.chunk_p[:, lanes] = pair[0]
            r.chunk_t[:, lanes] = pair[1]
            part_totals(r.chunk_p, r.chunk_t, sz, True, prefix, mine, lanes)
            flights.append(exchange_start(1, layer, part))
            carried = [units.expect(link, 16384) for link in ("core", "x", "x")]
            if part:
                units.hold("x", WINDOW)
            units.passed(0.8)
        need(keys.zc)
        if late:
            need(keys.gb)
            down_grad(layer, unit)
            up_grad(layer, unit + 2)
            out_grad(layer, unit + 4)
        unit += 5
        units.now = max(units.now, *carried)

        def gate_lanes(n):
            wide = 2 * LANES
            lanes = tile(n, wide)

            def walk(j, kept):
                m, bf, bi, bc = kept
                at = tile(j, sz.group)
                d = decay[at, lanes]
                q = ga[at, lanes] + m
                a, b, zc = r.a[at, lanes], r.b[at, lanes], r.zc[at, lanes]
                vm = jnp.concatenate([valid[at, :]] * 2, axis=1)
                km = jnp.concatenate([keep[at, :]] * 2, axis=1)
                fp, ip, inv = gate_weights(a, b)
                gf = q * (r.states[at, lanes] * km - zc * vm)
                parts = (
                    (gf * (a * inv) * fp).astype(BF16),
                    (-gf * (b * inv) * ip).astype(BF16),
                    (q * vm * ip).astype(BF16),
                )
                for part, value in enumerate(parts):
                    gz[at, pl.ds(pl.multiple_of(part * sz.hidden + n * wide, wide), wide)] = value
                return (d * q,) + tuple(
                    a + value.astype(F32) for a, value in zip((bf, bi, bc), parts)
                )

            zero = jnp.zeros((sz.group, wide), F32)
            _, *sums = steps_of(
                sz.steps, 4, walk, (enter[:, lanes], zero, zero, zero), reverse=True
            )
            for part, total in enumerate(sums):
                small[0, layer * 4 + part : layer * 4 + part + 1, lanes] = jnp.sum(
                    total, axis=0, keepdims=True
                )

        turns = sz.hidden // LANES // 4
        for part in range(2):
            exchange_end(*flights[part], True, part)
            over(turns, lambda n: gate_lanes(n + part * turns))
            units.passed(1.8)
        freed(keys.a, keys.b, keys.zc, keys.states)
        need(keys.u)
        wide_t[...] = r.u[...].T
        freed(keys.u)
        for k in range(2):
            units.room(unit + k)

        def gate_grad(b):
            cols = pl.ds(pl.multiple_of(b * 384, 128), 256)
            value = jnp.dot(wide_t[...], gz[:, cols], preferred_element_type=F32)
            for s in range(4):
                for h in range(2):
                    at = place(h, s // 2, b % 2, (b // 2) % 2, b // 4)
                    for t in range(2):
                        held[(unit + t) % HELD, s % 2, h, at] = value[
                            s * 128 + h * 64 : s * 128 + h * 64 + 64, t * 128 : t * 128 + 128
                        ]

        over(8, gate_grad)
        units.produced(3, unit, unit + 1)
        unit += 2
        units.room(unit)

        def gate_rest(z):
            right = jnp.concatenate(
                [
                    gz[:, pl.ds(pl.multiple_of((2 * z + y) * 384 + 256, 128), 128)]
                    for y in range(2)
                ],
                axis=1,
            )
            value = jnp.dot(wide_t[...], right, preferred_element_type=F32)
            for s in range(4):
                for h in range(2):
                    for y in range(2):
                        at = place(h, s // 2, y, z % 2, z // 2)
                        held[unit % HELD, s % 2, h, at] = value[
                            s * 128 + h * 64 : s * 128 + h * 64 + 64, y * 128 : y * 128 + 128
                        ]

        over(4, gate_rest)
        units.produced(1.5, unit)
        unit += 1
        need(keys.gate_w, keys.stream)
        contract(gz, r.gate_w, grad, sz.width)
        freed(keys.gate_w)
        units.passed(2.5)
        norm_back(r.stream, r.mix_gain.at[layer : layer + 1], grad, gy1, gx, r.mix_sum, sz.rows, 64)
        freed(keys.stream)
        row = slice(layer * 4 + 3, layer * 4 + 4)
        small[0, row, : sz.width] = jnp.sum(r.mix_sum[...], axis=0, keepdims=True)
        small[0, row, sz.width : 2 * sz.width] = jnp.sum(r.mlp_sum[...], axis=0, keepdims=True)
        units.passed(1.5)

    forward(0)
    keep_cotangent()
    for layer in range(1, layers):
        forward(layer)
    out_copies = from_steps(gy1, r.layer_out, r.out_sems)
    cast(low, gx)
    units.passed(2)
    for index, layer in enumerate(reversed(range(layers))):
        backward(layer, 8 * index)
    units.small_start()
    for copy in out_copies:
        copy.wait()
    out_copies = from_steps(gx, r.input_grad, r.out_sems)
    units.passed(1)
    units.drain()
    for copy in out_copies:
        copy.wait()
    total = small[STAGES]
    count = jnp.int32(0)
    for s in range(r.lens.shape[0]):
        for d in range(r.lens.shape[1]):
            count = count + r.lens[s, d]
    scale = 1.0 / (count.astype(F32) * sz.hidden)
    for layer in range(layers):
        for part in range(3):
            r.gate_bias_grad[layer : layer + 1, part * sz.hidden : (part + 1) * sz.hidden] = total[
                layer * 4 + part : layer * 4 + part + 1, : sz.hidden
            ]
        row = slice(layer * 4 + 3, layer * 4 + 4)
        r.mix_gain_grad[layer : layer + 1, :] = total[row, : sz.width]
        r.mlp_gain_grad[layer : layer + 1, :] = total[row, sz.width : 2 * sz.width]
        lanes = total[layer * 4 : layer * 4 + 1, sz.hidden : sz.hidden + LANES]
        r.forget_mean[layer : layer + 1, :] = (
            jnp.sum(lanes, axis=1, keepdims=True) * scale + jnp.zeros((1, LANES), F32)
        )


def run_whole_step(sz, layers, named):
    lengths = named["lengths"]
    rows, d, h, f = sz.rows, sz.width, sz.hidden, sz.inner
    vm = lambda *dims, kind=F32: pltpu.VMEM(dims, kind)
    sems = pltpu.SemaphoreType
    spec = dict(gate_bias=VMEM, mix_gain=VMEM, mlp_gain=VMEM)
    outputs = dict(
        layer_out=(shape(rows, d), ANY),
        input_grad=(shape(rows, d), ANY),
        gate_weight_grad=(shape(layers, 128, 384), VMEM),
        gate_bias_grad=(shape(layers, 3 * h), VMEM),
        out_weight_grad=(shape(layers, 64, 256), VMEM),
        up_weight_grad=(shape(layers, 128, 256), VMEM),
        down_weight_grad=(shape(layers, 64, 512), VMEM),
        mix_gain_grad=(shape(layers, d), VMEM),
        mlp_gain_grad=(shape(layers, d), VMEM),
        forget_mean=(shape(layers, LANES), VMEM),
    )
    results = len(outputs)
    kept = dict(
        u=((rows, d), BF16),
        a=((rows, h), F32),
        b=((rows, h), F32),
        zc=((rows, h), F32),
        states=((rows + sz.group, h), F32),
        y1=((rows, d), F32),
        v=((rows, d), BF16),
        p=((rows, f), F32),
        gb=((rows, f), BF16),
        stream=((rows, d), F32),
    )
    scratch = {}
    for name, (dims, kind) in kept.items():
        outputs[name + "_save"] = (shape(layers - 1, *dims, kind=kind), ANY)
        scratch[name] = vm(*dims, kind=kind)
    scratch.update(
        gate_w=vm(d, 3 * h, kind=BF16),
        out_w=vm(h, d, kind=BF16),
        up_w=vm(d, f, kind=BF16),
        down_w=vm(f, d, kind=BF16),
        valid=vm(rows, LANES),
        keep=vm(rows, LANES),
        gx=vm(rows, d),
        low=vm(rows, d, kind=BF16),
        low_t=vm(d, rows, kind=BF16),
        wide_t=vm(d, rows, kind=BF16),
        hb=vm(rows, h, kind=BF16),
        z1=vm(rows, 768),
        forget=vm(8, LANES),
        ga=vm(rows, h),
        gz=vm(rows, 3 * h, kind=BF16),
        grad=vm(rows, d),
        gy1=vm(rows, d),
        decay=vm(rows, h),
        chunk_p=vm(sz.group, h),
        chunk_t=vm(sz.group, h),
        prefix=vm(2, sz.group, h),
        enter=vm(sz.group, h),
        mine=vm(8, h),
        slots=vm(2, layers, sz.sections, 8, h),
        mlp_sum=vm(8, d),
        mix_sum=vm(8, d),
        held=vm(HELD, 2, 2, 16, BLOCK, LANES),
        small=vm(STAGES + 1, 8, SMALL),
        small_arrived=vm(STAGES, 8, SMALL),
        in_sems=sems.DMA((3,)),
        lens=pltpu.SMEM(lengths.shape, jnp.int32),
        out_sems=sems.DMA((d // LANES,)),
        natural=vm(d // LANES, rows, LANES),
        load_sems=sems.DMA((len(kept) + 4,)),
        save_sems=sems.DMA((len(kept) + 4,)),
        pair_send=sems.DMA((2, layers, 2, sz.sections - 1)),
        pair_recv=sems.DMA((2, layers, 2, sz.sections - 1)),
        send_sems=sems.DMA((SENDS, 2 * STAGES - 1)),
        recv_sems=sems.DMA((max(RINGS), 2 * STAGES - 1)),
        credits=sems.REGULAR((2 * STAGES - 1,)),
        small_send=sems.DMA((STAGES,)),
        small_recv=sems.DMA((STAGES,)),
    )
    for stage in range(STAGES):
        scratch[f"arrived{stage}"] = vm(RINGS[stage], 2, 16 >> stage, BLOCK, LANES)
    names = list(named) + list(outputs) + list(scratch)
    out = pl.pallas_call(
        functools.partial(whole_step, sz, layers, names),
        out_shape=tuple(value for value, _ in outputs.values()),
        in_specs=[spec.get(name, ANY) for name in named],
        out_specs=[place_of for _, place_of in outputs.values()],
        scratch_shapes=list(scratch.values()),
        compiler_params=pltpu.CompilerParams(
            collective_id=4, has_side_effects=True, vmem_limit_bytes=LIMIT
        ),
        name="whole_step",
    )(*named.values())
    return out[:results]


def deliver_kernel(count, *refs):
    sources, targets, held = refs[:count], refs[count : 2 * count], refs[2 * count : 3 * count - 1]
    sems = refs[3 * count - 1]
    arrivals = [
        pltpu.make_async_copy(sources[i], held[i], sems.at[0, i]) for i in range(count - 1)
    ]
    departures = [
        pltpu.make_async_copy(held[i], targets[i], sems.at[1, i]) for i in range(count - 1)
    ]
    for copy in arrivals:
        copy.start()
    for layer in range(targets[-1].shape[0]):
        targets[-1][layer] = sources[-1][layer, 0]
    for arrival, departure in zip(arrivals, departures):
        arrival.wait()
        departure.start()
    for copy in departures:
        copy.wait()


def deliver(values):
    count = len(values)
    scalars = pl.BlockSpec(memory_space=pltpu.SMEM)
    shapes = [shape(*value.shape) for value in values[:-1]] + [shape(values[-1].shape[0])]
    return pl.pallas_call(
        functools.partial(deliver_kernel, count),
        out_shape=tuple(shapes),
        in_specs=[ANY] * (count - 1) + [scalars],
        out_specs=[ANY] * (count - 1) + [scalars],
        scratch_shapes=[pltpu.VMEM(value.shape, F32) for value in values[:-1]]
        + [pltpu.SemaphoreType.DMA((2, count - 1))],
        compiler_params=pltpu.CompilerParams(vmem_limit_bytes=LIMIT),
        name="deliver",
    )(*values)


def mask_kernel(sizes, lens, valid, keep):
    fill_masks(lens, valid, keep, sizes)


def body(
    activations,
    cotangent,
    lengths,
    gate_weight,
    gate_bias,
    out_weight,
    up_weight,
    down_weight,
    mix_gain,
    mlp_gain,
):
    micro, span, width = activations.shape
    layers = gate_weight.shape[0]
    sz = Sizes(
        micro, span, width, out_weight.shape[1], up_weight.shape[2], lax.axis_size("section")
    )

    blocks = (width // 4, 3 * sz.hidden // 8, width // 8, sz.inner // 4, sz.hidden // 4)
    axes = (lax.axis_size("section"), lax.axis_size("batch"))
    if axes == (4, 8) and blocks == (128, 384, 64, 512, 256):
        out = run_whole_step(
            sz,
            layers,
            dict(
                activations=activations.reshape(sz.rows, width),
                cotangent=cotangent.reshape(sz.rows, width),
                lengths=lengths.T,
                gate_bias=gate_bias,
                mix_gain=mix_gain,
                mlp_gain=mlp_gain,
                gate_hbm=gate_weight,
                out_hbm=out_weight,
                up_hbm=up_weight,
                down_hbm=down_weight,
            ),
        )
        stream_out, input_grad, gate_g, bias_g, out_g, up_g, down_g, *rest = deliver(out)
        return (
            stream_out.reshape(activations.shape),
            input_grad.reshape(activations.shape),
            gate_g,
            bias_g,
            out_g.transpose(0, 2, 1),
            up_g,
            down_g.transpose(0, 2, 1),
            *rest,
        )

    def arranged(value):
        value = value.astype(F32).reshape(micro, CHUNKS, sz.steps, width)
        return value.transpose(2, 0, 1, 3).reshape(sz.rows, width)

    def restored(value):
        value = value.reshape(sz.steps, micro, CHUNKS, width).transpose(1, 2, 0, 3)
        return value.reshape(micro, span, width)

    masks = pl.pallas_call(
        functools.partial(mask_kernel, sz),
        out_shape=(shape(sz.rows, LANES), shape(sz.rows, LANES)),
        in_specs=[pl.BlockSpec(memory_space=pltpu.SMEM)],
        out_specs=[VMEM] * 2,
        name="masks",
    )(lengths)
    weights = (gate_weight, out_weight, up_weight, down_weight)
    stream = arranged(activations)
    streams, saved, forgets = [], [], []
    for layer in range(layers):
        streams.append(stream)
        stream, *kept, forget, pairs = run_forward(
            sz,
            layer,
            stream,
            masks,
            gate_bias[layer : layer + 1],
            mix_gain[layer : layer + 1],
            mlp_gain[layer : layer + 1],
            weights,
        )
        saved.append((*kept, pairs))
        forgets.append(forget)
    layer_out = restored(stream)
    gx = arranged(cotangent)
    true_count = jnp.sum(lengths).astype(F32)
    forgets = [jnp.sum(forget) for forget in forgets]
    sums, small = [None] * layers, [None] * layers
    for layer in reversed(range(layers)):
        gx, gate_g, out_g, up_g, down_g, bias_g, mix_g, mlp_g = run_backward(
            sz,
            layer,
            gx,
            streams[layer],
            masks,
            mix_gain[layer : layer + 1],
            mlp_gain[layer : layer + 1],
            saved[layer],
            weights,
        )
        sums[layer] = (gate_g, out_g.T, up_g, down_g.T)
        small[layer] = tuple(jnp.sum(part, axis=0) for part in (bias_g, mix_g, mlp_g))
    input_grad = restored(gx)
    stacked = tuple(jnp.stack(parts) for parts in zip(*sums))
    partial_sums = lax.psum_scatter(stacked, "section", scatter_dimension=1, tiled=True)
    large = lax.psum_scatter(partial_sums, "batch", scatter_dimension=2, tiled=True)
    bias_grad, mix_grad, mlp_grad = (jnp.stack(parts) for parts in zip(*small))
    bias_grad, mix_grad, mlp_grad, forget = lax.psum(
        (bias_grad, mix_grad, mlp_grad, jnp.stack(forgets)), ("section", "batch")
    )
    forget_mean = forget / (true_count * sz.hidden)
    return (
        layer_out,
        input_grad,
        large[0],
        bias_grad,
        large[1],
        large[2],
        large[3],
        mix_grad,
        mlp_grad,
        forget_mean,
    )


def solution(mesh):
    stream = P("batch", "section", None)
    block = P(None, "section", "batch")
    return jax.shard_map(
        body,
        mesh=mesh,
        in_specs=(stream, stream) + (P(),) * 8,
        out_specs=(stream, stream, block, P(), block, block, block, P(), P(), P()),
        check_vma=False,
    )
```

```python
import functools
import types

import jax
import jax.numpy as jnp
from jax import lax
from jax.experimental import pallas as pl
from jax.experimental.pallas import tpu as pltpu
from jax.sharding import PartitionSpec as P

epsilon = 1e-06
MESH = pl.DeviceIdType.MESH
F32, BF16 = jnp.float32, jnp.bfloat16
CHUNKS = 8
LANES = 128
ROOT_HALF = 0.7071067811865476
ROOT_TAU = 0.3989422804014327


def tile(index, size):
    return pl.ds(pl.multiple_of(index * size, size), size)


def inverse(value):
    r = pltpu.reciprocal(value, approx=True)
    return r * (2.0 - value * r)


def normal_below(p):
    return 0.5 + 0.5 * lax.erf(p * ROOT_HALF)


def steps_of(count, unroll, one, start, reverse=False):
    def turn(i, carry):
        for k in range(unroll):
            at = i * unroll + k
            carry = one(count - 1 - at if reverse else at, carry)
        return carry

    return lax.fori_loop(0, count // unroll, turn, start)


def odds(zf, zi):
    return jnp.exp(jnp.minimum(-zf, 86.0)), jnp.exp(jnp.minimum(-zi, 86.0))


def gate_weights(a, b):
    inv = inverse(2.0 + a + b)
    return (1.0 + b) * inv, (1.0 + a) * inv, inv


def greet_section(sections):
    me = lax.axis_index("section")
    barrier = pltpu.get_barrier_semaphore()
    for hop in range(1, sections):
        pl.semaphore_signal(
            barrier, inc=1, device_id={"section": lax.rem(me + hop, sections)}, device_id_type=MESH
        )
    pl.semaphore_wait(barrier, sections - 1)


def exchange(mine, slots, send_sems, recv_sems, sections):
    me = lax.axis_index("section")
    copies = []
    for hop in range(1, sections):
        copies.append(
            pltpu.make_async_remote_copy(
                src_ref=mine,
                dst_ref=slots.at[me],
                send_sem=send_sems.at[hop - 1],
                recv_sem=recv_sems.at[hop - 1],
                device_id={"section": lax.rem(me + hop, sections)},
                device_id_type=MESH,
            )
        )
    for copy in copies:
        copy.start()
    slots[me] = mine[...]
    for copy in copies:
        copy.wait()


def norm_rows(stream, gain, low, rows, step):
    def one(i, carry):
        at = tile(i, step)
        x = stream[at, :]
        r = lax.rsqrt(jnp.mean(x * x, axis=-1, keepdims=True) + epsilon)
        low[at, :] = (x * r * gain[...]).astype(BF16)
        return carry

    lax.fori_loop(0, rows // step, one, 0)


def norm_back(stream, gain, grad, through, out, gain_sum, rows, step, low=None):
    width = stream.shape[1]

    def one(i, total):
        at = tile(i, step)
        x = stream[at, :]
        r = lax.rsqrt(jnp.mean(x * x, axis=-1, keepdims=True) + epsilon)
        n = x * r
        g = grad[at, :]
        a = g * gain[...]
        value = through[at, :] + r * (a - n * jnp.mean(a * n, axis=-1, keepdims=True))
        out[at, :] = value
        if low is not None:
            low[at, :] = value.astype(BF16)
        return total + jnp.sum((g * n).reshape(step // 8, 8, width), axis=0)

    gain_sum[...] = lax.fori_loop(0, rows // step, one, jnp.zeros((8, width), F32))


def fill_masks(lens, valid, keep, sizes, turned=False):
    section = lax.axis_index("section")
    group = lax.axis_index("batch")
    starts, totals = [], []
    for s in range(sizes.micro):
        total, begin = 0, []
        for d in range(lens.shape[0 if turned else 1]):
            row = group * sizes.micro + s
            length = lens[d, row] if turned else lens[row, d]
            begin.append(jnp.where(length > 0, total, -1))
            total = total + length
        starts.append(begin)
        totals.append(total)
    chunk_place = lax.broadcasted_iota(jnp.int32, (8, LANES), 0) * sizes.steps

    def one(j, carry):
        for s in range(sizes.micro):
            place = section * sizes.span + j + chunk_place
            true = place < totals[s]
            first = place == starts[s][0]
            for begin in starts[s][1:]:
                first = first | (place == begin)
            at = pl.ds(pl.multiple_of(j * sizes.group + s * 8, 8), 8)
            valid[at, :] = jnp.where(true, 1.0, 0.0)
            keep[at, :] = jnp.where(true & jnp.logical_not(first), 1.0, 0.0)
        return carry

    lax.fori_loop(0, sizes.steps, one, 0)


def scan_totals(first, second, sizes, reverse, prefix, chunk, mine):
    for s in range(sizes.micro):
        p = jnp.ones((1, sizes.hidden), F32)
        t = jnp.zeros((1, sizes.hidden), F32)
        for c in reversed(range(CHUNKS)) if reverse else range(CHUNKS):
            at = s * 8 + c
            prefix[0, at : at + 1, :] = p
            prefix[1, at : at + 1, :] = t
            pc = first[at : at + 1, :]
            t = pc * t + second[at : at + 1, :]
            p = p * pc
        mine[s : s + 1, :] = p
        mine[sizes.micro + s : sizes.micro + s + 1, :] = t


def scan_enter(slots, prefix, enter, sizes, reverse):
    me = lax.axis_index("section")
    for s in range(sizes.micro):
        a = jnp.zeros((1, sizes.hidden), F32)
        order = range(sizes.sections - 1, 0, -1) if reverse else range(sizes.sections - 1)
        for k in order:
            reached = k > me if reverse else k < me
            pk = slots[k, s : s + 1, :]
            tk = slots[k, sizes.micro + s : sizes.micro + s + 1, :]
            a = jnp.where(reached, pk * a + tk, a)
        at = slice(s * 8, s * 8 + 8)
        enter[at, :] = prefix[0, at, :] * a + prefix[1, at, :]


def part_totals(first, second, sizes, reverse, prefix, mine, lanes):
    for s in range(sizes.micro):
        p = jnp.ones((1, lanes.stop - lanes.start), F32)
        t = jnp.zeros_like(p)
        for c in reversed(range(CHUNKS)) if reverse else range(CHUNKS):
            at = s * 8 + c
            prefix[0, at : at + 1, lanes] = p
            prefix[1, at : at + 1, lanes] = t
            pc = first[at : at + 1, lanes]
            t = pc * t + second[at : at + 1, lanes]
            p = p * pc
        mine[s : s + 1, lanes] = p
        mine[sizes.micro + s : sizes.micro + s + 1, lanes] = t


def part_enter(slots, prefix, enter, sizes, reverse, lanes):
    me = lax.axis_index("section")
    for s in range(sizes.micro):
        a = jnp.zeros((1, lanes.stop - lanes.start), F32)
        order = range(sizes.sections - 1, 0, -1) if reverse else range(sizes.sections - 1)
        for k in order:
            reached = k > me if reverse else k < me
            pk = slots[k, s : s + 1, lanes]
            tk = slots[k, sizes.micro + s : sizes.micro + s + 1, lanes]
            a = jnp.where(reached, pk * a + tk, a)
        at = slice(s * 8, s * 8 + 8)
        enter[at, lanes] = prefix[0, at, lanes] * a + prefix[1, at, lanes]


class Sizes:
    def __init__(self, micro, span, width, hidden, inner, sections):
        self.micro, self.span, self.width = micro, span, width
        self.hidden, self.inner, self.sections = hidden, inner, sections
        self.rows = micro * span
        self.steps = span // CHUNKS
        self.group = micro * CHUNKS


def forward_kernel(
    sizes,
    layer,
    stream,
    valid,
    keep,
    bias,
    mix_gain,
    mlp_gain,
    gate_hbm,
    out_hbm,
    up_hbm,
    down_hbm,
    next_stream,
    u,
    sf_out,
    si_out,
    zc_out,
    states,
    y1,
    v,
    p_out,
    gb,
    forget,
    pair_slots,
    gate_w,
    out_w,
    up_w,
    down_w,
    z,
    decay,
    drive,
    hb,
    chunk_p,
    chunk_t,
    prefix,
    enter,
    mine,
    weight_sems,
    send_sems,
    recv_sems,
):
    sz = sizes
    loads = [
        pltpu.make_async_copy(src.at[layer], dst, weight_sems.at[i])
        for i, (src, dst) in enumerate(
            ((gate_hbm, gate_w), (out_hbm, out_w), (up_hbm, up_w), (down_hbm, down_w))
        )
    ]
    for load in loads:
        load.start()
    greet_section(sz.sections)
    mine[...] = jnp.zeros_like(mine)
    norm_rows(stream, mix_gain, u, sz.rows, 64)
    loads[0].wait()
    forget[...] = jnp.zeros_like(forget)
    hw = 256

    def gate_tile(n, carry):
        for part in range(3):
            cols = pl.ds(pl.multiple_of(part * sz.hidden + n * hw, hw), hw)
            z[:, part * hw : (part + 1) * hw] = (
                jnp.dot(u[...], gate_w[:, cols], preferred_element_type=F32) + bias[:, cols]
            )

        def one(i, inner):
            at = tile(i, 64)
            for lane in range(hw // LANES):
                src = lambda part: z[
                    at, part * hw + lane * LANES : part * hw + (lane + 1) * LANES
                ]
                dst = pl.ds(pl.multiple_of(n * hw + lane * LANES, LANES), LANES)
                a = jnp.exp(jnp.minimum(-src(0), 86.0))
                b = jnp.exp(jnp.minimum(-src(1), 86.0))
                zc = src(2)
                fp, ip, _ = gate_weights(a, b)
                vm = valid[at, :]
                decay[at, dst] = fp * keep[at, :]
                drive[at, dst] = ip * zc * vm
                sf_out[at, dst] = a
                si_out[at, dst] = b
                zc_out[at, dst] = zc
                forget[...] += jnp.sum((fp * vm).reshape(8, 8, LANES), axis=0)
            return inner

        lax.fori_loop(0, sz.rows // 64, one, 0)
        return carry

    lax.fori_loop(0, sz.hidden // hw, gate_tile, 0)
    half = sz.hidden // 2
    for part in range(2):
        lanes = slice(part * half, (part + 1) * half)

        def totals(j, pair):
            at = tile(j, sz.group)
            d = decay[at, lanes]
            return pair[0] * d, pair[1] * d + drive[at, lanes]

        one = jnp.ones((sz.group, half), F32)
        pair = steps_of(sz.steps, 4, totals, (one, jnp.zeros_like(one)))
        chunk_p[:, lanes] = pair[0]
        chunk_t[:, lanes] = pair[1]
    scan_totals(chunk_p, chunk_t, sz, False, prefix, None, mine)
    exchange(mine, pair_slots, send_sems, recv_sems, sz.sections)
    scan_enter(pair_slots, prefix, enter, sz, False)
    states[0 : sz.group, :] = enter[...]
    for part in range(2):
        lanes = slice(part * half, (part + 1) * half)

        def walk(j, h):
            at = tile(j, sz.group)
            h = decay[at, lanes] * h + drive[at, lanes]
            states[tile(j + 1, sz.group), lanes] = h
            hb[at, lanes] = h.astype(BF16)
            return h

        steps_of(sz.steps, 4, walk, enter[:, lanes])
    loads[1].wait()

    def out_tile(n, carry):
        cols = tile(n, 256)
        y1[:, cols] = stream[:, cols] + jnp.dot(
            hb[...], out_w[:, cols], preferred_element_type=F32
        )
        return carry

    lax.fori_loop(0, sz.width // 256, out_tile, 0)
    norm_rows(y1, mlp_gain, v, sz.rows, 64)
    loads[2].wait()

    def up_tile(n, carry):
        cols = tile(n, 256)
        p_out[:, cols] = jnp.dot(v[...], up_w[:, cols], preferred_element_type=F32)

        def one(i, inner):
            at = tile(i, 64)
            p = p_out[at, cols]
            gb[at, cols] = (p * normal_below(p)).astype(BF16)
            return inner

        lax.fori_loop(0, sz.rows // 64, one, 0)
        return carry

    lax.fori_loop(0, sz.inner // 256, up_tile, 0)
    loads[3].wait()

    def down_tile(n, carry):
        cols = tile(n, 256)
        next_stream[:, cols] = y1[:, cols] + jnp.dot(
            gb[...], down_w[:, cols], preferred_element_type=F32
        )
        return carry

    lax.fori_loop(0, sz.width // 256, down_tile, 0)


def backward_kernel(
    sizes,
    layer,
    gx,
    stream,
    valid,
    keep,
    mix_gain,
    mlp_gain,
    u,
    sf_in,
    si_in,
    zc_in,
    states,
    y1,
    v,
    p_in,
    gb,
    pair_slots,
    gate_hbm,
    out_hbm,
    up_hbm,
    down_hbm,
    next_gx,
    gate_grad,
    out_grad,
    up_grad,
    down_grad,
    bias_sum,
    mix_sum,
    mlp_sum,
    gate_w,
    out_w,
    up_w,
    down_w,
    low,
    low_t,
    wide_t,
    hb,
    ga,
    gp,
    gz,
    grad,
    gy1,
    decay,
    chunk_p,
    chunk_t,
    prefix,
    enter,
    mine,
    slots,
    weight_sems,
    send_sems,
    recv_sems,
):
    sz = sizes
    loads = [
        pltpu.make_async_copy(src.at[layer], dst, weight_sems.at[i])
        for i, (src, dst) in enumerate(
            ((gate_hbm, gate_w), (out_hbm, out_w), (up_hbm, up_w), (down_hbm, down_w))
        )
    ]
    for load in reversed(loads):
        load.start()
    greet_section(sz.sections)
    mine[...] = jnp.zeros_like(mine)

    def cast(i, carry):
        at = tile(i, 64)
        low[at, :] = gx[at, :].astype(BF16)
        return carry

    lax.fori_loop(0, sz.rows // 64, cast, 0)
    low_t[...] = low[...].T

    def weight_grad(left_t, right, dst, step):
        def one(n, carry):
            cols = tile(n, step)
            dst[:, cols] = jnp.dot(left_t[...], right[:, cols], preferred_element_type=F32)
            return carry

        lax.fori_loop(0, right.shape[1] // step, one, 0)

    weight_grad(low_t, gb, down_grad, 256)
    loads[3].wait()

    def act_tile(n, carry):
        cols = tile(n, 256)
        ga[:, :256] = lax.dot_general(
            low[...], down_w[cols, :], (((1,), (1,)), ((), ())), preferred_element_type=F32
        )

        def one(i, inner):
            at = tile(i, 64)
            p = p_in[at, cols]
            slope = normal_below(p) + ROOT_TAU * p * jnp.exp(-0.5 * p * p)
            gp[at, cols] = (ga[at, :256] * slope).astype(BF16)
            return inner

        lax.fori_loop(0, sz.rows // 64, one, 0)
        return carry

    lax.fori_loop(0, sz.inner // 256, act_tile, 0)
    wide_t[...] = v[...].T
    weight_grad(wide_t, gp, up_grad, 256)
    loads[2].wait()

    def contract(left, weight, dst, step):
        def one(n, carry):
            cols = tile(n, step)
            dst[:, cols] = lax.dot_general(
                left[...], weight[cols, :], (((1,), (1,)), ((), ())), preferred_element_type=F32
            )
            return carry

        lax.fori_loop(0, weight.shape[0] // step, one, 0)

    contract(gp, up_w, grad, 256)
    norm_back(y1, mlp_gain, grad, gx, gy1, mlp_sum, sz.rows, 64)

    def cast_more(i, carry):
        at = tile(i, 64)
        low[at, :] = gy1[at, :].astype(BF16)
        return carry

    lax.fori_loop(0, sz.rows // 64, cast_more, 0)

    def cast_state(i, carry):
        hb[tile(i, sz.group), :] = states[tile(i + 1, sz.group), :].astype(BF16)
        return carry

    lax.fori_loop(0, sz.steps, cast_state, 0)
    low_t[...] = low[...].T
    weight_grad(low_t, hb, out_grad, 256)
    loads[1].wait()
    contract(low, out_w, ga, 256)
    half = sz.hidden // 2
    for part in range(2):
        lanes = slice(part * half, (part + 1) * half)

        def totals(i, pair):
            at = tile(sz.steps - 1 - i, sz.group)
            mask = jnp.concatenate([keep[at, :]] * (half // LANES), axis=1)
            d = gate_weights(sf_in[at, lanes], si_in[at, lanes])[0] * mask
            decay[at, lanes] = d
            return pair[0] * d, d * (ga[at, lanes] + pair[1])

        pair = lax.fori_loop(
            0,
            sz.steps,
            totals,
            (jnp.ones((sz.group, half), F32), jnp.zeros((sz.group, half), F32)),
        )
        chunk_p[:, lanes] = pair[0]
        chunk_t[:, lanes] = pair[1]
    scan_totals(chunk_p, chunk_t, sz, True, prefix, None, mine)
    exchange(mine, slots, send_sems, recv_sems, sz.sections)
    scan_enter(slots, prefix, enter, sz, True)

    def gate_lane(n, carry):
        lanes = tile(n, LANES)

        def walk(i, kept):
            m, bf, bi, bc = kept
            j = sz.steps - 1 - i
            at = tile(j, sz.group)
            d = decay[at, lanes]
            q = ga[at, lanes] + m
            a = sf_in[at, lanes]
            b = si_in[at, lanes]
            zc = zc_in[at, lanes]
            vm = valid[at, :]
            fp, ip, inv = gate_weights(a, b)
            gf = q * (states[at, lanes] * keep[at, :] - zc * vm)
            gzf = (gf * (a * inv) * fp).astype(BF16)
            gzi = (-gf * (b * inv) * ip).astype(BF16)
            gzc = (q * vm * ip).astype(BF16)
            gz[at, lanes] = gzf
            gz[at, pl.ds(pl.multiple_of(sz.hidden + n * LANES, LANES), LANES)] = gzi
            gz[at, pl.ds(pl.multiple_of(2 * sz.hidden + n * LANES, LANES), LANES)] = gzc
            return (
                d * q,
                bf + gzf.astype(F32),
                bi + gzi.astype(F32),
                bc + gzc.astype(F32),
            )

        zero = jnp.zeros((sz.group, LANES), F32)
        _, bf, bi, bc = lax.fori_loop(0, sz.steps, walk, (enter[:, lanes], zero, zero, zero))
        for part, total in enumerate((bf, bi, bc)):
            where = pl.ds(pl.multiple_of(part * sz.hidden + n * LANES, LANES), LANES)
            bias_sum[:, where] = jnp.sum(total.reshape(sz.group // 8, 8, LANES), axis=0)
        return carry

    lax.fori_loop(0, sz.hidden // LANES, gate_lane, 0)
    wide_t[...] = u[...].T
    weight_grad(wide_t, gz, gate_grad, 256)
    loads[0].wait()
    contract(gz, gate_w, grad, 256)
    norm_back(stream, mix_gain, grad, gy1, next_gx, mix_sum, sz.rows, 64)


VMEM = pl.BlockSpec(memory_space=pltpu.VMEM)
ANY = pl.BlockSpec(memory_space=pl.ANY)
LIMIT = 62 * 2**20


def shape(*dims, kind=F32):
    return jax.ShapeDtypeStruct(dims, kind)


def exchange_scratch(sz):
    return [
        pltpu.SemaphoreType.DMA((4,)),
        pltpu.SemaphoreType.DMA((sz.sections - 1,)),
        pltpu.SemaphoreType.DMA((sz.sections - 1,)),
    ]


def weight_scratch(sz):
    return [
        pltpu.VMEM((sz.width, 3 * sz.hidden), BF16),
        pltpu.VMEM((sz.hidden, sz.width), BF16),
        pltpu.VMEM((sz.width, sz.inner), BF16),
        pltpu.VMEM((sz.inner, sz.width), BF16),
    ]


def scan_scratch(sz):
    return [
        pltpu.VMEM((sz.group, sz.hidden), F32),
        pltpu.VMEM((sz.group, sz.hidden), F32),
        pltpu.VMEM((2, sz.group, sz.hidden), F32),
        pltpu.VMEM((sz.group, sz.hidden), F32),
        pltpu.VMEM((8, sz.hidden), F32),
    ]


def run_forward(sz, layer, stream, masks, bias, mix_gain, mlp_gain, weights):
    r, d, h, f = sz.rows, sz.width, sz.hidden, sz.inner
    return pl.pallas_call(
        functools.partial(forward_kernel, sz, layer),
        out_shape=(
            shape(r, d),
            shape(r, d, kind=BF16),
            shape(r, h),
            shape(r, h),
            shape(r, h),
            shape(r + sz.group, h),
            shape(r, d),
            shape(r, d, kind=BF16),
            shape(r, f),
            shape(r, f, kind=BF16),
            shape(8, LANES),
            shape(sz.sections, 8, h),
        ),
        in_specs=[VMEM] * 6 + [ANY] * 4,
        out_specs=[VMEM] * 12,
        scratch_shapes=weight_scratch(sz)
        + [
            pltpu.VMEM((r, 3 * 256), F32),
            pltpu.VMEM((r, h), F32),
            pltpu.VMEM((r, h), F32),
            pltpu.VMEM((r, h), BF16),
        ]
        + scan_scratch(sz)
        + exchange_scratch(sz),
        compiler_params=pltpu.CompilerParams(
            collective_id=layer, has_side_effects=True, vmem_limit_bytes=LIMIT
        ),
        name=f"forward_{layer}",
    )(stream, *masks, bias, mix_gain, mlp_gain, *weights)


def run_backward(sz, layer, gx, stream, masks, mix_gain, mlp_gain, saved, weights):
    r, d, h, f = sz.rows, sz.width, sz.hidden, sz.inner
    return pl.pallas_call(
        functools.partial(backward_kernel, sz, layer),
        out_shape=(
            shape(r, d),
            shape(d, 3 * h),
            shape(d, h),
            shape(d, f),
            shape(d, f),
            shape(8, 3 * h),
            shape(8, d),
            shape(8, d),
        ),
        in_specs=[VMEM] * 16 + [ANY] * 4,
        out_specs=[VMEM] * 8,
        scratch_shapes=weight_scratch(sz)
        + [
            pltpu.VMEM((r, d), BF16),
            pltpu.VMEM((d, r), BF16),
            pltpu.VMEM((d, r), BF16),
            pltpu.VMEM((r, h), BF16),
            pltpu.VMEM((r, h), F32),
            pltpu.VMEM((r, f), BF16),
            pltpu.VMEM((r, 3 * h), BF16),
            pltpu.VMEM((r, d), F32),
            pltpu.VMEM((r, d), F32),
            pltpu.VMEM((r, h), F32),
        ]
        + scan_scratch(sz)
        + [pltpu.VMEM((sz.sections, 8, h), F32)]
        + exchange_scratch(sz),
        compiler_params=pltpu.CompilerParams(
            collective_id=2 + layer, has_side_effects=True, vmem_limit_bytes=LIMIT
        ),
        name=f"backward_{layer}",
    )(gx, stream, *masks, mix_gain, mlp_gain, *saved, *weights)


BLOCK = 64
HELD = 3
RINGS = (4, 5, 6, 16, 16)
SENDS = 16
STAGES = 5
WINDOW = 4
DELAY = 1.5
SMALL = 1280


ORDERS = (((0, 2, 1, 3), (1, 2, 0, 3)),) * 16


class Units:
    def __init__(self, count, refs):
        self.count = count
        self.__dict__.update(vars(refs))
        self.arrived = [getattr(refs, f"arrived{stage}") for stage in range(STAGES)]
        section, batch = lax.axis_index("section"), lax.axis_index("batch")
        core, x = section % 2, section // 2
        y, za, zb = batch % 2, (batch // 2) % 2, batch // 4
        self.core = core
        self.where = (x, y, za, zb)
        self.partner = {
            "core": {"section": section + 1 - 2 * core},
            "x": {"section": section + 2 - 4 * x},
            "y": {"batch": batch + 1 - 2 * y},
            "za": {"batch": batch + 2 - 4 * za},
            "zb": {"batch": batch + 4 - 8 * zb},
        }
        self.now = 0.0
        self.links = ("core", "x", "y", "z")
        self.free_at = dict.fromkeys(self.links, 0.0)
        self.flying = dict.fromkeys(self.links, 0)
        self.queues = {link: [] for link in self.links}
        self.ready = {}
        self.summed = set()
        self.copies = {}
        self.small_left = None

    def greet(self):
        section = lax.axis_index("section")
        others = [self.partner["y"], self.partner["za"], self.partner["zb"]]
        others += [{"section": lax.rem(section + hop, 4)} for hop in range(1, 4)]
        for other in others:
            pl.semaphore_signal(
                pltpu.get_barrier_semaphore(), inc=1, device_id=other, device_id_type=MESH
            )

    def greeted(self):
        pl.semaphore_wait(pltpu.get_barrier_semaphore(), 6)

    def name(self, unit, stage, half):
        return "core" if stage == 0 else ("x", "y", "za", "zb")[ORDERS[unit][half][stage - 1]]

    def link(self, unit, stage, half):
        name = self.name(unit, stage, half)
        return "z" if name[0] == "z" else name

    def bit(self, unit, stage, half):
        return self.where[ORDERS[unit][half][stage - 1]]

    def arrival(self, unit, stage, half):
        ref = self.arrived[stage].at[unit % RINGS[stage]]
        return ref if stage == 0 else ref.at[half]

    def copy(self, unit, stage, half):
        at = 0 if stage == 0 else 2 * stage - 1 + half
        if stage == 0:
            src = self.held.at[unit % HELD, 1 - self.core]
        else:
            count = 16 >> stage
            src = self.arrived[stage - 1].at[unit % RINGS[stage - 1], half]
            src = src.at[pl.ds((1 - self.bit(unit, stage, half)) * count, count)]
        return pltpu.make_async_remote_copy(
            src_ref=src,
            dst_ref=self.arrival(unit, stage, half),
            send_sem=self.send_sems.at[unit % SENDS, at],
            recv_sem=self.recv_sems.at[unit % RINGS[stage], at],
            device_id=self.partner[self.name(unit, stage, half)],
            device_id_type=MESH,
        )

    def has_place(self, unit, stage, half):
        before = unit - RINGS[stage]
        if before < 0:
            return True
        if stage == 0:
            return (before, 1, 0) in self.summed and (before, 1, 1) in self.summed
        return (before, min(stage + 1, STAGES - 1), half) in self.summed

    def credit(self, unit, stage, half):
        after = unit + RINGS[stage]
        if after < self.count:
            pl.semaphore_signal(
                self.credits.at[0 if stage == 0 else 2 * stage - 1 + half, after],
                inc=1,
                device_id=self.partner[self.name(after, stage, half)],
                device_id_type=MESH,
            )

    def pump(self):
        for link, queue in self.queues.items():
            while self.flying[link] < WINDOW:
                key = next((key for key in queue if self.has_place(*key)), None)
                if key is None:
                    break
                queue.remove(key)
                self.flying[link] += 1
                unit, stage, half = key
                if unit >= RINGS[stage]:
                    at = 0 if stage == 0 else 2 * stage - 1 + half
                    pl.semaphore_wait(self.credits.at[at, unit], 1)
                self.copies[key] = self.copy(*key)
                self.copies[key].start()
                blocks = 32 if stage == 0 else 16 >> stage
                self.ready[key] = self.expect(link, blocks * BLOCK * LANES * 4)

    def expect(self, link, size):
        rate = 250e3 if link == "core" else 45e3
        self.free_at[link] = max(self.now, self.free_at[link]) + size / rate
        return self.free_at[link] + DELAY

    def push(self, unit, stage, half):
        self.queues[self.link(unit, stage, half)].append((unit, stage, half))
        self.pump()

    def produced(self, us, *which):
        self.now += us
        for unit in which:
            self.push(unit, 0, 0)
        self.passed(0)

    def add(self, dst, src, count):
        turn = min(count, 4)

        def one(i, carry):
            for k in range(turn):
                dst[i * turn + k] += src[i * turn + k]
            return carry

        if count == turn:
            one(0, 0)
        else:
            lax.fori_loop(0, count // turn, one, 0)

    def step(self, unit, stage, half):
        key = (unit, stage, half)
        del self.ready[key]
        self.copies[key].wait_recv()
        here = self.arrival(unit, stage, half)
        if stage == 0:
            for h in range(2):
                self.add(here.at[h], self.held.at[unit % HELD, self.core, h], 16)
        else:
            count = 16 >> stage
            before = self.arrived[stage - 1].at[unit % RINGS[stage - 1], half]
            self.add(here, before.at[pl.ds(self.bit(unit, stage, half) * count, count)], count)
            self.copies.pop(key).wait_send()
        self.summed.add(key)
        self.flying[self.link(unit, stage, half)] -= 1
        self.now += 0.25
        if stage > 1 or (unit, 1, 1 - half) in self.summed:
            if stage > 0:
                self.credit(unit, stage - 1, half if stage > 1 else 0)
        if stage == 0:
            for h in range(2):
                self.push(unit, 1, h)
        elif stage < STAGES - 1:
            self.push(unit, stage + 1, half)
        else:
            self.finish(unit, half, here[0])
            self.credit(unit, stage, half)
        self.pump()

    def finish(self, unit, half, block):
        layer, k = self.count // 8 - 1 - unit // 8, unit % 8
        if k < 2 or k == 4:
            ref, at = (self.down_weight_grad, k) if k < 2 else (self.out_weight_grad, 0)
            ref[layer, :, at * 256 + half * 128 : at * 256 + half * 128 + 128] = block
        else:
            ref, at = (self.up_weight_grad, k - 2) if k < 4 else (self.gate_weight_grad, k - 5)
            rows = slice(half * BLOCK, half * BLOCK + BLOCK)
            ref[layer, rows, at * LANES : at * LANES + LANES] = block

    def small_copy(self, stage):
        name = ("core", "x", "y", "za", "zb")[stage]
        return pltpu.make_async_remote_copy(
            src_ref=self.small.at[stage],
            dst_ref=self.small_arrived.at[stage],
            send_sem=self.small_send.at[stage],
            recv_sem=self.small_recv.at[stage],
            device_id=self.partner[name],
            device_id_type=MESH,
        )

    def small_start(self):
        self.small_left = 0
        self.small_copies = [self.small_copy(0)]
        self.small_copies[0].start()
        self.small_ready = self.now + 3.0

    def small_step(self):
        stage = self.small_left
        self.small_copies[stage].wait_recv()
        self.small[stage + 1] = self.small[stage] + self.small_arrived[stage]
        self.small_left += 1
        if self.small_left < STAGES:
            self.small_copies.append(self.small_copy(self.small_left))
            self.small_copies[-1].start()
            self.small_ready = self.now + 3.0
        else:
            for copy in self.small_copies:
                copy.wait_send()

    def open(self, unit, stage, half):
        halves = range(2) if stage == 0 else (half,)
        before = unit - RING
        return (
            before < 0
            or stage == STAGES - 1
            or all((before, stage + 1, h) in self.consumed for h in halves)
        )

    def next(self):
        best = min(self.ready.items(), key=lambda item: (item[1], item[0]), default=None)
        small = self.small_left is not None and self.small_left < STAGES
        if small and (best is None or self.small_ready <= best[1]):
            return self.small_ready, None
        return (best[1], best[0]) if best else None

    def take(self, item):
        self.now = max(self.now, item[0])
        if item[1] is None:
            self.small_step()
        else:
            self.step(*item[1])

    def passed(self, us):
        self.now += us
        while (item := self.next()) and item[0] <= self.now:
            self.take(item)

    def room(self, unit):
        before = (unit - HELD, 0, 0)
        while unit >= HELD and before not in self.summed:
            self.take(self.next())
        if before in self.copies:
            self.copies.pop(before).wait_send()

    def drain(self):
        while item := self.next():
            self.take(item)
        for key in list(self.copies):
            self.copies.pop(key).wait_send()


def place(unit, half, x, y, z):
    where = (x, y, z % 2, z // 2)
    order = ORDERS[unit][half]
    return where[order[0]] * 8 + where[order[1]] * 4 + where[order[2]] * 2 + where[order[3]]


def strided(start, steps):
    return pl.ds(start, CHUNKS, stride=steps)


def whole_step(sz, layers, names, *args):
    r = types.SimpleNamespace(**dict(zip(names, args)))
    units = Units(8 * layers, r)
    valid, keep, low, low_t, wide_t = r.valid, r.keep, r.low, r.low_t, r.wide_t
    hb, ga, gz, grad, gy1, gx = r.hb, r.ga, r.gz, r.grad, r.gy1, r.gx
    gp = gz.at[:, : sz.inner]
    decay, enter, prefix, mine = r.decay, r.enter, r.prefix, r.mine
    small, held = r.small, r.held
    natural = r.natural
    last = layers - 1
    half = sz.hidden // 2
    zs = (ga.at[:, :256], r.z1)
    drive = ga
    homes = dict(gate_w=r.gate_hbm, out_w=r.out_hbm, up_w=r.up_hbm, down_w=r.down_hbm)
    homes.update(u=r.u_save, zf=r.zf_save, zi=r.zi_save, zc=r.zc_save, states=r.states_save)
    homes.update(y1=r.y1_save, v=r.v_save, p=r.p_save, gb=r.gb_save, stream=r.stream_save)
    keys = types.SimpleNamespace(**{name: name for name in homes})
    index_of = {name: i for i, name in enumerate(homes)}
    loads, saves = {}, {}

    def load(layer, name):
        copy = pltpu.make_async_copy(
            homes[name].at[layer], getattr(r, name), r.load_sems.at[index_of[name]]
        )
        copy.start()
        loads[name] = copy

    def need(*wanted):
        for name in wanted:
            if name in loads:
                loads.pop(name).wait()

    def save(layer, name, ref=None):
        if layer < last:
            src = getattr(r, name) if ref is None else ref
            copy = pltpu.make_async_copy(
                src, homes[name].at[layer], r.save_sems.at[index_of[name]]
            )
            copy.start()
            saves[name] = copy

    def settled(*which):
        for name in which:
            if name in saves:
                saves.pop(name).wait()

    def over(count, one):
        def each(i, carry):
            one(i)
            return carry

        lax.fori_loop(0, count, each, 0)

    act_load = pltpu.make_async_copy(r.activations, hb.at[:, : sz.width], r.in_sems.at[0])
    cot_load = pltpu.make_async_copy(r.cotangent, wide_t, r.in_sems.at[1])
    len_load = pltpu.make_async_copy(r.lengths, r.lens, r.in_sems.at[2])
    len_load.start()
    act_load.start()
    for name in (keys.gate_w, keys.out_w, keys.up_w, keys.down_w):
        load(0, name)
    cot_load.start()
    units.greet()
    mine[...] = jnp.zeros_like(mine)
    small[0] = jnp.zeros((8, SMALL), F32)
    len_load.wait()
    fill_masks(r.lens, valid, keep, sz, True)

    def to_steps(src, put):
        def cast(i):
            at = tile(i, 64)
            for k in range(sz.width // LANES):
                natural[k, at, :] = src[at, k * LANES : (k + 1) * LANES].astype(F32)

        over(sz.rows // 64, cast)

        def gather(j):
            for k in range(sz.width // LANES):
                parts = [
                    natural[k, strided(s * sz.span + j, sz.steps), :] for s in range(sz.micro)
                ]
                put(tile(j, sz.group), slice(k * LANES, (k + 1) * LANES), jnp.concatenate(parts, axis=0))

        over(sz.steps, gather)

    def from_steps(src, dst, sem):
        def scatter(j):
            for k in range(sz.width // LANES):
                value = src[tile(j, sz.group), k * LANES : (k + 1) * LANES]
                for s in range(sz.micro):
                    natural[k, strided(s * sz.span + j, sz.steps), :] = value[s * 8 : s * 8 + 8]

        over(sz.steps, scatter)
        copies = []
        for k in range(sz.width // LANES):
            lanes = slice(k * LANES, (k + 1) * LANES)
            copies.append(pltpu.make_async_copy(natural.at[k], dst.at[:, lanes], sem.at[k]))
            copies[-1].start()
        return copies

    act_load.wait()

    def put_gx(at, lanes, value):
        gx[at, lanes] = value

    to_steps(hb.at[:, : sz.width], put_gx)

    parts = [slice(part * half, (part + 1) * half) for part in range(2)]

    def exchange_start(way, layer, part):
        lanes = parts[part]
        slots = r.slots.at[way, layer]
        me = lax.axis_index("section")
        copies = []
        for hop in range(1, sz.sections):
            copies.append(
                pltpu.make_async_remote_copy(
                    src_ref=mine.at[:, lanes],
                    dst_ref=slots.at[me, :, lanes],
                    send_sem=r.pair_send.at[way, layer, part, hop - 1],
                    recv_sem=r.pair_recv.at[way, layer, part, hop - 1],
                    device_id={"section": lax.rem(me + hop, sz.sections)},
                    device_id_type=MESH,
                )
            )
        for copy in copies:
            copy.start()
        slots[me, :, lanes] = mine[:, lanes]
        return slots, copies

    def exchange_end(slots, copies, reverse, part):
        for copy in copies:
            copy.wait()
        part_enter(slots, prefix, enter, sz, reverse, parts[part])

    def in_turn(count, dots, rest, after=None):
        over(sz.rows // 256, lambda i: dots(0, i))
        for n in range(count):

            def both(i):
                if n + 1 < count:
                    dots(n + 1, i)
                rest(n, i)

            over(sz.rows // 256, both)
            if after is not None:
                after(n)

    def keep_cotangent():
        cot_load.wait()

        def put_low(at, lanes, value):
            low[at, lanes] = value.astype(BF16)

        to_steps(wide_t, put_low)
        low_t[...] = low[...].T

    def forward(layer):
        stream = r.stream if layer > 0 else gx
        settled(keys.u)
        norm_rows(stream, r.mix_gain.at[layer : layer + 1], r.u, sz.rows, 128)
        save(layer, keys.u)
        if layer == 0:
            save(layer, keys.stream, gx)
        need(keys.gate_w)
        settled(keys.zf, keys.zi, keys.zc)
        hw = 256
        bias = r.gate_bias

        def gate_dots(n, i):
            rows, to = tile(i, 256), slice(n * hw, (n + 1) * hw)
            for part, z in enumerate((r.zf, r.zi, r.zc)):
                cols = slice(part * sz.hidden + n * hw, part * sz.hidden + (n + 1) * hw)
                z[rows, to] = (
                    jnp.dot(r.u[rows, :], r.gate_w[:, cols], preferred_element_type=F32)
                    + bias[layer : layer + 1, cols]
                )

        def gate_rest(n, i):
            for chunk in range(4):
                at = pl.ds(pl.multiple_of(i * 256 + chunk * 64, 64), 64)
                vm, km = valid[at, :], keep[at, :]
                for lane in range(hw // LANES):
                    cols = slice(n * hw + lane * LANES, n * hw + (lane + 1) * LANES)
                    fp, ip, _ = gate_weights(*odds(r.zf[at, cols], r.zi[at, cols]))
                    decay[at, cols] = fp * km
                    drive[at, cols] = ip * r.zc[at, cols] * vm
                    r.forget[...] += jnp.sum((fp * vm).reshape(8, 8, LANES), axis=0)

        flights = []

        def gate_after(n):
            if n % 2 == 0:
                return
            lanes = parts[n // 2]

            def totals(j, pair):
                at = tile(j, sz.group)
                d = decay[at, lanes]
                return pair[0] * d, pair[1] * d + drive[at, lanes]

            one = jnp.ones((sz.group, half), F32)
            pair = steps_of(sz.steps, 2, totals, (one, jnp.zeros_like(one)))
            r.chunk_p[:, lanes] = pair[0]
            r.chunk_t[:, lanes] = pair[1]
            part_totals(r.chunk_p, r.chunk_t, sz, False, prefix, mine, lanes)
            if layer == 0 and n == 1:
                units.greeted()
            flights.append(exchange_start(0, layer, n // 2))

        r.forget[...] = jnp.zeros_like(r.forget)
        in_turn(sz.hidden // hw, gate_dots, gate_rest, gate_after)
        small[0, layer * 4 : layer * 4 + 1, sz.hidden : sz.hidden + LANES] = jnp.sum(
            r.forget[...], axis=0, keepdims=True
        )
        for name in (keys.zf, keys.zi, keys.zc):
            save(layer, name)
        if layer < last:
            load(layer + 1, keys.gate_w)
        settled(keys.states, keys.y1, keys.v, keys.p, keys.gb, keys.stream)
        states = r.states
        for part, lanes in enumerate(parts):
            exchange_end(*flights[part], False, part)
            states[0 : sz.group, lanes] = enter[:, lanes]

            def walk(j, h):
                at = tile(j, sz.group)
                h = decay[at, lanes] * h + drive[at, lanes]
                states[tile(j + 1, sz.group), lanes] = h
                hb[at, lanes] = h.astype(BF16)
                return h

            steps_of(sz.steps, 4, walk, enter[:, lanes])
            if (layer, part) == (0, 0):
                keep_cotangent()
        save(layer, keys.states)
        need(keys.out_w)

        def out_tile(n):
            cols = tile(n, 256)
            r.y1[:, cols] = stream[:, cols] + jnp.dot(
                hb[...], r.out_w[:, cols], preferred_element_type=F32
            )

        over(sz.width // 256, out_tile)
        save(layer, keys.y1)
        if layer < last:
            load(layer + 1, keys.out_w)
        norm_rows(r.y1, r.mlp_gain.at[layer : layer + 1], r.v, sz.rows, 128)
        save(layer, keys.v)
        need(keys.up_w)

        def up_dots(n, i):
            rows, cols = tile(i, 256), slice(n * 256, (n + 1) * 256)
            r.p[rows, cols] = jnp.dot(
                r.v[rows, :], r.up_w[:, cols], preferred_element_type=F32
            )

        def up_rest(n, i):
            cols = slice(n * 256, (n + 1) * 256)
            for chunk in range(4):
                at = pl.ds(pl.multiple_of(i * 256 + chunk * 64, 64), 64)
                p = r.p[at, cols]
                r.gb[at, cols] = (p * normal_below(p)).astype(BF16)

        in_turn(sz.inner // 256, up_dots, up_rest)
        save(layer, keys.p)
        save(layer, keys.gb)
        if layer < last:
            load(layer + 1, keys.up_w)
        else:
            down_grad(layer, 0)
        need(keys.down_w)
        out = r.stream if layer < last else gy1

        def down_tile(n):
            cols = tile(n, 256)
            out[:, cols] = r.y1[:, cols] + jnp.dot(
                r.gb[...], r.down_w[:, cols], preferred_element_type=F32
            )

        over(sz.width // 256, down_tile)
        if layer < last:
            load(layer + 1, keys.down_w)

    def down_grad(layer, unit):
        for k in range(2):
            units.room(unit + k)

        def one(n):
            s, t = n // 2, n % 2
            value = jnp.dot(low_t[...], r.gb[:, tile(n, 256)], preferred_element_type=F32)
            for b in range(8):
                for h in range(2):
                    at = [place(unit + k, h, s // 2, b % 2, b // 2) for k in range(2)]
                    held[(unit + t) % HELD, s % 2, h, jnp.where(t == 0, *at)] = value[
                        b * 64 : b * 64 + 64, h * 128 : h * 128 + 128
                    ]

        over(8, one)
        units.produced(2, unit, unit + 1)

    def cast(src, dst):
        def one(i):
            at = tile(i, 64)
            dst[at, :] = src[at, :].astype(dst.dtype)

        over(sz.rows // 64, one)

    def turn_rows(src, dst, n):
        at = tile(n, 128)
        dst[:, at] = src[at, :].T

    def contract(left, weight, dst, count, beside=None):
        def one(n):
            if beside is not None:
                beside(n)
            cols = tile(n, 256)
            dst[:, cols] = lax.dot_general(
                left[...], weight[cols, :], (((1,), (1,)), ((), ())), preferred_element_type=F32
            )

        over(count // 256, one)

    def up_grad(layer, unit):
        for k in range(2):
            units.room(unit + k)

        def one(b):
            value = jnp.dot(wide_t[...], gp[:, tile(b, 256)], preferred_element_type=F32)
            for s in range(4):
                for h in range(2):
                    for t in range(2):
                        at = place(unit + t, h, s // 2, b % 2, b // 2)
                        held[(unit + t) % HELD, s % 2, h, at] = value[
                            s * 128 + h * 64 : s * 128 + h * 64 + 64, t * 128 : t * 128 + 128
                        ]

        over(8, one)
        units.produced(2.5, unit, unit + 1)

    def out_grad(layer, unit):
        def cast_state(i):
            hb[tile(i, sz.group), :] = r.states[tile(i + 1, sz.group), :].astype(BF16)

        if layer < last:
            over(sz.steps, cast_state)
        units.room(unit)

        def one(s):
            value = jnp.dot(r.go_t[...], hb[:, tile(s, 256)], preferred_element_type=F32)
            for b in range(8):
                for h in range(2):
                    at = place(unit, h, s // 2, b % 2, b // 2)
                    held[unit % HELD, s % 2, h, at] = value[
                        b * 64 : b * 64 + 64, h * 128 : h * 128 + 128
                    ]

        over(4, one)
        units.produced(1.2, unit)

    def backward(layer, unit):
        late = layer < last

        def freed(*which):
            if layer > 0:
                for name in which:
                    load(layer - 1, name)

        if not late:
            freed(keys.gb)
        need(keys.down_w, keys.p, keys.v)

        def act_dots(n, i):
            rows = tile(i, 256)
            zs[n % 2][rows, :] = lax.dot_general(
                low[rows, :],
                r.down_w[n * 256 : (n + 1) * 256, :],
                (((1,), (1,)), ((), ())),
                preferred_element_type=F32,
            )

        def act_rest(n, i):
            if n < 2:
                turn_rows(r.v, wide_t, 2 * n + i)
            elif n < 4 and late:
                turn_rows(low, low_t, 2 * (n - 2) + i)
            cols = slice(n * 256, (n + 1) * 256)
            for chunk in range(4):
                at = pl.ds(pl.multiple_of(i * 256 + chunk * 64, 64), 64)
                p = r.p[at, cols]
                slope = normal_below(p) + ROOT_TAU * p * jnp.exp(-0.5 * p * p)
                gp[at, cols] = (zs[n % 2][at, :] * slope).astype(BF16)

        in_turn(sz.inner // 256, act_dots, act_rest, lambda n: units.passed(0.6))
        freed(keys.down_w, keys.p, keys.v)
        if not late:
            up_grad(layer, unit + 2)
        need(keys.up_w, keys.y1, keys.u)

        def turn_u(n):
            for k in range(2):
                turn_rows(r.u, r.u_t, 2 * n + k)

        contract(gp, r.up_w, grad, sz.width, turn_u)
        freed(keys.u)
        freed(keys.up_w)
        units.passed(1.5)
        norm_back(r.y1, r.mlp_gain.at[layer : layer + 1], grad, gx, gy1, r.mlp_sum, sz.rows, 64, low)
        freed(keys.y1)
        need(keys.states)
        units.passed(2)
        need(keys.out_w, keys.zf, keys.zi)
        contract(low, r.out_w, ga, sz.hidden, lambda n: turn_rows(low, r.go_t, n))
        freed(keys.out_w)
        units.passed(1)
        if not late:
            out_grad(layer, unit + 4)
        flights = []
        for part, lanes in enumerate(parts):

            def totals(j, pair):
                at = tile(j, sz.group)
                if layer < last:
                    mask = jnp.concatenate([keep[at, :]] * (half // LANES), axis=1)
                    d = gate_weights(*odds(r.zf[at, lanes], r.zi[at, lanes]))[0] * mask
                    decay[at, lanes] = d
                else:
                    d = decay[at, lanes]
                return pair[0] * d, d * (ga[at, lanes] + pair[1])

            one = jnp.ones((sz.group, half), F32)
            pair = steps_of(sz.steps, 2, totals, (one, jnp.zeros_like(one)), reverse=True)
            r.chunk_p[:, lanes] = pair[0]
            r.chunk_t[:, lanes] = pair[1]
            part_totals(r.chunk_p, r.chunk_t, sz, True, prefix, mine, lanes)
            flights.append(exchange_start(1, layer, part))
            carried = [units.expect(link, 16384) for link in ("core", "x", "x")]
            units.passed(0.8)
        need(keys.zc)
        if late:
            need(keys.gb)
            down_grad(layer, unit)
            up_grad(layer, unit + 2)
            out_grad(layer, unit + 4)
        unit += 5
        units.now = max(units.now, *carried)

        def gate_lanes(n):
            wide = 2 * LANES
            lanes = tile(n, wide)

            def walk(j, kept):
                m, bf, bi, bc = kept
                at = tile(j, sz.group)
                d = decay[at, lanes]
                q = ga[at, lanes] + m
                (a, b), zc = odds(r.zf[at, lanes], r.zi[at, lanes]), r.zc[at, lanes]
                vm = jnp.concatenate([valid[at, :]] * 2, axis=1)
                km = jnp.concatenate([keep[at, :]] * 2, axis=1)
                fp, ip, inv = gate_weights(a, b)
                gf = q * (r.states[at, lanes] * km - zc * vm)
                parts = (
                    (gf * (a * inv) * fp).astype(BF16),
                    (-gf * (b * inv) * ip).astype(BF16),
                    (q * vm * ip).astype(BF16),
                )
                for part, value in enumerate(parts):
                    gz[at, pl.ds(pl.multiple_of(part * sz.hidden + n * wide, wide), wide)] = value
                return (d * q,) + tuple(
                    a + value.astype(F32) for a, value in zip((bf, bi, bc), parts)
                )

            zero = jnp.zeros((sz.group, wide), F32)
            _, *sums = steps_of(
                sz.steps, 4, walk, (enter[:, lanes], zero, zero, zero), reverse=True
            )
            for part, total in enumerate(sums):
                small[0, layer * 4 + part : layer * 4 + part + 1, lanes] = jnp.sum(
                    total, axis=0, keepdims=True
                )

        turns = sz.hidden // LANES // 4
        for part in range(2):
            exchange_end(*flights[part], True, part)
            over(turns, lambda n: gate_lanes(n + part * turns))
            units.passed(1.8)
        freed(keys.zf, keys.zi, keys.zc, keys.states)
        for k in range(2):
            units.room(unit + k)

        def gate_grad(b):
            cols = pl.ds(pl.multiple_of(b * 384, 128), 256)
            value = jnp.dot(r.u_t[...], gz[:, cols], preferred_element_type=F32)
            for s in range(4):
                for h in range(2):
                    for t in range(2):
                        at = place(unit + t, h, s // 2, b % 2, b // 2)
                        held[(unit + t) % HELD, s % 2, h, at] = value[
                            s * 128 + h * 64 : s * 128 + h * 64 + 64, t * 128 : t * 128 + 128
                        ]

        over(8, gate_grad)
        units.produced(3, unit, unit + 1)
        unit += 2
        units.room(unit)

        def gate_rest(z):
            right = jnp.concatenate(
                [
                    gz[:, pl.ds(pl.multiple_of((2 * z + y) * 384 + 256, 128), 128)]
                    for y in range(2)
                ],
                axis=1,
            )
            value = jnp.dot(r.u_t[...], right, preferred_element_type=F32)
            for s in range(4):
                for h in range(2):
                    for y in range(2):
                        at = place(unit, h, s // 2, y, z)
                        held[unit % HELD, s % 2, h, at] = value[
                            s * 128 + h * 64 : s * 128 + h * 64 + 64, y * 128 : y * 128 + 128
                        ]

        over(4, gate_rest)
        units.produced(1.5, unit)
        unit += 1
        need(keys.gate_w, keys.stream)
        contract(gz, r.gate_w, grad, sz.width)
        freed(keys.gate_w)
        units.passed(2.5)
        norm_back(r.stream, r.mix_gain.at[layer : layer + 1], grad, gy1, gx, r.mix_sum, sz.rows, 64, low)
        freed(keys.stream)
        row = slice(layer * 4 + 3, layer * 4 + 4)
        small[0, row, : sz.width] = jnp.sum(r.mix_sum[...], axis=0, keepdims=True)
        small[0, row, sz.width : 2 * sz.width] = jnp.sum(r.mlp_sum[...], axis=0, keepdims=True)
        units.passed(1.5)

    forward(0)
    for layer in range(1, layers):
        forward(layer)
    out_copies = from_steps(gy1, r.layer_out, r.out_sems)
    cast(low, gx)
    units.passed(2)
    for index, layer in enumerate(reversed(range(layers))):
        backward(layer, 8 * index)
    units.small_start()
    for copy in out_copies:
        copy.wait()
    out_copies = from_steps(gx, r.input_grad, r.out_sems)
    units.passed(1)
    units.drain()
    for copy in out_copies:
        copy.wait()
    total = small[STAGES]
    count = jnp.int32(0)
    for s in range(r.lens.shape[0]):
        for d in range(r.lens.shape[1]):
            count = count + r.lens[s, d]
    scale = 1.0 / (count.astype(F32) * sz.hidden)
    for layer in range(layers):
        for part in range(3):
            r.gate_bias_grad[layer : layer + 1, part * sz.hidden : (part + 1) * sz.hidden] = total[
                layer * 4 + part : layer * 4 + part + 1, : sz.hidden
            ]
        row = slice(layer * 4 + 3, layer * 4 + 4)
        r.mix_gain_grad[layer : layer + 1, :] = total[row, : sz.width]
        r.mlp_gain_grad[layer : layer + 1, :] = total[row, sz.width : 2 * sz.width]
        lanes = total[layer * 4 : layer * 4 + 1, sz.hidden : sz.hidden + LANES]
        r.forget_mean[layer : layer + 1, :] = (
            jnp.sum(lanes, axis=1, keepdims=True) * scale + jnp.zeros((1, LANES), F32)
        )


def run_whole_step(sz, layers, named):
    lengths = named["lengths"]
    rows, d, h, f = sz.rows, sz.width, sz.hidden, sz.inner
    vm = lambda *dims, kind=F32: pltpu.VMEM(dims, kind)
    sems = pltpu.SemaphoreType
    spec = dict(gate_bias=VMEM, mix_gain=VMEM, mlp_gain=VMEM)
    outputs = dict(
        layer_out=(shape(rows, d), ANY),
        input_grad=(shape(rows, d), ANY),
        gate_weight_grad=(shape(layers, 128, 384), VMEM),
        gate_bias_grad=(shape(layers, 3 * h), VMEM),
        out_weight_grad=(shape(layers, 64, 256), VMEM),
        up_weight_grad=(shape(layers, 128, 256), VMEM),
        down_weight_grad=(shape(layers, 64, 512), VMEM),
        mix_gain_grad=(shape(layers, d), VMEM),
        mlp_gain_grad=(shape(layers, d), VMEM),
        forget_mean=(shape(layers, LANES), VMEM),
    )
    results = len(outputs)
    kept = dict(
        u=((rows, d), BF16),
        zf=((rows, h), F32),
        zi=((rows, h), F32),
        zc=((rows, h), F32),
        states=((rows + sz.group, h), F32),
        y1=((rows, d), F32),
        v=((rows, d), BF16),
        p=((rows, f), F32),
        gb=((rows, f), BF16),
        stream=((rows, d), F32),
    )
    scratch = {}
    for name, (dims, kind) in kept.items():
        outputs[name + "_save"] = (shape(layers - 1, *dims, kind=kind), ANY)
        scratch[name] = vm(*dims, kind=kind)
    scratch.update(
        gate_w=vm(d, 3 * h, kind=BF16),
        out_w=vm(h, d, kind=BF16),
        up_w=vm(d, f, kind=BF16),
        down_w=vm(f, d, kind=BF16),
        valid=vm(rows, LANES),
        keep=vm(rows, LANES),
        gx=vm(rows, d),
        low=vm(rows, d, kind=BF16),
        low_t=vm(d, rows, kind=BF16),
        wide_t=vm(d, rows, kind=BF16),
        u_t=vm(d, rows, kind=BF16),
        go_t=vm(d, rows, kind=BF16),
        hb=vm(rows, h, kind=BF16),
        z1=vm(rows, 256),
        forget=vm(8, LANES),
        ga=vm(rows, h),
        gz=vm(rows, 3 * h, kind=BF16),
        grad=vm(rows, d),
        gy1=vm(rows, d),
        decay=vm(rows, h),
        chunk_p=vm(sz.group, h),
        chunk_t=vm(sz.group, h),
        prefix=vm(2, sz.group, h),
        enter=vm(sz.group, h),
        mine=vm(8, h),
        slots=vm(2, layers, sz.sections, 8, h),
        mlp_sum=vm(8, d),
        mix_sum=vm(8, d),
        held=vm(HELD, 2, 2, 16, BLOCK, LANES),
        small=vm(STAGES + 1, 8, SMALL),
        small_arrived=vm(STAGES, 8, SMALL),
        in_sems=sems.DMA((3,)),
        lens=pltpu.SMEM(lengths.shape, jnp.int32),
        out_sems=sems.DMA((d // LANES,)),
        natural=vm(d // LANES, rows, LANES),
        load_sems=sems.DMA((len(kept) + 4,)),
        save_sems=sems.DMA((len(kept) + 4,)),
        pair_send=sems.DMA((2, layers, 2, sz.sections - 1)),
        pair_recv=sems.DMA((2, layers, 2, sz.sections - 1)),
        send_sems=sems.DMA((SENDS, 2 * STAGES - 1)),
        recv_sems=sems.DMA((max(RINGS), 2 * STAGES - 1)),
        credits=sems.REGULAR((2 * STAGES - 1, 8 * layers)),
        small_send=sems.DMA((STAGES,)),
        small_recv=sems.DMA((STAGES,)),
    )
    for stage in range(STAGES):
        scratch[f"arrived{stage}"] = vm(RINGS[stage], 2, 16 >> stage, BLOCK, LANES)
    names = list(named) + list(outputs) + list(scratch)
    out = pl.pallas_call(
        functools.partial(whole_step, sz, layers, names),
        out_shape=tuple(value for value, _ in outputs.values()),
        in_specs=[spec.get(name, ANY) for name in named],
        out_specs=[place_of for _, place_of in outputs.values()],
        scratch_shapes=list(scratch.values()),
        compiler_params=pltpu.CompilerParams(
            collective_id=4, has_side_effects=True, vmem_limit_bytes=LIMIT
        ),
        name="whole_step",
    )(*named.values())
    return out[:results]


def deliver_kernel(count, *refs):
    sources, targets, held = refs[:count], refs[count : 2 * count], refs[2 * count : 3 * count - 1]
    sems = refs[3 * count - 1]
    arrivals = [
        pltpu.make_async_copy(sources[i], held[i], sems.at[0, i]) for i in range(count - 1)
    ]
    departures = [
        pltpu.make_async_copy(held[i], targets[i], sems.at[1, i]) for i in range(count - 1)
    ]
    for copy in arrivals:
        copy.start()
    for layer in range(targets[-1].shape[0]):
        targets[-1][layer] = sources[-1][layer, 0]
    for arrival, departure in zip(arrivals, departures):
        arrival.wait()
        departure.start()
    for copy in departures:
        copy.wait()


def deliver(values):
    count = len(values)
    scalars = pl.BlockSpec(memory_space=pltpu.SMEM)
    shapes = [shape(*value.shape) for value in values[:-1]] + [shape(values[-1].shape[0])]
    return pl.pallas_call(
        functools.partial(deliver_kernel, count),
        out_shape=tuple(shapes),
        in_specs=[ANY] * (count - 1) + [scalars],
        out_specs=[ANY] * (count - 1) + [scalars],
        scratch_shapes=[pltpu.VMEM(value.shape, F32) for value in values[:-1]]
        + [pltpu.SemaphoreType.DMA((2, count - 1))],
        compiler_params=pltpu.CompilerParams(vmem_limit_bytes=LIMIT),
        name="deliver",
    )(*values)


def mask_kernel(sizes, lens, valid, keep):
    fill_masks(lens, valid, keep, sizes)


def body(
    activations,
    cotangent,
    lengths,
    gate_weight,
    gate_bias,
    out_weight,
    up_weight,
    down_weight,
    mix_gain,
    mlp_gain,
):
    micro, span, width = activations.shape
    layers = gate_weight.shape[0]
    sz = Sizes(
        micro, span, width, out_weight.shape[1], up_weight.shape[2], lax.axis_size("section")
    )

    blocks = (width // 4, 3 * sz.hidden // 8, width // 8, sz.inner // 4, sz.hidden // 4)
    axes = (lax.axis_size("section"), lax.axis_size("batch"))
    if axes == (4, 8) and blocks == (128, 384, 64, 512, 256):
        out = run_whole_step(
            sz,
            layers,
            dict(
                activations=activations.reshape(sz.rows, width),
                cotangent=cotangent.reshape(sz.rows, width),
                lengths=lengths.T,
                gate_bias=gate_bias,
                mix_gain=mix_gain,
                mlp_gain=mlp_gain,
                gate_hbm=gate_weight,
                out_hbm=out_weight,
                up_hbm=up_weight,
                down_hbm=down_weight,
            ),
        )
        stream_out, input_grad, gate_g, bias_g, out_g, up_g, down_g, *rest = deliver(out)
        return (
            stream_out.reshape(activations.shape),
            input_grad.reshape(activations.shape),
            gate_g,
            bias_g,
            out_g.transpose(0, 2, 1),
            up_g,
            down_g.transpose(0, 2, 1),
            *rest,
        )

    def arranged(value):
        value = value.astype(F32).reshape(micro, CHUNKS, sz.steps, width)
        return value.transpose(2, 0, 1, 3).reshape(sz.rows, width)

    def restored(value):
        value = value.reshape(sz.steps, micro, CHUNKS, width).transpose(1, 2, 0, 3)
        return value.reshape(micro, span, width)

    masks = pl.pallas_call(
        functools.partial(mask_kernel, sz),
        out_shape=(shape(sz.rows, LANES), shape(sz.rows, LANES)),
        in_specs=[pl.BlockSpec(memory_space=pltpu.SMEM)],
        out_specs=[VMEM] * 2,
        name="masks",
    )(lengths)
    weights = (gate_weight, out_weight, up_weight, down_weight)
    stream = arranged(activations)
    streams, saved, forgets = [], [], []
    for layer in range(layers):
        streams.append(stream)
        stream, *kept, forget, pairs = run_forward(
            sz,
            layer,
            stream,
            masks,
            gate_bias[layer : layer + 1],
            mix_gain[layer : layer + 1],
            mlp_gain[layer : layer + 1],
            weights,
        )
        saved.append((*kept, pairs))
        forgets.append(forget)
    layer_out = restored(stream)
    gx = arranged(cotangent)
    true_count = jnp.sum(lengths).astype(F32)
    forgets = [jnp.sum(forget) for forget in forgets]
    sums, small = [None] * layers, [None] * layers
    for layer in reversed(range(layers)):
        gx, gate_g, out_g, up_g, down_g, bias_g, mix_g, mlp_g = run_backward(
            sz,
            layer,
            gx,
            streams[layer],
            masks,
            mix_gain[layer : layer + 1],
            mlp_gain[layer : layer + 1],
            saved[layer],
            weights,
        )
        sums[layer] = (gate_g, out_g.T, up_g, down_g.T)
        small[layer] = tuple(jnp.sum(part, axis=0) for part in (bias_g, mix_g, mlp_g))
    input_grad = restored(gx)
    stacked = tuple(jnp.stack(parts) for parts in zip(*sums))
    partial_sums = lax.psum_scatter(stacked, "section", scatter_dimension=1, tiled=True)
    large = lax.psum_scatter(partial_sums, "batch", scatter_dimension=2, tiled=True)
    bias_grad, mix_grad, mlp_grad = (jnp.stack(parts) for parts in zip(*small))
    bias_grad, mix_grad, mlp_grad, forget = lax.psum(
        (bias_grad, mix_grad, mlp_grad, jnp.stack(forgets)), ("section", "batch")
    )
    forget_mean = forget / (true_count * sz.hidden)
    return (
        layer_out,
        input_grad,
        large[0],
        bias_grad,
        large[1],
        large[2],
        large[3],
        mix_grad,
        mlp_grad,
        forget_mean,
    )


def solution(mesh):
    stream = P("batch", "section", None)
    block = P(None, "section", "batch")
    return jax.shard_map(
        body,
        mesh=mesh,
        in_specs=(stream, stream) + (P(),) * 8,
        out_specs=(stream, stream, block, P(), block, block, block, P(), P(), P()),
        check_vma=False,
    )
```

```python
import functools
import types

import jax
import jax.numpy as jnp
from jax import lax
from jax.experimental import pallas as pl
from jax.experimental.pallas import tpu as pltpu
from jax.sharding import PartitionSpec as P

epsilon = 1e-06
MESH = pl.DeviceIdType.MESH
F32, BF16 = jnp.float32, jnp.bfloat16
CHUNKS = 8
LANES = 128
ROOT_HALF = 0.7071067811865476
ROOT_TAU = 0.3989422804014327


def tile(index, size):
    return pl.ds(pl.multiple_of(index * size, size), size)


def inverse(value):
    r = pltpu.reciprocal(value, approx=True)
    return r * (2.0 - value * r)


def normal_below(p):
    return 0.5 + 0.5 * lax.erf(p * ROOT_HALF)


def steps_of(count, unroll, one, start, reverse=False):
    def turn(i, carry):
        for k in range(unroll):
            at = i * unroll + k
            carry = one(count - 1 - at if reverse else at, carry)
        return carry

    return lax.fori_loop(0, count // unroll, turn, start)


def odds(zf, zi):
    return jnp.exp(jnp.minimum(-zf, 86.0)), jnp.exp(jnp.minimum(-zi, 86.0))


def gate_weights(a, b):
    inv = inverse(2.0 + a + b)
    return (1.0 + b) * inv, (1.0 + a) * inv, inv


def greet_section(sections):
    me = lax.axis_index("section")
    barrier = pltpu.get_barrier_semaphore()
    for hop in range(1, sections):
        pl.semaphore_signal(
            barrier, inc=1, device_id={"section": lax.rem(me + hop, sections)}, device_id_type=MESH
        )
    pl.semaphore_wait(barrier, sections - 1)


def exchange(mine, slots, send_sems, recv_sems, sections):
    me = lax.axis_index("section")
    copies = []
    for hop in range(1, sections):
        copies.append(
            pltpu.make_async_remote_copy(
                src_ref=mine,
                dst_ref=slots.at[me],
                send_sem=send_sems.at[hop - 1],
                recv_sem=recv_sems.at[hop - 1],
                device_id={"section": lax.rem(me + hop, sections)},
                device_id_type=MESH,
            )
        )
    for copy in copies:
        copy.start()
    slots[me] = mine[...]
    for copy in copies:
        copy.wait()


def norm_rows(stream, gain, low, rows, step):
    def one(i, carry):
        at = tile(i, step)
        x = stream[at, :]
        r = lax.rsqrt(jnp.mean(x * x, axis=-1, keepdims=True) + epsilon)
        low[at, :] = (x * r * gain[...]).astype(BF16)
        return carry

    lax.fori_loop(0, rows // step, one, 0)


def norm_back(stream, gain, grad, through, out, gain_sum, rows, step, low=None):
    width = stream.shape[1]

    def one(i, total):
        at = tile(i, step)
        x = stream[at, :]
        r = lax.rsqrt(jnp.mean(x * x, axis=-1, keepdims=True) + epsilon)
        n = x * r
        g = grad[at, :]
        a = g * gain[...]
        value = through[at, :] + r * (a - n * jnp.mean(a * n, axis=-1, keepdims=True))
        out[at, :] = value
        if low is not None:
            low[at, :] = value.astype(BF16)
        return total + jnp.sum((g * n).reshape(step // 8, 8, width), axis=0)

    gain_sum[...] = lax.fori_loop(0, rows // step, one, jnp.zeros((8, width), F32))


def fill_masks(lens, valid, keep, sizes, turned=False):
    section = lax.axis_index("section")
    group = lax.axis_index("batch")
    starts, totals = [], []
    for s in range(sizes.micro):
        total, begin = 0, []
        for d in range(lens.shape[0 if turned else 1]):
            row = group * sizes.micro + s
            length = lens[d, row] if turned else lens[row, d]
            begin.append(jnp.where(length > 0, total, -1))
            total = total + length
        starts.append(begin)
        totals.append(total)
    chunk_place = lax.broadcasted_iota(jnp.int32, (8, LANES), 0) * sizes.steps

    def one(j, carry):
        for s in range(sizes.micro):
            place = section * sizes.span + j + chunk_place
            true = place < totals[s]
            first = place == starts[s][0]
            for begin in starts[s][1:]:
                first = first | (place == begin)
            at = pl.ds(pl.multiple_of(j * sizes.group + s * 8, 8), 8)
            valid[at, :] = jnp.where(true, 1.0, 0.0)
            keep[at, :] = jnp.where(true & jnp.logical_not(first), 1.0, 0.0)
        return carry

    lax.fori_loop(0, sizes.steps, one, 0)


def scan_totals(first, second, sizes, reverse, prefix, chunk, mine):
    for s in range(sizes.micro):
        p = jnp.ones((1, sizes.hidden), F32)
        t = jnp.zeros((1, sizes.hidden), F32)
        for c in reversed(range(CHUNKS)) if reverse else range(CHUNKS):
            at = s * 8 + c
            prefix[0, at : at + 1, :] = p
            prefix[1, at : at + 1, :] = t
            pc = first[at : at + 1, :]
            t = pc * t + second[at : at + 1, :]
            p = p * pc
        mine[s : s + 1, :] = p
        mine[sizes.micro + s : sizes.micro + s + 1, :] = t


def scan_enter(slots, prefix, enter, sizes, reverse):
    me = lax.axis_index("section")
    for s in range(sizes.micro):
        a = jnp.zeros((1, sizes.hidden), F32)
        order = range(sizes.sections - 1, 0, -1) if reverse else range(sizes.sections - 1)
        for k in order:
            reached = k > me if reverse else k < me
            pk = slots[k, s : s + 1, :]
            tk = slots[k, sizes.micro + s : sizes.micro + s + 1, :]
            a = jnp.where(reached, pk * a + tk, a)
        at = slice(s * 8, s * 8 + 8)
        enter[at, :] = prefix[0, at, :] * a + prefix[1, at, :]


def part_totals(first, second, sizes, reverse, prefix, mine, lanes):
    for s in range(sizes.micro):
        p = jnp.ones((1, lanes.stop - lanes.start), F32)
        t = jnp.zeros_like(p)
        for c in reversed(range(CHUNKS)) if reverse else range(CHUNKS):
            at = s * 8 + c
            prefix[0, at : at + 1, lanes] = p
            prefix[1, at : at + 1, lanes] = t
            pc = first[at : at + 1, lanes]
            t = pc * t + second[at : at + 1, lanes]
            p = p * pc
        mine[s : s + 1, lanes] = p
        mine[sizes.micro + s : sizes.micro + s + 1, lanes] = t


def part_enter(slots, prefix, enter, sizes, reverse, lanes):
    me = lax.axis_index("section")
    for s in range(sizes.micro):
        a = jnp.zeros((1, lanes.stop - lanes.start), F32)
        order = range(sizes.sections - 1, 0, -1) if reverse else range(sizes.sections - 1)
        for k in order:
            reached = k > me if reverse else k < me
            pk = slots[k, s : s + 1, lanes]
            tk = slots[k, sizes.micro + s : sizes.micro + s + 1, lanes]
            a = jnp.where(reached, pk * a + tk, a)
        at = slice(s * 8, s * 8 + 8)
        enter[at, lanes] = prefix[0, at, lanes] * a + prefix[1, at, lanes]


class Sizes:
    def __init__(self, micro, span, width, hidden, inner, sections):
        self.micro, self.span, self.width = micro, span, width
        self.hidden, self.inner, self.sections = hidden, inner, sections
        self.rows = micro * span
        self.steps = span // CHUNKS
        self.group = micro * CHUNKS


def forward_kernel(
    sizes,
    layer,
    stream,
    valid,
    keep,
    bias,
    mix_gain,
    mlp_gain,
    gate_hbm,
    out_hbm,
    up_hbm,
    down_hbm,
    next_stream,
    u,
    sf_out,
    si_out,
    zc_out,
    states,
    y1,
    v,
    p_out,
    gb,
    forget,
    pair_slots,
    gate_w,
    out_w,
    up_w,
    down_w,
    z,
    decay,
    drive,
    hb,
    chunk_p,
    chunk_t,
    prefix,
    enter,
    mine,
    weight_sems,
    send_sems,
    recv_sems,
):
    sz = sizes
    loads = [
        pltpu.make_async_copy(src.at[layer], dst, weight_sems.at[i])
        for i, (src, dst) in enumerate(
            ((gate_hbm, gate_w), (out_hbm, out_w), (up_hbm, up_w), (down_hbm, down_w))
        )
    ]
    for load in loads:
        load.start()
    greet_section(sz.sections)
    mine[...] = jnp.zeros_like(mine)
    norm_rows(stream, mix_gain, u, sz.rows, 64)
    loads[0].wait()
    forget[...] = jnp.zeros_like(forget)
    hw = 256

    def gate_tile(n, carry):
        for part in range(3):
            cols = pl.ds(pl.multiple_of(part * sz.hidden + n * hw, hw), hw)
            z[:, part * hw : (part + 1) * hw] = (
                jnp.dot(u[...], gate_w[:, cols], preferred_element_type=F32) + bias[:, cols]
            )

        def one(i, inner):
            at = tile(i, 64)
            for lane in range(hw // LANES):
                src = lambda part: z[
                    at, part * hw + lane * LANES : part * hw + (lane + 1) * LANES
                ]
                dst = pl.ds(pl.multiple_of(n * hw + lane * LANES, LANES), LANES)
                a = jnp.exp(jnp.minimum(-src(0), 86.0))
                b = jnp.exp(jnp.minimum(-src(1), 86.0))
                zc = src(2)
                fp, ip, _ = gate_weights(a, b)
                vm = valid[at, :]
                decay[at, dst] = fp * keep[at, :]
                drive[at, dst] = ip * zc * vm
                sf_out[at, dst] = a
                si_out[at, dst] = b
                zc_out[at, dst] = zc
                forget[...] += jnp.sum((fp * vm).reshape(8, 8, LANES), axis=0)
            return inner

        lax.fori_loop(0, sz.rows // 64, one, 0)
        return carry

    lax.fori_loop(0, sz.hidden // hw, gate_tile, 0)
    half = sz.hidden // 2
    for part in range(2):
        lanes = slice(part * half, (part + 1) * half)

        def totals(j, pair):
            at = tile(j, sz.group)
            d = decay[at, lanes]
            return pair[0] * d, pair[1] * d + drive[at, lanes]

        one = jnp.ones((sz.group, half), F32)
        pair = steps_of(sz.steps, 4, totals, (one, jnp.zeros_like(one)))
        chunk_p[:, lanes] = pair[0]
        chunk_t[:, lanes] = pair[1]
    scan_totals(chunk_p, chunk_t, sz, False, prefix, None, mine)
    exchange(mine, pair_slots, send_sems, recv_sems, sz.sections)
    scan_enter(pair_slots, prefix, enter, sz, False)
    states[0 : sz.group, :] = enter[...]
    for part in range(2):
        lanes = slice(part * half, (part + 1) * half)

        def walk(j, h):
            at = tile(j, sz.group)
            h = decay[at, lanes] * h + drive[at, lanes]
            states[tile(j + 1, sz.group), lanes] = h
            hb[at, lanes] = h.astype(BF16)
            return h

        steps_of(sz.steps, 4, walk, enter[:, lanes])
    loads[1].wait()

    def out_tile(n, carry):
        cols = tile(n, 256)
        y1[:, cols] = stream[:, cols] + jnp.dot(
            hb[...], out_w[:, cols], preferred_element_type=F32
        )
        return carry

    lax.fori_loop(0, sz.width // 256, out_tile, 0)
    norm_rows(y1, mlp_gain, v, sz.rows, 64)
    loads[2].wait()

    def up_tile(n, carry):
        cols = tile(n, 256)
        p_out[:, cols] = jnp.dot(v[...], up_w[:, cols], preferred_element_type=F32)

        def one(i, inner):
            at = tile(i, 64)
            p = p_out[at, cols]
            gb[at, cols] = (p * normal_below(p)).astype(BF16)
            return inner

        lax.fori_loop(0, sz.rows // 64, one, 0)
        return carry

    lax.fori_loop(0, sz.inner // 256, up_tile, 0)
    loads[3].wait()

    def down_tile(n, carry):
        cols = tile(n, 256)
        next_stream[:, cols] = y1[:, cols] + jnp.dot(
            gb[...], down_w[:, cols], preferred_element_type=F32
        )
        return carry

    lax.fori_loop(0, sz.width // 256, down_tile, 0)


def backward_kernel(
    sizes,
    layer,
    gx,
    stream,
    valid,
    keep,
    mix_gain,
    mlp_gain,
    u,
    sf_in,
    si_in,
    zc_in,
    states,
    y1,
    v,
    p_in,
    gb,
    pair_slots,
    gate_hbm,
    out_hbm,
    up_hbm,
    down_hbm,
    next_gx,
    gate_grad,
    out_grad,
    up_grad,
    down_grad,
    bias_sum,
    mix_sum,
    mlp_sum,
    gate_w,
    out_w,
    up_w,
    down_w,
    low,
    low_t,
    wide_t,
    hb,
    ga,
    gp,
    gz,
    grad,
    gy1,
    decay,
    chunk_p,
    chunk_t,
    prefix,
    enter,
    mine,
    slots,
    weight_sems,
    send_sems,
    recv_sems,
):
    sz = sizes
    loads = [
        pltpu.make_async_copy(src.at[layer], dst, weight_sems.at[i])
        for i, (src, dst) in enumerate(
            ((gate_hbm, gate_w), (out_hbm, out_w), (up_hbm, up_w), (down_hbm, down_w))
        )
    ]
    for load in reversed(loads):
        load.start()
    greet_section(sz.sections)
    mine[...] = jnp.zeros_like(mine)

    def cast(i, carry):
        at = tile(i, 64)
        low[at, :] = gx[at, :].astype(BF16)
        return carry

    lax.fori_loop(0, sz.rows // 64, cast, 0)
    low_t[...] = low[...].T

    def weight_grad(left_t, right, dst, step):
        def one(n, carry):
            cols = tile(n, step)
            dst[:, cols] = jnp.dot(left_t[...], right[:, cols], preferred_element_type=F32)
            return carry

        lax.fori_loop(0, right.shape[1] // step, one, 0)

    weight_grad(low_t, gb, down_grad, 256)
    loads[3].wait()

    def act_tile(n, carry):
        cols = tile(n, 256)
        ga[:, :256] = lax.dot_general(
            low[...], down_w[cols, :], (((1,), (1,)), ((), ())), preferred_element_type=F32
        )

        def one(i, inner):
            at = tile(i, 64)
            p = p_in[at, cols]
            slope = normal_below(p) + ROOT_TAU * p * jnp.exp(-0.5 * p * p)
            gp[at, cols] = (ga[at, :256] * slope).astype(BF16)
            return inner

        lax.fori_loop(0, sz.rows // 64, one, 0)
        return carry

    lax.fori_loop(0, sz.inner // 256, act_tile, 0)
    wide_t[...] = v[...].T
    weight_grad(wide_t, gp, up_grad, 256)
    loads[2].wait()

    def contract(left, weight, dst, step):
        def one(n, carry):
            cols = tile(n, step)
            dst[:, cols] = lax.dot_general(
                left[...], weight[cols, :], (((1,), (1,)), ((), ())), preferred_element_type=F32
            )
            return carry

        lax.fori_loop(0, weight.shape[0] // step, one, 0)

    contract(gp, up_w, grad, 256)
    norm_back(y1, mlp_gain, grad, gx, gy1, mlp_sum, sz.rows, 64)

    def cast_more(i, carry):
        at = tile(i, 64)
        low[at, :] = gy1[at, :].astype(BF16)
        return carry

    lax.fori_loop(0, sz.rows // 64, cast_more, 0)

    def cast_state(i, carry):
        hb[tile(i, sz.group), :] = states[tile(i + 1, sz.group), :].astype(BF16)
        return carry

    lax.fori_loop(0, sz.steps, cast_state, 0)
    low_t[...] = low[...].T
    weight_grad(low_t, hb, out_grad, 256)
    loads[1].wait()
    contract(low, out_w, ga, 256)
    half = sz.hidden // 2
    for part in range(2):
        lanes = slice(part * half, (part + 1) * half)

        def totals(i, pair):
            at = tile(sz.steps - 1 - i, sz.group)
            mask = jnp.concatenate([keep[at, :]] * (half // LANES), axis=1)
            d = gate_weights(sf_in[at, lanes], si_in[at, lanes])[0] * mask
            decay[at, lanes] = d
            return pair[0] * d, d * (ga[at, lanes] + pair[1])

        pair = lax.fori_loop(
            0,
            sz.steps,
            totals,
            (jnp.ones((sz.group, half), F32), jnp.zeros((sz.group, half), F32)),
        )
        chunk_p[:, lanes] = pair[0]
        chunk_t[:, lanes] = pair[1]
    scan_totals(chunk_p, chunk_t, sz, True, prefix, None, mine)
    exchange(mine, slots, send_sems, recv_sems, sz.sections)
    scan_enter(slots, prefix, enter, sz, True)

    def gate_lane(n, carry):
        lanes = tile(n, LANES)

        def walk(i, kept):
            m, bf, bi, bc = kept
            j = sz.steps - 1 - i
            at = tile(j, sz.group)
            d = decay[at, lanes]
            q = ga[at, lanes] + m
            a = sf_in[at, lanes]
            b = si_in[at, lanes]
            zc = zc_in[at, lanes]
            vm = valid[at, :]
            fp, ip, inv = gate_weights(a, b)
            gf = q * (states[at, lanes] * keep[at, :] - zc * vm)
            gzf = (gf * (a * inv) * fp).astype(BF16)
            gzi = (-gf * (b * inv) * ip).astype(BF16)
            gzc = (q * vm * ip).astype(BF16)
            gz[at, lanes] = gzf
            gz[at, pl.ds(pl.multiple_of(sz.hidden + n * LANES, LANES), LANES)] = gzi
            gz[at, pl.ds(pl.multiple_of(2 * sz.hidden + n * LANES, LANES), LANES)] = gzc
            return (
                d * q,
                bf + gzf.astype(F32),
                bi + gzi.astype(F32),
                bc + gzc.astype(F32),
            )

        zero = jnp.zeros((sz.group, LANES), F32)
        _, bf, bi, bc = lax.fori_loop(0, sz.steps, walk, (enter[:, lanes], zero, zero, zero))
        for part, total in enumerate((bf, bi, bc)):
            where = pl.ds(pl.multiple_of(part * sz.hidden + n * LANES, LANES), LANES)
            bias_sum[:, where] = jnp.sum(total.reshape(sz.group // 8, 8, LANES), axis=0)
        return carry

    lax.fori_loop(0, sz.hidden // LANES, gate_lane, 0)
    wide_t[...] = u[...].T
    weight_grad(wide_t, gz, gate_grad, 256)
    loads[0].wait()
    contract(gz, gate_w, grad, 256)
    norm_back(stream, mix_gain, grad, gy1, next_gx, mix_sum, sz.rows, 64)


VMEM = pl.BlockSpec(memory_space=pltpu.VMEM)
ANY = pl.BlockSpec(memory_space=pl.ANY)
LIMIT = 63 * 2**20


def shape(*dims, kind=F32):
    return jax.ShapeDtypeStruct(dims, kind)


def exchange_scratch(sz):
    return [
        pltpu.SemaphoreType.DMA((4,)),
        pltpu.SemaphoreType.DMA((sz.sections - 1,)),
        pltpu.SemaphoreType.DMA((sz.sections - 1,)),
    ]


def weight_scratch(sz):
    return [
        pltpu.VMEM((sz.width, 3 * sz.hidden), BF16),
        pltpu.VMEM((sz.hidden, sz.width), BF16),
        pltpu.VMEM((sz.width, sz.inner), BF16),
        pltpu.VMEM((sz.inner, sz.width), BF16),
    ]


def scan_scratch(sz):
    return [
        pltpu.VMEM((sz.group, sz.hidden), F32),
        pltpu.VMEM((sz.group, sz.hidden), F32),
        pltpu.VMEM((2, sz.group, sz.hidden), F32),
        pltpu.VMEM((sz.group, sz.hidden), F32),
        pltpu.VMEM((8, sz.hidden), F32),
    ]


def run_forward(sz, layer, stream, masks, bias, mix_gain, mlp_gain, weights):
    r, d, h, f = sz.rows, sz.width, sz.hidden, sz.inner
    return pl.pallas_call(
        functools.partial(forward_kernel, sz, layer),
        out_shape=(
            shape(r, d),
            shape(r, d, kind=BF16),
            shape(r, h),
            shape(r, h),
            shape(r, h),
            shape(r + sz.group, h),
            shape(r, d),
            shape(r, d, kind=BF16),
            shape(r, f),
            shape(r, f, kind=BF16),
            shape(8, LANES),
            shape(sz.sections, 8, h),
        ),
        in_specs=[VMEM] * 6 + [ANY] * 4,
        out_specs=[VMEM] * 12,
        scratch_shapes=weight_scratch(sz)
        + [
            pltpu.VMEM((r, 3 * 256), F32),
            pltpu.VMEM((r, h), F32),
            pltpu.VMEM((r, h), F32),
            pltpu.VMEM((r, h), BF16),
        ]
        + scan_scratch(sz)
        + exchange_scratch(sz),
        compiler_params=pltpu.CompilerParams(
            collective_id=layer, has_side_effects=True, vmem_limit_bytes=LIMIT
        ),
        name=f"forward_{layer}",
    )(stream, *masks, bias, mix_gain, mlp_gain, *weights)


def run_backward(sz, layer, gx, stream, masks, mix_gain, mlp_gain, saved, weights):
    r, d, h, f = sz.rows, sz.width, sz.hidden, sz.inner
    return pl.pallas_call(
        functools.partial(backward_kernel, sz, layer),
        out_shape=(
            shape(r, d),
            shape(d, 3 * h),
            shape(d, h),
            shape(d, f),
            shape(d, f),
            shape(8, 3 * h),
            shape(8, d),
            shape(8, d),
        ),
        in_specs=[VMEM] * 16 + [ANY] * 4,
        out_specs=[VMEM] * 8,
        scratch_shapes=weight_scratch(sz)
        + [
            pltpu.VMEM((r, d), BF16),
            pltpu.VMEM((d, r), BF16),
            pltpu.VMEM((d, r), BF16),
            pltpu.VMEM((r, h), BF16),
            pltpu.VMEM((r, h), F32),
            pltpu.VMEM((r, f), BF16),
            pltpu.VMEM((r, 3 * h), BF16),
            pltpu.VMEM((r, d), F32),
            pltpu.VMEM((r, d), F32),
            pltpu.VMEM((r, h), F32),
        ]
        + scan_scratch(sz)
        + [pltpu.VMEM((sz.sections, 8, h), F32)]
        + exchange_scratch(sz),
        compiler_params=pltpu.CompilerParams(
            collective_id=2 + layer, has_side_effects=True, vmem_limit_bytes=LIMIT
        ),
        name=f"backward_{layer}",
    )(gx, stream, *masks, mix_gain, mlp_gain, *saved, *weights)


BLOCK = 64
HELD = 3
RINGS = (4, 5, 5, 16, 16)
SENDS = 16
STAGES = 5
WINDOW = 4
DELAY = 1.5
SMALL = 1280


ORDERS = (((0, 2, 1, 3), (1, 2, 0, 3)),) * 16


class Units:
    def __init__(self, count, refs):
        self.count = count
        self.__dict__.update(vars(refs))
        self.arrived = [getattr(refs, f"arrived{stage}") for stage in range(STAGES)]
        section, batch = lax.axis_index("section"), lax.axis_index("batch")
        core, x = section % 2, section // 2
        y, za, zb = batch % 2, (batch // 2) % 2, batch // 4
        self.core = core
        self.where = (x, y, za, zb)
        self.partner = {
            "core": {"section": section + 1 - 2 * core},
            "x": {"section": section + 2 - 4 * x},
            "y": {"batch": batch + 1 - 2 * y},
            "za": {"batch": batch + 2 - 4 * za},
            "zb": {"batch": batch + 4 - 8 * zb},
        }
        self.now = 0.0
        self.links = ("core", "x", "y", "z")
        self.free_at = dict.fromkeys(self.links, 0.0)
        self.flying = dict.fromkeys(self.links, 0)
        self.queues = {link: [] for link in self.links}
        self.ready = {}
        self.summed = set()
        self.copies = {}
        self.small_left = None

    def greet(self):
        section = lax.axis_index("section")
        others = [self.partner["y"], self.partner["za"], self.partner["zb"]]
        others += [{"section": lax.rem(section + hop, 4)} for hop in range(1, 4)]
        for other in others:
            pl.semaphore_signal(
                pltpu.get_barrier_semaphore(), inc=1, device_id=other, device_id_type=MESH
            )

    def greeted(self):
        pl.semaphore_wait(pltpu.get_barrier_semaphore(), 6)

    def name(self, unit, stage, half):
        return "core" if stage == 0 else ("x", "y", "za", "zb")[ORDERS[unit][half][stage - 1]]

    def link(self, unit, stage, half):
        name = self.name(unit, stage, half)
        return "z" if name[0] == "z" else name

    def bit(self, unit, stage, half):
        return self.where[ORDERS[unit][half][stage - 1]]

    def arrival(self, unit, stage, half):
        ref = self.arrived[stage].at[unit % RINGS[stage]]
        return ref if stage == 0 else ref.at[half]

    def copy(self, unit, stage, half):
        at = 0 if stage == 0 else 2 * stage - 1 + half
        if stage == 0:
            src = self.held.at[unit % HELD, 1 - self.core]
        else:
            count = 16 >> stage
            src = self.arrived[stage - 1].at[unit % RINGS[stage - 1], half]
            src = src.at[pl.ds((1 - self.bit(unit, stage, half)) * count, count)]
        return pltpu.make_async_remote_copy(
            src_ref=src,
            dst_ref=self.arrival(unit, stage, half),
            send_sem=self.send_sems.at[unit % SENDS, at],
            recv_sem=self.recv_sems.at[unit % RINGS[stage], at],
            device_id=self.partner[self.name(unit, stage, half)],
            device_id_type=MESH,
        )

    def has_place(self, unit, stage, half):
        before = unit - RINGS[stage]
        if before < 0:
            return True
        if stage == 0:
            return (before, 1, 0) in self.summed and (before, 1, 1) in self.summed
        return (before, min(stage + 1, STAGES - 1), half) in self.summed

    def credit(self, unit, stage, half):
        after = unit + RINGS[stage]
        if after < self.count:
            pl.semaphore_signal(
                self.credits.at[0 if stage == 0 else 2 * stage - 1 + half, after],
                inc=1,
                device_id=self.partner[self.name(after, stage, half)],
                device_id_type=MESH,
            )

    def pump(self):
        for link, queue in self.queues.items():
            while self.flying[link] < WINDOW:
                key = next((key for key in queue if self.has_place(*key)), None)
                if key is None:
                    break
                queue.remove(key)
                self.flying[link] += 1
                unit, stage, half = key
                if unit >= RINGS[stage]:
                    at = 0 if stage == 0 else 2 * stage - 1 + half
                    pl.semaphore_wait(self.credits.at[at, unit], 1)
                self.copies[key] = self.copy(*key)
                self.copies[key].start()
                blocks = 32 if stage == 0 else 16 >> stage
                self.ready[key] = self.expect(link, blocks * BLOCK * LANES * 4)

    def expect(self, link, size):
        rate = 250e3 if link == "core" else 45e3
        self.free_at[link] = max(self.now, self.free_at[link]) + size / rate
        return self.free_at[link] + DELAY

    def push(self, unit, stage, half):
        self.queues[self.link(unit, stage, half)].append((unit, stage, half))
        self.pump()

    def produced(self, us, *which):
        self.now += us
        for unit in which:
            self.push(unit, 0, 0)
        self.passed(0)

    def add(self, dst, src, count):
        turn = min(count, 4)

        def one(i, carry):
            for k in range(turn):
                dst[i * turn + k] += src[i * turn + k]
            return carry

        if count == turn:
            one(0, 0)
        else:
            lax.fori_loop(0, count // turn, one, 0)

    def step(self, unit, stage, half):
        key = (unit, stage, half)
        del self.ready[key]
        self.copies[key].wait_recv()
        here = self.arrival(unit, stage, half)
        if stage == 0:
            for h in range(2):
                self.add(here.at[h], self.held.at[unit % HELD, self.core, h], 16)
        else:
            count = 16 >> stage
            before = self.arrived[stage - 1].at[unit % RINGS[stage - 1], half]
            self.add(here, before.at[pl.ds(self.bit(unit, stage, half) * count, count)], count)
            self.copies.pop(key).wait_send()
        self.summed.add(key)
        self.flying[self.link(unit, stage, half)] -= 1
        self.now += 0.25
        if stage > 1 or (unit, 1, 1 - half) in self.summed:
            if stage > 0:
                self.credit(unit, stage - 1, half if stage > 1 else 0)
        if stage == 0:
            for h in range(2):
                self.push(unit, 1, h)
        elif stage < STAGES - 1:
            self.push(unit, stage + 1, half)
        else:
            self.finish(unit, half, here[0])
            self.credit(unit, stage, half)
        self.pump()

    def finish(self, unit, half, block):
        layer, k = self.count // 8 - 1 - unit // 8, unit % 8
        if k < 2 or k == 4:
            ref, at = (self.down_weight_grad, k) if k < 2 else (self.out_weight_grad, 0)
            ref[layer, :, at * 256 + half * 128 : at * 256 + half * 128 + 128] = block
        else:
            ref, at = (self.up_weight_grad, k - 2) if k < 4 else (self.gate_weight_grad, k - 5)
            rows = slice(half * BLOCK, half * BLOCK + BLOCK)
            ref[layer, rows, at * LANES : at * LANES + LANES] = block

    def small_copy(self, stage):
        name = ("core", "x", "y", "za", "zb")[stage]
        return pltpu.make_async_remote_copy(
            src_ref=self.small.at[stage],
            dst_ref=self.small_arrived.at[stage],
            send_sem=self.small_send.at[stage],
            recv_sem=self.small_recv.at[stage],
            device_id=self.partner[name],
            device_id_type=MESH,
        )

    def small_start(self):
        self.small_left = 0
        self.small_copies = [self.small_copy(0)]
        self.small_copies[0].start()
        self.small_ready = self.now + 3.0

    def small_step(self):
        stage = self.small_left
        self.small_copies[stage].wait_recv()
        self.small[stage + 1] = self.small[stage] + self.small_arrived[stage]
        self.small_left += 1
        if self.small_left < STAGES:
            self.small_copies.append(self.small_copy(self.small_left))
            self.small_copies[-1].start()
            self.small_ready = self.now + 3.0
        else:
            for copy in self.small_copies:
                copy.wait_send()

    def open(self, unit, stage, half):
        halves = range(2) if stage == 0 else (half,)
        before = unit - RING
        return (
            before < 0
            or stage == STAGES - 1
            or all((before, stage + 1, h) in self.consumed for h in halves)
        )

    def next(self):
        best = min(self.ready.items(), key=lambda item: (item[1], item[0]), default=None)
        small = self.small_left is not None and self.small_left < STAGES
        if small and (best is None or self.small_ready <= best[1]):
            return self.small_ready, None
        return (best[1], best[0]) if best else None

    def take(self, item):
        self.now = max(self.now, item[0])
        if item[1] is None:
            self.small_step()
        else:
            self.step(*item[1])

    def passed(self, us):
        self.now += us
        while (item := self.next()) and item[0] <= self.now:
            self.take(item)

    def room(self, unit):
        before = (unit - HELD, 0, 0)
        while unit >= HELD and before not in self.summed:
            self.take(self.next())
        if before in self.copies:
            self.copies.pop(before).wait_send()

    def drain(self):
        while item := self.next():
            self.take(item)
        for key in list(self.copies):
            self.copies.pop(key).wait_send()


def place(unit, half, x, y, z):
    where = (x, y, z % 2, z // 2)
    order = ORDERS[unit][half]
    return where[order[0]] * 8 + where[order[1]] * 4 + where[order[2]] * 2 + where[order[3]]


def strided(start, steps):
    return pl.ds(start, CHUNKS, stride=steps)


def whole_step(sz, layers, names, *args):
    r = types.SimpleNamespace(**dict(zip(names, args)))
    units = Units(8 * layers, r)
    valid, keep, low, low_t, wide_t = r.valid, r.keep, r.low, r.low_t, r.wide_t
    hb, ga, gz, grad, gy1, gx = r.hb, r.ga, r.gz, r.grad, r.gy1, r.gx
    gp = gz.at[:, : sz.inner]
    decay, enter, prefix, mine = r.decay, r.enter, r.prefix, r.mine
    small, held = r.small, r.held
    natural = r.natural
    last = layers - 1
    half = sz.hidden // 2
    zs = (ga.at[:, :768], r.z1)
    drive = r.drive
    homes = dict(gate_w=r.gate_hbm, out_w=r.out_hbm, up_w=r.up_hbm, down_w=r.down_hbm)
    homes.update(u=r.u_save, a=r.a_save, b=r.b_save, zc=r.zc_save, states=r.states_save)
    homes.update(y1=r.y1_save, v=r.v_save, p=r.p_save, gb=r.gb_save, stream=r.stream_save)
    keys = types.SimpleNamespace(**{name: name for name in homes})
    index_of = {name: i for i, name in enumerate(homes)}
    loads, saves = {}, {}

    def load(layer, name):
        copy = pltpu.make_async_copy(
            homes[name].at[layer], getattr(r, name), r.load_sems.at[index_of[name]]
        )
        copy.start()
        loads[name] = copy

    def need(*wanted):
        for name in wanted:
            if name in loads:
                loads.pop(name).wait()

    def save(layer, name, ref=None):
        if layer < last:
            src = getattr(r, name) if ref is None else ref
            copy = pltpu.make_async_copy(
                src, homes[name].at[layer], r.save_sems.at[index_of[name]]
            )
            copy.start()
            saves[name] = copy

    def settled(*which):
        for name in which:
            if name in saves:
                saves.pop(name).wait()

    def over(count, one):
        def each(i, carry):
            one(i)
            return carry

        lax.fori_loop(0, count, each, 0)

    act_load = pltpu.make_async_copy(r.activations, hb.at[:, : sz.width], r.in_sems.at[0])
    cot_load = pltpu.make_async_copy(r.cotangent, wide_t, r.in_sems.at[1])
    len_load = pltpu.make_async_copy(r.lengths, r.lens, r.in_sems.at[2])
    len_load.start()
    act_load.start()
    for name in (keys.gate_w, keys.out_w, keys.up_w, keys.down_w):
        load(0, name)
    cot_load.start()
    units.greet()
    mine[...] = jnp.zeros_like(mine)
    small[0] = jnp.zeros((8, SMALL), F32)
    len_load.wait()
    fill_masks(r.lens, valid, keep, sz, True)

    def to_steps(src, put):
        def cast(i):
            at = tile(i, 64)
            for k in range(sz.width // LANES):
                natural[k, at, :] = src[at, k * LANES : (k + 1) * LANES].astype(F32)

        over(sz.rows // 64, cast)

        def gather(j):
            for k in range(sz.width // LANES):
                parts = [
                    natural[k, strided(s * sz.span + j, sz.steps), :] for s in range(sz.micro)
                ]
                put(tile(j, sz.group), slice(k * LANES, (k + 1) * LANES), jnp.concatenate(parts, axis=0))

        over(sz.steps, gather)

    def from_steps(src, dst, sem):
        def scatter(j):
            for k in range(sz.width // LANES):
                value = src[tile(j, sz.group), k * LANES : (k + 1) * LANES]
                for s in range(sz.micro):
                    natural[k, strided(s * sz.span + j, sz.steps), :] = value[s * 8 : s * 8 + 8]

        over(sz.steps, scatter)
        copies = []
        for k in range(sz.width // LANES):
            lanes = slice(k * LANES, (k + 1) * LANES)
            copies.append(pltpu.make_async_copy(natural.at[k], dst.at[:, lanes], sem.at[k]))
            copies[-1].start()
        return copies

    act_load.wait()

    def put_gx(at, lanes, value):
        gx[at, lanes] = value

    to_steps(hb.at[:, : sz.width], put_gx)

    parts = [slice(part * half, (part + 1) * half) for part in range(2)]

    def exchange_start(way, layer, part):
        lanes = parts[part]
        slots = r.slots.at[way, layer]
        me = lax.axis_index("section")
        copies = []
        for hop in range(1, sz.sections):
            copies.append(
                pltpu.make_async_remote_copy(
                    src_ref=mine.at[:, lanes],
                    dst_ref=slots.at[me, :, lanes],
                    send_sem=r.pair_send.at[way, layer, part, hop - 1],
                    recv_sem=r.pair_recv.at[way, layer, part, hop - 1],
                    device_id={"section": lax.rem(me + hop, sz.sections)},
                    device_id_type=MESH,
                )
            )
        for copy in copies:
            copy.start()
        slots[me, :, lanes] = mine[:, lanes]
        return slots, copies

    def exchange_end(slots, copies, reverse, part):
        for copy in copies:
            copy.wait()
        part_enter(slots, prefix, enter, sz, reverse, parts[part])

    def in_turn(count, dots, rest, after=None):
        over(sz.rows // 256, lambda i: dots(0, i))
        for n in range(count):

            def both(i):
                if n + 1 < count:
                    dots(n + 1, i)
                rest(n, i)

            over(sz.rows // 256, both)
            if after is not None:
                after(n)

    def keep_cotangent():
        cot_load.wait()

        def put_low(at, lanes, value):
            low[at, lanes] = value.astype(BF16)

        to_steps(wide_t, put_low)
        low_t[...] = low[...].T

    def forward(layer):
        stream = r.stream if layer > 0 else gx
        settled(keys.u)
        norm_rows(stream, r.mix_gain.at[layer : layer + 1], r.u, sz.rows, 128)
        save(layer, keys.u)
        if layer == 0:
            save(layer, keys.stream, gx)
        need(keys.gate_w)
        settled(keys.a, keys.b, keys.zc)
        hw = 256
        bias = r.gate_bias

        def gate_dots(n, i):
            rows = tile(i, 256)
            for part in range(3):
                cols = slice(part * sz.hidden + n * hw, part * sz.hidden + (n + 1) * hw)
                zs[n % 2][rows, part * hw : (part + 1) * hw] = (
                    jnp.dot(r.u[rows, :], r.gate_w[:, cols], preferred_element_type=F32)
                    + bias[layer : layer + 1, cols]
                )

        def gate_rest(n, i):
            for chunk in range(4):
                at = pl.ds(pl.multiple_of(i * 256 + chunk * 64, 64), 64)
                vm, km = valid[at, :], keep[at, :]
                for lane in range(hw // LANES):
                    zf, zi, zc = (
                        zs[n % 2][at, part * hw + lane * LANES : part * hw + (lane + 1) * LANES]
                        for part in range(3)
                    )
                    cols = slice(n * hw + lane * LANES, n * hw + (lane + 1) * LANES)
                    a, b = odds(zf, zi)
                    fp, ip, _ = gate_weights(a, b)
                    decay[at, cols] = fp * km
                    drive[at, cols] = ip * zc * vm
                    r.a[at, cols] = a
                    r.b[at, cols] = b
                    r.zc[at, cols] = zc
                    r.forget[...] += jnp.sum((fp * vm).reshape(8, 8, LANES), axis=0)

        flights = []

        def gate_after(n):
            if n % 2 == 0:
                return
            lanes = parts[n // 2]

            def totals(j, pair):
                at = tile(j, sz.group)
                d = decay[at, lanes]
                return pair[0] * d, pair[1] * d + drive[at, lanes]

            one = jnp.ones((sz.group, half), F32)
            pair = steps_of(sz.steps, 2, totals, (one, jnp.zeros_like(one)))
            r.chunk_p[:, lanes] = pair[0]
            r.chunk_t[:, lanes] = pair[1]
            part_totals(r.chunk_p, r.chunk_t, sz, False, prefix, mine, lanes)
            if layer == 0 and n == 1:
                units.greeted()
            flights.append(exchange_start(0, layer, n // 2))

        r.forget[...] = jnp.zeros_like(r.forget)
        in_turn(sz.hidden // hw, gate_dots, gate_rest, gate_after)
        small[0, layer * 4 : layer * 4 + 1, sz.hidden : sz.hidden + LANES] = jnp.sum(
            r.forget[...], axis=0, keepdims=True
        )
        for name in (keys.a, keys.b, keys.zc):
            save(layer, name)
        if layer < last:
            load(layer + 1, keys.gate_w)
        settled(keys.states, keys.y1, keys.v, keys.p, keys.gb, keys.stream)
        states = r.states
        for part, lanes in enumerate(parts):
            exchange_end(*flights[part], False, part)
            states[0 : sz.group, lanes] = enter[:, lanes]

            def walk(j, h):
                at = tile(j, sz.group)
                h = decay[at, lanes] * h + drive[at, lanes]
                states[tile(j + 1, sz.group), lanes] = h
                hb[at, lanes] = h.astype(BF16)
                return h

            steps_of(sz.steps, 4, walk, enter[:, lanes])
            if (layer, part) == (0, 0):
                keep_cotangent()
        save(layer, keys.states)
        need(keys.out_w)

        def out_tile(n):
            cols = tile(n, 256)
            r.y1[:, cols] = stream[:, cols] + jnp.dot(
                hb[...], r.out_w[:, cols], preferred_element_type=F32
            )

        over(sz.width // 256, out_tile)
        save(layer, keys.y1)
        if layer < last:
            load(layer + 1, keys.out_w)
        norm_rows(r.y1, r.mlp_gain.at[layer : layer + 1], r.v, sz.rows, 128)
        save(layer, keys.v)
        need(keys.up_w)

        def up_dots(n, i):
            rows, cols = tile(i, 256), slice(n * 256, (n + 1) * 256)
            zs[n % 2][rows, :256] = jnp.dot(
                r.v[rows, :], r.up_w[:, cols], preferred_element_type=F32
            )

        def up_rest(n, i):
            cols = slice(n * 256, (n + 1) * 256)
            for chunk in range(4):
                at = pl.ds(pl.multiple_of(i * 256 + chunk * 64, 64), 64)
                p = zs[n % 2][at, :256]
                r.p[at, cols] = p
                r.gb[at, cols] = (p * normal_below(p)).astype(BF16)

        in_turn(sz.inner // 256, up_dots, up_rest)
        save(layer, keys.p)
        save(layer, keys.gb)
        if layer < last:
            load(layer + 1, keys.up_w)
        else:
            down_grad(layer, 0)
        need(keys.down_w)
        out = r.stream if layer < last else gy1

        def down_tile(n):
            cols = tile(n, 256)
            out[:, cols] = r.y1[:, cols] + jnp.dot(
                r.gb[...], r.down_w[:, cols], preferred_element_type=F32
            )

        over(sz.width // 256, down_tile)
        if layer < last:
            load(layer + 1, keys.down_w)

    def down_grad(layer, unit):
        for k in range(2):
            units.room(unit + k)

        def one(n):
            s, t = n // 2, n % 2
            value = jnp.dot(low_t[...], r.gb[:, tile(n, 256)], preferred_element_type=F32)
            for b in range(8):
                for h in range(2):
                    at = [place(unit + k, h, s // 2, b % 2, b // 2) for k in range(2)]
                    held[(unit + t) % HELD, s % 2, h, jnp.where(t == 0, *at)] = value[
                        b * 64 : b * 64 + 64, h * 128 : h * 128 + 128
                    ]

        over(8, one)
        units.produced(2, unit, unit + 1)

    def cast(src, dst):
        def one(i):
            at = tile(i, 64)
            dst[at, :] = src[at, :].astype(dst.dtype)

        over(sz.rows // 64, one)

    def turn_rows(src, dst, n):
        at = tile(n, 128)
        dst[:, at] = src[at, :].T

    def contract(left, weight, dst, count, beside=None):
        def one(n):
            if beside is not None:
                beside(n)
            cols = tile(n, 256)
            dst[:, cols] = lax.dot_general(
                left[...], weight[cols, :], (((1,), (1,)), ((), ())), preferred_element_type=F32
            )

        over(count // 256, one)

    def up_grad(layer, unit):
        for k in range(2):
            units.room(unit + k)

        def one(b):
            value = jnp.dot(wide_t[...], gp[:, tile(b, 256)], preferred_element_type=F32)
            for s in range(4):
                for h in range(2):
                    for t in range(2):
                        at = place(unit + t, h, s // 2, b % 2, b // 2)
                        held[(unit + t) % HELD, s % 2, h, at] = value[
                            s * 128 + h * 64 : s * 128 + h * 64 + 64, t * 128 : t * 128 + 128
                        ]

        over(8, one)
        units.produced(2.5, unit, unit + 1)

    def out_grad(layer, unit):
        def cast_state(i):
            hb[tile(i, sz.group), :] = r.states[tile(i + 1, sz.group), :].astype(BF16)

        if layer < last:
            over(sz.steps, cast_state)
        units.room(unit)

        def one(s):
            value = jnp.dot(r.go_t[...], hb[:, tile(s, 256)], preferred_element_type=F32)
            for b in range(8):
                for h in range(2):
                    at = place(unit, h, s // 2, b % 2, b // 2)
                    held[unit % HELD, s % 2, h, at] = value[
                        b * 64 : b * 64 + 64, h * 128 : h * 128 + 128
                    ]

        over(4, one)
        units.produced(1.2, unit)

    def backward(layer, unit):
        late = layer < last

        def freed(*which):
            if layer > 0:
                for name in which:
                    load(layer - 1, name)

        if not late:
            freed(keys.gb)
        need(keys.down_w, keys.p, keys.v)

        def act_dots(n, i):
            rows = tile(i, 256)
            zs[n % 2][rows, :256] = lax.dot_general(
                low[rows, :],
                r.down_w[n * 256 : (n + 1) * 256, :],
                (((1,), (1,)), ((), ())),
                preferred_element_type=F32,
            )

        def act_rest(n, i):
            if n < 2:
                turn_rows(r.v, wide_t, 2 * n + i)
            elif n < 4 and late:
                turn_rows(low, low_t, 2 * (n - 2) + i)
            cols = slice(n * 256, (n + 1) * 256)
            for chunk in range(4):
                at = pl.ds(pl.multiple_of(i * 256 + chunk * 64, 64), 64)
                p = r.p[at, cols]
                slope = normal_below(p) + ROOT_TAU * p * jnp.exp(-0.5 * p * p)
                gp[at, cols] = (zs[n % 2][at, :256] * slope).astype(BF16)

        in_turn(sz.inner // 256, act_dots, act_rest, lambda n: units.passed(0.6))
        freed(keys.down_w, keys.p, keys.v)
        if not late:
            up_grad(layer, unit + 2)
        need(keys.up_w, keys.y1, keys.u)

        def turn_u(n):
            for k in range(2):
                turn_rows(r.u, r.u_t, 2 * n + k)

        contract(gp, r.up_w, grad, sz.width, turn_u)
        freed(keys.u)
        freed(keys.up_w)
        units.passed(1.5)
        norm_back(r.y1, r.mlp_gain.at[layer : layer + 1], grad, gx, gy1, r.mlp_sum, sz.rows, 64, low)
        freed(keys.y1)
        need(keys.states)
        units.passed(2)
        need(keys.out_w, keys.a, keys.b)
        contract(low, r.out_w, ga, sz.hidden, lambda n: turn_rows(low, r.go_t, n))
        freed(keys.out_w)
        units.passed(1)
        if not late:
            out_grad(layer, unit + 4)
        flights = []
        for part, lanes in enumerate(parts):

            def totals(j, pair):
                at = tile(j, sz.group)
                if layer < last:
                    mask = jnp.concatenate([keep[at, :]] * (half // LANES), axis=1)
                    d = gate_weights(r.a[at, lanes], r.b[at, lanes])[0] * mask
                    decay[at, lanes] = d
                else:
                    d = decay[at, lanes]
                return pair[0] * d, d * (ga[at, lanes] + pair[1])

            one = jnp.ones((sz.group, half), F32)
            pair = steps_of(sz.steps, 2, totals, (one, jnp.zeros_like(one)), reverse=True)
            r.chunk_p[:, lanes] = pair[0]
            r.chunk_t[:, lanes] = pair[1]
            part_totals(r.chunk_p, r.chunk_t, sz, True, prefix, mine, lanes)
            flights.append(exchange_start(1, layer, part))
            carried = [units.expect(link, 16384) for link in ("core", "x", "x")]
            units.passed(0.8)
        need(keys.zc)
        if late:
            need(keys.gb)
            down_grad(layer, unit)
            up_grad(layer, unit + 2)
            out_grad(layer, unit + 4)
        unit += 5
        units.now = max(units.now, *carried)

        def gate_lanes(n):
            wide = 2 * LANES
            lanes = tile(n, wide)

            def walk(j, kept):
                m, bf, bi, bc = kept
                at = tile(j, sz.group)
                d = decay[at, lanes]
                q = ga[at, lanes] + m
                a, b, zc = r.a[at, lanes], r.b[at, lanes], r.zc[at, lanes]
                vm = jnp.concatenate([valid[at, :]] * 2, axis=1)
                km = jnp.concatenate([keep[at, :]] * 2, axis=1)
                fp, ip, inv = gate_weights(a, b)
                gf = q * (r.states[at, lanes] * km - zc * vm)
                parts = (
                    (gf * (a * inv) * fp).astype(BF16),
                    (-gf * (b * inv) * ip).astype(BF16),
                    (q * vm * ip).astype(BF16),
                )
                for part, value in enumerate(parts):
                    gz[at, pl.ds(pl.multiple_of(part * sz.hidden + n * wide, wide), wide)] = value
                return (d * q,) + tuple(
                    a + value.astype(F32) for a, value in zip((bf, bi, bc), parts)
                )

            zero = jnp.zeros((sz.group, wide), F32)
            _, *sums = steps_of(
                sz.steps, 4, walk, (enter[:, lanes], zero, zero, zero), reverse=True
            )
            for part, total in enumerate(sums):
                small[0, layer * 4 + part : layer * 4 + part + 1, lanes] = jnp.sum(
                    total, axis=0, keepdims=True
                )

        turns = sz.hidden // LANES // 4
        for part in range(2):
            exchange_end(*flights[part], True, part)
            over(turns, lambda n: gate_lanes(n + part * turns))
            units.passed(1.8)
        freed(keys.a, keys.b, keys.zc, keys.states)
        for k in range(2):
            units.room(unit + k)

        def gate_grad(b):
            cols = pl.ds(pl.multiple_of(b * 384, 128), 256)
            value = jnp.dot(r.u_t[...], gz[:, cols], preferred_element_type=F32)
            for s in range(4):
                for h in range(2):
                    for t in range(2):
                        at = place(unit + t, h, s // 2, b % 2, b // 2)
                        held[(unit + t) % HELD, s % 2, h, at] = value[
                            s * 128 + h * 64 : s * 128 + h * 64 + 64, t * 128 : t * 128 + 128
                        ]

        over(8, gate_grad)
        units.produced(3, unit, unit + 1)
        unit += 2
        units.room(unit)

        def gate_rest(z):
            right = jnp.concatenate(
                [
                    gz[:, pl.ds(pl.multiple_of((2 * z + y) * 384 + 256, 128), 128)]
                    for y in range(2)
                ],
                axis=1,
            )
            value = jnp.dot(r.u_t[...], right, preferred_element_type=F32)
            for s in range(4):
                for h in range(2):
                    for y in range(2):
                        at = place(unit, h, s // 2, y, z)
                        held[unit % HELD, s % 2, h, at] = value[
                            s * 128 + h * 64 : s * 128 + h * 64 + 64, y * 128 : y * 128 + 128
                        ]

        over(4, gate_rest)
        units.produced(1.5, unit)
        unit += 1
        need(keys.gate_w, keys.stream)
        contract(gz, r.gate_w, grad, sz.width)
        freed(keys.gate_w)
        units.passed(2.5)
        norm_back(r.stream, r.mix_gain.at[layer : layer + 1], grad, gy1, gx, r.mix_sum, sz.rows, 64, low)
        freed(keys.stream)
        row = slice(layer * 4 + 3, layer * 4 + 4)
        small[0, row, : sz.width] = jnp.sum(r.mix_sum[...], axis=0, keepdims=True)
        small[0, row, sz.width : 2 * sz.width] = jnp.sum(r.mlp_sum[...], axis=0, keepdims=True)
        units.passed(1.5)

    forward(0)
    for layer in range(1, layers):
        forward(layer)
    out_copies = from_steps(gy1, r.layer_out, r.out_sems)
    cast(low, gx)
    units.passed(2)
    for index, layer in enumerate(reversed(range(layers))):
        backward(layer, 8 * index)
    units.small_start()
    for copy in out_copies:
        copy.wait()
    out_copies = from_steps(gx, r.input_grad, r.out_sems)
    units.passed(1)
    units.drain()
    for copy in out_copies:
        copy.wait()
    total = small[STAGES]
    count = jnp.int32(0)
    for s in range(r.lens.shape[0]):
        for d in range(r.lens.shape[1]):
            count = count + r.lens[s, d]
    scale = 1.0 / (count.astype(F32) * sz.hidden)
    for layer in range(layers):
        for part in range(3):
            r.gate_bias_grad[layer : layer + 1, part * sz.hidden : (part + 1) * sz.hidden] = total[
                layer * 4 + part : layer * 4 + part + 1, : sz.hidden
            ]
        row = slice(layer * 4 + 3, layer * 4 + 4)
        r.mix_gain_grad[layer : layer + 1, :] = total[row, : sz.width]
        r.mlp_gain_grad[layer : layer + 1, :] = total[row, sz.width : 2 * sz.width]
        lanes = total[layer * 4 : layer * 4 + 1, sz.hidden : sz.hidden + LANES]
        r.forget_mean[layer : layer + 1, :] = (
            jnp.sum(lanes, axis=1, keepdims=True) * scale + jnp.zeros((1, LANES), F32)
        )


def run_whole_step(sz, layers, named):
    lengths = named["lengths"]
    rows, d, h, f = sz.rows, sz.width, sz.hidden, sz.inner
    vm = lambda *dims, kind=F32: pltpu.VMEM(dims, kind)
    sems = pltpu.SemaphoreType
    spec = dict(gate_bias=VMEM, mix_gain=VMEM, mlp_gain=VMEM)
    outputs = dict(
        layer_out=(shape(rows, d), ANY),
        input_grad=(shape(rows, d), ANY),
        gate_weight_grad=(shape(layers, 128, 384), VMEM),
        gate_bias_grad=(shape(layers, 3 * h), VMEM),
        out_weight_grad=(shape(layers, 64, 256), VMEM),
        up_weight_grad=(shape(layers, 128, 256), VMEM),
        down_weight_grad=(shape(layers, 64, 512), VMEM),
        mix_gain_grad=(shape(layers, d), VMEM),
        mlp_gain_grad=(shape(layers, d), VMEM),
        forget_mean=(shape(layers, LANES), VMEM),
    )
    results = len(outputs)
    kept = dict(
        u=((rows, d), BF16),
        a=((rows, h), F32),
        b=((rows, h), F32),
        zc=((rows, h), F32),
        states=((rows + sz.group, h), F32),
        y1=((rows, d), F32),
        v=((rows, d), BF16),
        p=((rows, f), F32),
        gb=((rows, f), BF16),
        stream=((rows, d), F32),
    )
    scratch = {}
    for name, (dims, kind) in kept.items():
        outputs[name + "_save"] = (shape(layers - 1, *dims, kind=kind), ANY)
        scratch[name] = vm(*dims, kind=kind)
    scratch.update(
        gate_w=vm(d, 3 * h, kind=BF16),
        out_w=vm(h, d, kind=BF16),
        up_w=vm(d, f, kind=BF16),
        down_w=vm(f, d, kind=BF16),
        valid=vm(rows, LANES),
        keep=vm(rows, LANES),
        gx=vm(rows, d),
        low=vm(rows, d, kind=BF16),
        low_t=vm(d, rows, kind=BF16),
        wide_t=vm(d, rows, kind=BF16),
        u_t=vm(d, rows, kind=BF16),
        go_t=vm(d, rows, kind=BF16),
        hb=vm(rows, h, kind=BF16),
        z1=vm(rows, 768),
        drive=vm(rows, h),
        forget=vm(8, LANES),
        ga=vm(rows, h),
        gz=vm(rows, 3 * h, kind=BF16),
        grad=vm(rows, d),
        gy1=vm(rows, d),
        decay=vm(rows, h),
        chunk_p=vm(sz.group, h),
        chunk_t=vm(sz.group, h),
        prefix=vm(2, sz.group, h),
        enter=vm(sz.group, h),
        mine=vm(8, h),
        slots=vm(2, layers, sz.sections, 8, h),
        mlp_sum=vm(8, d),
        mix_sum=vm(8, d),
        held=vm(HELD, 2, 2, 16, BLOCK, LANES),
        small=vm(STAGES + 1, 8, SMALL),
        small_arrived=vm(STAGES, 8, SMALL),
        in_sems=sems.DMA((3,)),
        lens=pltpu.SMEM(lengths.shape, jnp.int32),
        out_sems=sems.DMA((d // LANES,)),
        natural=vm(d // LANES, rows, LANES),
        load_sems=sems.DMA((len(kept) + 4,)),
        save_sems=sems.DMA((len(kept) + 4,)),
        pair_send=sems.DMA((2, layers, 2, sz.sections - 1)),
        pair_recv=sems.DMA((2, layers, 2, sz.sections - 1)),
        send_sems=sems.DMA((SENDS, 2 * STAGES - 1)),
        recv_sems=sems.DMA((max(RINGS), 2 * STAGES - 1)),
        credits=sems.REGULAR((2 * STAGES - 1, 8 * layers)),
        small_send=sems.DMA((STAGES,)),
        small_recv=sems.DMA((STAGES,)),
    )
    for stage in range(STAGES):
        scratch[f"arrived{stage}"] = vm(RINGS[stage], 2, 16 >> stage, BLOCK, LANES)
    names = list(named) + list(outputs) + list(scratch)
    out = pl.pallas_call(
        functools.partial(whole_step, sz, layers, names),
        out_shape=tuple(value for value, _ in outputs.values()),
        in_specs=[spec.get(name, ANY) for name in named],
        out_specs=[place_of for _, place_of in outputs.values()],
        scratch_shapes=list(scratch.values()),
        compiler_params=pltpu.CompilerParams(
            collective_id=4, has_side_effects=True, vmem_limit_bytes=LIMIT
        ),
        name="whole_step",
    )(*named.values())
    return out[:results]


def deliver_kernel(count, *refs):
    sources, targets, held = refs[:count], refs[count : 2 * count], refs[2 * count : 3 * count - 1]
    sems = refs[3 * count - 1]
    arrivals = [
        pltpu.make_async_copy(sources[i], held[i], sems.at[0, i]) for i in range(count - 1)
    ]
    departures = [
        pltpu.make_async_copy(held[i], targets[i], sems.at[1, i]) for i in range(count - 1)
    ]
    for copy in arrivals:
        copy.start()
    for layer in range(targets[-1].shape[0]):
        targets[-1][layer] = sources[-1][layer, 0]
    for arrival, departure in zip(arrivals, departures):
        arrival.wait()
        departure.start()
    for copy in departures:
        copy.wait()


def deliver(values):
    count = len(values)
    scalars = pl.BlockSpec(memory_space=pltpu.SMEM)
    shapes = [shape(*value.shape) for value in values[:-1]] + [shape(values[-1].shape[0])]
    return pl.pallas_call(
        functools.partial(deliver_kernel, count),
        out_shape=tuple(shapes),
        in_specs=[ANY] * (count - 1) + [scalars],
        out_specs=[ANY] * (count - 1) + [scalars],
        scratch_shapes=[pltpu.VMEM(value.shape, F32) for value in values[:-1]]
        + [pltpu.SemaphoreType.DMA((2, count - 1))],
        compiler_params=pltpu.CompilerParams(vmem_limit_bytes=LIMIT),
        name="deliver",
    )(*values)


def mask_kernel(sizes, lens, valid, keep):
    fill_masks(lens, valid, keep, sizes)


def body(
    activations,
    cotangent,
    lengths,
    gate_weight,
    gate_bias,
    out_weight,
    up_weight,
    down_weight,
    mix_gain,
    mlp_gain,
):
    micro, span, width = activations.shape
    layers = gate_weight.shape[0]
    sz = Sizes(
        micro, span, width, out_weight.shape[1], up_weight.shape[2], lax.axis_size("section")
    )

    blocks = (width // 4, 3 * sz.hidden // 8, width // 8, sz.inner // 4, sz.hidden // 4)
    axes = (lax.axis_size("section"), lax.axis_size("batch"))
    if axes == (4, 8) and blocks == (128, 384, 64, 512, 256):
        out = run_whole_step(
            sz,
            layers,
            dict(
                activations=activations.reshape(sz.rows, width),
                cotangent=cotangent.reshape(sz.rows, width),
                lengths=lengths.T,
                gate_bias=gate_bias,
                mix_gain=mix_gain,
                mlp_gain=mlp_gain,
                gate_hbm=gate_weight,
                out_hbm=out_weight,
                up_hbm=up_weight,
                down_hbm=down_weight,
            ),
        )
        stream_out, input_grad, gate_g, bias_g, out_g, up_g, down_g, *rest = deliver(out)
        return (
            stream_out.reshape(activations.shape),
            input_grad.reshape(activations.shape),
            gate_g,
            bias_g,
            out_g.transpose(0, 2, 1),
            up_g,
            down_g.transpose(0, 2, 1),
            *rest,
        )

    def arranged(value):
        value = value.astype(F32).reshape(micro, CHUNKS, sz.steps, width)
        return value.transpose(2, 0, 1, 3).reshape(sz.rows, width)

    def restored(value):
        value = value.reshape(sz.steps, micro, CHUNKS, width).transpose(1, 2, 0, 3)
        return value.reshape(micro, span, width)

    masks = pl.pallas_call(
        functools.partial(mask_kernel, sz),
        out_shape=(shape(sz.rows, LANES), shape(sz.rows, LANES)),
        in_specs=[pl.BlockSpec(memory_space=pltpu.SMEM)],
        out_specs=[VMEM] * 2,
        name="masks",
    )(lengths)
    weights = (gate_weight, out_weight, up_weight, down_weight)
    stream = arranged(activations)
    streams, saved, forgets = [], [], []
    for layer in range(layers):
        streams.append(stream)
        stream, *kept, forget, pairs = run_forward(
            sz,
            layer,
            stream,
            masks,
            gate_bias[layer : layer + 1],
            mix_gain[layer : layer + 1],
            mlp_gain[layer : layer + 1],
            weights,
        )
        saved.append((*kept, pairs))
        forgets.append(forget)
    layer_out = restored(stream)
    gx = arranged(cotangent)
    true_count = jnp.sum(lengths).astype(F32)
    forgets = [jnp.sum(forget) for forget in forgets]
    sums, small = [None] * layers, [None] * layers
    for layer in reversed(range(layers)):
        gx, gate_g, out_g, up_g, down_g, bias_g, mix_g, mlp_g = run_backward(
            sz,
            layer,
            gx,
            streams[layer],
            masks,
            mix_gain[layer : layer + 1],
            mlp_gain[layer : layer + 1],
            saved[layer],
            weights,
        )
        sums[layer] = (gate_g, out_g.T, up_g, down_g.T)
        small[layer] = tuple(jnp.sum(part, axis=0) for part in (bias_g, mix_g, mlp_g))
    input_grad = restored(gx)
    stacked = tuple(jnp.stack(parts) for parts in zip(*sums))
    partial_sums = lax.psum_scatter(stacked, "section", scatter_dimension=1, tiled=True)
    large = lax.psum_scatter(partial_sums, "batch", scatter_dimension=2, tiled=True)
    bias_grad, mix_grad, mlp_grad = (jnp.stack(parts) for parts in zip(*small))
    bias_grad, mix_grad, mlp_grad, forget = lax.psum(
        (bias_grad, mix_grad, mlp_grad, jnp.stack(forgets)), ("section", "batch")
    )
    forget_mean = forget / (true_count * sz.hidden)
    return (
        layer_out,
        input_grad,
        large[0],
        bias_grad,
        large[1],
        large[2],
        large[3],
        mix_grad,
        mlp_grad,
        forget_mean,
    )


def solution(mesh):
    stream = P("batch", "section", None)
    block = P(None, "section", "batch")
    return jax.shard_map(
        body,
        mesh=mesh,
        in_specs=(stream, stream) + (P(),) * 8,
        out_specs=(stream, stream, block, P(), block, block, block, P(), P(), P()),
        check_vma=False,
    )
```

```python
import functools
import types

import jax
import jax.numpy as jnp
from jax import lax
from jax.experimental import pallas as pl
from jax.experimental.pallas import tpu as pltpu
from jax.sharding import PartitionSpec as P

epsilon = 1e-06
MESH = pl.DeviceIdType.MESH
F32, BF16 = jnp.float32, jnp.bfloat16
CHUNKS = 8
LANES = 128
ROOT_HALF = 0.7071067811865476
ROOT_TAU = 0.3989422804014327


def tile(index, size):
    return pl.ds(pl.multiple_of(index * size, size), size)


def inverse(value):
    r = pltpu.reciprocal(value, approx=True)
    return r * (2.0 - value * r)


def normal_below(p):
    return 0.5 + 0.5 * lax.erf(p * ROOT_HALF)


def steps_of(count, unroll, one, start, reverse=False):
    def turn(i, carry):
        for k in range(unroll):
            at = i * unroll + k
            carry = one(count - 1 - at if reverse else at, carry)
        return carry

    return lax.fori_loop(0, count // unroll, turn, start)


def odds(zf, zi):
    return jnp.exp(jnp.minimum(-zf, 86.0)), jnp.exp(jnp.minimum(-zi, 86.0))


def gate_weights(a, b):
    inv = inverse(2.0 + a + b)
    return (1.0 + b) * inv, (1.0 + a) * inv, inv


def greet_section(sections):
    me = lax.axis_index("section")
    barrier = pltpu.get_barrier_semaphore()
    for hop in range(1, sections):
        pl.semaphore_signal(
            barrier, inc=1, device_id={"section": lax.rem(me + hop, sections)}, device_id_type=MESH
        )
    pl.semaphore_wait(barrier, sections - 1)


def exchange(mine, slots, send_sems, recv_sems, sections):
    me = lax.axis_index("section")
    copies = []
    for hop in range(1, sections):
        copies.append(
            pltpu.make_async_remote_copy(
                src_ref=mine,
                dst_ref=slots.at[me],
                send_sem=send_sems.at[hop - 1],
                recv_sem=recv_sems.at[hop - 1],
                device_id={"section": lax.rem(me + hop, sections)},
                device_id_type=MESH,
            )
        )
    for copy in copies:
        copy.start()
    slots[me] = mine[...]
    for copy in copies:
        copy.wait()


def norm_rows(stream, gain, low, rows, step):
    def one(i, carry):
        at = tile(i, step)
        x = stream[at, :]
        r = lax.rsqrt(jnp.mean(x * x, axis=-1, keepdims=True) + epsilon)
        low[at, :] = (x * r * gain[...]).astype(BF16)
        return carry

    lax.fori_loop(0, rows // step, one, 0)


def norm_back(stream, gain, grad, through, out, gain_sum, rows, step, low=None):
    width = stream.shape[1]

    def one(i, total):
        at = tile(i, step)
        x = stream[at, :]
        r = lax.rsqrt(jnp.mean(x * x, axis=-1, keepdims=True) + epsilon)
        n = x * r
        g = grad[at, :]
        a = g * gain[...]
        value = through[at, :] + r * (a - n * jnp.mean(a * n, axis=-1, keepdims=True))
        out[at, :] = value
        if low is not None:
            low[at, :] = value.astype(BF16)
        return total + jnp.sum((g * n).reshape(step // 8, 8, width), axis=0)

    gain_sum[...] = lax.fori_loop(0, rows // step, one, jnp.zeros((8, width), F32))


def fill_masks(lens, valid, keep, sizes, turned=False):
    section = lax.axis_index("section")
    group = lax.axis_index("batch")
    starts, totals = [], []
    for s in range(sizes.micro):
        total, begin = 0, []
        for d in range(lens.shape[0 if turned else 1]):
            row = group * sizes.micro + s
            length = lens[d, row] if turned else lens[row, d]
            begin.append(jnp.where(length > 0, total, -1))
            total = total + length
        starts.append(begin)
        totals.append(total)
    chunk_place = lax.broadcasted_iota(jnp.int32, (8, LANES), 0) * sizes.steps

    def one(j, carry):
        for s in range(sizes.micro):
            place = section * sizes.span + j + chunk_place
            true = place < totals[s]
            first = place == starts[s][0]
            for begin in starts[s][1:]:
                first = first | (place == begin)
            at = pl.ds(pl.multiple_of(j * sizes.group + s * 8, 8), 8)
            valid[at, :] = jnp.where(true, 1.0, 0.0)
            keep[at, :] = jnp.where(true & jnp.logical_not(first), 1.0, 0.0)
        return carry

    lax.fori_loop(0, sizes.steps, one, 0)


def scan_totals(first, second, sizes, reverse, prefix, chunk, mine):
    for s in range(sizes.micro):
        p = jnp.ones((1, sizes.hidden), F32)
        t = jnp.zeros((1, sizes.hidden), F32)
        for c in reversed(range(CHUNKS)) if reverse else range(CHUNKS):
            at = s * 8 + c
            prefix[0, at : at + 1, :] = p
            prefix[1, at : at + 1, :] = t
            pc = first[at : at + 1, :]
            t = pc * t + second[at : at + 1, :]
            p = p * pc
        mine[s : s + 1, :] = p
        mine[sizes.micro + s : sizes.micro + s + 1, :] = t


def scan_enter(slots, prefix, enter, sizes, reverse):
    me = lax.axis_index("section")
    for s in range(sizes.micro):
        a = jnp.zeros((1, sizes.hidden), F32)
        order = range(sizes.sections - 1, 0, -1) if reverse else range(sizes.sections - 1)
        for k in order:
            reached = k > me if reverse else k < me
            pk = slots[k, s : s + 1, :]
            tk = slots[k, sizes.micro + s : sizes.micro + s + 1, :]
            a = jnp.where(reached, pk * a + tk, a)
        at = slice(s * 8, s * 8 + 8)
        enter[at, :] = prefix[0, at, :] * a + prefix[1, at, :]


def part_totals(first, second, sizes, reverse, prefix, mine, lanes):
    for s in range(sizes.micro):
        p = jnp.ones((1, lanes.stop - lanes.start), F32)
        t = jnp.zeros_like(p)
        for c in reversed(range(CHUNKS)) if reverse else range(CHUNKS):
            at = s * 8 + c
            prefix[0, at : at + 1, lanes] = p
            prefix[1, at : at + 1, lanes] = t
            pc = first[at : at + 1, lanes]
            t = pc * t + second[at : at + 1, lanes]
            p = p * pc
        mine[s : s + 1, lanes] = p
        mine[sizes.micro + s : sizes.micro + s + 1, lanes] = t


def part_enter(slots, prefix, enter, sizes, reverse, lanes):
    me = lax.axis_index("section")
    for s in range(sizes.micro):
        a = jnp.zeros((1, lanes.stop - lanes.start), F32)
        order = range(sizes.sections - 1, 0, -1) if reverse else range(sizes.sections - 1)
        for k in order:
            reached = k > me if reverse else k < me
            pk = slots[k, s : s + 1, lanes]
            tk = slots[k, sizes.micro + s : sizes.micro + s + 1, lanes]
            a = jnp.where(reached, pk * a + tk, a)
        at = slice(s * 8, s * 8 + 8)
        enter[at, lanes] = prefix[0, at, lanes] * a + prefix[1, at, lanes]


class Sizes:
    def __init__(self, micro, span, width, hidden, inner, sections):
        self.micro, self.span, self.width = micro, span, width
        self.hidden, self.inner, self.sections = hidden, inner, sections
        self.rows = micro * span
        self.steps = span // CHUNKS
        self.group = micro * CHUNKS


def forward_kernel(
    sizes,
    layer,
    stream,
    valid,
    keep,
    bias,
    mix_gain,
    mlp_gain,
    gate_hbm,
    out_hbm,
    up_hbm,
    down_hbm,
    next_stream,
    u,
    sf_out,
    si_out,
    zc_out,
    states,
    y1,
    v,
    p_out,
    gb,
    forget,
    pair_slots,
    gate_w,
    out_w,
    up_w,
    down_w,
    z,
    decay,
    drive,
    hb,
    chunk_p,
    chunk_t,
    prefix,
    enter,
    mine,
    weight_sems,
    send_sems,
    recv_sems,
):
    sz = sizes
    loads = [
        pltpu.make_async_copy(src.at[layer], dst, weight_sems.at[i])
        for i, (src, dst) in enumerate(
            ((gate_hbm, gate_w), (out_hbm, out_w), (up_hbm, up_w), (down_hbm, down_w))
        )
    ]
    for load in loads:
        load.start()
    greet_section(sz.sections)
    mine[...] = jnp.zeros_like(mine)
    norm_rows(stream, mix_gain, u, sz.rows, 64)
    loads[0].wait()
    forget[...] = jnp.zeros_like(forget)
    hw = 256

    def gate_tile(n, carry):
        for part in range(3):
            cols = pl.ds(pl.multiple_of(part * sz.hidden + n * hw, hw), hw)
            z[:, part * hw : (part + 1) * hw] = (
                jnp.dot(u[...], gate_w[:, cols], preferred_element_type=F32) + bias[:, cols]
            )

        def one(i, inner):
            at = tile(i, 64)
            for lane in range(hw // LANES):
                src = lambda part: z[
                    at, part * hw + lane * LANES : part * hw + (lane + 1) * LANES
                ]
                dst = pl.ds(pl.multiple_of(n * hw + lane * LANES, LANES), LANES)
                a = jnp.exp(jnp.minimum(-src(0), 86.0))
                b = jnp.exp(jnp.minimum(-src(1), 86.0))
                zc = src(2)
                fp, ip, _ = gate_weights(a, b)
                vm = valid[at, :]
                decay[at, dst] = fp * keep[at, :]
                drive[at, dst] = ip * zc * vm
                sf_out[at, dst] = a
                si_out[at, dst] = b
                zc_out[at, dst] = zc
                forget[...] += jnp.sum((fp * vm).reshape(8, 8, LANES), axis=0)
            return inner

        lax.fori_loop(0, sz.rows // 64, one, 0)
        return carry

    lax.fori_loop(0, sz.hidden // hw, gate_tile, 0)
    half = sz.hidden // 2
    for part in range(2):
        lanes = slice(part * half, (part + 1) * half)

        def totals(j, pair):
            at = tile(j, sz.group)
            d = decay[at, lanes]
            return pair[0] * d, pair[1] * d + drive[at, lanes]

        one = jnp.ones((sz.group, half), F32)
        pair = steps_of(sz.steps, 4, totals, (one, jnp.zeros_like(one)))
        chunk_p[:, lanes] = pair[0]
        chunk_t[:, lanes] = pair[1]
    scan_totals(chunk_p, chunk_t, sz, False, prefix, None, mine)
    exchange(mine, pair_slots, send_sems, recv_sems, sz.sections)
    scan_enter(pair_slots, prefix, enter, sz, False)
    states[0 : sz.group, :] = enter[...]
    for part in range(2):
        lanes = slice(part * half, (part + 1) * half)

        def walk(j, h):
            at = tile(j, sz.group)
            h = decay[at, lanes] * h + drive[at, lanes]
            states[tile(j + 1, sz.group), lanes] = h
            hb[at, lanes] = h.astype(BF16)
            return h

        steps_of(sz.steps, 4, walk, enter[:, lanes])
    loads[1].wait()

    def out_tile(n, carry):
        cols = tile(n, 256)
        y1[:, cols] = stream[:, cols] + jnp.dot(
            hb[...], out_w[:, cols], preferred_element_type=F32
        )
        return carry

    lax.fori_loop(0, sz.width // 256, out_tile, 0)
    norm_rows(y1, mlp_gain, v, sz.rows, 64)
    loads[2].wait()

    def up_tile(n, carry):
        cols = tile(n, 256)
        p_out[:, cols] = jnp.dot(v[...], up_w[:, cols], preferred_element_type=F32)

        def one(i, inner):
            at = tile(i, 64)
            p = p_out[at, cols]
            gb[at, cols] = (p * normal_below(p)).astype(BF16)
            return inner

        lax.fori_loop(0, sz.rows // 64, one, 0)
        return carry

    lax.fori_loop(0, sz.inner // 256, up_tile, 0)
    loads[3].wait()

    def down_tile(n, carry):
        cols = tile(n, 256)
        next_stream[:, cols] = y1[:, cols] + jnp.dot(
            gb[...], down_w[:, cols], preferred_element_type=F32
        )
        return carry

    lax.fori_loop(0, sz.width // 256, down_tile, 0)


def backward_kernel(
    sizes,
    layer,
    gx,
    stream,
    valid,
    keep,
    mix_gain,
    mlp_gain,
    u,
    sf_in,
    si_in,
    zc_in,
    states,
    y1,
    v,
    p_in,
    gb,
    pair_slots,
    gate_hbm,
    out_hbm,
    up_hbm,
    down_hbm,
    next_gx,
    gate_grad,
    out_grad,
    up_grad,
    down_grad,
    bias_sum,
    mix_sum,
    mlp_sum,
    gate_w,
    out_w,
    up_w,
    down_w,
    low,
    low_t,
    wide_t,
    hb,
    ga,
    gp,
    gz,
    grad,
    gy1,
    decay,
    chunk_p,
    chunk_t,
    prefix,
    enter,
    mine,
    slots,
    weight_sems,
    send_sems,
    recv_sems,
):
    sz = sizes
    loads = [
        pltpu.make_async_copy(src.at[layer], dst, weight_sems.at[i])
        for i, (src, dst) in enumerate(
            ((gate_hbm, gate_w), (out_hbm, out_w), (up_hbm, up_w), (down_hbm, down_w))
        )
    ]
    for load in reversed(loads):
        load.start()
    greet_section(sz.sections)
    mine[...] = jnp.zeros_like(mine)

    def cast(i, carry):
        at = tile(i, 64)
        low[at, :] = gx[at, :].astype(BF16)
        return carry

    lax.fori_loop(0, sz.rows // 64, cast, 0)
    low_t[...] = low[...].T

    def weight_grad(left_t, right, dst, step):
        def one(n, carry):
            cols = tile(n, step)
            dst[:, cols] = jnp.dot(left_t[...], right[:, cols], preferred_element_type=F32)
            return carry

        lax.fori_loop(0, right.shape[1] // step, one, 0)

    weight_grad(low_t, gb, down_grad, 256)
    loads[3].wait()

    def act_tile(n, carry):
        cols = tile(n, 256)
        ga[:, :256] = lax.dot_general(
            low[...], down_w[cols, :], (((1,), (1,)), ((), ())), preferred_element_type=F32
        )

        def one(i, inner):
            at = tile(i, 64)
            p = p_in[at, cols]
            slope = normal_below(p) + ROOT_TAU * p * jnp.exp(-0.5 * p * p)
            gp[at, cols] = (ga[at, :256] * slope).astype(BF16)
            return inner

        lax.fori_loop(0, sz.rows // 64, one, 0)
        return carry

    lax.fori_loop(0, sz.inner // 256, act_tile, 0)
    wide_t[...] = v[...].T
    weight_grad(wide_t, gp, up_grad, 256)
    loads[2].wait()

    def contract(left, weight, dst, step):
        def one(n, carry):
            cols = tile(n, step)
            dst[:, cols] = lax.dot_general(
                left[...], weight[cols, :], (((1,), (1,)), ((), ())), preferred_element_type=F32
            )
            return carry

        lax.fori_loop(0, weight.shape[0] // step, one, 0)

    contract(gp, up_w, grad, 256)
    norm_back(y1, mlp_gain, grad, gx, gy1, mlp_sum, sz.rows, 64)

    def cast_more(i, carry):
        at = tile(i, 64)
        low[at, :] = gy1[at, :].astype(BF16)
        return carry

    lax.fori_loop(0, sz.rows // 64, cast_more, 0)

    def cast_state(i, carry):
        hb[tile(i, sz.group), :] = states[tile(i + 1, sz.group), :].astype(BF16)
        return carry

    lax.fori_loop(0, sz.steps, cast_state, 0)
    low_t[...] = low[...].T
    weight_grad(low_t, hb, out_grad, 256)
    loads[1].wait()
    contract(low, out_w, ga, 256)
    half = sz.hidden // 2
    for part in range(2):
        lanes = slice(part * half, (part + 1) * half)

        def totals(i, pair):
            at = tile(sz.steps - 1 - i, sz.group)
            mask = jnp.concatenate([keep[at, :]] * (half // LANES), axis=1)
            d = gate_weights(sf_in[at, lanes], si_in[at, lanes])[0] * mask
            decay[at, lanes] = d
            return pair[0] * d, d * (ga[at, lanes] + pair[1])

        pair = lax.fori_loop(
            0,
            sz.steps,
            totals,
            (jnp.ones((sz.group, half), F32), jnp.zeros((sz.group, half), F32)),
        )
        chunk_p[:, lanes] = pair[0]
        chunk_t[:, lanes] = pair[1]
    scan_totals(chunk_p, chunk_t, sz, True, prefix, None, mine)
    exchange(mine, slots, send_sems, recv_sems, sz.sections)
    scan_enter(slots, prefix, enter, sz, True)

    def gate_lane(n, carry):
        lanes = tile(n, LANES)

        def walk(i, kept):
            m, bf, bi, bc = kept
            j = sz.steps - 1 - i
            at = tile(j, sz.group)
            d = decay[at, lanes]
            q = ga[at, lanes] + m
            a = sf_in[at, lanes]
            b = si_in[at, lanes]
            zc = zc_in[at, lanes]
            vm = valid[at, :]
            fp, ip, inv = gate_weights(a, b)
            gf = q * (states[at, lanes] * keep[at, :] - zc * vm)
            gzf = (gf * (a * inv) * fp).astype(BF16)
            gzi = (-gf * (b * inv) * ip).astype(BF16)
            gzc = (q * vm * ip).astype(BF16)
            gz[at, lanes] = gzf
            gz[at, pl.ds(pl.multiple_of(sz.hidden + n * LANES, LANES), LANES)] = gzi
            gz[at, pl.ds(pl.multiple_of(2 * sz.hidden + n * LANES, LANES), LANES)] = gzc
            return (
                d * q,
                bf + gzf.astype(F32),
                bi + gzi.astype(F32),
                bc + gzc.astype(F32),
            )

        zero = jnp.zeros((sz.group, LANES), F32)
        _, bf, bi, bc = lax.fori_loop(0, sz.steps, walk, (enter[:, lanes], zero, zero, zero))
        for part, total in enumerate((bf, bi, bc)):
            where = pl.ds(pl.multiple_of(part * sz.hidden + n * LANES, LANES), LANES)
            bias_sum[:, where] = jnp.sum(total.reshape(sz.group // 8, 8, LANES), axis=0)
        return carry

    lax.fori_loop(0, sz.hidden // LANES, gate_lane, 0)
    wide_t[...] = u[...].T
    weight_grad(wide_t, gz, gate_grad, 256)
    loads[0].wait()
    contract(gz, gate_w, grad, 256)
    norm_back(stream, mix_gain, grad, gy1, next_gx, mix_sum, sz.rows, 64)


VMEM = pl.BlockSpec(memory_space=pltpu.VMEM)
ANY = pl.BlockSpec(memory_space=pl.ANY)
LIMIT = 63 * 2**20


def shape(*dims, kind=F32):
    return jax.ShapeDtypeStruct(dims, kind)


def exchange_scratch(sz):
    return [
        pltpu.SemaphoreType.DMA((4,)),
        pltpu.SemaphoreType.DMA((sz.sections - 1,)),
        pltpu.SemaphoreType.DMA((sz.sections - 1,)),
    ]


def weight_scratch(sz):
    return [
        pltpu.VMEM((sz.width, 3 * sz.hidden), BF16),
        pltpu.VMEM((sz.hidden, sz.width), BF16),
        pltpu.VMEM((sz.width, sz.inner), BF16),
        pltpu.VMEM((sz.inner, sz.width), BF16),
    ]


def scan_scratch(sz):
    return [
        pltpu.VMEM((sz.group, sz.hidden), F32),
        pltpu.VMEM((sz.group, sz.hidden), F32),
        pltpu.VMEM((2, sz.group, sz.hidden), F32),
        pltpu.VMEM((sz.group, sz.hidden), F32),
        pltpu.VMEM((8, sz.hidden), F32),
    ]


def run_forward(sz, layer, stream, masks, bias, mix_gain, mlp_gain, weights):
    r, d, h, f = sz.rows, sz.width, sz.hidden, sz.inner
    return pl.pallas_call(
        functools.partial(forward_kernel, sz, layer),
        out_shape=(
            shape(r, d),
            shape(r, d, kind=BF16),
            shape(r, h),
            shape(r, h),
            shape(r, h),
            shape(r + sz.group, h),
            shape(r, d),
            shape(r, d, kind=BF16),
            shape(r, f),
            shape(r, f, kind=BF16),
            shape(8, LANES),
            shape(sz.sections, 8, h),
        ),
        in_specs=[VMEM] * 6 + [ANY] * 4,
        out_specs=[VMEM] * 12,
        scratch_shapes=weight_scratch(sz)
        + [
            pltpu.VMEM((r, 3 * 256), F32),
            pltpu.VMEM((r, h), F32),
            pltpu.VMEM((r, h), F32),
            pltpu.VMEM((r, h), BF16),
        ]
        + scan_scratch(sz)
        + exchange_scratch(sz),
        compiler_params=pltpu.CompilerParams(
            collective_id=layer, has_side_effects=True, vmem_limit_bytes=LIMIT
        ),
        name=f"forward_{layer}",
    )(stream, *masks, bias, mix_gain, mlp_gain, *weights)


def run_backward(sz, layer, gx, stream, masks, mix_gain, mlp_gain, saved, weights):
    r, d, h, f = sz.rows, sz.width, sz.hidden, sz.inner
    return pl.pallas_call(
        functools.partial(backward_kernel, sz, layer),
        out_shape=(
            shape(r, d),
            shape(d, 3 * h),
            shape(d, h),
            shape(d, f),
            shape(d, f),
            shape(8, 3 * h),
            shape(8, d),
            shape(8, d),
        ),
        in_specs=[VMEM] * 16 + [ANY] * 4,
        out_specs=[VMEM] * 8,
        scratch_shapes=weight_scratch(sz)
        + [
            pltpu.VMEM((r, d), BF16),
            pltpu.VMEM((d, r), BF16),
            pltpu.VMEM((d, r), BF16),
            pltpu.VMEM((r, h), BF16),
            pltpu.VMEM((r, h), F32),
            pltpu.VMEM((r, f), BF16),
            pltpu.VMEM((r, 3 * h), BF16),
            pltpu.VMEM((r, d), F32),
            pltpu.VMEM((r, d), F32),
            pltpu.VMEM((r, h), F32),
        ]
        + scan_scratch(sz)
        + [pltpu.VMEM((sz.sections, 8, h), F32)]
        + exchange_scratch(sz),
        compiler_params=pltpu.CompilerParams(
            collective_id=2 + layer, has_side_effects=True, vmem_limit_bytes=LIMIT
        ),
        name=f"backward_{layer}",
    )(gx, stream, *masks, mix_gain, mlp_gain, *saved, *weights)


BLOCK = 64
HELD = 3
RINGS = (4, 5, 5, 16, 16)
SENDS = 16
STAGES = 5
WINDOW = 4
DELAY = 1.5
SMALL = 1280


ORDERS = (((0, 2, 1, 3), (1, 2, 0, 3)),) * 16


class Units:
    def __init__(self, count, refs):
        self.count = count
        self.__dict__.update(vars(refs))
        self.arrived = [getattr(refs, f"arrived{stage}") for stage in range(STAGES)]
        section, batch = lax.axis_index("section"), lax.axis_index("batch")
        core, x = section % 2, section // 2
        y, za, zb = batch % 2, (batch // 2) % 2, batch // 4
        self.core = core
        self.where = (x, y, za, zb)
        self.partner = {
            "core": {"section": section + 1 - 2 * core},
            "x": {"section": section + 2 - 4 * x},
            "y": {"batch": batch + 1 - 2 * y},
            "za": {"batch": batch + 2 - 4 * za},
            "zb": {"batch": batch + 4 - 8 * zb},
        }
        self.now = 0.0
        self.links = ("core", "x", "y", "z")
        self.free_at = dict.fromkeys(self.links, 0.0)
        self.flying = dict.fromkeys(self.links, 0)
        self.queues = {link: [] for link in self.links}
        self.ready = {}
        self.summed = set()
        self.copies = {}
        self.small_left = None

    def greet(self):
        section = lax.axis_index("section")
        others = [self.partner["y"], self.partner["za"], self.partner["zb"]]
        others += [{"section": lax.rem(section + hop, 4)} for hop in range(1, 4)]
        for other in others:
            pl.semaphore_signal(
                pltpu.get_barrier_semaphore(), inc=1, device_id=other, device_id_type=MESH
            )

    def greeted(self):
        pl.semaphore_wait(pltpu.get_barrier_semaphore(), 6)

    def name(self, unit, stage, half):
        return "core" if stage == 0 else ("x", "y", "za", "zb")[ORDERS[unit][half][stage - 1]]

    def link(self, unit, stage, half):
        name = self.name(unit, stage, half)
        return "z" if name[0] == "z" else name

    def bit(self, unit, stage, half):
        return self.where[ORDERS[unit][half][stage - 1]]

    def arrival(self, unit, stage, half):
        ref = self.arrived[stage].at[unit % RINGS[stage]]
        return ref if stage == 0 else ref.at[half]

    def copy(self, unit, stage, half):
        at = 0 if stage == 0 else 2 * stage - 1 + half
        if stage == 0:
            src = self.held.at[unit % HELD, 1 - self.core]
        else:
            count = 16 >> stage
            src = self.arrived[stage - 1].at[unit % RINGS[stage - 1], half]
            src = src.at[pl.ds((1 - self.bit(unit, stage, half)) * count, count)]
        return pltpu.make_async_remote_copy(
            src_ref=src,
            dst_ref=self.arrival(unit, stage, half),
            send_sem=self.send_sems.at[unit % SENDS, at],
            recv_sem=self.recv_sems.at[unit % RINGS[stage], at],
            device_id=self.partner[self.name(unit, stage, half)],
            device_id_type=MESH,
        )

    def has_place(self, unit, stage, half):
        before = unit - RINGS[stage]
        if before < 0:
            return True
        if stage == 0:
            return (before, 1, 0) in self.summed and (before, 1, 1) in self.summed
        return (before, min(stage + 1, STAGES - 1), half) in self.summed

    def credit(self, unit, stage, half):
        after = unit + RINGS[stage]
        if after < self.count:
            pl.semaphore_signal(
                self.credits.at[0 if stage == 0 else 2 * stage - 1 + half, after],
                inc=1,
                device_id=self.partner[self.name(after, stage, half)],
                device_id_type=MESH,
            )

    def pump(self):
        for link, queue in self.queues.items():
            while self.flying[link] < WINDOW:
                key = next((key for key in queue if self.has_place(*key)), None)
                if key is None:
                    break
                queue.remove(key)
                self.flying[link] += 1
                unit, stage, half = key
                if unit >= RINGS[stage]:
                    at = 0 if stage == 0 else 2 * stage - 1 + half
                    pl.semaphore_wait(self.credits.at[at, unit], 1)
                self.copies[key] = self.copy(*key)
                self.copies[key].start()
                blocks = 32 if stage == 0 else 16 >> stage
                self.ready[key] = self.expect(link, blocks * BLOCK * LANES * 4)

    def expect(self, link, size):
        rate = 250e3 if link == "core" else 45e3
        self.free_at[link] = max(self.now, self.free_at[link]) + size / rate
        return self.free_at[link] + DELAY

    def push(self, unit, stage, half):
        self.queues[self.link(unit, stage, half)].append((unit, stage, half))
        self.pump()

    def produced(self, us, *which):
        self.now += us
        for unit in which:
            self.push(unit, 0, 0)
        self.passed(0)

    def add(self, dst, src, count):
        turn = min(count, 4)

        def one(i, carry):
            for k in range(turn):
                dst[i * turn + k] += src[i * turn + k]
            return carry

        if count == turn:
            one(0, 0)
        else:
            lax.fori_loop(0, count // turn, one, 0)

    def step(self, unit, stage, half):
        key = (unit, stage, half)
        del self.ready[key]
        self.copies[key].wait_recv()
        here = self.arrival(unit, stage, half)
        if stage == 0:
            for h in range(2):
                self.add(here.at[h], self.held.at[unit % HELD, self.core, h], 16)
        else:
            count = 16 >> stage
            before = self.arrived[stage - 1].at[unit % RINGS[stage - 1], half]
            self.add(here, before.at[pl.ds(self.bit(unit, stage, half) * count, count)], count)
            self.copies.pop(key).wait_send()
        self.summed.add(key)
        self.flying[self.link(unit, stage, half)] -= 1
        self.now += 0.25
        if stage > 1 or (unit, 1, 1 - half) in self.summed:
            if stage > 0:
                self.credit(unit, stage - 1, half if stage > 1 else 0)
        if stage == 0:
            for h in range(2):
                self.push(unit, 1, h)
        elif stage < STAGES - 1:
            self.push(unit, stage + 1, half)
        else:
            self.finish(unit, half, here[0])
            self.credit(unit, stage, half)
        self.pump()

    def finish(self, unit, half, block):
        layer, k = self.count // 8 - 1 - unit // 8, unit % 8
        if k < 2 or k == 4:
            ref, at = (self.down_weight_grad, k) if k < 2 else (self.out_weight_grad, 0)
            ref[layer, :, at * 256 + half * 128 : at * 256 + half * 128 + 128] = block
        else:
            ref, at = (self.up_weight_grad, k - 2) if k < 4 else (self.gate_weight_grad, k - 5)
            rows = slice(half * BLOCK, half * BLOCK + BLOCK)
            ref[layer, rows, at * LANES : at * LANES + LANES] = block

    def small_copy(self, stage):
        name = ("core", "x", "y", "za", "zb")[stage]
        return pltpu.make_async_remote_copy(
            src_ref=self.small.at[stage],
            dst_ref=self.small_arrived.at[stage],
            send_sem=self.small_send.at[stage],
            recv_sem=self.small_recv.at[stage],
            device_id=self.partner[name],
            device_id_type=MESH,
        )

    def small_start(self):
        self.small_left = 0
        self.small_copies = [self.small_copy(0)]
        self.small_copies[0].start()
        self.small_ready = self.now + 3.0

    def small_step(self):
        stage = self.small_left
        self.small_copies[stage].wait_recv()
        self.small[stage + 1] = self.small[stage] + self.small_arrived[stage]
        self.small_left += 1
        if self.small_left < STAGES:
            self.small_copies.append(self.small_copy(self.small_left))
            self.small_copies[-1].start()
            self.small_ready = self.now + 3.0
        else:
            for copy in self.small_copies:
                copy.wait_send()

    def open(self, unit, stage, half):
        halves = range(2) if stage == 0 else (half,)
        before = unit - RING
        return (
            before < 0
            or stage == STAGES - 1
            or all((before, stage + 1, h) in self.consumed for h in halves)
        )

    def next(self):
        best = min(self.ready.items(), key=lambda item: (item[1], item[0]), default=None)
        small = self.small_left is not None and self.small_left < STAGES
        if small and (best is None or self.small_ready <= best[1]):
            return self.small_ready, None
        return (best[1], best[0]) if best else None

    def take(self, item):
        self.now = max(self.now, item[0])
        if item[1] is None:
            self.small_step()
        else:
            self.step(*item[1])

    def passed(self, us):
        self.now += us
        while (item := self.next()) and item[0] <= self.now:
            self.take(item)

    def room(self, unit):
        before = (unit - HELD, 0, 0)
        while unit >= HELD and before not in self.summed:
            self.take(self.next())
        if before in self.copies:
            self.copies.pop(before).wait_send()

    def drain(self):
        while item := self.next():
            self.take(item)
        for key in list(self.copies):
            self.copies.pop(key).wait_send()


def place(unit, half, x, y, z):
    return spot(unit, half, (x, y, z % 2, z // 2))


def spot(unit, half, where):
    order = ORDERS[unit][half]
    return where[order[0]] * 8 + where[order[1]] * 4 + where[order[2]] * 2 + where[order[3]]


def strided(start, steps):
    return pl.ds(start, CHUNKS, stride=steps)


def whole_step(sz, layers, names, *args):
    r = types.SimpleNamespace(**dict(zip(names, args)))
    units = Units(8 * layers, r)
    valid, keep, low, low_t, wide_t = r.valid, r.keep, r.low, r.low_t, r.wide_t
    hb, ga, gz, grad, gy1, gx = r.hb, r.ga, r.gz, r.grad, r.gy1, r.gx
    gp = gz.at[:, : sz.inner]
    decay, enter, prefix, mine = r.decay, r.enter, r.prefix, r.mine
    small, held = r.small, r.held
    natural = r.natural
    last = layers - 1
    half = sz.hidden // 2
    zs = (ga.at[:, :768], r.z1)
    drive = r.drive
    homes = dict(gate_w=r.gate_hbm, out_w=r.out_hbm, up_w=r.up_hbm, down_w=r.down_hbm)
    homes.update(u=r.u_save, a=r.a_save, b=r.b_save, zc=r.zc_save, states=r.states_save)
    homes.update(y1=r.y1_save, v=r.v_save, p=r.p_save, gb=r.gb_save, stream=r.stream_save)
    keys = types.SimpleNamespace(**{name: name for name in homes})
    index_of = {name: i for i, name in enumerate(homes)}
    loads, saves = {}, {}

    def load(layer, name):
        copy = pltpu.make_async_copy(
            homes[name].at[layer], getattr(r, name), r.load_sems.at[index_of[name]]
        )
        copy.start()
        loads[name] = copy

    def need(*wanted):
        for name in wanted:
            if name in loads:
                loads.pop(name).wait()

    def save(layer, name, ref=None):
        if layer < last:
            src = getattr(r, name) if ref is None else ref
            copy = pltpu.make_async_copy(
                src, homes[name].at[layer], r.save_sems.at[index_of[name]]
            )
            copy.start()
            saves[name] = copy

    def settled(*which):
        for name in which:
            if name in saves:
                saves.pop(name).wait()

    def over(count, one):
        def each(i, carry):
            one(i)
            return carry

        lax.fori_loop(0, count, each, 0)

    act_load = pltpu.make_async_copy(r.activations, hb.at[:, : sz.width], r.in_sems.at[0])
    cot_load = pltpu.make_async_copy(r.cotangent, wide_t, r.in_sems.at[1])
    len_load = pltpu.make_async_copy(r.lengths, r.lens, r.in_sems.at[2])
    len_load.start()
    act_load.start()
    load(0, keys.gate_w)
    units.greet()
    mine[...] = jnp.zeros_like(mine)
    small[0] = jnp.zeros((8, SMALL), F32)
    len_load.wait()
    fill_masks(r.lens, valid, keep, sz, True)

    def to_steps(src, put):
        def cast(i):
            at = tile(i, 64)
            for k in range(sz.width // LANES):
                natural[k, at, :] = src[at, k * LANES : (k + 1) * LANES].astype(F32)

        over(sz.rows // 64, cast)

        def gather(j):
            for k in range(sz.width // LANES):
                parts = [
                    natural[k, strided(s * sz.span + j, sz.steps), :] for s in range(sz.micro)
                ]
                put(tile(j, sz.group), slice(k * LANES, (k + 1) * LANES), jnp.concatenate(parts, axis=0))

        over(sz.steps, gather)

    def from_steps(src, dst, sem):
        def scatter(j):
            for k in range(sz.width // LANES):
                value = src[tile(j, sz.group), k * LANES : (k + 1) * LANES]
                for s in range(sz.micro):
                    natural[k, strided(s * sz.span + j, sz.steps), :] = value[s * 8 : s * 8 + 8]

        over(sz.steps, scatter)
        copies = []
        for k in range(sz.width // LANES):
            lanes = slice(k * LANES, (k + 1) * LANES)
            copies.append(pltpu.make_async_copy(natural.at[k], dst.at[:, lanes], sem.at[k]))
            copies[-1].start()
        return copies

    act_load.wait()

    def put_gx(at, lanes, value):
        gx[at, lanes] = value

    to_steps(hb.at[:, : sz.width], put_gx)

    parts = [slice(part * half, (part + 1) * half) for part in range(2)]

    def exchange_start(way, layer, part):
        lanes = parts[part]
        slots = r.slots.at[way, layer]
        me = lax.axis_index("section")
        copies = []
        for hop in range(1, sz.sections):
            copies.append(
                pltpu.make_async_remote_copy(
                    src_ref=mine.at[:, lanes],
                    dst_ref=slots.at[me, :, lanes],
                    send_sem=r.pair_send.at[way, layer, part, hop - 1],
                    recv_sem=r.pair_recv.at[way, layer, part, hop - 1],
                    device_id={"section": lax.rem(me + hop, sz.sections)},
                    device_id_type=MESH,
                )
            )
        for copy in copies:
            copy.start()
        slots[me, :, lanes] = mine[:, lanes]
        return slots, copies

    def exchange_end(slots, copies, reverse, part):
        for copy in copies:
            copy.wait()
        part_enter(slots, prefix, enter, sz, reverse, parts[part])

    def in_turn(count, dots, rest, after=None, third=None):
        over(sz.rows // 256, lambda i: dots(0, i))
        for n in range(count):

            def both(i):
                if n + 1 < count:
                    dots(n + 1, i)
                if third is not None and n > 0:
                    third(n - 1, i)
                rest(n, i)

            over(sz.rows // 256, both)
            if after is not None:
                after(n)

    def keep_cotangent():
        cot_load.wait()

        def put_low(at, lanes, value):
            low[at, lanes] = value.astype(BF16)

        to_steps(wide_t, put_low)
        low_t[...] = low[...].T

    def forward(layer):
        stream = r.stream if layer > 0 else gx
        settled(keys.u)
        norm_rows(stream, r.mix_gain.at[layer : layer + 1], r.u, sz.rows, 128)
        save(layer, keys.u)
        if layer == 0:
            save(layer, keys.stream, gx)
        need(keys.gate_w)
        if layer == 0:
            for name in (keys.out_w, keys.up_w, keys.down_w):
                load(0, name)
            cot_load.start()
        settled(keys.a, keys.b, keys.zc)
        hw = 256
        bias = r.gate_bias

        def gate_dots(n, i):
            rows = tile(i, 256)
            for part in range(3):
                cols = slice(part * sz.hidden + n * hw, part * sz.hidden + (n + 1) * hw)
                zs[n % 2][rows, part * hw : (part + 1) * hw] = (
                    jnp.dot(r.u[rows, :], r.gate_w[:, cols], preferred_element_type=F32)
                    + bias[layer : layer + 1, cols]
                )

        def gate_rest(n, i):
            for chunk in range(4):
                at = pl.ds(pl.multiple_of(i * 256 + chunk * 64, 64), 64)
                vm, km = valid[at, :], keep[at, :]
                for lane in range(hw // LANES):
                    zf, zi, zc = (
                        zs[n % 2][at, part * hw + lane * LANES : part * hw + (lane + 1) * LANES]
                        for part in range(3)
                    )
                    cols = slice(n * hw + lane * LANES, n * hw + (lane + 1) * LANES)
                    a, b = odds(zf, zi)
                    fp, ip, _ = gate_weights(a, b)
                    decay[at, cols] = fp * km
                    drive[at, cols] = ip * zc * vm
                    r.a[at, cols] = a
                    r.b[at, cols] = b
                    r.zc[at, cols] = zc
                    r.forget[...] += jnp.sum((fp * vm).reshape(8, 8, LANES), axis=0)

        flights = []

        def gate_after(n):
            if n % 2 == 0:
                return
            lanes = parts[n // 2]

            def totals(j, pair):
                at = tile(j, sz.group)
                d = decay[at, lanes]
                return pair[0] * d, pair[1] * d + drive[at, lanes]

            one = jnp.ones((sz.group, half), F32)
            pair = steps_of(sz.steps, 2, totals, (one, jnp.zeros_like(one)))
            r.chunk_p[:, lanes] = pair[0]
            r.chunk_t[:, lanes] = pair[1]
            part_totals(r.chunk_p, r.chunk_t, sz, False, prefix, mine, lanes)
            if layer == 0 and n == 1:
                units.greeted()
            flights.append(exchange_start(0, layer, n // 2))

        r.forget[...] = jnp.zeros_like(r.forget)
        in_turn(sz.hidden // hw, gate_dots, gate_rest, gate_after)
        small[0, layer * 4 : layer * 4 + 1, sz.hidden : sz.hidden + LANES] = jnp.sum(
            r.forget[...], axis=0, keepdims=True
        )
        for name in (keys.a, keys.b, keys.zc):
            save(layer, name)
        if layer < last:
            load(layer + 1, keys.gate_w)
        settled(keys.states, keys.y1, keys.v, keys.p, keys.gb, keys.stream)
        states = r.states
        for part, lanes in enumerate(parts):
            exchange_end(*flights[part], False, part)
            states[0 : sz.group, lanes] = enter[:, lanes]

            def walk(j, h):
                at = tile(j, sz.group)
                h = decay[at, lanes] * h + drive[at, lanes]
                states[tile(j + 1, sz.group), lanes] = h
                hb[at, lanes] = h.astype(BF16)
                return h

            steps_of(sz.steps, 4, walk, enter[:, lanes])
            if (layer, part) == (0, 0):
                keep_cotangent()
        save(layer, keys.states)
        need(keys.out_w)

        def out_tile(n):
            cols = tile(n, 256)
            r.y1[:, cols] = stream[:, cols] + jnp.dot(
                hb[...], r.out_w[:, cols], preferred_element_type=F32
            )

        over(sz.width // 256, out_tile)
        save(layer, keys.y1)
        if layer < last:
            load(layer + 1, keys.out_w)
        norm_rows(r.y1, r.mlp_gain.at[layer : layer + 1], r.v, sz.rows, 128)
        save(layer, keys.v)
        need(keys.up_w)

        tiles = range(8) if layer < last else (0, 2, 4, 6, 1, 3, 5, 7)

        def up_dots(n, i):
            rows, cols = tile(i, 256), slice(tiles[n] * 256, (tiles[n] + 1) * 256)
            zs[n % 2][rows, :256] = jnp.dot(
                r.v[rows, :], r.up_w[:, cols], preferred_element_type=F32
            )

        def up_rest(n, i):
            cols = slice(tiles[n] * 256, (tiles[n] + 1) * 256)
            for chunk in range(4):
                at = pl.ds(pl.multiple_of(i * 256 + chunk * 64, 64), 64)
                p = zs[n % 2][at, :256]
                r.p[at, cols] = p
                r.gb[at, cols] = (p * normal_below(p)).astype(BF16)

        def down_part(n, i):
            s, unit = tiles[n] // 2, tiles[n] % 2
            value = jnp.dot(
                low_t[tile(i, 256), :],
                r.gb[:, tiles[n] * 256 : (tiles[n] + 1) * 256],
                preferred_element_type=F32,
            )
            for k in range(4):
                for h in range(2):
                    at = spot(unit, h, (s // 2, k % 2, k // 2, i))
                    held[unit, s % 2, h, at] = value[
                        k * 64 : k * 64 + 64, h * 128 : h * 128 + 128
                    ]

        def up_after(n):
            units.passed(0.3)
            if n == 4:
                units.produced(0, 0)

        if layer < last:
            in_turn(8, up_dots, up_rest)
        else:
            in_turn(8, up_dots, up_rest, up_after, down_part)
            over(2, lambda i: down_part(7, i))
            units.produced(0.2, 1)
        save(layer, keys.p)
        save(layer, keys.gb)
        if layer < last:
            load(layer + 1, keys.up_w)
        need(keys.down_w)
        out = r.stream if layer < last else gy1

        def down_tile(n):
            cols = tile(n, 256)
            out[:, cols] = r.y1[:, cols] + jnp.dot(
                r.gb[...], r.down_w[:, cols], preferred_element_type=F32
            )

        over(sz.width // 256, down_tile)
        if layer < last:
            load(layer + 1, keys.down_w)

    def down_grad(layer, unit):
        for k in range(2):
            units.room(unit + k)

        def one(n):
            s, t = n // 2, n % 2
            value = jnp.dot(low_t[...], r.gb[:, tile(n, 256)], preferred_element_type=F32)
            for b in range(8):
                for h in range(2):
                    at = [place(unit + k, h, s // 2, b % 2, b // 2) for k in range(2)]
                    held[(unit + t) % HELD, s % 2, h, jnp.where(t == 0, *at)] = value[
                        b * 64 : b * 64 + 64, h * 128 : h * 128 + 128
                    ]

        over(8, one)
        units.produced(2, unit, unit + 1)

    def cast(src, dst):
        def one(i):
            at = tile(i, 64)
            dst[at, :] = src[at, :].astype(dst.dtype)

        over(sz.rows // 64, one)

    def turn_rows(src, dst, n):
        at = tile(n, 128)
        dst[:, at] = src[at, :].T

    def contract(left, weight, dst, count, beside=None):
        def one(n):
            if beside is not None:
                beside(n)
            cols = tile(n, 256)
            dst[:, cols] = lax.dot_general(
                left[...], weight[cols, :], (((1,), (1,)), ((), ())), preferred_element_type=F32
            )

        over(count // 256, one)

    def up_grad(layer, unit):
        for k in range(2):
            units.room(unit + k)

        def one(b):
            value = jnp.dot(wide_t[...], gp[:, tile(b, 256)], preferred_element_type=F32)
            for s in range(4):
                for h in range(2):
                    for t in range(2):
                        at = place(unit + t, h, s // 2, b % 2, b // 2)
                        held[(unit + t) % HELD, s % 2, h, at] = value[
                            s * 128 + h * 64 : s * 128 + h * 64 + 64, t * 128 : t * 128 + 128
                        ]

        over(8, one)
        units.produced(2.5, unit, unit + 1)

    def out_grad(layer, unit):
        def cast_state(i):
            hb[tile(i, sz.group), :] = r.states[tile(i + 1, sz.group), :].astype(BF16)

        if layer < last:
            over(sz.steps, cast_state)
        units.room(unit)

        def one(s):
            value = jnp.dot(r.go_t[...], hb[:, tile(s, 256)], preferred_element_type=F32)
            for b in range(8):
                for h in range(2):
                    at = place(unit, h, s // 2, b % 2, b // 2)
                    held[unit % HELD, s % 2, h, at] = value[
                        b * 64 : b * 64 + 64, h * 128 : h * 128 + 128
                    ]

        over(4, one)
        units.produced(1.2, unit)

    def backward(layer, unit):
        late = layer < last

        def freed(*which):
            if layer > 0:
                for name in which:
                    load(layer - 1, name)

        if not late:
            freed(keys.gb)
        need(keys.down_w, keys.p, keys.v)

        def act_dots(n, i):
            rows = tile(i, 256)
            zs[n % 2][rows, :256] = lax.dot_general(
                low[rows, :],
                r.down_w[n * 256 : (n + 1) * 256, :],
                (((1,), (1,)), ((), ())),
                preferred_element_type=F32,
            )

        def act_rest(n, i):
            if n < 2:
                turn_rows(r.v, wide_t, 2 * n + i)
            elif n < 4 and late:
                turn_rows(low, low_t, 2 * (n - 2) + i)
            cols = slice(n * 256, (n + 1) * 256)
            for chunk in range(4):
                at = pl.ds(pl.multiple_of(i * 256 + chunk * 64, 64), 64)
                p = r.p[at, cols]
                slope = normal_below(p) + ROOT_TAU * p * jnp.exp(-0.5 * p * p)
                gp[at, cols] = (zs[n % 2][at, :256] * slope).astype(BF16)

        in_turn(sz.inner // 256, act_dots, act_rest, lambda n: units.passed(0.6))
        freed(keys.down_w, keys.p, keys.v)
        if not late:
            up_grad(layer, unit + 2)
        need(keys.up_w, keys.y1, keys.u)

        def turn_u(n):
            for k in range(2):
                turn_rows(r.u, r.u_t, 2 * n + k)

        contract(gp, r.up_w, grad, sz.width, turn_u)
        freed(keys.u)
        freed(keys.up_w)
        units.passed(1.5)
        norm_back(r.y1, r.mlp_gain.at[layer : layer + 1], grad, gx, gy1, r.mlp_sum, sz.rows, 64, low)
        freed(keys.y1)
        need(keys.states)
        units.passed(2)
        need(keys.out_w, keys.a, keys.b)
        contract(low, r.out_w, ga, sz.hidden, lambda n: turn_rows(low, r.go_t, n))
        freed(keys.out_w)
        units.passed(1)
        if not late:
            out_grad(layer, unit + 4)
        flights = []
        for part, lanes in enumerate(parts):

            def totals(j, pair):
                at = tile(j, sz.group)
                if layer < last:
                    mask = jnp.concatenate([keep[at, :]] * (half // LANES), axis=1)
                    d = gate_weights(r.a[at, lanes], r.b[at, lanes])[0] * mask
                    decay[at, lanes] = d
                else:
                    d = decay[at, lanes]
                return pair[0] * d, d * (ga[at, lanes] + pair[1])

            one = jnp.ones((sz.group, half), F32)
            pair = steps_of(sz.steps, 2, totals, (one, jnp.zeros_like(one)), reverse=True)
            r.chunk_p[:, lanes] = pair[0]
            r.chunk_t[:, lanes] = pair[1]
            part_totals(r.chunk_p, r.chunk_t, sz, True, prefix, mine, lanes)
            flights.append(exchange_start(1, layer, part))
            carried = [units.expect(link, 16384) for link in ("core", "x", "x")]
            units.passed(0.8)
        need(keys.zc)
        if late:
            need(keys.gb)
            down_grad(layer, unit)
            up_grad(layer, unit + 2)
            out_grad(layer, unit + 4)
        unit += 5
        units.now = max(units.now, *carried)

        def gate_lanes(n):
            wide = 2 * LANES
            lanes = tile(n, wide)

            def walk(j, kept):
                m, bf, bi, bc = kept
                at = tile(j, sz.group)
                d = decay[at, lanes]
                q = ga[at, lanes] + m
                a, b, zc = r.a[at, lanes], r.b[at, lanes], r.zc[at, lanes]
                vm = jnp.concatenate([valid[at, :]] * 2, axis=1)
                km = jnp.concatenate([keep[at, :]] * 2, axis=1)
                fp, ip, inv = gate_weights(a, b)
                gf = q * (r.states[at, lanes] * km - zc * vm)
                parts = (
                    (gf * (a * inv) * fp).astype(BF16),
                    (-gf * (b * inv) * ip).astype(BF16),
                    (q * vm * ip).astype(BF16),
                )
                for part, value in enumerate(parts):
                    gz[at, pl.ds(pl.multiple_of(part * sz.hidden + n * wide, wide), wide)] = value
                return (d * q,) + tuple(
                    a + value.astype(F32) for a, value in zip((bf, bi, bc), parts)
                )

            zero = jnp.zeros((sz.group, wide), F32)
            _, *sums = steps_of(
                sz.steps, 4, walk, (enter[:, lanes], zero, zero, zero), reverse=True
            )
            for part, total in enumerate(sums):
                small[0, layer * 4 + part : layer * 4 + part + 1, lanes] = jnp.sum(
                    total, axis=0, keepdims=True
                )

        turns = sz.hidden // LANES // 4
        for part in range(2):
            exchange_end(*flights[part], True, part)
            over(turns, lambda n: gate_lanes(n + part * turns))
            units.passed(1.8)
        freed(keys.a, keys.b, keys.zc, keys.states)
        for k in range(2):
            units.room(unit + k)

        def gate_grad(b):
            cols = pl.ds(pl.multiple_of(b * 384, 128), 256)
            value = jnp.dot(r.u_t[...], gz[:, cols], preferred_element_type=F32)
            for s in range(4):
                for h in range(2):
                    for t in range(2):
                        at = place(unit + t, h, s // 2, b % 2, b // 2)
                        held[(unit + t) % HELD, s % 2, h, at] = value[
                            s * 128 + h * 64 : s * 128 + h * 64 + 64, t * 128 : t * 128 + 128
                        ]

        over(8, gate_grad)
        units.produced(3, unit, unit + 1)
        unit += 2
        units.room(unit)

        def gate_rest(z):
            right = jnp.concatenate(
                [
                    gz[:, pl.ds(pl.multiple_of((2 * z + y) * 384 + 256, 128), 128)]
                    for y in range(2)
                ],
                axis=1,
            )
            value = jnp.dot(r.u_t[...], right, preferred_element_type=F32)
            for s in range(4):
                for h in range(2):
                    for y in range(2):
                        at = place(unit, h, s // 2, y, z)
                        held[unit % HELD, s % 2, h, at] = value[
                            s * 128 + h * 64 : s * 128 + h * 64 + 64, y * 128 : y * 128 + 128
                        ]

        over(4, gate_rest)
        units.produced(1.5, unit)
        unit += 1
        need(keys.gate_w, keys.stream)
        contract(gz, r.gate_w, grad, sz.width)
        freed(keys.gate_w)
        units.passed(2.5)
        norm_back(r.stream, r.mix_gain.at[layer : layer + 1], grad, gy1, gx, r.mix_sum, sz.rows, 64, low)
        freed(keys.stream)
        row = slice(layer * 4 + 3, layer * 4 + 4)
        small[0, row, : sz.width] = jnp.sum(r.mix_sum[...], axis=0, keepdims=True)
        small[0, row, sz.width : 2 * sz.width] = jnp.sum(r.mlp_sum[...], axis=0, keepdims=True)
        units.passed(1.5)

    forward(0)
    for layer in range(1, layers):
        forward(layer)
    out_copies = from_steps(gy1, r.layer_out, r.out_sems)
    cast(low, gx)
    units.passed(2)
    for index, layer in enumerate(reversed(range(layers))):
        backward(layer, 8 * index)
    units.small_start()
    for copy in out_copies:
        copy.wait()
    out_copies = from_steps(gx, r.input_grad, r.out_sems)
    units.passed(1)
    units.drain()
    for copy in out_copies:
        copy.wait()
    total = small[STAGES]
    count = jnp.int32(0)
    for s in range(r.lens.shape[0]):
        for d in range(r.lens.shape[1]):
            count = count + r.lens[s, d]
    scale = 1.0 / (count.astype(F32) * sz.hidden)
    for layer in range(layers):
        for part in range(3):
            r.gate_bias_grad[layer : layer + 1, part * sz.hidden : (part + 1) * sz.hidden] = total[
                layer * 4 + part : layer * 4 + part + 1, : sz.hidden
            ]
        row = slice(layer * 4 + 3, layer * 4 + 4)
        r.mix_gain_grad[layer : layer + 1, :] = total[row, : sz.width]
        r.mlp_gain_grad[layer : layer + 1, :] = total[row, sz.width : 2 * sz.width]
        lanes = total[layer * 4 : layer * 4 + 1, sz.hidden : sz.hidden + LANES]
        r.forget_mean[layer : layer + 1, :] = (
            jnp.sum(lanes, axis=1, keepdims=True) * scale + jnp.zeros((1, LANES), F32)
        )


def run_whole_step(sz, layers, named):
    lengths = named["lengths"]
    rows, d, h, f = sz.rows, sz.width, sz.hidden, sz.inner
    vm = lambda *dims, kind=F32: pltpu.VMEM(dims, kind)
    sems = pltpu.SemaphoreType
    spec = dict(gate_bias=VMEM, mix_gain=VMEM, mlp_gain=VMEM)
    outputs = dict(
        layer_out=(shape(rows, d), ANY),
        input_grad=(shape(rows, d), ANY),
        gate_weight_grad=(shape(layers, 128, 384), VMEM),
        gate_bias_grad=(shape(layers, 3 * h), VMEM),
        out_weight_grad=(shape(layers, 64, 256), VMEM),
        up_weight_grad=(shape(layers, 128, 256), VMEM),
        down_weight_grad=(shape(layers, 64, 512), VMEM),
        mix_gain_grad=(shape(layers, d), VMEM),
        mlp_gain_grad=(shape(layers, d), VMEM),
        forget_mean=(shape(layers, LANES), VMEM),
    )
    results = len(outputs)
    kept = dict(
        u=((rows, d), BF16),
        a=((rows, h), F32),
        b=((rows, h), F32),
        zc=((rows, h), F32),
        states=((rows + sz.group, h), F32),
        y1=((rows, d), F32),
        v=((rows, d), BF16),
        p=((rows, f), F32),
        gb=((rows, f), BF16),
        stream=((rows, d), F32),
    )
    scratch = {}
    for name, (dims, kind) in kept.items():
        outputs[name + "_save"] = (shape(layers - 1, *dims, kind=kind), ANY)
        scratch[name] = vm(*dims, kind=kind)
    scratch.update(
        gate_w=vm(d, 3 * h, kind=BF16),
        out_w=vm(h, d, kind=BF16),
        up_w=vm(d, f, kind=BF16),
        down_w=vm(f, d, kind=BF16),
        valid=vm(rows, LANES),
        keep=vm(rows, LANES),
        gx=vm(rows, d),
        low=vm(rows, d, kind=BF16),
        low_t=vm(d, rows, kind=BF16),
        wide_t=vm(d, rows, kind=BF16),
        u_t=vm(d, rows, kind=BF16),
        go_t=vm(d, rows, kind=BF16),
        hb=vm(rows, h, kind=BF16),
        z1=vm(rows, 768),
        drive=vm(rows, h),
        forget=vm(8, LANES),
        ga=vm(rows, h),
        gz=vm(rows, 3 * h, kind=BF16),
        grad=vm(rows, d),
        gy1=vm(rows, d),
        decay=vm(rows, h),
        chunk_p=vm(sz.group, h),
        chunk_t=vm(sz.group, h),
        prefix=vm(2, sz.group, h),
        enter=vm(sz.group, h),
        mine=vm(8, h),
        slots=vm(2, layers, sz.sections, 8, h),
        mlp_sum=vm(8, d),
        mix_sum=vm(8, d),
        held=vm(HELD, 2, 2, 16, BLOCK, LANES),
        small=vm(STAGES + 1, 8, SMALL),
        small_arrived=vm(STAGES, 8, SMALL),
        in_sems=sems.DMA((3,)),
        lens=pltpu.SMEM(lengths.shape, jnp.int32),
        out_sems=sems.DMA((d // LANES,)),
        natural=vm(d // LANES, rows, LANES),
        load_sems=sems.DMA((len(kept) + 4,)),
        save_sems=sems.DMA((len(kept) + 4,)),
        pair_send=sems.DMA((2, layers, 2, sz.sections - 1)),
        pair_recv=sems.DMA((2, layers, 2, sz.sections - 1)),
        send_sems=sems.DMA((SENDS, 2 * STAGES - 1)),
        recv_sems=sems.DMA((max(RINGS), 2 * STAGES - 1)),
        credits=sems.REGULAR((2 * STAGES - 1, 8 * layers)),
        small_send=sems.DMA((STAGES,)),
        small_recv=sems.DMA((STAGES,)),
    )
    for stage in range(STAGES):
        scratch[f"arrived{stage}"] = vm(RINGS[stage], 2, 16 >> stage, BLOCK, LANES)
    names = list(named) + list(outputs) + list(scratch)
    out = pl.pallas_call(
        functools.partial(whole_step, sz, layers, names),
        out_shape=tuple(value for value, _ in outputs.values()),
        in_specs=[spec.get(name, ANY) for name in named],
        out_specs=[place_of for _, place_of in outputs.values()],
        scratch_shapes=list(scratch.values()),
        compiler_params=pltpu.CompilerParams(
            collective_id=4, has_side_effects=True, vmem_limit_bytes=LIMIT
        ),
        name="whole_step",
    )(*named.values())
    return out[:results]


def deliver_kernel(count, *refs):
    sources, targets, held = refs[:count], refs[count : 2 * count], refs[2 * count : 3 * count - 1]
    sems = refs[3 * count - 1]
    arrivals = [
        pltpu.make_async_copy(sources[i], held[i], sems.at[0, i]) for i in range(count - 1)
    ]
    departures = [
        pltpu.make_async_copy(held[i], targets[i], sems.at[1, i]) for i in range(count - 1)
    ]
    for copy in arrivals:
        copy.start()
    for layer in range(targets[-1].shape[0]):
        targets[-1][layer] = sources[-1][layer, 0]
    for arrival, departure in zip(arrivals, departures):
        arrival.wait()
        departure.start()
    for copy in departures:
        copy.wait()


def deliver(values):
    count = len(values)
    scalars = pl.BlockSpec(memory_space=pltpu.SMEM)
    shapes = [shape(*value.shape) for value in values[:-1]] + [shape(values[-1].shape[0])]
    return pl.pallas_call(
        functools.partial(deliver_kernel, count),
        out_shape=tuple(shapes),
        in_specs=[ANY] * (count - 1) + [scalars],
        out_specs=[ANY] * (count - 1) + [scalars],
        scratch_shapes=[pltpu.VMEM(value.shape, F32) for value in values[:-1]]
        + [pltpu.SemaphoreType.DMA((2, count - 1))],
        compiler_params=pltpu.CompilerParams(vmem_limit_bytes=LIMIT),
        name="deliver",
    )(*values)


def mask_kernel(sizes, lens, valid, keep):
    fill_masks(lens, valid, keep, sizes)


def body(
    activations,
    cotangent,
    lengths,
    gate_weight,
    gate_bias,
    out_weight,
    up_weight,
    down_weight,
    mix_gain,
    mlp_gain,
):
    micro, span, width = activations.shape
    layers = gate_weight.shape[0]
    sz = Sizes(
        micro, span, width, out_weight.shape[1], up_weight.shape[2], lax.axis_size("section")
    )

    blocks = (width // 4, 3 * sz.hidden // 8, width // 8, sz.inner // 4, sz.hidden // 4)
    axes = (lax.axis_size("section"), lax.axis_size("batch"))
    if axes == (4, 8) and blocks == (128, 384, 64, 512, 256):
        out = run_whole_step(
            sz,
            layers,
            dict(
                activations=activations.reshape(sz.rows, width),
                cotangent=cotangent.reshape(sz.rows, width),
                lengths=lengths.T,
                gate_bias=gate_bias,
                mix_gain=mix_gain,
                mlp_gain=mlp_gain,
                gate_hbm=gate_weight,
                out_hbm=out_weight,
                up_hbm=up_weight,
                down_hbm=down_weight,
            ),
        )
        stream_out, input_grad, gate_g, bias_g, out_g, up_g, down_g, *rest = deliver(out)
        return (
            stream_out.reshape(activations.shape),
            input_grad.reshape(activations.shape),
            gate_g,
            bias_g,
            out_g.transpose(0, 2, 1),
            up_g,
            down_g.transpose(0, 2, 1),
            *rest,
        )

    def arranged(value):
        value = value.astype(F32).reshape(micro, CHUNKS, sz.steps, width)
        return value.transpose(2, 0, 1, 3).reshape(sz.rows, width)

    def restored(value):
        value = value.reshape(sz.steps, micro, CHUNKS, width).transpose(1, 2, 0, 3)
        return value.reshape(micro, span, width)

    masks = pl.pallas_call(
        functools.partial(mask_kernel, sz),
        out_shape=(shape(sz.rows, LANES), shape(sz.rows, LANES)),
        in_specs=[pl.BlockSpec(memory_space=pltpu.SMEM)],
        out_specs=[VMEM] * 2,
        name="masks",
    )(lengths)
    weights = (gate_weight, out_weight, up_weight, down_weight)
    stream = arranged(activations)
    streams, saved, forgets = [], [], []
    for layer in range(layers):
        streams.append(stream)
        stream, *kept, forget, pairs = run_forward(
            sz,
            layer,
            stream,
            masks,
            gate_bias[layer : layer + 1],
            mix_gain[layer : layer + 1],
            mlp_gain[layer : layer + 1],
            weights,
        )
        saved.append((*kept, pairs))
        forgets.append(forget)
    layer_out = restored(stream)
    gx = arranged(cotangent)
    true_count = jnp.sum(lengths).astype(F32)
    forgets = [jnp.sum(forget) for forget in forgets]
    sums, small = [None] * layers, [None] * layers
    for layer in reversed(range(layers)):
        gx, gate_g, out_g, up_g, down_g, bias_g, mix_g, mlp_g = run_backward(
            sz,
            layer,
            gx,
            streams[layer],
            masks,
            mix_gain[layer : layer + 1],
            mlp_gain[layer : layer + 1],
            saved[layer],
            weights,
        )
        sums[layer] = (gate_g, out_g.T, up_g, down_g.T)
        small[layer] = tuple(jnp.sum(part, axis=0) for part in (bias_g, mix_g, mlp_g))
    input_grad = restored(gx)
    stacked = tuple(jnp.stack(parts) for parts in zip(*sums))
    partial_sums = lax.psum_scatter(stacked, "section", scatter_dimension=1, tiled=True)
    large = lax.psum_scatter(partial_sums, "batch", scatter_dimension=2, tiled=True)
    bias_grad, mix_grad, mlp_grad = (jnp.stack(parts) for parts in zip(*small))
    bias_grad, mix_grad, mlp_grad, forget = lax.psum(
        (bias_grad, mix_grad, mlp_grad, jnp.stack(forgets)), ("section", "batch")
    )
    forget_mean = forget / (true_count * sz.hidden)
    return (
        layer_out,
        input_grad,
        large[0],
        bias_grad,
        large[1],
        large[2],
        large[3],
        mix_grad,
        mlp_grad,
        forget_mean,
    )


def solution(mesh):
    stream = P("batch", "section", None)
    block = P(None, "section", "batch")
    return jax.shard_map(
        body,
        mesh=mesh,
        in_specs=(stream, stream) + (P(),) * 8,
        out_specs=(stream, stream, block, P(), block, block, block, P(), P(), P()),
        check_vma=False,
    )
```

```python
import functools
import types

import jax
import jax.numpy as jnp
from jax import lax
from jax.experimental import pallas as pl
from jax.experimental.pallas import tpu as pltpu
from jax.sharding import PartitionSpec as P

epsilon = 1e-06
MESH = pl.DeviceIdType.MESH
F32, BF16 = jnp.float32, jnp.bfloat16
CHUNKS = 8
LANES = 128
ROOT_HALF = 0.7071067811865476
ROOT_TAU = 0.3989422804014327


def tile(index, size):
    return pl.ds(pl.multiple_of(index * size, size), size)


def inverse(value):
    r = pltpu.reciprocal(value, approx=True)
    return r * (2.0 - value * r)


def normal_below(p):
    return 0.5 + 0.5 * lax.erf(p * ROOT_HALF)


def steps_of(count, unroll, one, start, reverse=False):
    def turn(i, carry):
        for k in range(unroll):
            at = i * unroll + k
            carry = one(count - 1 - at if reverse else at, carry)
        return carry

    return lax.fori_loop(0, count // unroll, turn, start)


def odds(zf, zi):
    return jnp.exp(jnp.minimum(-zf, 86.0)), jnp.exp(jnp.minimum(-zi, 86.0))


def gate_weights(a, b):
    inv = inverse(2.0 + a + b)
    return (1.0 + b) * inv, (1.0 + a) * inv, inv


def greet_section(sections):
    me = lax.axis_index("section")
    barrier = pltpu.get_barrier_semaphore()
    for hop in range(1, sections):
        pl.semaphore_signal(
            barrier, inc=1, device_id={"section": lax.rem(me + hop, sections)}, device_id_type=MESH
        )
    pl.semaphore_wait(barrier, sections - 1)


def exchange(mine, slots, send_sems, recv_sems, sections):
    me = lax.axis_index("section")
    copies = []
    for hop in range(1, sections):
        copies.append(
            pltpu.make_async_remote_copy(
                src_ref=mine,
                dst_ref=slots.at[me],
                send_sem=send_sems.at[hop - 1],
                recv_sem=recv_sems.at[hop - 1],
                device_id={"section": lax.rem(me + hop, sections)},
                device_id_type=MESH,
            )
        )
    for copy in copies:
        copy.start()
    slots[me] = mine[...]
    for copy in copies:
        copy.wait()


def norm_rows(stream, gain, low, rows, step):
    def one(i, carry):
        at = tile(i, step)
        x = stream[at, :]
        r = lax.rsqrt(jnp.mean(x * x, axis=-1, keepdims=True) + epsilon)
        low[at, :] = (x * r * gain[...]).astype(BF16)
        return carry

    lax.fori_loop(0, rows // step, one, 0)


def norm_back(stream, gain, grad, through, out, gain_sum, rows, step, low=None):
    width = stream.shape[1]

    def one(i, total):
        at = tile(i, step)
        x = stream[at, :]
        r = lax.rsqrt(jnp.mean(x * x, axis=-1, keepdims=True) + epsilon)
        n = x * r
        g = grad[at, :]
        a = g * gain[...]
        value = through[at, :] + r * (a - n * jnp.mean(a * n, axis=-1, keepdims=True))
        out[at, :] = value
        if low is not None:
            low[at, :] = value.astype(BF16)
        return total + jnp.sum((g * n).reshape(step // 8, 8, width), axis=0)

    gain_sum[...] = lax.fori_loop(0, rows // step, one, jnp.zeros((8, width), F32))


def fill_masks(lens, valid, keep, sizes, turned=False):
    section = lax.axis_index("section")
    group = lax.axis_index("batch")
    starts, totals = [], []
    for s in range(sizes.micro):
        total, begin = 0, []
        for d in range(lens.shape[0 if turned else 1]):
            row = group * sizes.micro + s
            length = lens[d, row] if turned else lens[row, d]
            begin.append(jnp.where(length > 0, total, -1))
            total = total + length
        starts.append(begin)
        totals.append(total)
    chunk_place = lax.broadcasted_iota(jnp.int32, (8, LANES), 0) * sizes.steps

    def one(j, carry):
        for s in range(sizes.micro):
            place = section * sizes.span + j + chunk_place
            true = place < totals[s]
            first = place == starts[s][0]
            for begin in starts[s][1:]:
                first = first | (place == begin)
            at = pl.ds(pl.multiple_of(j * sizes.group + s * 8, 8), 8)
            valid[at, :] = jnp.where(true, 1.0, 0.0)
            keep[at, :] = jnp.where(true & jnp.logical_not(first), 1.0, 0.0)
        return carry

    lax.fori_loop(0, sizes.steps, one, 0)


def scan_totals(first, second, sizes, reverse, prefix, chunk, mine):
    for s in range(sizes.micro):
        p = jnp.ones((1, sizes.hidden), F32)
        t = jnp.zeros((1, sizes.hidden), F32)
        for c in reversed(range(CHUNKS)) if reverse else range(CHUNKS):
            at = s * 8 + c
            prefix[0, at : at + 1, :] = p
            prefix[1, at : at + 1, :] = t
            pc = first[at : at + 1, :]
            t = pc * t + second[at : at + 1, :]
            p = p * pc
        mine[s : s + 1, :] = p
        mine[sizes.micro + s : sizes.micro + s + 1, :] = t


def scan_enter(slots, prefix, enter, sizes, reverse):
    me = lax.axis_index("section")
    for s in range(sizes.micro):
        a = jnp.zeros((1, sizes.hidden), F32)
        order = range(sizes.sections - 1, 0, -1) if reverse else range(sizes.sections - 1)
        for k in order:
            reached = k > me if reverse else k < me
            pk = slots[k, s : s + 1, :]
            tk = slots[k, sizes.micro + s : sizes.micro + s + 1, :]
            a = jnp.where(reached, pk * a + tk, a)
        at = slice(s * 8, s * 8 + 8)
        enter[at, :] = prefix[0, at, :] * a + prefix[1, at, :]


def part_totals(first, second, sizes, reverse, prefix, mine, lanes):
    for s in range(sizes.micro):
        p = jnp.ones((1, lanes.stop - lanes.start), F32)
        t = jnp.zeros_like(p)
        for c in reversed(range(CHUNKS)) if reverse else range(CHUNKS):
            at = s * 8 + c
            prefix[0, at : at + 1, lanes] = p
            prefix[1, at : at + 1, lanes] = t
            pc = first[at : at + 1, lanes]
            t = pc * t + second[at : at + 1, lanes]
            p = p * pc
        mine[s : s + 1, lanes] = p
        mine[sizes.micro + s : sizes.micro + s + 1, lanes] = t


def part_enter(slots, prefix, enter, sizes, reverse, lanes):
    me = lax.axis_index("section")
    for s in range(sizes.micro):
        a = jnp.zeros((1, lanes.stop - lanes.start), F32)
        order = range(sizes.sections - 1, 0, -1) if reverse else range(sizes.sections - 1)
        for k in order:
            reached = k > me if reverse else k < me
            pk = slots[k, s : s + 1, lanes]
            tk = slots[k, sizes.micro + s : sizes.micro + s + 1, lanes]
            a = jnp.where(reached, pk * a + tk, a)
        at = slice(s * 8, s * 8 + 8)
        enter[at, lanes] = prefix[0, at, lanes] * a + prefix[1, at, lanes]


class Sizes:
    def __init__(self, micro, span, width, hidden, inner, sections):
        self.micro, self.span, self.width = micro, span, width
        self.hidden, self.inner, self.sections = hidden, inner, sections
        self.rows = micro * span
        self.steps = span // CHUNKS
        self.group = micro * CHUNKS


def forward_kernel(
    sizes,
    layer,
    stream,
    valid,
    keep,
    bias,
    mix_gain,
    mlp_gain,
    gate_hbm,
    out_hbm,
    up_hbm,
    down_hbm,
    next_stream,
    u,
    sf_out,
    si_out,
    zc_out,
    states,
    y1,
    v,
    p_out,
    gb,
    forget,
    pair_slots,
    gate_w,
    out_w,
    up_w,
    down_w,
    z,
    decay,
    drive,
    hb,
    chunk_p,
    chunk_t,
    prefix,
    enter,
    mine,
    weight_sems,
    send_sems,
    recv_sems,
):
    sz = sizes
    loads = [
        pltpu.make_async_copy(src.at[layer], dst, weight_sems.at[i])
        for i, (src, dst) in enumerate(
            ((gate_hbm, gate_w), (out_hbm, out_w), (up_hbm, up_w), (down_hbm, down_w))
        )
    ]
    for load in loads:
        load.start()
    greet_section(sz.sections)
    mine[...] = jnp.zeros_like(mine)
    norm_rows(stream, mix_gain, u, sz.rows, 64)
    loads[0].wait()
    forget[...] = jnp.zeros_like(forget)
    hw = 256

    def gate_tile(n, carry):
        for part in range(3):
            cols = pl.ds(pl.multiple_of(part * sz.hidden + n * hw, hw), hw)
            z[:, part * hw : (part + 1) * hw] = (
                jnp.dot(u[...], gate_w[:, cols], preferred_element_type=F32) + bias[:, cols]
            )

        def one(i, inner):
            at = tile(i, 64)
            for lane in range(hw // LANES):
                src = lambda part: z[
                    at, part * hw + lane * LANES : part * hw + (lane + 1) * LANES
                ]
                dst = pl.ds(pl.multiple_of(n * hw + lane * LANES, LANES), LANES)
                a = jnp.exp(jnp.minimum(-src(0), 86.0))
                b = jnp.exp(jnp.minimum(-src(1), 86.0))
                zc = src(2)
                fp, ip, _ = gate_weights(a, b)
                vm = valid[at, :]
                decay[at, dst] = fp * keep[at, :]
                drive[at, dst] = ip * zc * vm
                sf_out[at, dst] = a
                si_out[at, dst] = b
                zc_out[at, dst] = zc
                forget[...] += jnp.sum((fp * vm).reshape(8, 8, LANES), axis=0)
            return inner

        lax.fori_loop(0, sz.rows // 64, one, 0)
        return carry

    lax.fori_loop(0, sz.hidden // hw, gate_tile, 0)
    half = sz.hidden // 2
    for part in range(2):
        lanes = slice(part * half, (part + 1) * half)

        def totals(j, pair):
            at = tile(j, sz.group)
            d = decay[at, lanes]
            return pair[0] * d, pair[1] * d + drive[at, lanes]

        one = jnp.ones((sz.group, half), F32)
        pair = steps_of(sz.steps, 4, totals, (one, jnp.zeros_like(one)))
        chunk_p[:, lanes] = pair[0]
        chunk_t[:, lanes] = pair[1]
    scan_totals(chunk_p, chunk_t, sz, False, prefix, None, mine)
    exchange(mine, pair_slots, send_sems, recv_sems, sz.sections)
    scan_enter(pair_slots, prefix, enter, sz, False)
    states[0 : sz.group, :] = enter[...]
    for part in range(2):
        lanes = slice(part * half, (part + 1) * half)

        def walk(j, h):
            at = tile(j, sz.group)
            h = decay[at, lanes] * h + drive[at, lanes]
            states[tile(j + 1, sz.group), lanes] = h
            hb[at, lanes] = h.astype(BF16)
            return h

        steps_of(sz.steps, 4, walk, enter[:, lanes])
    loads[1].wait()

    def out_tile(n, carry):
        cols = tile(n, 256)
        y1[:, cols] = stream[:, cols] + jnp.dot(
            hb[...], out_w[:, cols], preferred_element_type=F32
        )
        return carry

    lax.fori_loop(0, sz.width // 256, out_tile, 0)
    norm_rows(y1, mlp_gain, v, sz.rows, 64)
    loads[2].wait()

    def up_tile(n, carry):
        cols = tile(n, 256)
        p_out[:, cols] = jnp.dot(v[...], up_w[:, cols], preferred_element_type=F32)

        def one(i, inner):
            at = tile(i, 64)
            p = p_out[at, cols]
            gb[at, cols] = (p * normal_below(p)).astype(BF16)
            return inner

        lax.fori_loop(0, sz.rows // 64, one, 0)
        return carry

    lax.fori_loop(0, sz.inner // 256, up_tile, 0)
    loads[3].wait()

    def down_tile(n, carry):
        cols = tile(n, 256)
        next_stream[:, cols] = y1[:, cols] + jnp.dot(
            gb[...], down_w[:, cols], preferred_element_type=F32
        )
        return carry

    lax.fori_loop(0, sz.width // 256, down_tile, 0)


def backward_kernel(
    sizes,
    layer,
    gx,
    stream,
    valid,
    keep,
    mix_gain,
    mlp_gain,
    u,
    sf_in,
    si_in,
    zc_in,
    states,
    y1,
    v,
    p_in,
    gb,
    pair_slots,
    gate_hbm,
    out_hbm,
    up_hbm,
    down_hbm,
    next_gx,
    gate_grad,
    out_grad,
    up_grad,
    down_grad,
    bias_sum,
    mix_sum,
    mlp_sum,
    gate_w,
    out_w,
    up_w,
    down_w,
    low,
    low_t,
    wide_t,
    hb,
    ga,
    gp,
    gz,
    grad,
    gy1,
    decay,
    chunk_p,
    chunk_t,
    prefix,
    enter,
    mine,
    slots,
    weight_sems,
    send_sems,
    recv_sems,
):
    sz = sizes
    loads = [
        pltpu.make_async_copy(src.at[layer], dst, weight_sems.at[i])
        for i, (src, dst) in enumerate(
            ((gate_hbm, gate_w), (out_hbm, out_w), (up_hbm, up_w), (down_hbm, down_w))
        )
    ]
    for load in reversed(loads):
        load.start()
    greet_section(sz.sections)
    mine[...] = jnp.zeros_like(mine)

    def cast(i, carry):
        at = tile(i, 64)
        low[at, :] = gx[at, :].astype(BF16)
        return carry

    lax.fori_loop(0, sz.rows // 64, cast, 0)
    low_t[...] = low[...].T

    def weight_grad(left_t, right, dst, step):
        def one(n, carry):
            cols = tile(n, step)
            dst[:, cols] = jnp.dot(left_t[...], right[:, cols], preferred_element_type=F32)
            return carry

        lax.fori_loop(0, right.shape[1] // step, one, 0)

    weight_grad(low_t, gb, down_grad, 256)
    loads[3].wait()

    def act_tile(n, carry):
        cols = tile(n, 256)
        ga[:, :256] = lax.dot_general(
            low[...], down_w[cols, :], (((1,), (1,)), ((), ())), preferred_element_type=F32
        )

        def one(i, inner):
            at = tile(i, 64)
            p = p_in[at, cols]
            slope = normal_below(p) + ROOT_TAU * p * jnp.exp(-0.5 * p * p)
            gp[at, cols] = (ga[at, :256] * slope).astype(BF16)
            return inner

        lax.fori_loop(0, sz.rows // 64, one, 0)
        return carry

    lax.fori_loop(0, sz.inner // 256, act_tile, 0)
    wide_t[...] = v[...].T
    weight_grad(wide_t, gp, up_grad, 256)
    loads[2].wait()

    def contract(left, weight, dst, step):
        def one(n, carry):
            cols = tile(n, step)
            dst[:, cols] = lax.dot_general(
                left[...], weight[cols, :], (((1,), (1,)), ((), ())), preferred_element_type=F32
            )
            return carry

        lax.fori_loop(0, weight.shape[0] // step, one, 0)

    contract(gp, up_w, grad, 256)
    norm_back(y1, mlp_gain, grad, gx, gy1, mlp_sum, sz.rows, 64)

    def cast_more(i, carry):
        at = tile(i, 64)
        low[at, :] = gy1[at, :].astype(BF16)
        return carry

    lax.fori_loop(0, sz.rows // 64, cast_more, 0)

    def cast_state(i, carry):
        hb[tile(i, sz.group), :] = states[tile(i + 1, sz.group), :].astype(BF16)
        return carry

    lax.fori_loop(0, sz.steps, cast_state, 0)
    low_t[...] = low[...].T
    weight_grad(low_t, hb, out_grad, 256)
    loads[1].wait()
    contract(low, out_w, ga, 256)
    half = sz.hidden // 2
    for part in range(2):
        lanes = slice(part * half, (part + 1) * half)

        def totals(i, pair):
            at = tile(sz.steps - 1 - i, sz.group)
            mask = jnp.concatenate([keep[at, :]] * (half // LANES), axis=1)
            d = gate_weights(sf_in[at, lanes], si_in[at, lanes])[0] * mask
            decay[at, lanes] = d
            return pair[0] * d, d * (ga[at, lanes] + pair[1])

        pair = lax.fori_loop(
            0,
            sz.steps,
            totals,
            (jnp.ones((sz.group, half), F32), jnp.zeros((sz.group, half), F32)),
        )
        chunk_p[:, lanes] = pair[0]
        chunk_t[:, lanes] = pair[1]
    scan_totals(chunk_p, chunk_t, sz, True, prefix, None, mine)
    exchange(mine, slots, send_sems, recv_sems, sz.sections)
    scan_enter(slots, prefix, enter, sz, True)

    def gate_lane(n, carry):
        lanes = tile(n, LANES)

        def walk(i, kept):
            m, bf, bi, bc = kept
            j = sz.steps - 1 - i
            at = tile(j, sz.group)
            d = decay[at, lanes]
            q = ga[at, lanes] + m
            a = sf_in[at, lanes]
            b = si_in[at, lanes]
            zc = zc_in[at, lanes]
            vm = valid[at, :]
            fp, ip, inv = gate_weights(a, b)
            gf = q * (states[at, lanes] * keep[at, :] - zc * vm)
            gzf = (gf * (a * inv) * fp).astype(BF16)
            gzi = (-gf * (b * inv) * ip).astype(BF16)
            gzc = (q * vm * ip).astype(BF16)
            gz[at, lanes] = gzf
            gz[at, pl.ds(pl.multiple_of(sz.hidden + n * LANES, LANES), LANES)] = gzi
            gz[at, pl.ds(pl.multiple_of(2 * sz.hidden + n * LANES, LANES), LANES)] = gzc
            return (
                d * q,
                bf + gzf.astype(F32),
                bi + gzi.astype(F32),
                bc + gzc.astype(F32),
            )

        zero = jnp.zeros((sz.group, LANES), F32)
        _, bf, bi, bc = lax.fori_loop(0, sz.steps, walk, (enter[:, lanes], zero, zero, zero))
        for part, total in enumerate((bf, bi, bc)):
            where = pl.ds(pl.multiple_of(part * sz.hidden + n * LANES, LANES), LANES)
            bias_sum[:, where] = jnp.sum(total.reshape(sz.group // 8, 8, LANES), axis=0)
        return carry

    lax.fori_loop(0, sz.hidden // LANES, gate_lane, 0)
    wide_t[...] = u[...].T
    weight_grad(wide_t, gz, gate_grad, 256)
    loads[0].wait()
    contract(gz, gate_w, grad, 256)
    norm_back(stream, mix_gain, grad, gy1, next_gx, mix_sum, sz.rows, 64)


VMEM = pl.BlockSpec(memory_space=pltpu.VMEM)
ANY = pl.BlockSpec(memory_space=pl.ANY)
LIMIT = 63 * 2**20


def shape(*dims, kind=F32):
    return jax.ShapeDtypeStruct(dims, kind)


def exchange_scratch(sz):
    return [
        pltpu.SemaphoreType.DMA((4,)),
        pltpu.SemaphoreType.DMA((sz.sections - 1,)),
        pltpu.SemaphoreType.DMA((sz.sections - 1,)),
    ]


def weight_scratch(sz):
    return [
        pltpu.VMEM((sz.width, 3 * sz.hidden), BF16),
        pltpu.VMEM((sz.hidden, sz.width), BF16),
        pltpu.VMEM((sz.width, sz.inner), BF16),
        pltpu.VMEM((sz.inner, sz.width), BF16),
    ]


def scan_scratch(sz):
    return [
        pltpu.VMEM((sz.group, sz.hidden), F32),
        pltpu.VMEM((sz.group, sz.hidden), F32),
        pltpu.VMEM((2, sz.group, sz.hidden), F32),
        pltpu.VMEM((sz.group, sz.hidden), F32),
        pltpu.VMEM((8, sz.hidden), F32),
    ]


def run_forward(sz, layer, stream, masks, bias, mix_gain, mlp_gain, weights):
    r, d, h, f = sz.rows, sz.width, sz.hidden, sz.inner
    return pl.pallas_call(
        functools.partial(forward_kernel, sz, layer),
        out_shape=(
            shape(r, d),
            shape(r, d, kind=BF16),
            shape(r, h),
            shape(r, h),
            shape(r, h),
            shape(r + sz.group, h),
            shape(r, d),
            shape(r, d, kind=BF16),
            shape(r, f),
            shape(r, f, kind=BF16),
            shape(8, LANES),
            shape(sz.sections, 8, h),
        ),
        in_specs=[VMEM] * 6 + [ANY] * 4,
        out_specs=[VMEM] * 12,
        scratch_shapes=weight_scratch(sz)
        + [
            pltpu.VMEM((r, 3 * 256), F32),
            pltpu.VMEM((r, h), F32),
            pltpu.VMEM((r, h), F32),
            pltpu.VMEM((r, h), BF16),
        ]
        + scan_scratch(sz)
        + exchange_scratch(sz),
        compiler_params=pltpu.CompilerParams(
            collective_id=layer, has_side_effects=True, vmem_limit_bytes=LIMIT
        ),
        name=f"forward_{layer}",
    )(stream, *masks, bias, mix_gain, mlp_gain, *weights)


def run_backward(sz, layer, gx, stream, masks, mix_gain, mlp_gain, saved, weights):
    r, d, h, f = sz.rows, sz.width, sz.hidden, sz.inner
    return pl.pallas_call(
        functools.partial(backward_kernel, sz, layer),
        out_shape=(
            shape(r, d),
            shape(d, 3 * h),
            shape(d, h),
            shape(d, f),
            shape(d, f),
            shape(8, 3 * h),
            shape(8, d),
            shape(8, d),
        ),
        in_specs=[VMEM] * 16 + [ANY] * 4,
        out_specs=[VMEM] * 8,
        scratch_shapes=weight_scratch(sz)
        + [
            pltpu.VMEM((r, d), BF16),
            pltpu.VMEM((d, r), BF16),
            pltpu.VMEM((d, r), BF16),
            pltpu.VMEM((r, h), BF16),
            pltpu.VMEM((r, h), F32),
            pltpu.VMEM((r, f), BF16),
            pltpu.VMEM((r, 3 * h), BF16),
            pltpu.VMEM((r, d), F32),
            pltpu.VMEM((r, d), F32),
            pltpu.VMEM((r, h), F32),
        ]
        + scan_scratch(sz)
        + [pltpu.VMEM((sz.sections, 8, h), F32)]
        + exchange_scratch(sz),
        compiler_params=pltpu.CompilerParams(
            collective_id=2 + layer, has_side_effects=True, vmem_limit_bytes=LIMIT
        ),
        name=f"backward_{layer}",
    )(gx, stream, *masks, mix_gain, mlp_gain, *saved, *weights)


BLOCK = 64
HELD = 3
RINGS = (4, 5, 5, 16, 16)
SENDS = 16
STAGES = 5
WINDOW = 4
DELAY = 1.5
SMALL = 1280


EVEN = ((0, 2, 1, 3), (1, 2, 0, 3))
PLANE = ((0, 1, 2, 3), (1, 0, 2, 3))
ORDERS = [EVEN] * 16
ORDERS[0] = ((0, 2, 1, 3), (2, 1, 3, 0))
ORDERS[1] = ((1, 2, 0, 3), (0, 2, 1, 3))
ORDERS[6] = ORDERS[9] = PLANE


class Units:
    def __init__(self, count, refs):
        self.count = count
        self.__dict__.update(vars(refs))
        self.arrived = [getattr(refs, f"arrived{stage}") for stage in range(STAGES)]
        section, batch = lax.axis_index("section"), lax.axis_index("batch")
        core, x = section % 2, section // 2
        y, za, zb = batch % 2, (batch // 2) % 2, batch // 4
        self.core = core
        self.where = (x, y, za, zb)
        self.partner = {
            "core": {"section": section + 1 - 2 * core},
            "x": {"section": section + 2 - 4 * x},
            "y": {"batch": batch + 1 - 2 * y},
            "za": {"batch": batch + 2 - 4 * za},
            "zb": {"batch": batch + 4 - 8 * zb},
        }
        self.now = 0.0
        self.links = ("core", "x", "y", "z")
        self.free_at = dict.fromkeys(self.links, 0.0)
        self.flying = dict.fromkeys(self.links, 0)
        self.queues = {link: [] for link in self.links}
        self.ready = {}
        self.summed = set()
        self.copies = {}
        self.small_left = None
        self.leaving = []

    def greet(self):
        section = lax.axis_index("section")
        others = [self.partner["y"], self.partner["za"], self.partner["zb"]]
        others += [{"section": lax.rem(section + hop, 4)} for hop in range(1, 4)]
        for other in others:
            pl.semaphore_signal(
                pltpu.get_barrier_semaphore(), inc=1, device_id=other, device_id_type=MESH
            )

    def greeted(self):
        pl.semaphore_wait(pltpu.get_barrier_semaphore(), 6)

    def name(self, unit, stage, half):
        return "core" if stage == 0 else ("x", "y", "za", "zb")[ORDERS[unit][half][stage - 1]]

    def link(self, unit, stage, half):
        name = self.name(unit, stage, half)
        return "z" if name[0] == "z" else name

    def bit(self, unit, stage, half):
        return self.where[ORDERS[unit][half][stage - 1]]

    def arrival(self, unit, stage, half):
        ref = self.arrived[stage].at[unit % RINGS[stage]]
        return ref if stage == 0 else ref.at[half]

    def copy(self, unit, stage, half):
        at = 0 if stage == 0 else 2 * stage - 1 + half
        if stage == 0:
            src = self.held.at[unit % HELD, 1 - self.core]
        else:
            count = 16 >> stage
            src = self.arrived[stage - 1].at[unit % RINGS[stage - 1], half]
            src = src.at[pl.ds((1 - self.bit(unit, stage, half)) * count, count)]
        return pltpu.make_async_remote_copy(
            src_ref=src,
            dst_ref=self.arrival(unit, stage, half),
            send_sem=self.send_sems.at[unit % SENDS, at],
            recv_sem=self.recv_sems.at[unit % RINGS[stage], at],
            device_id=self.partner[self.name(unit, stage, half)],
            device_id_type=MESH,
        )

    def has_place(self, unit, stage, half):
        before = unit - RINGS[stage]
        if before < 0:
            return True
        if stage == 0:
            return (before, 1, 0) in self.summed and (before, 1, 1) in self.summed
        return (before, min(stage + 1, STAGES - 1), half) in self.summed

    def credit(self, unit, stage, half):
        after = unit + RINGS[stage]
        if after < self.count:
            pl.semaphore_signal(
                self.credits.at[0 if stage == 0 else 2 * stage - 1 + half, after],
                inc=1,
                device_id=self.partner[self.name(after, stage, half)],
                device_id_type=MESH,
            )

    def pump(self):
        for link, queue in self.queues.items():
            while self.flying[link] < WINDOW:
                key = next((key for key in queue if self.has_place(*key)), None)
                if key is None:
                    break
                queue.remove(key)
                self.flying[link] += 1
                unit, stage, half = key
                if unit >= RINGS[stage]:
                    at = 0 if stage == 0 else 2 * stage - 1 + half
                    pl.semaphore_wait(self.credits.at[at, unit], 1)
                self.copies[key] = self.copy(*key)
                self.copies[key].start()
                blocks = 32 if stage == 0 else 16 >> stage
                self.ready[key] = self.expect(link, blocks * BLOCK * LANES * 4)

    def expect(self, link, size):
        rate = 250e3 if link == "core" else 45e3
        self.free_at[link] = max(self.now, self.free_at[link]) + size / rate
        return self.free_at[link] + DELAY

    def push(self, unit, stage, half):
        self.queues[self.link(unit, stage, half)].append((unit, stage, half))
        self.pump()

    def produced(self, us, *which):
        self.now += us
        for unit in which:
            self.push(unit, 0, 0)
        self.passed(0)

    def add(self, dst, src, count):
        turn = min(count, 4)

        def one(i, carry):
            for k in range(turn):
                dst[i * turn + k] += src[i * turn + k]
            return carry

        if count == turn:
            one(0, 0)
        else:
            lax.fori_loop(0, count // turn, one, 0)

    def step(self, unit, stage, half):
        key = (unit, stage, half)
        del self.ready[key]
        self.copies[key].wait_recv()
        here = self.arrival(unit, stage, half)
        if stage == 0:
            for h in range(2):
                self.add(here.at[h], self.held.at[unit % HELD, self.core, h], 16)
        else:
            count = 16 >> stage
            before = self.arrived[stage - 1].at[unit % RINGS[stage - 1], half]
            self.add(here, before.at[pl.ds(self.bit(unit, stage, half) * count, count)], count)
            self.copies.pop(key).wait_send()
        self.summed.add(key)
        self.flying[self.link(unit, stage, half)] -= 1
        self.now += 0.25
        if stage > 1 or (unit, 1, 1 - half) in self.summed:
            if stage > 0:
                self.credit(unit, stage - 1, half if stage > 1 else 0)
        if stage == 0:
            for h in range(2):
                self.push(unit, 1, h)
        elif stage < STAGES - 1:
            self.push(unit, stage + 1, half)
        else:
            self.finish(unit, half, here.at[0])
            self.credit(unit, stage, half)
        self.pump()

    def finish(self, unit, half, block):
        layer, k = self.count // 8 - 1 - unit // 8, unit % 8
        if k < 2 or k == 4:
            ref, at = (self.down_weight_grad, k) if k < 2 else (self.out_weight_grad, 0)
            to = ref.at[layer, :, at * 256 + half * 128 : at * 256 + half * 128 + 128]
        else:
            ref, at = (self.up_weight_grad, k - 2) if k < 4 else (self.gate_weight_grad, k - 5)
            rows = slice(half * BLOCK, half * BLOCK + BLOCK)
            to = ref.at[layer, rows, at * LANES : at * LANES + LANES]
        copy = pltpu.make_async_copy(block, to, self.result_sems.at[unit, half])
        copy.start()
        self.leaving.append(copy)

    def small_copy(self, stage):
        name = ("core", "x", "y", "za", "zb")[stage]
        return pltpu.make_async_remote_copy(
            src_ref=self.small.at[stage],
            dst_ref=self.small_arrived.at[stage],
            send_sem=self.small_send.at[stage],
            recv_sem=self.small_recv.at[stage],
            device_id=self.partner[name],
            device_id_type=MESH,
        )

    def small_start(self):
        self.small_left = 0
        self.small_copies = [self.small_copy(0)]
        self.small_copies[0].start()
        self.small_ready = self.now + 3.0

    def small_step(self):
        stage = self.small_left
        self.small_copies[stage].wait_recv()
        self.small[stage + 1] = self.small[stage] + self.small_arrived[stage]
        self.small_left += 1
        if self.small_left < STAGES:
            self.small_copies.append(self.small_copy(self.small_left))
            self.small_copies[-1].start()
            self.small_ready = self.now + 3.0
        else:
            for copy in self.small_copies:
                copy.wait_send()
            self.small_done()

    def open(self, unit, stage, half):
        halves = range(2) if stage == 0 else (half,)
        before = unit - RING
        return (
            before < 0
            or stage == STAGES - 1
            or all((before, stage + 1, h) in self.consumed for h in halves)
        )

    def next(self):
        best = min(self.ready.items(), key=lambda item: (item[1], item[0]), default=None)
        small = self.small_left is not None and self.small_left < STAGES
        if small and (best is None or self.small_ready <= best[1]):
            return self.small_ready, None
        return (best[1], best[0]) if best else None

    def take(self, item):
        self.now = max(self.now, item[0])
        if item[1] is None:
            self.small_step()
        else:
            self.step(*item[1])

    def passed(self, us):
        self.now += us
        while (item := self.next()) and item[0] <= self.now:
            self.take(item)

    def room(self, unit):
        before = (unit - HELD, 0, 0)
        while unit >= HELD and before not in self.summed:
            self.take(self.next())
        if before in self.copies:
            self.copies.pop(before).wait_send()

    def drain(self):
        while item := self.next():
            self.take(item)
        for key in list(self.copies):
            self.copies.pop(key).wait_send()
        for copy in self.leaving:
            copy.wait()


def place(unit, half, x, y, z):
    return spot(unit, half, (x, y, z % 2, z // 2))


def spot(unit, half, where):
    order = ORDERS[unit][half]
    return where[order[0]] * 8 + where[order[1]] * 4 + where[order[2]] * 2 + where[order[3]]


def strided(start, steps):
    return pl.ds(start, CHUNKS, stride=steps)


def whole_step(sz, layers, names, *args):
    r = types.SimpleNamespace(**dict(zip(names, args)))
    units = Units(8 * layers, r)
    valid, keep, low, low_t, wide_t = r.valid, r.keep, r.low, r.low_t, r.wide_t
    hb, ga, gz, grad, gy1, gx = r.hb, r.ga, r.gz, r.grad, r.gy1, r.gx
    gp = gz.at[:, : sz.inner]
    decay, enter, prefix, mine = r.decay, r.enter, r.prefix, r.mine
    small, held = r.small, r.held
    natural = r.natural
    last = layers - 1
    half = sz.hidden // 2
    zs = (ga.at[:, :768], r.z1)
    drive = r.drive
    homes = dict(gate_w=r.gate_hbm, out_w=r.out_hbm, up_w=r.up_hbm, down_w=r.down_hbm)
    homes.update(u=r.u_save, a=r.a_save, b=r.b_save, zc=r.zc_save, states=r.states_save)
    homes.update(y1=r.y1_save, v=r.v_save, p=r.p_save, gb=r.gb_save, stream=r.stream_save)
    keys = types.SimpleNamespace(**{name: name for name in homes})
    index_of = {name: i for i, name in enumerate(homes)}
    loads, saves = {}, {}

    def load(layer, name):
        copy = pltpu.make_async_copy(
            homes[name].at[layer], getattr(r, name), r.load_sems.at[index_of[name]]
        )
        copy.start()
        loads[name] = copy

    def need(*wanted):
        for name in wanted:
            if name in loads:
                loads.pop(name).wait()

    def save(layer, name, ref=None):
        if layer < last:
            src = getattr(r, name) if ref is None else ref
            copy = pltpu.make_async_copy(
                src, homes[name].at[layer], r.save_sems.at[index_of[name]]
            )
            copy.start()
            saves[name] = copy

    def settled(*which):
        for name in which:
            if name in saves:
                saves.pop(name).wait()

    def over(count, one):
        def each(i, carry):
            one(i)
            return carry

        lax.fori_loop(0, count, each, 0)

    act_load = pltpu.make_async_copy(r.activations, hb.at[:, : sz.width], r.in_sems.at[0])
    cot_load = pltpu.make_async_copy(r.cotangent, wide_t, r.in_sems.at[1])
    len_load = pltpu.make_async_copy(r.lengths, r.lens, r.in_sems.at[2])
    len_load.start()
    act_load.start()
    load(0, keys.gate_w)
    units.greet()
    mine[...] = jnp.zeros_like(mine)
    small[0] = jnp.zeros((8, SMALL), F32)
    len_load.wait()
    fill_masks(r.lens, valid, keep, sz, True)

    def to_steps(src, put):
        def cast(i):
            at = tile(i, 64)
            for k in range(sz.width // LANES):
                natural[k, at, :] = src[at, k * LANES : (k + 1) * LANES].astype(F32)

        over(sz.rows // 64, cast)

        def gather(j):
            for k in range(sz.width // LANES):
                parts = [
                    natural[k, strided(s * sz.span + j, sz.steps), :] for s in range(sz.micro)
                ]
                put(tile(j, sz.group), slice(k * LANES, (k + 1) * LANES), jnp.concatenate(parts, axis=0))

        over(sz.steps, gather)

    def from_steps(src, dst, sem):
        def scatter(j):
            for k in range(sz.width // LANES):
                value = src[tile(j, sz.group), k * LANES : (k + 1) * LANES]
                for s in range(sz.micro):
                    natural[k, strided(s * sz.span + j, sz.steps), :] = value[s * 8 : s * 8 + 8]

        over(sz.steps, scatter)
        copies = []
        for k in range(sz.width // LANES):
            lanes = slice(k * LANES, (k + 1) * LANES)
            copies.append(pltpu.make_async_copy(natural.at[k], dst.at[:, lanes], sem.at[k]))
            copies[-1].start()
        return copies

    act_load.wait()

    def put_gx(at, lanes, value):
        gx[at, lanes] = value

    to_steps(hb.at[:, : sz.width], put_gx)

    parts = [slice(part * half, (part + 1) * half) for part in range(2)]

    def exchange_start(way, layer, part):
        lanes = parts[part]
        slots = r.slots.at[way, layer]
        me = lax.axis_index("section")
        copies = []
        for hop in range(1, sz.sections):
            copies.append(
                pltpu.make_async_remote_copy(
                    src_ref=mine.at[:, lanes],
                    dst_ref=slots.at[me, :, lanes],
                    send_sem=r.pair_send.at[way, layer, part, hop - 1],
                    recv_sem=r.pair_recv.at[way, layer, part, hop - 1],
                    device_id={"section": lax.rem(me + hop, sz.sections)},
                    device_id_type=MESH,
                )
            )
        for copy in copies:
            copy.start()
        slots[me, :, lanes] = mine[:, lanes]
        return slots, copies

    sent = {}

    def sends_settled(part):
        for copy in sent.pop(part, ()):
            copy.wait_send()

    def exchange_end(slots, copies, reverse, part):
        for copy in copies:
            copy.wait_recv()
        sent[part] = copies
        part_enter(slots, prefix, enter, sz, reverse, parts[part])

    def in_turn(count, dots, rest, after=None, third=None):
        over(sz.rows // 256, lambda i: dots(0, i))
        for n in range(count):

            def both(i):
                if n + 1 < count:
                    dots(n + 1, i)
                if third is not None and n > 0:
                    third(n - 1, i)
                rest(n, i)

            over(sz.rows // 256, both)
            if after is not None:
                after(n)

    def keep_cotangent():
        cot_load.wait()

        def put_low(at, lanes, value):
            low[at, lanes] = value.astype(BF16)

        to_steps(wide_t, put_low)
        low_t[...] = low[...].T

    def forward(layer):
        stream = r.stream if layer > 0 else gx
        settled(keys.u)
        norm_rows(stream, r.mix_gain.at[layer : layer + 1], r.u, sz.rows, 128)
        save(layer, keys.u)
        if layer == 0:
            save(layer, keys.stream, gx)
        need(keys.gate_w)
        if layer == 0:
            for name in (keys.out_w, keys.up_w, keys.down_w):
                load(0, name)
            cot_load.start()
        settled(keys.a, keys.b, keys.zc)
        hw = 256
        bias = r.gate_bias

        def gate_dots(n, i):
            rows = tile(i, 256)
            for part in range(3):
                cols = slice(part * sz.hidden + n * hw, part * sz.hidden + (n + 1) * hw)
                zs[n % 2][rows, part * hw : (part + 1) * hw] = (
                    jnp.dot(r.u[rows, :], r.gate_w[:, cols], preferred_element_type=F32)
                    + bias[layer : layer + 1, cols]
                )

        def gate_rest(n, i):
            for chunk in range(4):
                at = pl.ds(pl.multiple_of(i * 256 + chunk * 64, 64), 64)
                vm, km = valid[at, :], keep[at, :]
                for lane in range(hw // LANES):
                    zf, zi, zc = (
                        zs[n % 2][at, part * hw + lane * LANES : part * hw + (lane + 1) * LANES]
                        for part in range(3)
                    )
                    cols = slice(n * hw + lane * LANES, n * hw + (lane + 1) * LANES)
                    a, b = odds(zf, zi)
                    fp, ip, _ = gate_weights(a, b)
                    decay[at, cols] = fp * km
                    drive[at, cols] = ip * zc * vm
                    r.a[at, cols] = a
                    r.b[at, cols] = b
                    r.zc[at, cols] = zc
                    r.forget[...] += jnp.sum((fp * vm).reshape(8, 8, LANES), axis=0)

        flights = []

        def gate_after(n):
            if n % 2 == 0:
                return
            lanes = parts[n // 2]

            def totals(j, pair):
                at = tile(j, sz.group)
                d = decay[at, lanes]
                return pair[0] * d, pair[1] * d + drive[at, lanes]

            one = jnp.ones((sz.group, half), F32)
            pair = steps_of(sz.steps, 2, totals, (one, jnp.zeros_like(one)))
            r.chunk_p[:, lanes] = pair[0]
            r.chunk_t[:, lanes] = pair[1]
            sends_settled(n // 2)
            part_totals(r.chunk_p, r.chunk_t, sz, False, prefix, mine, lanes)
            if layer == 0 and n == 1:
                units.greeted()
            flights.append(exchange_start(0, layer, n // 2))

        r.forget[...] = jnp.zeros_like(r.forget)
        in_turn(sz.hidden // hw, gate_dots, gate_rest, gate_after)
        small[0, layer * 4 : layer * 4 + 1, sz.hidden : sz.hidden + LANES] = jnp.sum(
            r.forget[...], axis=0, keepdims=True
        )
        for name in (keys.a, keys.b, keys.zc):
            save(layer, name)
        if layer < last:
            load(layer + 1, keys.gate_w)
        settled(keys.states, keys.y1, keys.v, keys.p, keys.gb, keys.stream)
        states = r.states
        for part, lanes in enumerate(parts):
            exchange_end(*flights[part], False, part)
            states[0 : sz.group, lanes] = enter[:, lanes]

            def walk(j, h):
                at = tile(j, sz.group)
                h = decay[at, lanes] * h + drive[at, lanes]
                states[tile(j + 1, sz.group), lanes] = h
                hb[at, lanes] = h.astype(BF16)
                return h

            steps_of(sz.steps, 4, walk, enter[:, lanes])
            if (layer, part) == (0, 0):
                keep_cotangent()
        save(layer, keys.states)
        need(keys.out_w)

        def out_tile(n):
            cols = tile(n, 256)
            r.y1[:, cols] = stream[:, cols] + jnp.dot(
                hb[...], r.out_w[:, cols], preferred_element_type=F32
            )

        over(sz.width // 256, out_tile)
        save(layer, keys.y1)
        if layer < last:
            load(layer + 1, keys.out_w)
        norm_rows(r.y1, r.mlp_gain.at[layer : layer + 1], r.v, sz.rows, 128)
        save(layer, keys.v)
        need(keys.up_w)

        tiles = range(8) if layer < last else (0, 2, 4, 6, 1, 3, 5, 7)

        def up_dots(n, i):
            rows, cols = tile(i, 256), slice(tiles[n] * 256, (tiles[n] + 1) * 256)
            zs[n % 2][rows, :256] = jnp.dot(
                r.v[rows, :], r.up_w[:, cols], preferred_element_type=F32
            )

        def up_rest(n, i):
            cols = slice(tiles[n] * 256, (tiles[n] + 1) * 256)
            for chunk in range(4):
                at = pl.ds(pl.multiple_of(i * 256 + chunk * 64, 64), 64)
                p = zs[n % 2][at, :256]
                r.p[at, cols] = p
                r.gb[at, cols] = (p * normal_below(p)).astype(BF16)

        def down_part(n, i):
            s, unit = tiles[n] // 2, tiles[n] % 2
            value = jnp.dot(
                low_t[tile(i, 256), :],
                r.gb[:, tiles[n] * 256 : (tiles[n] + 1) * 256],
                preferred_element_type=F32,
            )
            for k in range(4):
                for h in range(2):
                    at = spot(unit, h, (s // 2, k % 2, k // 2, i))
                    held[unit, s % 2, h, at] = value[
                        k * 64 : k * 64 + 64, h * 128 : h * 128 + 128
                    ]

        def up_after(n):
            units.passed(0.3)
            if n == 4:
                units.produced(0, 0)

        if layer < last:
            in_turn(8, up_dots, up_rest)
        else:
            in_turn(8, up_dots, up_rest, up_after, down_part)
            over(2, lambda i: down_part(7, i))
            units.produced(0.2, 1)
        save(layer, keys.p)
        save(layer, keys.gb)
        if layer < last:
            load(layer + 1, keys.up_w)
        need(keys.down_w)
        out = r.stream if layer < last else gy1

        def down_tile(n):
            cols = tile(n, 256)
            out[:, cols] = r.y1[:, cols] + jnp.dot(
                r.gb[...], r.down_w[:, cols], preferred_element_type=F32
            )

        over(sz.width // 256, down_tile)
        if layer < last:
            load(layer + 1, keys.down_w)

    def down_grad(layer, unit):
        for k in range(2):
            units.room(unit + k)

        def one(n):
            s, t = n // 2, n % 2
            value = jnp.dot(low_t[...], r.gb[:, tile(n, 256)], preferred_element_type=F32)
            for b in range(8):
                for h in range(2):
                    at = [place(unit + k, h, s // 2, b % 2, b // 2) for k in range(2)]
                    held[(unit + t) % HELD, s % 2, h, jnp.where(t == 0, *at)] = value[
                        b * 64 : b * 64 + 64, h * 128 : h * 128 + 128
                    ]

        over(8, one)
        units.produced(2, unit, unit + 1)

    def cast(src, dst):
        def one(i):
            at = tile(i, 64)
            dst[at, :] = src[at, :].astype(dst.dtype)

        over(sz.rows // 64, one)

    def turn_rows(src, dst, n):
        at = tile(n, 128)
        dst[:, at] = src[at, :].T

    def contract(left, weight, dst, count, beside=None):
        def one(n):
            if beside is not None:
                beside(n)
            cols = tile(n, 256)
            dst[:, cols] = lax.dot_general(
                left[...], weight[cols, :], (((1,), (1,)), ((), ())), preferred_element_type=F32
            )

        over(count // 256, one)

    def up_grad(layer, unit):
        for k in range(2):
            units.room(unit + k)

        def one(b):
            value = jnp.dot(wide_t[...], gp[:, tile(b, 256)], preferred_element_type=F32)
            for s in range(4):
                for h in range(2):
                    for t in range(2):
                        at = place(unit + t, h, s // 2, b % 2, b // 2)
                        held[(unit + t) % HELD, s % 2, h, at] = value[
                            s * 128 + h * 64 : s * 128 + h * 64 + 64, t * 128 : t * 128 + 128
                        ]

        over(8, one)
        units.produced(2.5, unit, unit + 1)

    def out_grad(layer, unit):
        def cast_state(i):
            hb[tile(i, sz.group), :] = r.states[tile(i + 1, sz.group), :].astype(BF16)

        if layer < last:
            over(sz.steps, cast_state)
        units.room(unit)

        def one(s):
            value = jnp.dot(r.go_t[...], hb[:, tile(s, 256)], preferred_element_type=F32)
            for b in range(8):
                for h in range(2):
                    at = place(unit, h, s // 2, b % 2, b // 2)
                    held[unit % HELD, s % 2, h, at] = value[
                        b * 64 : b * 64 + 64, h * 128 : h * 128 + 128
                    ]

        over(4, one)
        units.produced(1.2, unit)

    def backward(layer, unit):
        late = layer < last

        def freed(*which):
            if layer > 0:
                for name in which:
                    load(layer - 1, name)

        if not late:
            freed(keys.gb)
        need(keys.down_w, keys.p, keys.v)

        def act_dots(n, i):
            rows = tile(i, 256)
            zs[n % 2][rows, :256] = lax.dot_general(
                low[rows, :],
                r.down_w[n * 256 : (n + 1) * 256, :],
                (((1,), (1,)), ((), ())),
                preferred_element_type=F32,
            )

        def act_rest(n, i):
            if n < 2:
                turn_rows(r.v, wide_t, 2 * n + i)
            elif n < 4 and late:
                turn_rows(low, low_t, 2 * (n - 2) + i)
            cols = slice(n * 256, (n + 1) * 256)
            for chunk in range(4):
                at = pl.ds(pl.multiple_of(i * 256 + chunk * 64, 64), 64)
                p = r.p[at, cols]
                slope = normal_below(p) + ROOT_TAU * p * jnp.exp(-0.5 * p * p)
                gp[at, cols] = (zs[n % 2][at, :256] * slope).astype(BF16)

        in_turn(sz.inner // 256, act_dots, act_rest, lambda n: units.passed(0.6))
        freed(keys.down_w, keys.p, keys.v)
        if not late:
            up_grad(layer, unit + 2)
        need(keys.up_w, keys.y1, keys.u)

        def turn_u(n):
            for k in range(2):
                turn_rows(r.u, r.u_t, 2 * n + k)

        contract(gp, r.up_w, grad, sz.width, turn_u)
        freed(keys.u)
        freed(keys.up_w)
        units.passed(1.5)
        norm_back(r.y1, r.mlp_gain.at[layer : layer + 1], grad, gx, gy1, r.mlp_sum, sz.rows, 64, low)
        freed(keys.y1)
        need(keys.states)
        units.passed(2)
        need(keys.out_w, keys.a, keys.b)
        contract(low, r.out_w, ga, sz.hidden, lambda n: turn_rows(low, r.go_t, n))
        freed(keys.out_w)
        units.passed(1)
        if not late:
            out_grad(layer, unit + 4)
        flights = []
        for part, lanes in enumerate(parts):

            def totals(j, pair):
                at = tile(j, sz.group)
                if layer < last:
                    mask = jnp.concatenate([keep[at, :]] * (half // LANES), axis=1)
                    d = gate_weights(r.a[at, lanes], r.b[at, lanes])[0] * mask
                    decay[at, lanes] = d
                else:
                    d = decay[at, lanes]
                return pair[0] * d, d * (ga[at, lanes] + pair[1])

            one = jnp.ones((sz.group, half), F32)
            pair = steps_of(sz.steps, 2, totals, (one, jnp.zeros_like(one)), reverse=True)
            r.chunk_p[:, lanes] = pair[0]
            r.chunk_t[:, lanes] = pair[1]
            sends_settled(part)
            part_totals(r.chunk_p, r.chunk_t, sz, True, prefix, mine, lanes)
            flights.append(exchange_start(1, layer, part))
            carried = [units.expect(link, 16384) for link in ("core", "x", "x")]
            units.passed(0.8)
        need(keys.zc)
        if late:
            need(keys.gb)
            down_grad(layer, unit)
            up_grad(layer, unit + 2)
            out_grad(layer, unit + 4)
        unit += 5
        units.now = max(units.now, *carried)

        def gate_lanes(n):
            wide = 2 * LANES
            lanes = tile(n, wide)

            def walk(j, kept):
                m, bf, bi, bc = kept
                at = tile(j, sz.group)
                d = decay[at, lanes]
                q = ga[at, lanes] + m
                a, b, zc = r.a[at, lanes], r.b[at, lanes], r.zc[at, lanes]
                vm = jnp.concatenate([valid[at, :]] * 2, axis=1)
                km = jnp.concatenate([keep[at, :]] * 2, axis=1)
                fp, ip, inv = gate_weights(a, b)
                gf = q * (r.states[at, lanes] * km - zc * vm)
                parts = (
                    (gf * (a * inv) * fp).astype(BF16),
                    (-gf * (b * inv) * ip).astype(BF16),
                    (q * vm * ip).astype(BF16),
                )
                for part, value in enumerate(parts):
                    gz[at, pl.ds(pl.multiple_of(part * sz.hidden + n * wide, wide), wide)] = value
                return (d * q,) + tuple(
                    a + value.astype(F32) for a, value in zip((bf, bi, bc), parts)
                )

            zero = jnp.zeros((sz.group, wide), F32)
            _, *sums = steps_of(
                sz.steps, 4, walk, (enter[:, lanes], zero, zero, zero), reverse=True
            )
            for part, total in enumerate(sums):
                small[0, layer * 4 + part : layer * 4 + part + 1, lanes] = jnp.sum(
                    total, axis=0, keepdims=True
                )

        turns = sz.hidden // LANES // 4
        for part in range(2):
            exchange_end(*flights[part], True, part)
            over(turns, lambda n: gate_lanes(n + part * turns))
            units.passed(1.8)
        freed(keys.a, keys.b, keys.zc, keys.states)
        for k in range(2):
            units.room(unit + k)

        def gate_grad(b):
            cols = pl.ds(pl.multiple_of(b * 384, 128), 256)
            value = jnp.dot(r.u_t[...], gz[:, cols], preferred_element_type=F32)
            for s in range(4):
                for h in range(2):
                    for t in range(2):
                        at = place(unit + t, h, s // 2, b % 2, b // 2)
                        held[(unit + t) % HELD, s % 2, h, at] = value[
                            s * 128 + h * 64 : s * 128 + h * 64 + 64, t * 128 : t * 128 + 128
                        ]

        over(8, gate_grad)
        units.produced(3, unit, unit + 1)
        unit += 2
        units.room(unit)

        def gate_rest(z):
            right = jnp.concatenate(
                [
                    gz[:, pl.ds(pl.multiple_of((2 * z + y) * 384 + 256, 128), 128)]
                    for y in range(2)
                ],
                axis=1,
            )
            value = jnp.dot(r.u_t[...], right, preferred_element_type=F32)
            for s in range(4):
                for h in range(2):
                    for y in range(2):
                        at = place(unit, h, s // 2, y, z)
                        held[unit % HELD, s % 2, h, at] = value[
                            s * 128 + h * 64 : s * 128 + h * 64 + 64, y * 128 : y * 128 + 128
                        ]

        over(4, gate_rest)
        units.produced(1.5, unit)
        unit += 1
        need(keys.gate_w, keys.stream)
        contract(gz, r.gate_w, grad, sz.width)
        freed(keys.gate_w)
        units.passed(2.5)
        norm_back(r.stream, r.mix_gain.at[layer : layer + 1], grad, gy1, gx, r.mix_sum, sz.rows, 64, low)
        freed(keys.stream)
        row = slice(layer * 4 + 3, layer * 4 + 4)
        small[0, row, : sz.width] = jnp.sum(r.mix_sum[...], axis=0, keepdims=True)
        small[0, row, sz.width : 2 * sz.width] = jnp.sum(r.mlp_sum[...], axis=0, keepdims=True)
        units.passed(1.5)

    forward(0)
    for layer in range(1, layers):
        forward(layer)
    out_copies = from_steps(gy1, r.layer_out, r.out_sems)
    cast(low, gx)
    units.passed(2)
    for index, layer in enumerate(reversed(range(layers))):
        backward(layer, 8 * index)
    def small_done():
        total = small[STAGES]
        count = jnp.int32(0)
        for s in range(r.lens.shape[0]):
            for d in range(r.lens.shape[1]):
                count = count + r.lens[s, d]
        scale = 1.0 / (count.astype(F32) * sz.hidden)
        for layer in range(layers):
            one = slice(layer, layer + 1)
            for part in range(3):
                r.bias_out[one, part * sz.hidden : (part + 1) * sz.hidden] = total[
                    layer * 4 + part : layer * 4 + part + 1, : sz.hidden
                ]
            row = slice(layer * 4 + 3, layer * 4 + 4)
            r.mix_out[one, :] = total[row, : sz.width]
            r.mlp_out[one, :] = total[row, sz.width : 2 * sz.width]
            lanes = total[layer * 4 : layer * 4 + 1, sz.hidden : sz.hidden + LANES]
            r.forget_out[one, :] = jnp.sum(lanes, axis=1, keepdims=True) * scale + jnp.zeros(
                (1, LANES), F32
            )
        pairs = (
            (r.bias_out, r.gate_bias_grad),
            (r.mix_out, r.mix_gain_grad),
            (r.mlp_out, r.mlp_gain_grad),
            (r.forget_out, r.forget_mean),
        )
        for k, (src, dst) in enumerate(pairs):
            copy = pltpu.make_async_copy(src, dst, r.small_out_sems.at[k])
            copy.start()
            units.leaving.append(copy)

    units.small_done = small_done
    units.small_start()
    for copy in out_copies:
        copy.wait()
    out_copies = from_steps(gx, r.input_grad, r.out_sems)
    units.passed(1)
    units.drain()
    for copy in out_copies:
        copy.wait()
    for part in range(2):
        sends_settled(part)


def run_whole_step(sz, layers, named):
    lengths = named["lengths"]
    rows, d, h, f = sz.rows, sz.width, sz.hidden, sz.inner
    vm = lambda *dims, kind=F32: pltpu.VMEM(dims, kind)
    sems = pltpu.SemaphoreType
    spec = dict(gate_bias=VMEM, mix_gain=VMEM, mlp_gain=VMEM)
    outputs = dict(
        layer_out=(shape(rows, d), ANY),
        input_grad=(shape(rows, d), ANY),
        gate_weight_grad=(shape(layers, 128, 384), ANY),
        gate_bias_grad=(shape(layers, 3 * h), ANY),
        out_weight_grad=(shape(layers, 64, 256), ANY),
        up_weight_grad=(shape(layers, 128, 256), ANY),
        down_weight_grad=(shape(layers, 64, 512), ANY),
        mix_gain_grad=(shape(layers, d), ANY),
        mlp_gain_grad=(shape(layers, d), ANY),
        forget_mean=(shape(layers, LANES), ANY),
    )
    results = len(outputs)
    kept = dict(
        u=((rows, d), BF16),
        a=((rows, h), F32),
        b=((rows, h), F32),
        zc=((rows, h), F32),
        states=((rows + sz.group, h), F32),
        y1=((rows, d), F32),
        v=((rows, d), BF16),
        p=((rows, f), F32),
        gb=((rows, f), BF16),
        stream=((rows, d), F32),
    )
    scratch = {}
    for name, (dims, kind) in kept.items():
        outputs[name + "_save"] = (shape(layers - 1, *dims, kind=kind), ANY)
        scratch[name] = vm(*dims, kind=kind)
    scratch.update(
        gate_w=vm(d, 3 * h, kind=BF16),
        out_w=vm(h, d, kind=BF16),
        up_w=vm(d, f, kind=BF16),
        down_w=vm(f, d, kind=BF16),
        valid=vm(rows, LANES),
        keep=vm(rows, LANES),
        gx=vm(rows, d),
        low=vm(rows, d, kind=BF16),
        low_t=vm(d, rows, kind=BF16),
        wide_t=vm(d, rows, kind=BF16),
        u_t=vm(d, rows, kind=BF16),
        go_t=vm(d, rows, kind=BF16),
        hb=vm(rows, h, kind=BF16),
        z1=vm(rows, 768),
        drive=vm(rows, h),
        forget=vm(8, LANES),
        ga=vm(rows, h),
        gz=vm(rows, 3 * h, kind=BF16),
        grad=vm(rows, d),
        gy1=vm(rows, d),
        decay=vm(rows, h),
        chunk_p=vm(sz.group, h),
        chunk_t=vm(sz.group, h),
        prefix=vm(2, sz.group, h),
        enter=vm(sz.group, h),
        mine=vm(8, h),
        slots=vm(2, layers, sz.sections, 8, h),
        mlp_sum=vm(8, d),
        mix_sum=vm(8, d),
        held=vm(HELD, 2, 2, 16, BLOCK, LANES),
        small=vm(STAGES + 1, 8, SMALL),
        small_arrived=vm(STAGES, 8, SMALL),
        in_sems=sems.DMA((3,)),
        bias_out=vm(layers, 3 * h),
        mix_out=vm(layers, d),
        mlp_out=vm(layers, d),
        forget_out=vm(layers, LANES),
        small_out_sems=sems.DMA((4,)),
        result_sems=sems.DMA((8 * layers, 2)),
        lens=pltpu.SMEM(lengths.shape, jnp.int32),
        out_sems=sems.DMA((d // LANES,)),
        natural=vm(d // LANES, rows, LANES),
        load_sems=sems.DMA((len(kept) + 4,)),
        save_sems=sems.DMA((len(kept) + 4,)),
        pair_send=sems.DMA((2, layers, 2, sz.sections - 1)),
        pair_recv=sems.DMA((2, layers, 2, sz.sections - 1)),
        send_sems=sems.DMA((SENDS, 2 * STAGES - 1)),
        recv_sems=sems.DMA((max(RINGS), 2 * STAGES - 1)),
        credits=sems.REGULAR((2 * STAGES - 1, 8 * layers)),
        small_send=sems.DMA((STAGES,)),
        small_recv=sems.DMA((STAGES,)),
    )
    for stage in range(STAGES):
        scratch[f"arrived{stage}"] = vm(RINGS[stage], 2, 16 >> stage, BLOCK, LANES)
    names = list(named) + list(outputs) + list(scratch)
    out = pl.pallas_call(
        functools.partial(whole_step, sz, layers, names),
        out_shape=tuple(value for value, _ in outputs.values()),
        in_specs=[spec.get(name, ANY) for name in named],
        out_specs=[place_of for _, place_of in outputs.values()],
        scratch_shapes=list(scratch.values()),
        compiler_params=pltpu.CompilerParams(
            collective_id=4, has_side_effects=True, vmem_limit_bytes=LIMIT
        ),
        name="whole_step",
    )(*named.values())
    return out[:results]


def deliver_kernel(count, *refs):
    sources, targets, held = refs[:count], refs[count : 2 * count], refs[2 * count : 3 * count - 1]
    sems = refs[3 * count - 1]
    arrivals = [
        pltpu.make_async_copy(sources[i], held[i], sems.at[0, i]) for i in range(count - 1)
    ]
    departures = [
        pltpu.make_async_copy(held[i], targets[i], sems.at[1, i]) for i in range(count - 1)
    ]
    for copy in arrivals:
        copy.start()
    for layer in range(targets[-1].shape[0]):
        targets[-1][layer] = sources[-1][layer, 0]
    for arrival, departure in zip(arrivals, departures):
        arrival.wait()
        departure.start()
    for copy in departures:
        copy.wait()


def deliver(values):
    count = len(values)
    scalars = pl.BlockSpec(memory_space=pltpu.SMEM)
    shapes = [shape(*value.shape) for value in values[:-1]] + [shape(values[-1].shape[0])]
    return pl.pallas_call(
        functools.partial(deliver_kernel, count),
        out_shape=tuple(shapes),
        in_specs=[ANY] * (count - 1) + [scalars],
        out_specs=[ANY] * (count - 1) + [scalars],
        scratch_shapes=[pltpu.VMEM(value.shape, F32) for value in values[:-1]]
        + [pltpu.SemaphoreType.DMA((2, count - 1))],
        compiler_params=pltpu.CompilerParams(vmem_limit_bytes=LIMIT),
        name="deliver",
    )(*values)


def mask_kernel(sizes, lens, valid, keep):
    fill_masks(lens, valid, keep, sizes)


def body(
    activations,
    cotangent,
    lengths,
    gate_weight,
    gate_bias,
    out_weight,
    up_weight,
    down_weight,
    mix_gain,
    mlp_gain,
):
    micro, span, width = activations.shape
    layers = gate_weight.shape[0]
    sz = Sizes(
        micro, span, width, out_weight.shape[1], up_weight.shape[2], lax.axis_size("section")
    )

    blocks = (width // 4, 3 * sz.hidden // 8, width // 8, sz.inner // 4, sz.hidden // 4)
    axes = (lax.axis_size("section"), lax.axis_size("batch"))
    if axes == (4, 8) and blocks == (128, 384, 64, 512, 256):
        out = run_whole_step(
            sz,
            layers,
            dict(
                activations=activations.reshape(sz.rows, width),
                cotangent=cotangent.reshape(sz.rows, width),
                lengths=lengths.T,
                gate_bias=gate_bias,
                mix_gain=mix_gain,
                mlp_gain=mlp_gain,
                gate_hbm=gate_weight,
                out_hbm=out_weight,
                up_hbm=up_weight,
                down_hbm=down_weight,
            ),
        )
        stream_out, input_grad, gate_g, bias_g, out_g, up_g, down_g, *rest = deliver(out)
        return (
            stream_out.reshape(activations.shape),
            input_grad.reshape(activations.shape),
            gate_g,
            bias_g,
            out_g.transpose(0, 2, 1),
            up_g,
            down_g.transpose(0, 2, 1),
            *rest,
        )

    def arranged(value):
        value = value.astype(F32).reshape(micro, CHUNKS, sz.steps, width)
        return value.transpose(2, 0, 1, 3).reshape(sz.rows, width)

    def restored(value):
        value = value.reshape(sz.steps, micro, CHUNKS, width).transpose(1, 2, 0, 3)
        return value.reshape(micro, span, width)

    masks = pl.pallas_call(
        functools.partial(mask_kernel, sz),
        out_shape=(shape(sz.rows, LANES), shape(sz.rows, LANES)),
        in_specs=[pl.BlockSpec(memory_space=pltpu.SMEM)],
        out_specs=[VMEM] * 2,
        name="masks",
    )(lengths)
    weights = (gate_weight, out_weight, up_weight, down_weight)
    stream = arranged(activations)
    streams, saved, forgets = [], [], []
    for layer in range(layers):
        streams.append(stream)
        stream, *kept, forget, pairs = run_forward(
            sz,
            layer,
            stream,
            masks,
            gate_bias[layer : layer + 1],
            mix_gain[layer : layer + 1],
            mlp_gain[layer : layer + 1],
            weights,
        )
        saved.append((*kept, pairs))
        forgets.append(forget)
    layer_out = restored(stream)
    gx = arranged(cotangent)
    true_count = jnp.sum(lengths).astype(F32)
    forgets = [jnp.sum(forget) for forget in forgets]
    sums, small = [None] * layers, [None] * layers
    for layer in reversed(range(layers)):
        gx, gate_g, out_g, up_g, down_g, bias_g, mix_g, mlp_g = run_backward(
            sz,
            layer,
            gx,
            streams[layer],
            masks,
            mix_gain[layer : layer + 1],
            mlp_gain[layer : layer + 1],
            saved[layer],
            weights,
        )
        sums[layer] = (gate_g, out_g.T, up_g, down_g.T)
        small[layer] = tuple(jnp.sum(part, axis=0) for part in (bias_g, mix_g, mlp_g))
    input_grad = restored(gx)
    stacked = tuple(jnp.stack(parts) for parts in zip(*sums))
    partial_sums = lax.psum_scatter(stacked, "section", scatter_dimension=1, tiled=True)
    large = lax.psum_scatter(partial_sums, "batch", scatter_dimension=2, tiled=True)
    bias_grad, mix_grad, mlp_grad = (jnp.stack(parts) for parts in zip(*small))
    bias_grad, mix_grad, mlp_grad, forget = lax.psum(
        (bias_grad, mix_grad, mlp_grad, jnp.stack(forgets)), ("section", "batch")
    )
    forget_mean = forget / (true_count * sz.hidden)
    return (
        layer_out,
        input_grad,
        large[0],
        bias_grad,
        large[1],
        large[2],
        large[3],
        mix_grad,
        mlp_grad,
        forget_mean,
    )


def solution(mesh):
    stream = P("batch", "section", None)
    block = P(None, "section", "batch")
    return jax.shard_map(
        body,
        mesh=mesh,
        in_specs=(stream, stream) + (P(),) * 8,
        out_specs=(stream, stream, block, P(), block, block, block, P(), P(), P()),
        check_vma=False,
    )
```

```python
import functools
import types

import jax
import jax.numpy as jnp
from jax import lax
from jax.experimental import pallas as pl
from jax.experimental.pallas import tpu as pltpu
from jax.sharding import PartitionSpec as P

epsilon = 1e-06
MESH = pl.DeviceIdType.MESH
F32, BF16 = jnp.float32, jnp.bfloat16
CHUNKS = 8
LANES = 128
ROOT_HALF = 0.7071067811865476
ROOT_TAU = 0.3989422804014327


def tile(index, size):
    return pl.ds(pl.multiple_of(index * size, size), size)


def inverse(value):
    r = pltpu.reciprocal(value, approx=True)
    return r * (2.0 - value * r)


def normal_below(p):
    return 0.5 + 0.5 * lax.erf(p * ROOT_HALF)


def steps_of(count, unroll, one, start, reverse=False):
    def turn(i, carry):
        for k in range(unroll):
            at = i * unroll + k
            carry = one(count - 1 - at if reverse else at, carry)
        return carry

    return lax.fori_loop(0, count // unroll, turn, start)


def odds(zf, zi):
    return jnp.exp(jnp.minimum(-zf, 86.0)), jnp.exp(jnp.minimum(-zi, 86.0))


def gate_weights(a, b):
    inv = inverse(2.0 + a + b)
    return (1.0 + b) * inv, (1.0 + a) * inv, inv


def greet_section(sections):
    me = lax.axis_index("section")
    barrier = pltpu.get_barrier_semaphore()
    for hop in range(1, sections):
        pl.semaphore_signal(
            barrier, inc=1, device_id={"section": lax.rem(me + hop, sections)}, device_id_type=MESH
        )
    pl.semaphore_wait(barrier, sections - 1)


def exchange(mine, slots, send_sems, recv_sems, sections):
    me = lax.axis_index("section")
    copies = []
    for hop in range(1, sections):
        copies.append(
            pltpu.make_async_remote_copy(
                src_ref=mine,
                dst_ref=slots.at[me],
                send_sem=send_sems.at[hop - 1],
                recv_sem=recv_sems.at[hop - 1],
                device_id={"section": lax.rem(me + hop, sections)},
                device_id_type=MESH,
            )
        )
    for copy in copies:
        copy.start()
    slots[me] = mine[...]
    for copy in copies:
        copy.wait()


def norm_rows(stream, gain, low, rows, step):
    def one(i, carry):
        at = tile(i, step)
        x = stream[at, :]
        r = lax.rsqrt(jnp.mean(x * x, axis=-1, keepdims=True) + epsilon)
        low[at, :] = (x * r * gain[...]).astype(BF16)
        return carry

    lax.fori_loop(0, rows // step, one, 0)


def norm_back(stream, gain, grad, through, out, gain_sum, rows, step, low=None):
    width = stream.shape[1]

    def one(i, total):
        at = tile(i, step)
        x = stream[at, :]
        r = lax.rsqrt(jnp.mean(x * x, axis=-1, keepdims=True) + epsilon)
        n = x * r
        g = grad[at, :]
        a = g * gain[...]
        value = through[at, :] + r * (a - n * jnp.mean(a * n, axis=-1, keepdims=True))
        out[at, :] = value
        if low is not None:
            low[at, :] = value.astype(BF16)
        return total + jnp.sum((g * n).reshape(step // 8, 8, width), axis=0)

    gain_sum[...] = lax.fori_loop(0, rows // step, one, jnp.zeros((8, width), F32))


def fill_masks(lens, valid, keep, sizes, turned=False):
    section = lax.axis_index("section")
    group = lax.axis_index("batch")
    starts, totals = [], []
    for s in range(sizes.micro):
        total, begin = 0, []
        for d in range(lens.shape[0 if turned else 1]):
            row = group * sizes.micro + s
            length = lens[d, row] if turned else lens[row, d]
            begin.append(jnp.where(length > 0, total, -1))
            total = total + length
        starts.append(begin)
        totals.append(total)
    chunk_place = lax.broadcasted_iota(jnp.int32, (8, LANES), 0) * sizes.steps

    def one(j, carry):
        for s in range(sizes.micro):
            place = section * sizes.span + j + chunk_place
            true = place < totals[s]
            first = place == starts[s][0]
            for begin in starts[s][1:]:
                first = first | (place == begin)
            at = pl.ds(pl.multiple_of(j * sizes.group + s * 8, 8), 8)
            valid[at, :] = jnp.where(true, 1.0, 0.0)
            keep[at, :] = jnp.where(true & jnp.logical_not(first), 1.0, 0.0)
        return carry

    lax.fori_loop(0, sizes.steps, one, 0)


def scan_totals(first, second, sizes, reverse, prefix, chunk, mine):
    for s in range(sizes.micro):
        p = jnp.ones((1, sizes.hidden), F32)
        t = jnp.zeros((1, sizes.hidden), F32)
        for c in reversed(range(CHUNKS)) if reverse else range(CHUNKS):
            at = s * 8 + c
            prefix[0, at : at + 1, :] = p
            prefix[1, at : at + 1, :] = t
            pc = first[at : at + 1, :]
            t = pc * t + second[at : at + 1, :]
            p = p * pc
        mine[s : s + 1, :] = p
        mine[sizes.micro + s : sizes.micro + s + 1, :] = t


def scan_enter(slots, prefix, enter, sizes, reverse):
    me = lax.axis_index("section")
    for s in range(sizes.micro):
        a = jnp.zeros((1, sizes.hidden), F32)
        order = range(sizes.sections - 1, 0, -1) if reverse else range(sizes.sections - 1)
        for k in order:
            reached = k > me if reverse else k < me
            pk = slots[k, s : s + 1, :]
            tk = slots[k, sizes.micro + s : sizes.micro + s + 1, :]
            a = jnp.where(reached, pk * a + tk, a)
        at = slice(s * 8, s * 8 + 8)
        enter[at, :] = prefix[0, at, :] * a + prefix[1, at, :]


def part_totals(first, second, sizes, reverse, prefix, mine, lanes):
    for s in range(sizes.micro):
        p = jnp.ones((1, lanes.stop - lanes.start), F32)
        t = jnp.zeros_like(p)
        for c in reversed(range(CHUNKS)) if reverse else range(CHUNKS):
            at = s * 8 + c
            prefix[0, at : at + 1, lanes] = p
            prefix[1, at : at + 1, lanes] = t
            pc = first[at : at + 1, lanes]
            t = pc * t + second[at : at + 1, lanes]
            p = p * pc
        mine[s : s + 1, lanes] = p
        mine[sizes.micro + s : sizes.micro + s + 1, lanes] = t


def part_enter(slots, prefix, enter, sizes, reverse, lanes):
    me = lax.axis_index("section")
    for s in range(sizes.micro):
        a = jnp.zeros((1, lanes.stop - lanes.start), F32)
        order = range(sizes.sections - 1, 0, -1) if reverse else range(sizes.sections - 1)
        for k in order:
            reached = k > me if reverse else k < me
            pk = slots[k, s : s + 1, lanes]
            tk = slots[k, sizes.micro + s : sizes.micro + s + 1, lanes]
            a = jnp.where(reached, pk * a + tk, a)
        at = slice(s * 8, s * 8 + 8)
        enter[at, lanes] = prefix[0, at, lanes] * a + prefix[1, at, lanes]


class Sizes:
    def __init__(self, micro, span, width, hidden, inner, sections):
        self.micro, self.span, self.width = micro, span, width
        self.hidden, self.inner, self.sections = hidden, inner, sections
        self.rows = micro * span
        self.steps = span // CHUNKS
        self.group = micro * CHUNKS


def forward_kernel(
    sizes,
    layer,
    stream,
    valid,
    keep,
    bias,
    mix_gain,
    mlp_gain,
    gate_hbm,
    out_hbm,
    up_hbm,
    down_hbm,
    next_stream,
    u,
    sf_out,
    si_out,
    zc_out,
    states,
    y1,
    v,
    p_out,
    gb,
    forget,
    pair_slots,
    gate_w,
    out_w,
    up_w,
    down_w,
    z,
    decay,
    drive,
    hb,
    chunk_p,
    chunk_t,
    prefix,
    enter,
    mine,
    weight_sems,
    send_sems,
    recv_sems,
):
    sz = sizes
    loads = [
        pltpu.make_async_copy(src.at[layer], dst, weight_sems.at[i])
        for i, (src, dst) in enumerate(
            ((gate_hbm, gate_w), (out_hbm, out_w), (up_hbm, up_w), (down_hbm, down_w))
        )
    ]
    for load in loads:
        load.start()
    greet_section(sz.sections)
    mine[...] = jnp.zeros_like(mine)
    norm_rows(stream, mix_gain, u, sz.rows, 64)
    loads[0].wait()
    forget[...] = jnp.zeros_like(forget)
    hw = 256

    def gate_tile(n, carry):
        for part in range(3):
            cols = pl.ds(pl.multiple_of(part * sz.hidden + n * hw, hw), hw)
            z[:, part * hw : (part + 1) * hw] = (
                jnp.dot(u[...], gate_w[:, cols], preferred_element_type=F32) + bias[:, cols]
            )

        def one(i, inner):
            at = tile(i, 64)
            for lane in range(hw // LANES):
                src = lambda part: z[
                    at, part * hw + lane * LANES : part * hw + (lane + 1) * LANES
                ]
                dst = pl.ds(pl.multiple_of(n * hw + lane * LANES, LANES), LANES)
                a = jnp.exp(jnp.minimum(-src(0), 86.0))
                b = jnp.exp(jnp.minimum(-src(1), 86.0))
                zc = src(2)
                fp, ip, _ = gate_weights(a, b)
                vm = valid[at, :]
                decay[at, dst] = fp * keep[at, :]
                drive[at, dst] = ip * zc * vm
                sf_out[at, dst] = a
                si_out[at, dst] = b
                zc_out[at, dst] = zc
                forget[...] += jnp.sum((fp * vm).reshape(8, 8, LANES), axis=0)
            return inner

        lax.fori_loop(0, sz.rows // 64, one, 0)
        return carry

    lax.fori_loop(0, sz.hidden // hw, gate_tile, 0)
    half = sz.hidden // 2
    for part in range(2):
        lanes = slice(part * half, (part + 1) * half)

        def totals(j, pair):
            at = tile(j, sz.group)
            d = decay[at, lanes]
            return pair[0] * d, pair[1] * d + drive[at, lanes]

        one = jnp.ones((sz.group, half), F32)
        pair = steps_of(sz.steps, 4, totals, (one, jnp.zeros_like(one)))
        chunk_p[:, lanes] = pair[0]
        chunk_t[:, lanes] = pair[1]
    scan_totals(chunk_p, chunk_t, sz, False, prefix, None, mine)
    exchange(mine, pair_slots, send_sems, recv_sems, sz.sections)
    scan_enter(pair_slots, prefix, enter, sz, False)
    states[0 : sz.group, :] = enter[...]
    for part in range(2):
        lanes = slice(part * half, (part + 1) * half)

        def walk(j, h):
            at = tile(j, sz.group)
            h = decay[at, lanes] * h + drive[at, lanes]
            states[tile(j + 1, sz.group), lanes] = h
            hb[at, lanes] = h.astype(BF16)
            return h

        steps_of(sz.steps, 4, walk, enter[:, lanes])
    loads[1].wait()

    def out_tile(n, carry):
        cols = tile(n, 256)
        y1[:, cols] = stream[:, cols] + jnp.dot(
            hb[...], out_w[:, cols], preferred_element_type=F32
        )
        return carry

    lax.fori_loop(0, sz.width // 256, out_tile, 0)
    norm_rows(y1, mlp_gain, v, sz.rows, 64)
    loads[2].wait()

    def up_tile(n, carry):
        cols = tile(n, 256)
        p_out[:, cols] = jnp.dot(v[...], up_w[:, cols], preferred_element_type=F32)

        def one(i, inner):
            at = tile(i, 64)
            p = p_out[at, cols]
            gb[at, cols] = (p * normal_below(p)).astype(BF16)
            return inner

        lax.fori_loop(0, sz.rows // 64, one, 0)
        return carry

    lax.fori_loop(0, sz.inner // 256, up_tile, 0)
    loads[3].wait()

    def down_tile(n, carry):
        cols = tile(n, 256)
        next_stream[:, cols] = y1[:, cols] + jnp.dot(
            gb[...], down_w[:, cols], preferred_element_type=F32
        )
        return carry

    lax.fori_loop(0, sz.width // 256, down_tile, 0)


def backward_kernel(
    sizes,
    layer,
    gx,
    stream,
    valid,
    keep,
    mix_gain,
    mlp_gain,
    u,
    sf_in,
    si_in,
    zc_in,
    states,
    y1,
    v,
    p_in,
    gb,
    pair_slots,
    gate_hbm,
    out_hbm,
    up_hbm,
    down_hbm,
    next_gx,
    gate_grad,
    out_grad,
    up_grad,
    down_grad,
    bias_sum,
    mix_sum,
    mlp_sum,
    gate_w,
    out_w,
    up_w,
    down_w,
    low,
    low_t,
    wide_t,
    hb,
    ga,
    gp,
    gz,
    grad,
    gy1,
    decay,
    chunk_p,
    chunk_t,
    prefix,
    enter,
    mine,
    slots,
    weight_sems,
    send_sems,
    recv_sems,
):
    sz = sizes
    loads = [
        pltpu.make_async_copy(src.at[layer], dst, weight_sems.at[i])
        for i, (src, dst) in enumerate(
            ((gate_hbm, gate_w), (out_hbm, out_w), (up_hbm, up_w), (down_hbm, down_w))
        )
    ]
    for load in reversed(loads):
        load.start()
    greet_section(sz.sections)
    mine[...] = jnp.zeros_like(mine)

    def cast(i, carry):
        at = tile(i, 64)
        low[at, :] = gx[at, :].astype(BF16)
        return carry

    lax.fori_loop(0, sz.rows // 64, cast, 0)
    low_t[...] = low[...].T

    def weight_grad(left_t, right, dst, step):
        def one(n, carry):
            cols = tile(n, step)
            dst[:, cols] = jnp.dot(left_t[...], right[:, cols], preferred_element_type=F32)
            return carry

        lax.fori_loop(0, right.shape[1] // step, one, 0)

    weight_grad(low_t, gb, down_grad, 256)
    loads[3].wait()

    def act_tile(n, carry):
        cols = tile(n, 256)
        ga[:, :256] = lax.dot_general(
            low[...], down_w[cols, :], (((1,), (1,)), ((), ())), preferred_element_type=F32
        )

        def one(i, inner):
            at = tile(i, 64)
            p = p_in[at, cols]
            slope = normal_below(p) + ROOT_TAU * p * jnp.exp(-0.5 * p * p)
            gp[at, cols] = (ga[at, :256] * slope).astype(BF16)
            return inner

        lax.fori_loop(0, sz.rows // 64, one, 0)
        return carry

    lax.fori_loop(0, sz.inner // 256, act_tile, 0)
    wide_t[...] = v[...].T
    weight_grad(wide_t, gp, up_grad, 256)
    loads[2].wait()

    def contract(left, weight, dst, step):
        def one(n, carry):
            cols = tile(n, step)
            dst[:, cols] = lax.dot_general(
                left[...], weight[cols, :], (((1,), (1,)), ((), ())), preferred_element_type=F32
            )
            return carry

        lax.fori_loop(0, weight.shape[0] // step, one, 0)

    contract(gp, up_w, grad, 256)
    norm_back(y1, mlp_gain, grad, gx, gy1, mlp_sum, sz.rows, 64)

    def cast_more(i, carry):
        at = tile(i, 64)
        low[at, :] = gy1[at, :].astype(BF16)
        return carry

    lax.fori_loop(0, sz.rows // 64, cast_more, 0)

    def cast_state(i, carry):
        hb[tile(i, sz.group), :] = states[tile(i + 1, sz.group), :].astype(BF16)
        return carry

    lax.fori_loop(0, sz.steps, cast_state, 0)
    low_t[...] = low[...].T
    weight_grad(low_t, hb, out_grad, 256)
    loads[1].wait()
    contract(low, out_w, ga, 256)
    half = sz.hidden // 2
    for part in range(2):
        lanes = slice(part * half, (part + 1) * half)

        def totals(i, pair):
            at = tile(sz.steps - 1 - i, sz.group)
            mask = jnp.concatenate([keep[at, :]] * (half // LANES), axis=1)
            d = gate_weights(sf_in[at, lanes], si_in[at, lanes])[0] * mask
            decay[at, lanes] = d
            return pair[0] * d, d * (ga[at, lanes] + pair[1])

        pair = lax.fori_loop(
            0,
            sz.steps,
            totals,
            (jnp.ones((sz.group, half), F32), jnp.zeros((sz.group, half), F32)),
        )
        chunk_p[:, lanes] = pair[0]
        chunk_t[:, lanes] = pair[1]
    scan_totals(chunk_p, chunk_t, sz, True, prefix, None, mine)
    exchange(mine, slots, send_sems, recv_sems, sz.sections)
    scan_enter(slots, prefix, enter, sz, True)

    def gate_lane(n, carry):
        lanes = tile(n, LANES)

        def walk(i, kept):
            m, bf, bi, bc = kept
            j = sz.steps - 1 - i
            at = tile(j, sz.group)
            d = decay[at, lanes]
            q = ga[at, lanes] + m
            a = sf_in[at, lanes]
            b = si_in[at, lanes]
            zc = zc_in[at, lanes]
            vm = valid[at, :]
            fp, ip, inv = gate_weights(a, b)
            gf = q * (states[at, lanes] * keep[at, :] - zc * vm)
            gzf = (gf * (a * inv) * fp).astype(BF16)
            gzi = (-gf * (b * inv) * ip).astype(BF16)
            gzc = (q * vm * ip).astype(BF16)
            gz[at, lanes] = gzf
            gz[at, pl.ds(pl.multiple_of(sz.hidden + n * LANES, LANES), LANES)] = gzi
            gz[at, pl.ds(pl.multiple_of(2 * sz.hidden + n * LANES, LANES), LANES)] = gzc
            return (
                d * q,
                bf + gzf.astype(F32),
                bi + gzi.astype(F32),
                bc + gzc.astype(F32),
            )

        zero = jnp.zeros((sz.group, LANES), F32)
        _, bf, bi, bc = lax.fori_loop(0, sz.steps, walk, (enter[:, lanes], zero, zero, zero))
        for part, total in enumerate((bf, bi, bc)):
            where = pl.ds(pl.multiple_of(part * sz.hidden + n * LANES, LANES), LANES)
            bias_sum[:, where] = jnp.sum(total.reshape(sz.group // 8, 8, LANES), axis=0)
        return carry

    lax.fori_loop(0, sz.hidden // LANES, gate_lane, 0)
    wide_t[...] = u[...].T
    weight_grad(wide_t, gz, gate_grad, 256)
    loads[0].wait()
    contract(gz, gate_w, grad, 256)
    norm_back(stream, mix_gain, grad, gy1, next_gx, mix_sum, sz.rows, 64)


VMEM = pl.BlockSpec(memory_space=pltpu.VMEM)
ANY = pl.BlockSpec(memory_space=pl.ANY)
LIMIT = 63 * 2**20


def shape(*dims, kind=F32):
    return jax.ShapeDtypeStruct(dims, kind)


def exchange_scratch(sz):
    return [
        pltpu.SemaphoreType.DMA((4,)),
        pltpu.SemaphoreType.DMA((sz.sections - 1,)),
        pltpu.SemaphoreType.DMA((sz.sections - 1,)),
    ]


def weight_scratch(sz):
    return [
        pltpu.VMEM((sz.width, 3 * sz.hidden), BF16),
        pltpu.VMEM((sz.hidden, sz.width), BF16),
        pltpu.VMEM((sz.width, sz.inner), BF16),
        pltpu.VMEM((sz.inner, sz.width), BF16),
    ]


def scan_scratch(sz):
    return [
        pltpu.VMEM((sz.group, sz.hidden), F32),
        pltpu.VMEM((sz.group, sz.hidden), F32),
        pltpu.VMEM((2, sz.group, sz.hidden), F32),
        pltpu.VMEM((sz.group, sz.hidden), F32),
        pltpu.VMEM((8, sz.hidden), F32),
    ]


def run_forward(sz, layer, stream, masks, bias, mix_gain, mlp_gain, weights):
    r, d, h, f = sz.rows, sz.width, sz.hidden, sz.inner
    return pl.pallas_call(
        functools.partial(forward_kernel, sz, layer),
        out_shape=(
            shape(r, d),
            shape(r, d, kind=BF16),
            shape(r, h),
            shape(r, h),
            shape(r, h),
            shape(r + sz.group, h),
            shape(r, d),
            shape(r, d, kind=BF16),
            shape(r, f),
            shape(r, f, kind=BF16),
            shape(8, LANES),
            shape(sz.sections, 8, h),
        ),
        in_specs=[VMEM] * 6 + [ANY] * 4,
        out_specs=[VMEM] * 12,
        scratch_shapes=weight_scratch(sz)
        + [
            pltpu.VMEM((r, 3 * 256), F32),
            pltpu.VMEM((r, h), F32),
            pltpu.VMEM((r, h), F32),
            pltpu.VMEM((r, h), BF16),
        ]
        + scan_scratch(sz)
        + exchange_scratch(sz),
        compiler_params=pltpu.CompilerParams(
            collective_id=layer, has_side_effects=True, vmem_limit_bytes=LIMIT
        ),
        name=f"forward_{layer}",
    )(stream, *masks, bias, mix_gain, mlp_gain, *weights)


def run_backward(sz, layer, gx, stream, masks, mix_gain, mlp_gain, saved, weights):
    r, d, h, f = sz.rows, sz.width, sz.hidden, sz.inner
    return pl.pallas_call(
        functools.partial(backward_kernel, sz, layer),
        out_shape=(
            shape(r, d),
            shape(d, 3 * h),
            shape(d, h),
            shape(d, f),
            shape(d, f),
            shape(8, 3 * h),
            shape(8, d),
            shape(8, d),
        ),
        in_specs=[VMEM] * 16 + [ANY] * 4,
        out_specs=[VMEM] * 8,
        scratch_shapes=weight_scratch(sz)
        + [
            pltpu.VMEM((r, d), BF16),
            pltpu.VMEM((d, r), BF16),
            pltpu.VMEM((d, r), BF16),
            pltpu.VMEM((r, h), BF16),
            pltpu.VMEM((r, h), F32),
            pltpu.VMEM((r, f), BF16),
            pltpu.VMEM((r, 3 * h), BF16),
            pltpu.VMEM((r, d), F32),
            pltpu.VMEM((r, d), F32),
            pltpu.VMEM((r, h), F32),
        ]
        + scan_scratch(sz)
        + [pltpu.VMEM((sz.sections, 8, h), F32)]
        + exchange_scratch(sz),
        compiler_params=pltpu.CompilerParams(
            collective_id=2 + layer, has_side_effects=True, vmem_limit_bytes=LIMIT
        ),
        name=f"backward_{layer}",
    )(gx, stream, *masks, mix_gain, mlp_gain, *saved, *weights)


BLOCK = 64
HELD = 3
RINGS = (4, 5, 5, 16, 16)
SENDS = 16
STAGES = 5
WINDOW = 4
DELAY = 1.5
SMALL = 1280


EVEN = ((0, 2, 1, 3), (1, 2, 0, 3))
ORDERS = [EVEN] * 16


class Units:
    def __init__(self, count, refs):
        self.count = count
        self.__dict__.update(vars(refs))
        self.arrived = [getattr(refs, f"arrived{stage}") for stage in range(STAGES)]
        section, batch = lax.axis_index("section"), lax.axis_index("batch")
        core, x = section % 2, section // 2
        y, za, zb = batch % 2, (batch // 2) % 2, batch // 4
        self.core = core
        self.where = (x, y, za, zb)
        self.partner = {
            "core": {"section": section + 1 - 2 * core},
            "x": {"section": section + 2 - 4 * x},
            "y": {"batch": batch + 1 - 2 * y},
            "za": {"batch": batch + 2 - 4 * za},
            "zb": {"batch": batch + 4 - 8 * zb},
        }
        self.now = 0.0
        self.links = ("core", "x", "y", "z")
        self.free_at = dict.fromkeys(self.links, 0.0)
        self.flying = dict.fromkeys(self.links, 0)
        self.queues = {link: [] for link in self.links}
        self.ready = {}
        self.summed = set()
        self.copies = {}
        self.small_left = None
        self.leaving = []

    def greet(self):
        section = lax.axis_index("section")
        others = [self.partner["y"], self.partner["za"], self.partner["zb"]]
        others += [{"section": lax.rem(section + hop, 4)} for hop in range(1, 4)]
        for other in others:
            pl.semaphore_signal(
                pltpu.get_barrier_semaphore(), inc=1, device_id=other, device_id_type=MESH
            )

    def greeted(self):
        pl.semaphore_wait(pltpu.get_barrier_semaphore(), 6)

    def name(self, unit, stage, half):
        return "core" if stage == 0 else ("x", "y", "za", "zb")[ORDERS[unit][half][stage - 1]]

    def link(self, unit, stage, half):
        name = self.name(unit, stage, half)
        return "z" if name[0] == "z" else name

    def bit(self, unit, stage, half):
        return self.where[ORDERS[unit][half][stage - 1]]

    def arrival(self, unit, stage, half):
        return self.arrived[stage].at[unit % RINGS[stage], half]

    def copy(self, unit, stage, half):
        at = 2 * stage + half
        if stage == 0:
            src = self.held.at[unit % HELD, 1 - self.core, half]
        else:
            count = 16 >> stage
            src = self.arrival(unit, stage - 1, half)
            src = src.at[pl.ds((1 - self.bit(unit, stage, half)) * count, count)]
        return pltpu.make_async_remote_copy(
            src_ref=src,
            dst_ref=self.arrival(unit, stage, half),
            send_sem=self.send_sems.at[unit % SENDS, at],
            recv_sem=self.recv_sems.at[unit % RINGS[stage], at],
            device_id=self.partner[self.name(unit, stage, half)],
            device_id_type=MESH,
        )

    def has_place(self, unit, stage, half):
        before = unit - RINGS[stage]
        return before < 0 or (before, min(stage + 1, STAGES - 1), half) in self.summed

    def credit(self, unit, stage, half):
        after = unit + RINGS[stage]
        if after < self.count:
            pl.semaphore_signal(
                self.credits.at[2 * stage + half, after],
                inc=1,
                device_id=self.partner[self.name(after, stage, half)],
                device_id_type=MESH,
            )

    def pump(self):
        for link, queue in self.queues.items():
            while self.flying[link] < WINDOW:
                key = next((key for key in queue if self.has_place(*key)), None)
                if key is None:
                    break
                queue.remove(key)
                self.flying[link] += 1
                unit, stage, half = key
                if unit >= RINGS[stage]:
                    pl.semaphore_wait(self.credits.at[2 * stage + half, unit], 1)
                self.copies[key] = self.copy(*key)
                self.copies[key].start()
                self.ready[key] = self.expect(link, (16 >> stage) * BLOCK * LANES * 4)

    def expect(self, link, size):
        rate = 250e3 if link == "core" else 45e3
        self.free_at[link] = max(self.now, self.free_at[link]) + size / rate
        return self.free_at[link] + DELAY

    def push(self, unit, stage, half):
        self.queues[self.link(unit, stage, half)].append((unit, stage, half))
        self.pump()

    def produced(self, us, *which):
        self.now += us
        for unit in which:
            for half in range(2):
                self.push(unit, 0, half)
        self.passed(0)

    def add(self, dst, src, count):
        turn = min(count, 4)

        def one(i, carry):
            for k in range(turn):
                dst[i * turn + k] += src[i * turn + k]
            return carry

        if count == turn:
            one(0, 0)
        else:
            lax.fori_loop(0, count // turn, one, 0)

    def step(self, unit, stage, half):
        key = (unit, stage, half)
        del self.ready[key]
        self.copies[key].wait_recv()
        here = self.arrival(unit, stage, half)
        if stage == 0:
            self.add(here, self.held.at[unit % HELD, self.core, half], 16)
        else:
            count = 16 >> stage
            before = self.arrival(unit, stage - 1, half)
            self.add(here, before.at[pl.ds(self.bit(unit, stage, half) * count, count)], count)
            self.copies.pop(key).wait_send()
        self.summed.add(key)
        self.flying[self.link(unit, stage, half)] -= 1
        self.now += 0.25
        if stage > 0:
            self.credit(unit, stage - 1, half)
        if stage < STAGES - 1:
            self.push(unit, stage + 1, half)
        else:
            self.finish(unit, half, here.at[0])
            self.credit(unit, stage, half)
        self.pump()

    def finish(self, unit, half, block):
        layer, k = self.count // 8 - 1 - unit // 8, unit % 8
        if k < 2 or k == 4:
            ref, at = (self.down_weight_grad, k) if k < 2 else (self.out_weight_grad, 0)
            to = ref.at[layer, :, at * 256 + half * 128 : at * 256 + half * 128 + 128]
        else:
            ref, at = (self.up_weight_grad, k - 2) if k < 4 else (self.gate_weight_grad, k - 5)
            rows = slice(half * BLOCK, half * BLOCK + BLOCK)
            to = ref.at[layer, rows, at * LANES : at * LANES + LANES]
        copy = pltpu.make_async_copy(block, to, self.result_sems.at[unit, half])
        copy.start()
        self.leaving.append(copy)

    def small_copy(self, stage):
        name = ("core", "x", "y", "za", "zb")[stage]
        return pltpu.make_async_remote_copy(
            src_ref=self.small.at[stage],
            dst_ref=self.small_arrived.at[stage],
            send_sem=self.small_send.at[stage],
            recv_sem=self.small_recv.at[stage],
            device_id=self.partner[name],
            device_id_type=MESH,
        )

    def small_start(self):
        self.small_left = 0
        self.small_copies = [self.small_copy(0)]
        self.small_copies[0].start()
        self.small_ready = self.now + 3.0

    def small_step(self):
        stage = self.small_left
        self.small_copies[stage].wait_recv()
        self.small[stage + 1] = self.small[stage] + self.small_arrived[stage]
        self.small_left += 1
        if self.small_left < STAGES:
            self.small_copies.append(self.small_copy(self.small_left))
            self.small_copies[-1].start()
            self.small_ready = self.now + 3.0
        else:
            for copy in self.small_copies:
                copy.wait_send()
            self.small_done()

    def open(self, unit, stage, half):
        halves = range(2) if stage == 0 else (half,)
        before = unit - RING
        return (
            before < 0
            or stage == STAGES - 1
            or all((before, stage + 1, h) in self.consumed for h in halves)
        )

    def next(self):
        best = min(self.ready.items(), key=lambda item: (item[1], item[0]), default=None)
        small = self.small_left is not None and self.small_left < STAGES
        if small and (best is None or self.small_ready <= best[1]):
            return self.small_ready, None
        return (best[1], best[0]) if best else None

    def take(self, item):
        self.now = max(self.now, item[0])
        if item[1] is None:
            self.small_step()
        else:
            self.step(*item[1])

    def passed(self, us):
        self.now += us
        while (item := self.next()) and item[0] <= self.now:
            self.take(item)

    def room(self, unit):
        for half in range(2):
            before = (unit - HELD, 0, half)
            while unit >= HELD and before not in self.summed:
                self.take(self.next())
            if before in self.copies:
                self.copies.pop(before).wait_send()

    def drain(self):
        while item := self.next():
            self.take(item)
        for key in list(self.copies):
            self.copies.pop(key).wait_send()
        for copy in self.leaving:
            copy.wait()


def place(unit, half, x, y, z):
    return spot(unit, half, (x, y, z % 2, z // 2))


def spot(unit, half, where):
    order = ORDERS[unit][half]
    return where[order[0]] * 8 + where[order[1]] * 4 + where[order[2]] * 2 + where[order[3]]


def strided(start, steps):
    return pl.ds(start, CHUNKS, stride=steps)


def whole_step(sz, layers, names, *args):
    r = types.SimpleNamespace(**dict(zip(names, args)))
    units = Units(8 * layers, r)
    valid, keep, low, low_t, wide_t = r.valid, r.keep, r.low, r.low_t, r.wide_t
    hb, ga, gz, grad, gy1, gx = r.hb, r.ga, r.gz, r.grad, r.gy1, r.gx
    gp = gz.at[:, : sz.inner]
    decay, enter, prefix, mine = r.decay, r.enter, r.prefix, r.mine
    small, held = r.small, r.held
    natural = r.natural
    last = layers - 1
    half = sz.hidden // 2
    zs = (ga.at[:, :768], r.z1)
    drive = r.drive
    homes = dict(gate_w=r.gate_hbm, out_w=r.out_hbm, up_w=r.up_hbm, down_w=r.down_hbm)
    homes.update(u=r.u_save, a=r.a_save, b=r.b_save, zc=r.zc_save, states=r.states_save)
    homes.update(y1=r.y1_save, v=r.v_save, p=r.p_save, gb=r.gb_save, stream=r.stream_save)
    keys = types.SimpleNamespace(**{name: name for name in homes})
    index_of = {name: i for i, name in enumerate(homes)}
    loads, saves = {}, {}

    def load(layer, name):
        copy = pltpu.make_async_copy(
            homes[name].at[layer], getattr(r, name), r.load_sems.at[index_of[name]]
        )
        copy.start()
        loads[name] = copy

    def need(*wanted):
        for name in wanted:
            if name in loads:
                loads.pop(name).wait()

    def save(layer, name, ref=None):
        if layer < last:
            src = getattr(r, name) if ref is None else ref
            copy = pltpu.make_async_copy(
                src, homes[name].at[layer], r.save_sems.at[index_of[name]]
            )
            copy.start()
            saves[name] = copy

    def settled(*which):
        for name in which:
            if name in saves:
                saves.pop(name).wait()

    def over(count, one):
        def each(i, carry):
            one(i)
            return carry

        lax.fori_loop(0, count, each, 0)

    act_load = pltpu.make_async_copy(r.activations, hb.at[:, : sz.width], r.in_sems.at[0])
    cot_load = pltpu.make_async_copy(r.cotangent, wide_t, r.in_sems.at[1])
    len_load = pltpu.make_async_copy(r.lengths, r.lens, r.in_sems.at[2])
    len_load.start()
    act_load.start()
    load(0, keys.gate_w)
    units.greet()
    mine[...] = jnp.zeros_like(mine)
    small[0] = jnp.zeros((8, SMALL), F32)
    len_load.wait()
    fill_masks(r.lens, valid, keep, sz, True)

    def to_steps(src, put):
        def cast(i):
            at = tile(i, 64)
            for k in range(sz.width // LANES):
                natural[k, at, :] = src[at, k * LANES : (k + 1) * LANES].astype(F32)

        over(sz.rows // 64, cast)

        def gather(j):
            for k in range(sz.width // LANES):
                parts = [
                    natural[k, strided(s * sz.span + j, sz.steps), :] for s in range(sz.micro)
                ]
                put(tile(j, sz.group), slice(k * LANES, (k + 1) * LANES), jnp.concatenate(parts, axis=0))

        over(sz.steps, gather)

    def from_steps(src, dst, sem):
        def scatter(j):
            for k in range(sz.width // LANES):
                value = src[tile(j, sz.group), k * LANES : (k + 1) * LANES]
                for s in range(sz.micro):
                    natural[k, strided(s * sz.span + j, sz.steps), :] = value[s * 8 : s * 8 + 8]

        over(sz.steps, scatter)
        copies = []
        for k in range(sz.width // LANES):
            lanes = slice(k * LANES, (k + 1) * LANES)
            copies.append(pltpu.make_async_copy(natural.at[k], dst.at[:, lanes], sem.at[k]))
            copies[-1].start()
        return copies

    act_load.wait()

    def put_gx(at, lanes, value):
        gx[at, lanes] = value

    to_steps(hb.at[:, : sz.width], put_gx)

    parts = [slice(part * half, (part + 1) * half) for part in range(2)]

    def exchange_start(way, layer, part):
        lanes = parts[part]
        slots = r.slots.at[way, layer]
        me = lax.axis_index("section")
        copies = []
        for hop in range(1, sz.sections):
            copies.append(
                pltpu.make_async_remote_copy(
                    src_ref=mine.at[:, lanes],
                    dst_ref=slots.at[me, :, lanes],
                    send_sem=r.pair_send.at[way, layer, part, hop - 1],
                    recv_sem=r.pair_recv.at[way, layer, part, hop - 1],
                    device_id={"section": lax.rem(me + hop, sz.sections)},
                    device_id_type=MESH,
                )
            )
        for copy in copies:
            copy.start()
        slots[me, :, lanes] = mine[:, lanes]
        return slots, copies

    sent = {}

    def sends_settled(part):
        for copy in sent.pop(part, ()):
            copy.wait_send()

    def exchange_end(slots, copies, reverse, part):
        for copy in copies:
            copy.wait_recv()
        sent[part] = copies
        part_enter(slots, prefix, enter, sz, reverse, parts[part])

    def in_turn(count, dots, rest, after=None, third=None):
        over(sz.rows // 256, lambda i: dots(0, i))
        for n in range(count):

            def both(i):
                if n + 1 < count:
                    dots(n + 1, i)
                if third is not None and n > 0:
                    third(n - 1, i)
                rest(n, i)

            over(sz.rows // 256, both)
            if after is not None:
                after(n)

    def keep_cotangent():
        cot_load.wait()

        def put_low(at, lanes, value):
            low[at, lanes] = value.astype(BF16)

        to_steps(wide_t, put_low)
        low_t[...] = low[...].T

    def forward(layer):
        stream = r.stream if layer > 0 else gx
        settled(keys.u)
        norm_rows(stream, r.mix_gain.at[layer : layer + 1], r.u, sz.rows, 128)
        save(layer, keys.u)
        if layer == 0:
            save(layer, keys.stream, gx)
        need(keys.gate_w)
        if layer == 0:
            for name in (keys.out_w, keys.up_w, keys.down_w):
                load(0, name)
            cot_load.start()
        settled(keys.a, keys.b, keys.zc)
        hw = 256
        bias = r.gate_bias

        def gate_dots(n, i):
            rows = tile(i, 256)
            for part in range(3):
                cols = slice(part * sz.hidden + n * hw, part * sz.hidden + (n + 1) * hw)
                zs[n % 2][rows, part * hw : (part + 1) * hw] = (
                    jnp.dot(r.u[rows, :], r.gate_w[:, cols], preferred_element_type=F32)
                    + bias[layer : layer + 1, cols]
                )

        def gate_rest(n, i):
            for chunk in range(4):
                at = pl.ds(pl.multiple_of(i * 256 + chunk * 64, 64), 64)
                vm, km = valid[at, :], keep[at, :]
                for lane in range(hw // LANES):
                    zf, zi, zc = (
                        zs[n % 2][at, part * hw + lane * LANES : part * hw + (lane + 1) * LANES]
                        for part in range(3)
                    )
                    cols = slice(n * hw + lane * LANES, n * hw + (lane + 1) * LANES)
                    a, b = odds(zf, zi)
                    fp, ip, _ = gate_weights(a, b)
                    decay[at, cols] = fp * km
                    drive[at, cols] = ip * zc * vm
                    r.a[at, cols] = a
                    r.b[at, cols] = b
                    r.zc[at, cols] = zc
                    r.forget[...] += jnp.sum((fp * vm).reshape(8, 8, LANES), axis=0)

        flights = []

        def gate_after(n):
            if n % 2 == 0:
                return
            lanes = parts[n // 2]

            def totals(j, pair):
                at = tile(j, sz.group)
                d = decay[at, lanes]
                return pair[0] * d, pair[1] * d + drive[at, lanes]

            one = jnp.ones((sz.group, half), F32)
            pair = steps_of(sz.steps, 2, totals, (one, jnp.zeros_like(one)))
            r.chunk_p[:, lanes] = pair[0]
            r.chunk_t[:, lanes] = pair[1]
            sends_settled(n // 2)
            part_totals(r.chunk_p, r.chunk_t, sz, False, prefix, mine, lanes)
            if layer == 0 and n == 1:
                units.greeted()
            flights.append(exchange_start(0, layer, n // 2))

        r.forget[...] = jnp.zeros_like(r.forget)
        in_turn(sz.hidden // hw, gate_dots, gate_rest, gate_after)
        small[0, layer * 4 : layer * 4 + 1, sz.hidden : sz.hidden + LANES] = jnp.sum(
            r.forget[...], axis=0, keepdims=True
        )
        for name in (keys.a, keys.b, keys.zc):
            save(layer, name)
        if layer < last:
            load(layer + 1, keys.gate_w)
        settled(keys.states, keys.y1, keys.v, keys.p, keys.gb, keys.stream)
        states = r.states
        for part, lanes in enumerate(parts):
            exchange_end(*flights[part], False, part)
            states[0 : sz.group, lanes] = enter[:, lanes]

            def walk(j, h):
                at = tile(j, sz.group)
                h = decay[at, lanes] * h + drive[at, lanes]
                states[tile(j + 1, sz.group), lanes] = h
                hb[at, lanes] = h.astype(BF16)
                return h

            steps_of(sz.steps, 4, walk, enter[:, lanes])
            if (layer, part) == (0, 0):
                keep_cotangent()
        save(layer, keys.states)
        need(keys.out_w)

        r.y1[...] = stream[...] + jnp.dot(hb[...], r.out_w[...], preferred_element_type=F32)
        save(layer, keys.y1)
        if layer < last:
            load(layer + 1, keys.out_w)
        norm_rows(r.y1, r.mlp_gain.at[layer : layer + 1], r.v, sz.rows, 128)
        save(layer, keys.v)
        need(keys.up_w)

        tiles = range(8) if layer < last else (0, 2, 4, 6, 1, 3, 5, 7)

        def up_dots(n, i):
            rows, cols = tile(i, 256), slice(tiles[n] * 256, (tiles[n] + 1) * 256)
            zs[n % 2][rows, :256] = jnp.dot(
                r.v[rows, :], r.up_w[:, cols], preferred_element_type=F32
            )

        def up_rest(n, i):
            cols = slice(tiles[n] * 256, (tiles[n] + 1) * 256)
            for chunk in range(4):
                at = pl.ds(pl.multiple_of(i * 256 + chunk * 64, 64), 64)
                p = zs[n % 2][at, :256]
                r.p[at, cols] = p
                r.gb[at, cols] = (p * normal_below(p)).astype(BF16)

        def down_part(n, i):
            s, unit = tiles[n] // 2, tiles[n] % 2
            value = jnp.dot(
                low_t[tile(i, 256), :],
                r.gb[:, tiles[n] * 256 : (tiles[n] + 1) * 256],
                preferred_element_type=F32,
            )
            for k in range(4):
                for h in range(2):
                    at = spot(unit, h, (s // 2, k % 2, k // 2, i))
                    held[unit, s % 2, h, at] = value[
                        k * 64 : k * 64 + 64, h * 128 : h * 128 + 128
                    ]

        def up_after(n):
            units.passed(0.3)
            if n == 4:
                units.produced(0, 0)

        if layer < last:
            in_turn(8, up_dots, up_rest)
        else:
            in_turn(8, up_dots, up_rest, up_after, down_part)
            over(2, lambda i: down_part(7, i))
            units.produced(0.2, 1)
        save(layer, keys.p)
        save(layer, keys.gb)
        if layer < last:
            load(layer + 1, keys.up_w)
        need(keys.down_w)
        out = r.stream if layer < last else gy1

        out[...] = r.y1[...] + jnp.dot(r.gb[...], r.down_w[...], preferred_element_type=F32)
        if layer < last:
            load(layer + 1, keys.down_w)

    def down_grad(layer, unit):
        for k in range(2):
            units.room(unit + k)

        def one(n):
            s, t = n // 2, n % 2
            value = jnp.dot(low_t[...], r.gb[:, tile(n, 256)], preferred_element_type=F32)
            for b in range(8):
                for h in range(2):
                    at = [place(unit + k, h, s // 2, b % 2, b // 2) for k in range(2)]
                    held[(unit + t) % HELD, s % 2, h, jnp.where(t == 0, *at)] = value[
                        b * 64 : b * 64 + 64, h * 128 : h * 128 + 128
                    ]

        over(8, one)
        units.produced(2, unit, unit + 1)

    def cast(src, dst):
        def one(i):
            at = tile(i, 64)
            dst[at, :] = src[at, :].astype(dst.dtype)

        over(sz.rows // 64, one)

    def turn_rows(src, dst, n):
        at = tile(n, 128)
        dst[:, at] = src[at, :].T

    def contract(left, weight, dst, count, beside=None):
        def one(n):
            if beside is not None:
                beside(n)
            cols = tile(n, 256)
            dst[:, cols] = lax.dot_general(
                left[...], weight[cols, :], (((1,), (1,)), ((), ())), preferred_element_type=F32
            )

        over(count // 256, one)

    def up_grad(layer, unit):
        for k in range(2):
            units.room(unit + k)

        def one(b):
            value = jnp.dot(wide_t[...], gp[:, tile(b, 256)], preferred_element_type=F32)
            for s in range(4):
                for h in range(2):
                    for t in range(2):
                        at = place(unit + t, h, s // 2, b % 2, b // 2)
                        held[(unit + t) % HELD, s % 2, h, at] = value[
                            s * 128 + h * 64 : s * 128 + h * 64 + 64, t * 128 : t * 128 + 128
                        ]

        over(8, one)
        units.produced(2.5, unit, unit + 1)

    def out_grad(layer, unit):
        def cast_state(i):
            hb[tile(i, sz.group), :] = r.states[tile(i + 1, sz.group), :].astype(BF16)

        if layer < last:
            over(sz.steps, cast_state)
        units.room(unit)

        def one(s):
            value = jnp.dot(r.go_t[...], hb[:, tile(s, 256)], preferred_element_type=F32)
            for b in range(8):
                for h in range(2):
                    at = place(unit, h, s // 2, b % 2, b // 2)
                    held[unit % HELD, s % 2, h, at] = value[
                        b * 64 : b * 64 + 64, h * 128 : h * 128 + 128
                    ]

        over(4, one)
        units.produced(1.2, unit)

    def backward(layer, unit):
        late = layer < last

        def freed(*which):
            if layer > 0:
                for name in which:
                    load(layer - 1, name)

        if not late:
            freed(keys.gb)
        need(keys.down_w, keys.p, keys.v)

        def act_dots(n, i):
            rows = tile(i, 256)
            zs[n % 2][rows, :256] = lax.dot_general(
                low[rows, :],
                r.down_w[n * 256 : (n + 1) * 256, :],
                (((1,), (1,)), ((), ())),
                preferred_element_type=F32,
            )

        def act_rest(n, i):
            if n < 2:
                turn_rows(r.v, wide_t, 2 * n + i)
            elif n < 4 and late:
                turn_rows(low, low_t, 2 * (n - 2) + i)
            cols = slice(n * 256, (n + 1) * 256)
            for chunk in range(4):
                at = pl.ds(pl.multiple_of(i * 256 + chunk * 64, 64), 64)
                p = r.p[at, cols]
                slope = normal_below(p) + ROOT_TAU * p * jnp.exp(-0.5 * p * p)
                gp[at, cols] = (zs[n % 2][at, :256] * slope).astype(BF16)

        in_turn(sz.inner // 256, act_dots, act_rest, lambda n: units.passed(0.6))
        freed(keys.down_w, keys.p, keys.v)
        if not late:
            up_grad(layer, unit + 2)
        need(keys.up_w, keys.y1, keys.u)

        def turn_u(n):
            for k in range(2):
                turn_rows(r.u, r.u_t, 2 * n + k)

        contract(gp, r.up_w, grad, sz.width, turn_u)
        freed(keys.u)
        freed(keys.up_w)
        units.passed(1.5)
        norm_back(r.y1, r.mlp_gain.at[layer : layer + 1], grad, gx, gy1, r.mlp_sum, sz.rows, 64, low)
        freed(keys.y1)
        need(keys.states)
        units.passed(2)
        need(keys.out_w, keys.a, keys.b)
        contract(low, r.out_w, ga, sz.hidden, lambda n: turn_rows(low, r.go_t, n))
        freed(keys.out_w)
        units.passed(1)
        if not late:
            out_grad(layer, unit + 4)
        flights = []
        for part, lanes in enumerate(parts):

            def totals(j, pair):
                at = tile(j, sz.group)
                if layer < last:
                    mask = jnp.concatenate([keep[at, :]] * (half // LANES), axis=1)
                    d = gate_weights(r.a[at, lanes], r.b[at, lanes])[0] * mask
                    decay[at, lanes] = d
                else:
                    d = decay[at, lanes]
                return pair[0] * d, d * (ga[at, lanes] + pair[1])

            one = jnp.ones((sz.group, half), F32)
            pair = steps_of(sz.steps, 2, totals, (one, jnp.zeros_like(one)), reverse=True)
            r.chunk_p[:, lanes] = pair[0]
            r.chunk_t[:, lanes] = pair[1]
            sends_settled(part)
            part_totals(r.chunk_p, r.chunk_t, sz, True, prefix, mine, lanes)
            flights.append(exchange_start(1, layer, part))
            carried = [units.expect(link, 16384) for link in ("core", "x", "x")]
            units.passed(0.8)
        need(keys.zc)
        if late:
            need(keys.gb)
            down_grad(layer, unit)
            up_grad(layer, unit + 2)
            out_grad(layer, unit + 4)
        unit += 5
        units.now = max(units.now, *carried)

        def gate_lanes(n):
            wide = 2 * LANES
            lanes = tile(n, wide)

            def walk(j, kept):
                m, bf, bi, bc = kept
                at = tile(j, sz.group)
                d = decay[at, lanes]
                q = ga[at, lanes] + m
                a, b, zc = r.a[at, lanes], r.b[at, lanes], r.zc[at, lanes]
                vm = jnp.concatenate([valid[at, :]] * 2, axis=1)
                km = jnp.concatenate([keep[at, :]] * 2, axis=1)
                fp, ip, inv = gate_weights(a, b)
                gf = q * (r.states[at, lanes] * km - zc * vm)
                parts = (
                    (gf * (a * inv) * fp).astype(BF16),
                    (-gf * (b * inv) * ip).astype(BF16),
                    (q * vm * ip).astype(BF16),
                )
                for part, value in enumerate(parts):
                    gz[at, pl.ds(pl.multiple_of(part * sz.hidden + n * wide, wide), wide)] = value
                return (d * q,) + tuple(
                    a + value.astype(F32) for a, value in zip((bf, bi, bc), parts)
                )

            zero = jnp.zeros((sz.group, wide), F32)
            _, *sums = steps_of(
                sz.steps, 4, walk, (enter[:, lanes], zero, zero, zero), reverse=True
            )
            for part, total in enumerate(sums):
                small[0, layer * 4 + part : layer * 4 + part + 1, lanes] = jnp.sum(
                    total, axis=0, keepdims=True
                )

        turns = sz.hidden // LANES // 4
        for part in range(2):
            exchange_end(*flights[part], True, part)
            over(turns, lambda n: gate_lanes(n + part * turns))
            units.passed(1.8)
        freed(keys.a, keys.b, keys.zc, keys.states)
        for k in range(2):
            units.room(unit + k)

        def gate_grad(b):
            cols = pl.ds(pl.multiple_of(b * 384, 128), 256)
            value = jnp.dot(r.u_t[...], gz[:, cols], preferred_element_type=F32)
            for s in range(4):
                for h in range(2):
                    for t in range(2):
                        at = place(unit + t, h, s // 2, b % 2, b // 2)
                        held[(unit + t) % HELD, s % 2, h, at] = value[
                            s * 128 + h * 64 : s * 128 + h * 64 + 64, t * 128 : t * 128 + 128
                        ]

        over(8, gate_grad)
        units.produced(3, unit, unit + 1)
        unit += 2
        units.room(unit)

        def gate_rest(z):
            right = jnp.concatenate(
                [
                    gz[:, pl.ds(pl.multiple_of((2 * z + y) * 384 + 256, 128), 128)]
                    for y in range(2)
                ],
                axis=1,
            )
            value = jnp.dot(r.u_t[...], right, preferred_element_type=F32)
            for s in range(4):
                for h in range(2):
                    for y in range(2):
                        at = place(unit, h, s // 2, y, z)
                        held[unit % HELD, s % 2, h, at] = value[
                            s * 128 + h * 64 : s * 128 + h * 64 + 64, y * 128 : y * 128 + 128
                        ]

        over(4, gate_rest)
        units.produced(1.5, unit)
        unit += 1
        need(keys.gate_w, keys.stream)
        contract(gz, r.gate_w, grad, sz.width)
        freed(keys.gate_w)
        units.passed(2.5)
        norm_back(r.stream, r.mix_gain.at[layer : layer + 1], grad, gy1, gx, r.mix_sum, sz.rows, 64, low)
        freed(keys.stream)
        row = slice(layer * 4 + 3, layer * 4 + 4)
        small[0, row, : sz.width] = jnp.sum(r.mix_sum[...], axis=0, keepdims=True)
        small[0, row, sz.width : 2 * sz.width] = jnp.sum(r.mlp_sum[...], axis=0, keepdims=True)
        units.passed(1.5)

    forward(0)
    for layer in range(1, layers):
        forward(layer)
    out_copies = from_steps(gy1, r.layer_out, r.out_sems)
    cast(low, gx)
    units.passed(2)
    for index, layer in enumerate(reversed(range(layers))):
        backward(layer, 8 * index)
    def small_done():
        total = small[STAGES]
        count = jnp.int32(0)
        for s in range(r.lens.shape[0]):
            for d in range(r.lens.shape[1]):
                count = count + r.lens[s, d]
        scale = 1.0 / (count.astype(F32) * sz.hidden)
        for layer in range(layers):
            one = slice(layer, layer + 1)
            for part in range(3):
                r.bias_out[one, part * sz.hidden : (part + 1) * sz.hidden] = total[
                    layer * 4 + part : layer * 4 + part + 1, : sz.hidden
                ]
            row = slice(layer * 4 + 3, layer * 4 + 4)
            r.mix_out[one, :] = total[row, : sz.width]
            r.mlp_out[one, :] = total[row, sz.width : 2 * sz.width]
            lanes = total[layer * 4 : layer * 4 + 1, sz.hidden : sz.hidden + LANES]
            r.forget_out[one, :] = jnp.sum(lanes, axis=1, keepdims=True) * scale + jnp.zeros(
                (1, LANES), F32
            )
        pairs = (
            (r.bias_out, r.gate_bias_grad),
            (r.mix_out, r.mix_gain_grad),
            (r.mlp_out, r.mlp_gain_grad),
            (r.forget_out, r.forget_mean),
        )
        for k, (src, dst) in enumerate(pairs):
            copy = pltpu.make_async_copy(src, dst, r.small_out_sems.at[k])
            copy.start()
            units.leaving.append(copy)

    units.small_done = small_done
    units.small_start()
    for copy in out_copies:
        copy.wait()
    out_copies = from_steps(gx, r.input_grad, r.out_sems)
    units.passed(1)
    units.drain()
    for copy in out_copies:
        copy.wait()
    for part in range(2):
        sends_settled(part)


def run_whole_step(sz, layers, named):
    lengths = named["lengths"]
    rows, d, h, f = sz.rows, sz.width, sz.hidden, sz.inner
    vm = lambda *dims, kind=F32: pltpu.VMEM(dims, kind)
    sems = pltpu.SemaphoreType
    spec = dict(gate_bias=VMEM, mix_gain=VMEM, mlp_gain=VMEM)
    outputs = dict(
        layer_out=(shape(rows, d), ANY),
        input_grad=(shape(rows, d), ANY),
        gate_weight_grad=(shape(layers, 128, 384), ANY),
        gate_bias_grad=(shape(layers, 3 * h), ANY),
        out_weight_grad=(shape(layers, 64, 256), ANY),
        up_weight_grad=(shape(layers, 128, 256), ANY),
        down_weight_grad=(shape(layers, 64, 512), ANY),
        mix_gain_grad=(shape(layers, d), ANY),
        mlp_gain_grad=(shape(layers, d), ANY),
        forget_mean=(shape(layers, LANES), ANY),
    )
    results = len(outputs)
    kept = dict(
        u=((rows, d), BF16),
        a=((rows, h), F32),
        b=((rows, h), F32),
        zc=((rows, h), F32),
        states=((rows + sz.group, h), F32),
        y1=((rows, d), F32),
        v=((rows, d), BF16),
        p=((rows, f), F32),
        gb=((rows, f), BF16),
        stream=((rows, d), F32),
    )
    scratch = {}
    for name, (dims, kind) in kept.items():
        outputs[name + "_save"] = (shape(layers - 1, *dims, kind=kind), ANY)
        scratch[name] = vm(*dims, kind=kind)
    scratch.update(
        gate_w=vm(d, 3 * h, kind=BF16),
        out_w=vm(h, d, kind=BF16),
        up_w=vm(d, f, kind=BF16),
        down_w=vm(f, d, kind=BF16),
        valid=vm(rows, LANES),
        keep=vm(rows, LANES),
        gx=vm(rows, d),
        low=vm(rows, d, kind=BF16),
        low_t=vm(d, rows, kind=BF16),
        wide_t=vm(d, rows, kind=BF16),
        u_t=vm(d, rows, kind=BF16),
        go_t=vm(d, rows, kind=BF16),
        hb=vm(rows, h, kind=BF16),
        z1=vm(rows, 768),
        drive=vm(rows, h),
        forget=vm(8, LANES),
        ga=vm(rows, h),
        gz=vm(rows, 3 * h, kind=BF16),
        grad=vm(rows, d),
        gy1=vm(rows, d),
        decay=vm(rows, h),
        chunk_p=vm(sz.group, h),
        chunk_t=vm(sz.group, h),
        prefix=vm(2, sz.group, h),
        enter=vm(sz.group, h),
        mine=vm(8, h),
        slots=vm(2, layers, sz.sections, 8, h),
        mlp_sum=vm(8, d),
        mix_sum=vm(8, d),
        held=vm(HELD, 2, 2, 16, BLOCK, LANES),
        small=vm(STAGES + 1, 8, SMALL),
        small_arrived=vm(STAGES, 8, SMALL),
        in_sems=sems.DMA((3,)),
        bias_out=vm(layers, 3 * h),
        mix_out=vm(layers, d),
        mlp_out=vm(layers, d),
        forget_out=vm(layers, LANES),
        small_out_sems=sems.DMA((4,)),
        result_sems=sems.DMA((8 * layers, 2)),
        lens=pltpu.SMEM(lengths.shape, jnp.int32),
        out_sems=sems.DMA((d // LANES,)),
        natural=vm(d // LANES, rows, LANES),
        load_sems=sems.DMA((len(kept) + 4,)),
        save_sems=sems.DMA((len(kept) + 4,)),
        pair_send=sems.DMA((2, layers, 2, sz.sections - 1)),
        pair_recv=sems.DMA((2, layers, 2, sz.sections - 1)),
        send_sems=sems.DMA((SENDS, 2 * STAGES)),
        recv_sems=sems.DMA((max(RINGS), 2 * STAGES)),
        credits=sems.REGULAR((2 * STAGES, 8 * layers)),
        small_send=sems.DMA((STAGES,)),
        small_recv=sems.DMA((STAGES,)),
    )
    for stage in range(STAGES):
        scratch[f"arrived{stage}"] = vm(RINGS[stage], 2, 16 >> stage, BLOCK, LANES)
    names = list(named) + list(outputs) + list(scratch)
    out = pl.pallas_call(
        functools.partial(whole_step, sz, layers, names),
        out_shape=tuple(value for value, _ in outputs.values()),
        in_specs=[spec.get(name, ANY) for name in named],
        out_specs=[place_of for _, place_of in outputs.values()],
        scratch_shapes=list(scratch.values()),
        compiler_params=pltpu.CompilerParams(
            collective_id=4, has_side_effects=True, vmem_limit_bytes=LIMIT
        ),
        name="whole_step",
    )(*named.values())
    return out[:results]


def deliver_kernel(count, *refs):
    sources, targets, held = refs[:count], refs[count : 2 * count], refs[2 * count : 3 * count - 1]
    sems = refs[3 * count - 1]
    arrivals, departures = [], []
    for i in range(count - 1):
        pieces = 4 if len(held[i].shape) == 2 and held[i].shape[0] >= 256 else 1
        size = held[i].shape[0] // pieces
        for k in range(pieces):
            at, sem = pl.ds(k * size, size), 4 * i + k
            arrivals.append(
                pltpu.make_async_copy(sources[i].at[at], held[i].at[at], sems.at[0, sem])
            )
            departures.append(
                pltpu.make_async_copy(held[i].at[at], targets[i].at[at], sems.at[1, sem])
            )
    for copy in arrivals:
        copy.start()
    for layer in range(targets[-1].shape[0]):
        targets[-1][layer] = sources[-1][layer, 0]
    for arrival, departure in zip(arrivals, departures):
        arrival.wait()
        departure.start()
    for copy in departures:
        copy.wait()


def deliver(values):
    count = len(values)
    scalars = pl.BlockSpec(memory_space=pltpu.SMEM)
    shapes = [shape(*value.shape) for value in values[:-1]] + [shape(values[-1].shape[0])]
    return pl.pallas_call(
        functools.partial(deliver_kernel, count),
        out_shape=tuple(shapes),
        in_specs=[ANY] * (count - 1) + [scalars],
        out_specs=[ANY] * (count - 1) + [scalars],
        scratch_shapes=[pltpu.VMEM(value.shape, F32) for value in values[:-1]]
        + [pltpu.SemaphoreType.DMA((2, 4 * count))],
        compiler_params=pltpu.CompilerParams(vmem_limit_bytes=LIMIT),
        name="deliver",
    )(*values)


def mask_kernel(sizes, lens, valid, keep):
    fill_masks(lens, valid, keep, sizes)


def body(
    activations,
    cotangent,
    lengths,
    gate_weight,
    gate_bias,
    out_weight,
    up_weight,
    down_weight,
    mix_gain,
    mlp_gain,
):
    micro, span, width = activations.shape
    layers = gate_weight.shape[0]
    sz = Sizes(
        micro, span, width, out_weight.shape[1], up_weight.shape[2], lax.axis_size("section")
    )

    blocks = (width // 4, 3 * sz.hidden // 8, width // 8, sz.inner // 4, sz.hidden // 4)
    axes = (lax.axis_size("section"), lax.axis_size("batch"))
    if axes == (4, 8) and blocks == (128, 384, 64, 512, 256):
        out = run_whole_step(
            sz,
            layers,
            dict(
                activations=activations.reshape(sz.rows, width),
                cotangent=cotangent.reshape(sz.rows, width),
                lengths=lengths.T,
                gate_bias=gate_bias,
                mix_gain=mix_gain,
                mlp_gain=mlp_gain,
                gate_hbm=gate_weight,
                out_hbm=out_weight,
                up_hbm=up_weight,
                down_hbm=down_weight,
            ),
        )
        stream_out, input_grad, gate_g, bias_g, out_g, up_g, down_g, *rest = deliver(out)
        return (
            stream_out.reshape(activations.shape),
            input_grad.reshape(activations.shape),
            gate_g,
            bias_g,
            out_g.transpose(0, 2, 1),
            up_g,
            down_g.transpose(0, 2, 1),
            *rest,
        )

    def arranged(value):
        value = value.astype(F32).reshape(micro, CHUNKS, sz.steps, width)
        return value.transpose(2, 0, 1, 3).reshape(sz.rows, width)

    def restored(value):
        value = value.reshape(sz.steps, micro, CHUNKS, width).transpose(1, 2, 0, 3)
        return value.reshape(micro, span, width)

    masks = pl.pallas_call(
        functools.partial(mask_kernel, sz),
        out_shape=(shape(sz.rows, LANES), shape(sz.rows, LANES)),
        in_specs=[pl.BlockSpec(memory_space=pltpu.SMEM)],
        out_specs=[VMEM] * 2,
        name="masks",
    )(lengths)
    weights = (gate_weight, out_weight, up_weight, down_weight)
    stream = arranged(activations)
    streams, saved, forgets = [], [], []
    for layer in range(layers):
        streams.append(stream)
        stream, *kept, forget, pairs = run_forward(
            sz,
            layer,
            stream,
            masks,
            gate_bias[layer : layer + 1],
            mix_gain[layer : layer + 1],
            mlp_gain[layer : layer + 1],
            weights,
        )
        saved.append((*kept, pairs))
        forgets.append(forget)
    layer_out = restored(stream)
    gx = arranged(cotangent)
    true_count = jnp.sum(lengths).astype(F32)
    forgets = [jnp.sum(forget) for forget in forgets]
    sums, small = [None] * layers, [None] * layers
    for layer in reversed(range(layers)):
        gx, gate_g, out_g, up_g, down_g, bias_g, mix_g, mlp_g = run_backward(
            sz,
            layer,
            gx,
            streams[layer],
            masks,
            mix_gain[layer : layer + 1],
            mlp_gain[layer : layer + 1],
            saved[layer],
            weights,
        )
        sums[layer] = (gate_g, out_g.T, up_g, down_g.T)
        small[layer] = tuple(jnp.sum(part, axis=0) for part in (bias_g, mix_g, mlp_g))
    input_grad = restored(gx)
    stacked = tuple(jnp.stack(parts) for parts in zip(*sums))
    partial_sums = lax.psum_scatter(stacked, "section", scatter_dimension=1, tiled=True)
    large = lax.psum_scatter(partial_sums, "batch", scatter_dimension=2, tiled=True)
    bias_grad, mix_grad, mlp_grad = (jnp.stack(parts) for parts in zip(*small))
    bias_grad, mix_grad, mlp_grad, forget = lax.psum(
        (bias_grad, mix_grad, mlp_grad, jnp.stack(forgets)), ("section", "batch")
    )
    forget_mean = forget / (true_count * sz.hidden)
    return (
        layer_out,
        input_grad,
        large[0],
        bias_grad,
        large[1],
        large[2],
        large[3],
        mix_grad,
        mlp_grad,
        forget_mean,
    )


def solution(mesh):
    stream = P("batch", "section", None)
    block = P(None, "section", "batch")
    return jax.shard_map(
        body,
        mesh=mesh,
        in_specs=(stream, stream) + (P(),) * 8,
        out_specs=(stream, stream, block, P(), block, block, block, P(), P(), P()),
        check_vma=False,
    )
```

```python
import functools
import types

import jax
import jax.numpy as jnp
from jax import lax
from jax.experimental import pallas as pl
from jax.experimental.pallas import tpu as pltpu
from jax.sharding import PartitionSpec as P

epsilon = 1e-06
MESH = pl.DeviceIdType.MESH
F32, BF16 = jnp.float32, jnp.bfloat16
CHUNKS = 8
LANES = 128
ROOT_HALF = 0.7071067811865476
ROOT_TAU = 0.3989422804014327


def tile(index, size):
    return pl.ds(pl.multiple_of(index * size, size), size)


def inverse(value):
    r = pltpu.reciprocal(value, approx=True)
    return r * (2.0 - value * r)


def normal_below(p):
    return 0.5 + 0.5 * lax.erf(p * ROOT_HALF)


def steps_of(count, unroll, one, start, reverse=False):
    def turn(i, carry):
        for k in range(unroll):
            at = i * unroll + k
            carry = one(count - 1 - at if reverse else at, carry)
        return carry

    return lax.fori_loop(0, count // unroll, turn, start)


def odds(zf, zi):
    return jnp.exp(jnp.minimum(-zf, 86.0)), jnp.exp(jnp.minimum(-zi, 86.0))


def gate_weights(a, b):
    inv = inverse(2.0 + a + b)
    return (1.0 + b) * inv, (1.0 + a) * inv, inv


def greet_section(sections):
    me = lax.axis_index("section")
    barrier = pltpu.get_barrier_semaphore()
    for hop in range(1, sections):
        pl.semaphore_signal(
            barrier, inc=1, device_id={"section": lax.rem(me + hop, sections)}, device_id_type=MESH
        )
    pl.semaphore_wait(barrier, sections - 1)


def exchange(mine, slots, send_sems, recv_sems, sections):
    me = lax.axis_index("section")
    copies = []
    for hop in range(1, sections):
        copies.append(
            pltpu.make_async_remote_copy(
                src_ref=mine,
                dst_ref=slots.at[me],
                send_sem=send_sems.at[hop - 1],
                recv_sem=recv_sems.at[hop - 1],
                device_id={"section": lax.rem(me + hop, sections)},
                device_id_type=MESH,
            )
        )
    for copy in copies:
        copy.start()
    slots[me] = mine[...]
    for copy in copies:
        copy.wait()


def norm_rows(stream, gain, low, rows, step):
    def one(i, carry):
        at = tile(i, step)
        x = stream[at, :]
        r = lax.rsqrt(jnp.mean(x * x, axis=-1, keepdims=True) + epsilon)
        low[at, :] = (x * r * gain[...]).astype(BF16)
        return carry

    lax.fori_loop(0, rows // step, one, 0)


def norm_back(stream, gain, grad, through, out, gain_sum, rows, step, low=None):
    width = stream.shape[1]

    def one(i, total):
        at = tile(i, step)
        x = stream[at, :]
        r = lax.rsqrt(jnp.mean(x * x, axis=-1, keepdims=True) + epsilon)
        n = x * r
        g = grad[at, :]
        a = g * gain[...]
        value = through[at, :] + r * (a - n * jnp.mean(a * n, axis=-1, keepdims=True))
        out[at, :] = value
        if low is not None:
            low[at, :] = value.astype(BF16)
        return total + jnp.sum((g * n).reshape(step // 8, 8, width), axis=0)

    gain_sum[...] = lax.fori_loop(0, rows // step, one, jnp.zeros((8, width), F32))


def fill_masks(lens, valid, keep, sizes, turned=False):
    section = lax.axis_index("section")
    group = lax.axis_index("batch")
    starts, totals = [], []
    for s in range(sizes.micro):
        total, begin = 0, []
        for d in range(lens.shape[0 if turned else 1]):
            row = group * sizes.micro + s
            length = lens[d, row] if turned else lens[row, d]
            begin.append(jnp.where(length > 0, total, -1))
            total = total + length
        starts.append(begin)
        totals.append(total)
    chunk_place = lax.broadcasted_iota(jnp.int32, (8, LANES), 0) * sizes.steps

    def one(j, carry):
        for s in range(sizes.micro):
            place = section * sizes.span + j + chunk_place
            true = place < totals[s]
            first = place == starts[s][0]
            for begin in starts[s][1:]:
                first = first | (place == begin)
            at = pl.ds(pl.multiple_of(j * sizes.group + s * 8, 8), 8)
            valid[at, :] = jnp.where(true, 1.0, 0.0)
            keep[at, :] = jnp.where(true & jnp.logical_not(first), 1.0, 0.0)
        return carry

    lax.fori_loop(0, sizes.steps, one, 0)


def scan_totals(first, second, sizes, reverse, prefix, chunk, mine):
    for s in range(sizes.micro):
        p = jnp.ones((1, sizes.hidden), F32)
        t = jnp.zeros((1, sizes.hidden), F32)
        for c in reversed(range(CHUNKS)) if reverse else range(CHUNKS):
            at = s * 8 + c
            prefix[0, at : at + 1, :] = p
            prefix[1, at : at + 1, :] = t
            pc = first[at : at + 1, :]
            t = pc * t + second[at : at + 1, :]
            p = p * pc
        mine[s : s + 1, :] = p
        mine[sizes.micro + s : sizes.micro + s + 1, :] = t


def scan_enter(slots, prefix, enter, sizes, reverse):
    me = lax.axis_index("section")
    for s in range(sizes.micro):
        a = jnp.zeros((1, sizes.hidden), F32)
        order = range(sizes.sections - 1, 0, -1) if reverse else range(sizes.sections - 1)
        for k in order:
            reached = k > me if reverse else k < me
            pk = slots[k, s : s + 1, :]
            tk = slots[k, sizes.micro + s : sizes.micro + s + 1, :]
            a = jnp.where(reached, pk * a + tk, a)
        at = slice(s * 8, s * 8 + 8)
        enter[at, :] = prefix[0, at, :] * a + prefix[1, at, :]


def part_totals(first, second, sizes, reverse, prefix, mine, lanes):
    for s in range(sizes.micro):
        p = jnp.ones((1, lanes.stop - lanes.start), F32)
        t = jnp.zeros_like(p)
        for c in reversed(range(CHUNKS)) if reverse else range(CHUNKS):
            at = s * 8 + c
            prefix[0, at : at + 1, lanes] = p
            prefix[1, at : at + 1, lanes] = t
            pc = first[at : at + 1, lanes]
            t = pc * t + second[at : at + 1, lanes]
            p = p * pc
        mine[s : s + 1, lanes] = p
        mine[sizes.micro + s : sizes.micro + s + 1, lanes] = t


def part_enter(slots, prefix, enter, sizes, reverse, lanes):
    me = lax.axis_index("section")
    for s in range(sizes.micro):
        a = jnp.zeros((1, lanes.stop - lanes.start), F32)
        order = range(sizes.sections - 1, 0, -1) if reverse else range(sizes.sections - 1)
        for k in order:
            reached = k > me if reverse else k < me
            pk = slots[k, s : s + 1, lanes]
            tk = slots[k, sizes.micro + s : sizes.micro + s + 1, lanes]
            a = jnp.where(reached, pk * a + tk, a)
        at = slice(s * 8, s * 8 + 8)
        enter[at, lanes] = prefix[0, at, lanes] * a + prefix[1, at, lanes]


class Sizes:
    def __init__(self, micro, span, width, hidden, inner, sections):
        self.micro, self.span, self.width = micro, span, width
        self.hidden, self.inner, self.sections = hidden, inner, sections
        self.rows = micro * span
        self.steps = span // CHUNKS
        self.group = micro * CHUNKS


def forward_kernel(
    sizes,
    layer,
    stream,
    valid,
    keep,
    bias,
    mix_gain,
    mlp_gain,
    gate_hbm,
    out_hbm,
    up_hbm,
    down_hbm,
    next_stream,
    u,
    sf_out,
    si_out,
    zc_out,
    states,
    y1,
    v,
    p_out,
    gb,
    forget,
    pair_slots,
    gate_w,
    out_w,
    up_w,
    down_w,
    z,
    decay,
    drive,
    hb,
    chunk_p,
    chunk_t,
    prefix,
    enter,
    mine,
    weight_sems,
    send_sems,
    recv_sems,
):
    sz = sizes
    loads = [
        pltpu.make_async_copy(src.at[layer], dst, weight_sems.at[i])
        for i, (src, dst) in enumerate(
            ((gate_hbm, gate_w), (out_hbm, out_w), (up_hbm, up_w), (down_hbm, down_w))
        )
    ]
    for load in loads:
        load.start()
    greet_section(sz.sections)
    mine[...] = jnp.zeros_like(mine)
    norm_rows(stream, mix_gain, u, sz.rows, 64)
    loads[0].wait()
    forget[...] = jnp.zeros_like(forget)
    hw = 256

    def gate_tile(n, carry):
        for part in range(3):
            cols = pl.ds(pl.multiple_of(part * sz.hidden + n * hw, hw), hw)
            z[:, part * hw : (part + 1) * hw] = (
                jnp.dot(u[...], gate_w[:, cols], preferred_element_type=F32) + bias[:, cols]
            )

        def one(i, inner):
            at = tile(i, 64)
            for lane in range(hw // LANES):
                src = lambda part: z[
                    at, part * hw + lane * LANES : part * hw + (lane + 1) * LANES
                ]
                dst = pl.ds(pl.multiple_of(n * hw + lane * LANES, LANES), LANES)
                a = jnp.exp(jnp.minimum(-src(0), 86.0))
                b = jnp.exp(jnp.minimum(-src(1), 86.0))
                zc = src(2)
                fp, ip, _ = gate_weights(a, b)
                vm = valid[at, :]
                decay[at, dst] = fp * keep[at, :]
                drive[at, dst] = ip * zc * vm
                sf_out[at, dst] = a
                si_out[at, dst] = b
                zc_out[at, dst] = zc
                forget[...] += jnp.sum((fp * vm).reshape(8, 8, LANES), axis=0)
            return inner

        lax.fori_loop(0, sz.rows // 64, one, 0)
        return carry

    lax.fori_loop(0, sz.hidden // hw, gate_tile, 0)
    half = sz.hidden // 2
    for part in range(2):
        lanes = slice(part * half, (part + 1) * half)

        def totals(j, pair):
            at = tile(j, sz.group)
            d = decay[at, lanes]
            return pair[0] * d, pair[1] * d + drive[at, lanes]

        one = jnp.ones((sz.group, half), F32)
        pair = steps_of(sz.steps, 4, totals, (one, jnp.zeros_like(one)))
        chunk_p[:, lanes] = pair[0]
        chunk_t[:, lanes] = pair[1]
    scan_totals(chunk_p, chunk_t, sz, False, prefix, None, mine)
    exchange(mine, pair_slots, send_sems, recv_sems, sz.sections)
    scan_enter(pair_slots, prefix, enter, sz, False)
    states[0 : sz.group, :] = enter[...]
    for part in range(2):
        lanes = slice(part * half, (part + 1) * half)

        def walk(j, h):
            at = tile(j, sz.group)
            h = decay[at, lanes] * h + drive[at, lanes]
            states[tile(j + 1, sz.group), lanes] = h
            hb[at, lanes] = h.astype(BF16)
            return h

        steps_of(sz.steps, 4, walk, enter[:, lanes])
    loads[1].wait()

    def out_tile(n, carry):
        cols = tile(n, 256)
        y1[:, cols] = stream[:, cols] + jnp.dot(
            hb[...], out_w[:, cols], preferred_element_type=F32
        )
        return carry

    lax.fori_loop(0, sz.width // 256, out_tile, 0)
    norm_rows(y1, mlp_gain, v, sz.rows, 64)
    loads[2].wait()

    def up_tile(n, carry):
        cols = tile(n, 256)
        p_out[:, cols] = jnp.dot(v[...], up_w[:, cols], preferred_element_type=F32)

        def one(i, inner):
            at = tile(i, 64)
            p = p_out[at, cols]
            gb[at, cols] = (p * normal_below(p)).astype(BF16)
            return inner

        lax.fori_loop(0, sz.rows // 64, one, 0)
        return carry

    lax.fori_loop(0, sz.inner // 256, up_tile, 0)
    loads[3].wait()

    def down_tile(n, carry):
        cols = tile(n, 256)
        next_stream[:, cols] = y1[:, cols] + jnp.dot(
            gb[...], down_w[:, cols], preferred_element_type=F32
        )
        return carry

    lax.fori_loop(0, sz.width // 256, down_tile, 0)


def backward_kernel(
    sizes,
    layer,
    gx,
    stream,
    valid,
    keep,
    mix_gain,
    mlp_gain,
    u,
    sf_in,
    si_in,
    zc_in,
    states,
    y1,
    v,
    p_in,
    gb,
    pair_slots,
    gate_hbm,
    out_hbm,
    up_hbm,
    down_hbm,
    next_gx,
    gate_grad,
    out_grad,
    up_grad,
    down_grad,
    bias_sum,
    mix_sum,
    mlp_sum,
    gate_w,
    out_w,
    up_w,
    down_w,
    low,
    low_t,
    wide_t,
    hb,
    ga,
    gp,
    gz,
    grad,
    gy1,
    decay,
    chunk_p,
    chunk_t,
    prefix,
    enter,
    mine,
    slots,
    weight_sems,
    send_sems,
    recv_sems,
):
    sz = sizes
    loads = [
        pltpu.make_async_copy(src.at[layer], dst, weight_sems.at[i])
        for i, (src, dst) in enumerate(
            ((gate_hbm, gate_w), (out_hbm, out_w), (up_hbm, up_w), (down_hbm, down_w))
        )
    ]
    for load in reversed(loads):
        load.start()
    greet_section(sz.sections)
    mine[...] = jnp.zeros_like(mine)

    def cast(i, carry):
        at = tile(i, 64)
        low[at, :] = gx[at, :].astype(BF16)
        return carry

    lax.fori_loop(0, sz.rows // 64, cast, 0)
    low_t[...] = low[...].T

    def weight_grad(left_t, right, dst, step):
        def one(n, carry):
            cols = tile(n, step)
            dst[:, cols] = jnp.dot(left_t[...], right[:, cols], preferred_element_type=F32)
            return carry

        lax.fori_loop(0, right.shape[1] // step, one, 0)

    weight_grad(low_t, gb, down_grad, 256)
    loads[3].wait()

    def act_tile(n, carry):
        cols = tile(n, 256)
        ga[:, :256] = lax.dot_general(
            low[...], down_w[cols, :], (((1,), (1,)), ((), ())), preferred_element_type=F32
        )

        def one(i, inner):
            at = tile(i, 64)
            p = p_in[at, cols]
            slope = normal_below(p) + ROOT_TAU * p * jnp.exp(-0.5 * p * p)
            gp[at, cols] = (ga[at, :256] * slope).astype(BF16)
            return inner

        lax.fori_loop(0, sz.rows // 64, one, 0)
        return carry

    lax.fori_loop(0, sz.inner // 256, act_tile, 0)
    wide_t[...] = v[...].T
    weight_grad(wide_t, gp, up_grad, 256)
    loads[2].wait()

    def contract(left, weight, dst, step):
        def one(n, carry):
            cols = tile(n, step)
            dst[:, cols] = lax.dot_general(
                left[...], weight[cols, :], (((1,), (1,)), ((), ())), preferred_element_type=F32
            )
            return carry

        lax.fori_loop(0, weight.shape[0] // step, one, 0)

    contract(gp, up_w, grad, 256)
    norm_back(y1, mlp_gain, grad, gx, gy1, mlp_sum, sz.rows, 64)

    def cast_more(i, carry):
        at = tile(i, 64)
        low[at, :] = gy1[at, :].astype(BF16)
        return carry

    lax.fori_loop(0, sz.rows // 64, cast_more, 0)

    def cast_state(i, carry):
        hb[tile(i, sz.group), :] = states[tile(i + 1, sz.group), :].astype(BF16)
        return carry

    lax.fori_loop(0, sz.steps, cast_state, 0)
    low_t[...] = low[...].T
    weight_grad(low_t, hb, out_grad, 256)
    loads[1].wait()
    contract(low, out_w, ga, 256)
    half = sz.hidden // 2
    for part in range(2):
        lanes = slice(part * half, (part + 1) * half)

        def totals(i, pair):
            at = tile(sz.steps - 1 - i, sz.group)
            mask = jnp.concatenate([keep[at, :]] * (half // LANES), axis=1)
            d = gate_weights(sf_in[at, lanes], si_in[at, lanes])[0] * mask
            decay[at, lanes] = d
            return pair[0] * d, d * (ga[at, lanes] + pair[1])

        pair = lax.fori_loop(
            0,
            sz.steps,
            totals,
            (jnp.ones((sz.group, half), F32), jnp.zeros((sz.group, half), F32)),
        )
        chunk_p[:, lanes] = pair[0]
        chunk_t[:, lanes] = pair[1]
    scan_totals(chunk_p, chunk_t, sz, True, prefix, None, mine)
    exchange(mine, slots, send_sems, recv_sems, sz.sections)
    scan_enter(slots, prefix, enter, sz, True)

    def gate_lane(n, carry):
        lanes = tile(n, LANES)

        def walk(i, kept):
            m, bf, bi, bc = kept
            j = sz.steps - 1 - i
            at = tile(j, sz.group)
            d = decay[at, lanes]
            q = ga[at, lanes] + m
            a = sf_in[at, lanes]
            b = si_in[at, lanes]
            zc = zc_in[at, lanes]
            vm = valid[at, :]
            fp, ip, inv = gate_weights(a, b)
            gf = q * (states[at, lanes] * keep[at, :] - zc * vm)
            gzf = (gf * (a * inv) * fp).astype(BF16)
            gzi = (-gf * (b * inv) * ip).astype(BF16)
            gzc = (q * vm * ip).astype(BF16)
            gz[at, lanes] = gzf
            gz[at, pl.ds(pl.multiple_of(sz.hidden + n * LANES, LANES), LANES)] = gzi
            gz[at, pl.ds(pl.multiple_of(2 * sz.hidden + n * LANES, LANES), LANES)] = gzc
            return (
                d * q,
                bf + gzf.astype(F32),
                bi + gzi.astype(F32),
                bc + gzc.astype(F32),
            )

        zero = jnp.zeros((sz.group, LANES), F32)
        _, bf, bi, bc = lax.fori_loop(0, sz.steps, walk, (enter[:, lanes], zero, zero, zero))
        for part, total in enumerate((bf, bi, bc)):
            where = pl.ds(pl.multiple_of(part * sz.hidden + n * LANES, LANES), LANES)
            bias_sum[:, where] = jnp.sum(total.reshape(sz.group // 8, 8, LANES), axis=0)
        return carry

    lax.fori_loop(0, sz.hidden // LANES, gate_lane, 0)
    wide_t[...] = u[...].T
    weight_grad(wide_t, gz, gate_grad, 256)
    loads[0].wait()
    contract(gz, gate_w, grad, 256)
    norm_back(stream, mix_gain, grad, gy1, next_gx, mix_sum, sz.rows, 64)


VMEM = pl.BlockSpec(memory_space=pltpu.VMEM)
ANY = pl.BlockSpec(memory_space=pl.ANY)
LIMIT = 63 * 2**20


def shape(*dims, kind=F32):
    return jax.ShapeDtypeStruct(dims, kind)


def exchange_scratch(sz):
    return [
        pltpu.SemaphoreType.DMA((4,)),
        pltpu.SemaphoreType.DMA((sz.sections - 1,)),
        pltpu.SemaphoreType.DMA((sz.sections - 1,)),
    ]


def weight_scratch(sz):
    return [
        pltpu.VMEM((sz.width, 3 * sz.hidden), BF16),
        pltpu.VMEM((sz.hidden, sz.width), BF16),
        pltpu.VMEM((sz.width, sz.inner), BF16),
        pltpu.VMEM((sz.inner, sz.width), BF16),
    ]


def scan_scratch(sz):
    return [
        pltpu.VMEM((sz.group, sz.hidden), F32),
        pltpu.VMEM((sz.group, sz.hidden), F32),
        pltpu.VMEM((2, sz.group, sz.hidden), F32),
        pltpu.VMEM((sz.group, sz.hidden), F32),
        pltpu.VMEM((8, sz.hidden), F32),
    ]


def run_forward(sz, layer, stream, masks, bias, mix_gain, mlp_gain, weights):
    r, d, h, f = sz.rows, sz.width, sz.hidden, sz.inner
    return pl.pallas_call(
        functools.partial(forward_kernel, sz, layer),
        out_shape=(
            shape(r, d),
            shape(r, d, kind=BF16),
            shape(r, h),
            shape(r, h),
            shape(r, h),
            shape(r + sz.group, h),
            shape(r, d),
            shape(r, d, kind=BF16),
            shape(r, f),
            shape(r, f, kind=BF16),
            shape(8, LANES),
            shape(sz.sections, 8, h),
        ),
        in_specs=[VMEM] * 6 + [ANY] * 4,
        out_specs=[VMEM] * 12,
        scratch_shapes=weight_scratch(sz)
        + [
            pltpu.VMEM((r, 3 * 256), F32),
            pltpu.VMEM((r, h), F32),
            pltpu.VMEM((r, h), F32),
            pltpu.VMEM((r, h), BF16),
        ]
        + scan_scratch(sz)
        + exchange_scratch(sz),
        compiler_params=pltpu.CompilerParams(
            collective_id=layer, has_side_effects=True, vmem_limit_bytes=LIMIT
        ),
        name=f"forward_{layer}",
    )(stream, *masks, bias, mix_gain, mlp_gain, *weights)


def run_backward(sz, layer, gx, stream, masks, mix_gain, mlp_gain, saved, weights):
    r, d, h, f = sz.rows, sz.width, sz.hidden, sz.inner
    return pl.pallas_call(
        functools.partial(backward_kernel, sz, layer),
        out_shape=(
            shape(r, d),
            shape(d, 3 * h),
            shape(d, h),
            shape(d, f),
            shape(d, f),
            shape(8, 3 * h),
            shape(8, d),
            shape(8, d),
        ),
        in_specs=[VMEM] * 16 + [ANY] * 4,
        out_specs=[VMEM] * 8,
        scratch_shapes=weight_scratch(sz)
        + [
            pltpu.VMEM((r, d), BF16),
            pltpu.VMEM((d, r), BF16),
            pltpu.VMEM((d, r), BF16),
            pltpu.VMEM((r, h), BF16),
            pltpu.VMEM((r, h), F32),
            pltpu.VMEM((r, f), BF16),
            pltpu.VMEM((r, 3 * h), BF16),
            pltpu.VMEM((r, d), F32),
            pltpu.VMEM((r, d), F32),
            pltpu.VMEM((r, h), F32),
        ]
        + scan_scratch(sz)
        + [pltpu.VMEM((sz.sections, 8, h), F32)]
        + exchange_scratch(sz),
        compiler_params=pltpu.CompilerParams(
            collective_id=2 + layer, has_side_effects=True, vmem_limit_bytes=LIMIT
        ),
        name=f"backward_{layer}",
    )(gx, stream, *masks, mix_gain, mlp_gain, *saved, *weights)


BLOCK = 64
HELD = 3
RINGS = (4, 5, 5, 16, 16)
SENDS = 16
STAGES = 5
WINDOW = 4
DELAY = 1.5
SMALL = 1280


EVEN = ((0, 2, 1, 3), (1, 2, 0, 3))
ORDERS = [EVEN] * 16


class Units:
    def __init__(self, count, refs):
        self.count = count
        self.__dict__.update(vars(refs))
        self.arrived = [getattr(refs, f"arrived{stage}") for stage in range(STAGES)]
        section, batch = lax.axis_index("section"), lax.axis_index("batch")
        core, x = section % 2, section // 2
        y, za, zb = batch % 2, (batch // 2) % 2, batch // 4
        self.core = core
        self.where = (x, y, za, zb)
        self.partner = {
            "core": {"section": section + 1 - 2 * core},
            "x": {"section": section + 2 - 4 * x},
            "y": {"batch": batch + 1 - 2 * y},
            "za": {"batch": batch + 2 - 4 * za},
            "zb": {"batch": batch + 4 - 8 * zb},
        }
        self.now = 0.0
        self.links = ("core", "x", "y", "z")
        self.free_at = dict.fromkeys(self.links, 0.0)
        self.flying = dict.fromkeys(self.links, 0)
        self.queues = {link: [] for link in self.links}
        self.ready = {}
        self.summed = set()
        self.copies = {}
        self.small_left = None
        self.leaving = []

    def greet(self):
        section = lax.axis_index("section")
        others = [self.partner["y"], self.partner["za"], self.partner["zb"]]
        others += [{"section": lax.rem(section + hop, 4)} for hop in range(1, 4)]
        for other in others:
            pl.semaphore_signal(
                pltpu.get_barrier_semaphore(), inc=1, device_id=other, device_id_type=MESH
            )

    def greeted(self):
        pl.semaphore_wait(pltpu.get_barrier_semaphore(), 6)

    def name(self, unit, stage, half):
        return "core" if stage == 0 else ("x", "y", "za", "zb")[ORDERS[unit][half][stage - 1]]

    def link(self, unit, stage, half):
        name = self.name(unit, stage, half)
        return "z" if name[0] == "z" else name

    def bit(self, unit, stage, half):
        return self.where[ORDERS[unit][half][stage - 1]]

    def arrival(self, unit, stage, half):
        ref = self.arrived[stage].at[unit % RINGS[stage]]
        return ref if stage == 0 else ref.at[half]

    def copy(self, unit, stage, half):
        at = 0 if stage == 0 else 2 * stage - 1 + half
        if stage == 0:
            src = self.held.at[unit % HELD, 1 - self.core]
        else:
            count = 16 >> stage
            src = self.arrived[stage - 1].at[unit % RINGS[stage - 1], half]
            src = src.at[pl.ds((1 - self.bit(unit, stage, half)) * count, count)]
        return pltpu.make_async_remote_copy(
            src_ref=src,
            dst_ref=self.arrival(unit, stage, half),
            send_sem=self.send_sems.at[unit % SENDS, at],
            recv_sem=self.recv_sems.at[unit % RINGS[stage], at],
            device_id=self.partner[self.name(unit, stage, half)],
            device_id_type=MESH,
        )

    def has_place(self, unit, stage, half):
        before = unit - RINGS[stage]
        if before < 0:
            return True
        if stage == 0:
            return (before, 1, 0) in self.summed and (before, 1, 1) in self.summed
        return (before, min(stage + 1, STAGES - 1), half) in self.summed

    def credit(self, unit, stage, half):
        after = unit + RINGS[stage]
        if after < self.count:
            pl.semaphore_signal(
                self.credits.at[0 if stage == 0 else 2 * stage - 1 + half, after],
                inc=1,
                device_id=self.partner[self.name(after, stage, half)],
                device_id_type=MESH,
            )

    def pump(self):
        for link, queue in self.queues.items():
            while self.flying[link] < WINDOW:
                key = next((key for key in queue if self.has_place(*key)), None)
                if key is None:
                    break
                queue.remove(key)
                self.flying[link] += 1
                unit, stage, half = key
                if unit >= RINGS[stage]:
                    at = 0 if stage == 0 else 2 * stage - 1 + half
                    pl.semaphore_wait(self.credits.at[at, unit], 1)
                self.copies[key] = self.copy(*key)
                self.copies[key].start()
                blocks = 32 if stage == 0 else 16 >> stage
                self.ready[key] = self.expect(link, blocks * BLOCK * LANES * 4)

    def expect(self, link, size):
        rate = 250e3 if link == "core" else 45e3
        self.free_at[link] = max(self.now, self.free_at[link]) + size / rate
        return self.free_at[link] + DELAY

    def push(self, unit, stage, half):
        self.queues[self.link(unit, stage, half)].append((unit, stage, half))
        self.pump()

    def produced(self, us, *which):
        self.now += us
        for unit in which:
            self.push(unit, 0, 0)
        self.passed(0)

    def add(self, dst, src, count):
        turn = min(count, 4)

        def one(i, carry):
            for k in range(turn):
                dst[i * turn + k] += src[i * turn + k]
            return carry

        if count == turn:
            one(0, 0)
        else:
            lax.fori_loop(0, count // turn, one, 0)

    def step(self, unit, stage, half):
        key = (unit, stage, half)
        del self.ready[key]
        self.copies[key].wait_recv()
        here = self.arrival(unit, stage, half)
        if stage == 0:
            for h in range(2):
                self.add(here.at[h], self.held.at[unit % HELD, self.core, h], 16)
        else:
            count = 16 >> stage
            before = self.arrived[stage - 1].at[unit % RINGS[stage - 1], half]
            self.add(here, before.at[pl.ds(self.bit(unit, stage, half) * count, count)], count)
            self.copies.pop(key).wait_send()
        self.summed.add(key)
        self.flying[self.link(unit, stage, half)] -= 1
        self.now += 0.25
        if stage > 1 or (unit, 1, 1 - half) in self.summed:
            if stage > 0:
                self.credit(unit, stage - 1, half if stage > 1 else 0)
        if stage == 0:
            for h in range(2):
                self.push(unit, 1, h)
        elif stage < STAGES - 1:
            self.push(unit, stage + 1, half)
        else:
            self.finish(unit, half, here.at[0])
            self.credit(unit, stage, half)
        self.pump()

    def finish(self, unit, half, block):
        layer, k = self.count // 8 - 1 - unit // 8, unit % 8
        if k < 2 or k == 4:
            ref, at = (self.down_weight_grad, k) if k < 2 else (self.out_weight_grad, 0)
            to = ref.at[layer, :, at * 256 + half * 128 : at * 256 + half * 128 + 128]
        else:
            ref, at = (self.up_weight_grad, k - 2) if k < 4 else (self.gate_weight_grad, k - 5)
            rows = slice(half * BLOCK, half * BLOCK + BLOCK)
            to = ref.at[layer, rows, at * LANES : at * LANES + LANES]
        copy = pltpu.make_async_copy(block, to, self.result_sems.at[unit, half])
        copy.start()
        self.leaving.append(copy)

    def small_copy(self, stage):
        name = ("core", "x", "y", "za", "zb")[stage]
        return pltpu.make_async_remote_copy(
            src_ref=self.small.at[stage],
            dst_ref=self.small_arrived.at[stage],
            send_sem=self.small_send.at[stage],
            recv_sem=self.small_recv.at[stage],
            device_id=self.partner[name],
            device_id_type=MESH,
        )

    def small_start(self):
        self.small_left = 0
        self.small_copies = [self.small_copy(0)]
        self.small_copies[0].start()
        self.small_ready = self.now + 3.0

    def small_step(self):
        stage = self.small_left
        self.small_copies[stage].wait_recv()
        self.small[stage + 1] = self.small[stage] + self.small_arrived[stage]
        self.small_left += 1
        if self.small_left < STAGES:
            self.small_copies.append(self.small_copy(self.small_left))
            self.small_copies[-1].start()
            self.small_ready = self.now + 3.0
        else:
            for copy in self.small_copies:
                copy.wait_send()
            self.small_done()

    def open(self, unit, stage, half):
        halves = range(2) if stage == 0 else (half,)
        before = unit - RING
        return (
            before < 0
            or stage == STAGES - 1
            or all((before, stage + 1, h) in self.consumed for h in halves)
        )

    def next(self):
        best = min(self.ready.items(), key=lambda item: (item[1], item[0]), default=None)
        small = self.small_left is not None and self.small_left < STAGES
        if small and (best is None or self.small_ready <= best[1]):
            return self.small_ready, None
        return (best[1], best[0]) if best else None

    def take(self, item):
        self.now = max(self.now, item[0])
        if item[1] is None:
            self.small_step()
        else:
            self.step(*item[1])

    def passed(self, us):
        self.now += us
        while (item := self.next()) and item[0] <= self.now:
            self.take(item)

    def room(self, unit):
        before = (unit - HELD, 0, 0)
        while unit >= HELD and before not in self.summed:
            self.take(self.next())
        if before in self.copies:
            self.copies.pop(before).wait_send()

    def drain(self):
        while item := self.next():
            self.take(item)
        for key in list(self.copies):
            self.copies.pop(key).wait_send()
        for copy in self.leaving:
            copy.wait()


def place(unit, half, x, y, z):
    return spot(unit, half, (x, y, z % 2, z // 2))


def spot(unit, half, where):
    order = ORDERS[unit][half]
    return where[order[0]] * 8 + where[order[1]] * 4 + where[order[2]] * 2 + where[order[3]]


def strided(start, steps):
    return pl.ds(start, CHUNKS, stride=steps)


def whole_step(sz, layers, names, *args):
    r = types.SimpleNamespace(**dict(zip(names, args)))
    units = Units(8 * layers, r)
    valid, keep, low, low_t, wide_t = r.valid, r.keep, r.low, r.low_t, r.wide_t
    hb, ga, gz, grad, gy1, gx = r.hb, r.ga, r.gz, r.grad, r.gy1, r.gx
    gp = gz.at[:, : sz.inner]
    decay, enter, prefix, mine = r.decay, r.enter, r.prefix, r.mine
    small, held = r.small, r.held
    natural = r.natural
    last = layers - 1
    half = sz.hidden // 2
    zs = (ga.at[:, :768], r.z1)
    drive = r.drive
    homes = dict(gate_w=r.gate_hbm, out_w=r.out_hbm, up_w=r.up_hbm, down_w=r.down_hbm)
    homes.update(u=r.u_save, a=r.a_save, b=r.b_save, zc=r.zc_save, states=r.states_save)
    homes.update(y1=r.y1_save, v=r.v_save, p=r.p_save, gb=r.gb_save, stream=r.stream_save)
    keys = types.SimpleNamespace(**{name: name for name in homes})
    index_of = {name: i for i, name in enumerate(homes)}
    loads, saves = {}, {}

    def load(layer, name):
        copy = pltpu.make_async_copy(
            homes[name].at[layer], getattr(r, name), r.load_sems.at[index_of[name]]
        )
        copy.start()
        loads[name] = copy

    def need(*wanted):
        for name in wanted:
            if name in loads:
                loads.pop(name).wait()

    def save(layer, name, ref=None):
        if layer < last:
            src = getattr(r, name) if ref is None else ref
            copy = pltpu.make_async_copy(
                src, homes[name].at[layer], r.save_sems.at[index_of[name]]
            )
            copy.start()
            saves[name] = copy

    def settled(*which):
        for name in which:
            if name in saves:
                saves.pop(name).wait()

    def over(count, one):
        def each(i, carry):
            one(i)
            return carry

        lax.fori_loop(0, count, each, 0)

    act_load = pltpu.make_async_copy(r.activations, hb.at[:, : sz.width], r.in_sems.at[0])
    cot_load = pltpu.make_async_copy(r.cotangent, wide_t, r.in_sems.at[1])
    len_load = pltpu.make_async_copy(r.lengths, r.lens, r.in_sems.at[2])
    len_load.start()
    act_load.start()
    load(0, keys.gate_w)
    units.greet()
    mine[...] = jnp.zeros_like(mine)
    small[0] = jnp.zeros((8, SMALL), F32)
    len_load.wait()
    fill_masks(r.lens, valid, keep, sz, True)

    def to_steps(src, put):
        def cast(i):
            at = tile(i, 64)
            for k in range(sz.width // LANES):
                natural[k, at, :] = src[at, k * LANES : (k + 1) * LANES].astype(F32)

        over(sz.rows // 64, cast)

        def gather(j):
            for k in range(sz.width // LANES):
                parts = [
                    natural[k, strided(s * sz.span + j, sz.steps), :] for s in range(sz.micro)
                ]
                put(tile(j, sz.group), slice(k * LANES, (k + 1) * LANES), jnp.concatenate(parts, axis=0))

        over(sz.steps, gather)

    def from_steps(src, dst, sem):
        def scatter(j):
            for k in range(sz.width // LANES):
                value = src[tile(j, sz.group), k * LANES : (k + 1) * LANES]
                for s in range(sz.micro):
                    natural[k, strided(s * sz.span + j, sz.steps), :] = value[s * 8 : s * 8 + 8]

        over(sz.steps, scatter)
        copies = []
        for k in range(sz.width // LANES):
            lanes = slice(k * LANES, (k + 1) * LANES)
            copies.append(pltpu.make_async_copy(natural.at[k], dst.at[:, lanes], sem.at[k]))
            copies[-1].start()
        return copies

    act_load.wait()

    def put_gx(at, lanes, value):
        gx[at, lanes] = value

    to_steps(hb.at[:, : sz.width], put_gx)

    parts = [slice(part * half, (part + 1) * half) for part in range(2)]

    def exchange_start(way, layer, part):
        lanes = parts[part]
        slots = r.slots.at[way, layer]
        me = lax.axis_index("section")
        copies = []
        for hop in range(1, sz.sections):
            copies.append(
                pltpu.make_async_remote_copy(
                    src_ref=mine.at[:, lanes],
                    dst_ref=slots.at[me, :, lanes],
                    send_sem=r.pair_send.at[way, layer, part, hop - 1],
                    recv_sem=r.pair_recv.at[way, layer, part, hop - 1],
                    device_id={"section": lax.rem(me + hop, sz.sections)},
                    device_id_type=MESH,
                )
            )
        for copy in copies:
            copy.start()
        slots[me, :, lanes] = mine[:, lanes]
        return slots, copies

    sent = {}

    def sends_settled(part):
        for copy in sent.pop(part, ()):
            copy.wait_send()

    def exchange_end(slots, copies, reverse, part):
        for copy in copies:
            copy.wait_recv()
        sent[part] = copies
        part_enter(slots, prefix, enter, sz, reverse, parts[part])

    def in_turn(count, dots, rest, after=None, third=None):
        dots(0)
        for n in range(count):
            if n + 1 < count:
                dots(n + 1)
            if third is not None and n > 0:
                third(n - 1)
            rest(n)
            if after is not None:
                after(n)

    def keep_cotangent():
        cot_load.wait()

        def put_low(at, lanes, value):
            low[at, lanes] = value.astype(BF16)

        to_steps(wide_t, put_low)
        low_t[...] = low[...].T

    def forward(layer):
        stream = r.stream if layer > 0 else gx
        settled(keys.u)
        norm_rows(stream, r.mix_gain.at[layer : layer + 1], r.u, sz.rows, 128)
        save(layer, keys.u)
        if layer == 0:
            save(layer, keys.stream, gx)
        need(keys.gate_w)
        if layer == 0:
            for name in (keys.out_w, keys.up_w, keys.down_w):
                load(0, name)
            cot_load.start()
        settled(keys.a, keys.b, keys.zc)
        hw = 256
        bias = r.gate_bias

        def gate_dots(n):
            for part in range(3):
                cols = slice(part * sz.hidden + n * hw, part * sz.hidden + (n + 1) * hw)
                zs[n % 2][:, part * hw : (part + 1) * hw] = (
                    jnp.dot(r.u[...], r.gate_w[:, cols], preferred_element_type=F32)
                    + bias[layer : layer + 1, cols]
                )

        def gate_rest(n):
            for chunk in range(sz.rows // 64):
                at = slice(chunk * 64, chunk * 64 + 64)
                vm, km = valid[at, :], keep[at, :]
                for lane in range(hw // LANES):
                    zf, zi, zc = (
                        zs[n % 2][at, part * hw + lane * LANES : part * hw + (lane + 1) * LANES]
                        for part in range(3)
                    )
                    cols = slice(n * hw + lane * LANES, n * hw + (lane + 1) * LANES)
                    a, b = odds(zf, zi)
                    fp, ip, _ = gate_weights(a, b)
                    decay[at, cols] = fp * km
                    drive[at, cols] = ip * zc * vm
                    r.a[at, cols] = a
                    r.b[at, cols] = b
                    r.zc[at, cols] = zc
                    r.forget[...] += jnp.sum((fp * vm).reshape(8, 8, LANES), axis=0)

        flights = []

        def gate_after(n):
            if n % 2 == 0:
                return
            lanes = parts[n // 2]

            def totals(j, pair):
                at = tile(j, sz.group)
                d = decay[at, lanes]
                return pair[0] * d, pair[1] * d + drive[at, lanes]

            one = jnp.ones((sz.group, half), F32)
            pair = steps_of(sz.steps, 2, totals, (one, jnp.zeros_like(one)))
            r.chunk_p[:, lanes] = pair[0]
            r.chunk_t[:, lanes] = pair[1]
            sends_settled(n // 2)
            part_totals(r.chunk_p, r.chunk_t, sz, False, prefix, mine, lanes)
            if layer == 0 and n == 1:
                units.greeted()
            flights.append(exchange_start(0, layer, n // 2))

        r.forget[...] = jnp.zeros_like(r.forget)
        in_turn(sz.hidden // hw, gate_dots, gate_rest, gate_after)
        small[0, layer * 4 : layer * 4 + 1, sz.hidden : sz.hidden + LANES] = jnp.sum(
            r.forget[...], axis=0, keepdims=True
        )
        for name in (keys.a, keys.b, keys.zc):
            save(layer, name)
        if layer < last:
            load(layer + 1, keys.gate_w)
        settled(keys.states, keys.y1, keys.v, keys.p, keys.gb, keys.stream)
        states = r.states
        for part, lanes in enumerate(parts):
            exchange_end(*flights[part], False, part)
            states[0 : sz.group, lanes] = enter[:, lanes]

            def walk(j, h):
                at = tile(j, sz.group)
                h = decay[at, lanes] * h + drive[at, lanes]
                states[tile(j + 1, sz.group), lanes] = h
                hb[at, lanes] = h.astype(BF16)
                return h

            steps_of(sz.steps, 4, walk, enter[:, lanes])
            if (layer, part) == (0, 0):
                keep_cotangent()
        save(layer, keys.states)
        need(keys.out_w)

        r.y1[...] = stream[...] + jnp.dot(hb[...], r.out_w[...], preferred_element_type=F32)
        save(layer, keys.y1)
        if layer < last:
            load(layer + 1, keys.out_w)
        norm_rows(r.y1, r.mlp_gain.at[layer : layer + 1], r.v, sz.rows, 128)
        save(layer, keys.v)
        need(keys.up_w)

        tiles = range(8) if layer < last else (0, 2, 4, 6, 1, 3, 5, 7)

        def up_dots(n):
            cols = slice(tiles[n] * 256, (tiles[n] + 1) * 256)
            zs[n % 2][:, :256] = jnp.dot(
                r.v[...], r.up_w[:, cols], preferred_element_type=F32
            )

        def up_rest(n):
            cols = slice(tiles[n] * 256, (tiles[n] + 1) * 256)
            for chunk in range(sz.rows // 64):
                at = slice(chunk * 64, chunk * 64 + 64)
                p = zs[n % 2][at, :256]
                r.p[at, cols] = p
                r.gb[at, cols] = (p * normal_below(p)).astype(BF16)

        def down_part(n):
            s, unit = tiles[n] // 2, tiles[n] % 2
            value = jnp.dot(
                low_t[...],
                r.gb[:, tiles[n] * 256 : (tiles[n] + 1) * 256],
                preferred_element_type=F32,
            )
            for k in range(8):
                for h in range(2):
                    at = place(unit, h, s // 2, k % 2, k // 2)
                    held[unit, s % 2, h, at] = value[
                        k * 64 : k * 64 + 64, h * 128 : h * 128 + 128
                    ]

        def up_after(n):
            units.passed(0.3)
            if n == 4:
                units.produced(0, 0)

        if layer < last:
            in_turn(8, up_dots, up_rest)
        else:
            in_turn(8, up_dots, up_rest, up_after, down_part)
            down_part(7)
            units.produced(0.2, 1)
        save(layer, keys.p)
        save(layer, keys.gb)
        if layer < last:
            load(layer + 1, keys.up_w)
        need(keys.down_w)
        out = r.stream if layer < last else gy1

        out[...] = r.y1[...] + jnp.dot(r.gb[...], r.down_w[...], preferred_element_type=F32)
        if layer < last:
            load(layer + 1, keys.down_w)

    def down_grad(layer, unit):
        for k in range(2):
            units.room(unit + k)

        def one(n):
            s, t = n // 2, n % 2
            value = jnp.dot(low_t[...], r.gb[:, tile(n, 256)], preferred_element_type=F32)
            for b in range(8):
                for h in range(2):
                    at = [place(unit + k, h, s // 2, b % 2, b // 2) for k in range(2)]
                    held[(unit + t) % HELD, s % 2, h, jnp.where(t == 0, *at)] = value[
                        b * 64 : b * 64 + 64, h * 128 : h * 128 + 128
                    ]

        over(8, one)
        units.produced(2, unit, unit + 1)

    def cast(src, dst):
        def one(i):
            at = tile(i, 64)
            dst[at, :] = src[at, :].astype(dst.dtype)

        over(sz.rows // 64, one)

    def turn_rows(src, dst, n):
        at = tile(n, 128)
        dst[:, at] = src[at, :].T

    def contract(left, weight, dst, count, beside=None):
        def one(n):
            if beside is not None:
                beside(n)
            cols = tile(n, 256)
            dst[:, cols] = lax.dot_general(
                left[...], weight[cols, :], (((1,), (1,)), ((), ())), preferred_element_type=F32
            )

        over(count // 256, one)

    def up_grad(layer, unit):
        for k in range(2):
            units.room(unit + k)

        def one(b):
            value = jnp.dot(wide_t[...], gp[:, tile(b, 256)], preferred_element_type=F32)
            for s in range(4):
                for h in range(2):
                    for t in range(2):
                        at = place(unit + t, h, s // 2, b % 2, b // 2)
                        held[(unit + t) % HELD, s % 2, h, at] = value[
                            s * 128 + h * 64 : s * 128 + h * 64 + 64, t * 128 : t * 128 + 128
                        ]

        over(8, one)
        units.produced(2.5, unit, unit + 1)

    def out_grad(layer, unit):
        def cast_state(i):
            hb[tile(i, sz.group), :] = r.states[tile(i + 1, sz.group), :].astype(BF16)

        if layer < last:
            over(sz.steps, cast_state)
        units.room(unit)

        def one(s):
            value = jnp.dot(r.go_t[...], hb[:, tile(s, 256)], preferred_element_type=F32)
            for b in range(8):
                for h in range(2):
                    at = place(unit, h, s // 2, b % 2, b // 2)
                    held[unit % HELD, s % 2, h, at] = value[
                        b * 64 : b * 64 + 64, h * 128 : h * 128 + 128
                    ]

        over(4, one)
        units.produced(1.2, unit)

    def backward(layer, unit):
        late = layer < last

        def freed(*which):
            if layer > 0:
                for name in which:
                    load(layer - 1, name)

        if not late:
            freed(keys.gb)
        need(keys.down_w, keys.p, keys.v)

        def act_dots(n):
            zs[n % 2][:, :256] = lax.dot_general(
                low[...],
                r.down_w[n * 256 : (n + 1) * 256, :],
                (((1,), (1,)), ((), ())),
                preferred_element_type=F32,
            )

        def act_rest(n):
            if n < 4:
                turn_rows(r.v, wide_t, n)
            elif late:
                turn_rows(low, low_t, n - 4)
            cols = slice(n * 256, (n + 1) * 256)
            for chunk in range(sz.rows // 64):
                at = slice(chunk * 64, chunk * 64 + 64)
                p = r.p[at, cols]
                slope = normal_below(p) + ROOT_TAU * p * jnp.exp(-0.5 * p * p)
                gp[at, cols] = (zs[n % 2][at, :256] * slope).astype(BF16)

        in_turn(sz.inner // 256, act_dots, act_rest, lambda n: units.passed(0.6))
        freed(keys.down_w, keys.p, keys.v)
        if not late:
            up_grad(layer, unit + 2)
        need(keys.up_w, keys.y1, keys.u)

        def turn_u(n):
            for k in range(2):
                turn_rows(r.u, r.u_t, 2 * n + k)

        contract(gp, r.up_w, grad, sz.width, turn_u)
        freed(keys.u)
        freed(keys.up_w)
        units.passed(1.5)
        norm_back(r.y1, r.mlp_gain.at[layer : layer + 1], grad, gx, gy1, r.mlp_sum, sz.rows, 64, low)
        freed(keys.y1)
        need(keys.states)
        units.passed(2)
        need(keys.out_w, keys.a, keys.b)
        contract(low, r.out_w, ga, sz.hidden, lambda n: turn_rows(low, r.go_t, n))
        freed(keys.out_w)
        units.passed(1)
        if not late:
            out_grad(layer, unit + 4)
        flights = []
        for part, lanes in enumerate(parts):

            def totals(j, pair):
                at = tile(j, sz.group)
                if layer < last:
                    mask = jnp.concatenate([keep[at, :]] * (half // LANES), axis=1)
                    d = gate_weights(r.a[at, lanes], r.b[at, lanes])[0] * mask
                    decay[at, lanes] = d
                else:
                    d = decay[at, lanes]
                return pair[0] * d, d * (ga[at, lanes] + pair[1])

            one = jnp.ones((sz.group, half), F32)
            pair = steps_of(sz.steps, 2, totals, (one, jnp.zeros_like(one)), reverse=True)
            r.chunk_p[:, lanes] = pair[0]
            r.chunk_t[:, lanes] = pair[1]
            sends_settled(part)
            part_totals(r.chunk_p, r.chunk_t, sz, True, prefix, mine, lanes)
            flights.append(exchange_start(1, layer, part))
            carried = [units.expect(link, 16384) for link in ("core", "x", "x")]
            units.passed(0.8)
        need(keys.zc)
        if late:
            need(keys.gb)
            down_grad(layer, unit)
            up_grad(layer, unit + 2)
            out_grad(layer, unit + 4)
        unit += 5
        units.now = max(units.now, *carried)

        def gate_lanes(n):
            wide = 2 * LANES
            lanes = tile(n, wide)

            def walk(j, kept):
                m, bf, bi, bc = kept
                at = tile(j, sz.group)
                d = decay[at, lanes]
                q = ga[at, lanes] + m
                a, b, zc = r.a[at, lanes], r.b[at, lanes], r.zc[at, lanes]
                vm = jnp.concatenate([valid[at, :]] * 2, axis=1)
                km = jnp.concatenate([keep[at, :]] * 2, axis=1)
                fp, ip, inv = gate_weights(a, b)
                gf = q * (r.states[at, lanes] * km - zc * vm)
                parts = (
                    (gf * (a * inv) * fp).astype(BF16),
                    (-gf * (b * inv) * ip).astype(BF16),
                    (q * vm * ip).astype(BF16),
                )
                for part, value in enumerate(parts):
                    gz[at, pl.ds(pl.multiple_of(part * sz.hidden + n * wide, wide), wide)] = value
                return (d * q,) + tuple(
                    a + value.astype(F32) for a, value in zip((bf, bi, bc), parts)
                )

            zero = jnp.zeros((sz.group, wide), F32)
            _, *sums = steps_of(
                sz.steps, 4, walk, (enter[:, lanes], zero, zero, zero), reverse=True
            )
            for part, total in enumerate(sums):
                small[0, layer * 4 + part : layer * 4 + part + 1, lanes] = jnp.sum(
                    total, axis=0, keepdims=True
                )

        turns = sz.hidden // LANES // 4
        for part in range(2):
            exchange_end(*flights[part], True, part)
            over(turns, lambda n: gate_lanes(n + part * turns))
            units.passed(1.8)
        freed(keys.a, keys.b, keys.zc, keys.states)
        for k in range(2):
            units.room(unit + k)

        def gate_grad(b):
            cols = pl.ds(pl.multiple_of(b * 384, 128), 256)
            value = jnp.dot(r.u_t[...], gz[:, cols], preferred_element_type=F32)
            for s in range(4):
                for h in range(2):
                    for t in range(2):
                        at = place(unit + t, h, s // 2, b % 2, b // 2)
                        held[(unit + t) % HELD, s % 2, h, at] = value[
                            s * 128 + h * 64 : s * 128 + h * 64 + 64, t * 128 : t * 128 + 128
                        ]

        over(8, gate_grad)
        units.produced(3, unit, unit + 1)
        unit += 2
        units.room(unit)

        def gate_rest(z):
            right = jnp.concatenate(
                [
                    gz[:, pl.ds(pl.multiple_of((2 * z + y) * 384 + 256, 128), 128)]
                    for y in range(2)
                ],
                axis=1,
            )
            value = jnp.dot(r.u_t[...], right, preferred_element_type=F32)
            for s in range(4):
                for h in range(2):
                    for y in range(2):
                        at = place(unit, h, s // 2, y, z)
                        held[unit % HELD, s % 2, h, at] = value[
                            s * 128 + h * 64 : s * 128 + h * 64 + 64, y * 128 : y * 128 + 128
                        ]

        over(4, gate_rest)
        units.produced(1.5, unit)
        unit += 1
        need(keys.gate_w, keys.stream)
        contract(gz, r.gate_w, grad, sz.width)
        freed(keys.gate_w)
        units.passed(2.5)
        norm_back(r.stream, r.mix_gain.at[layer : layer + 1], grad, gy1, gx, r.mix_sum, sz.rows, 64, low)
        freed(keys.stream)
        row = slice(layer * 4 + 3, layer * 4 + 4)
        small[0, row, : sz.width] = jnp.sum(r.mix_sum[...], axis=0, keepdims=True)
        small[0, row, sz.width : 2 * sz.width] = jnp.sum(r.mlp_sum[...], axis=0, keepdims=True)
        units.passed(1.5)

    forward(0)
    for layer in range(1, layers):
        forward(layer)
    out_copies = from_steps(gy1, r.layer_out, r.out_sems)
    cast(low, gx)
    units.passed(2)
    for index, layer in enumerate(reversed(range(layers))):
        backward(layer, 8 * index)
    def small_done():
        total = small[STAGES]
        count = jnp.int32(0)
        for s in range(r.lens.shape[0]):
            for d in range(r.lens.shape[1]):
                count = count + r.lens[s, d]
        scale = 1.0 / (count.astype(F32) * sz.hidden)
        for layer in range(layers):
            one = slice(layer, layer + 1)
            for part in range(3):
                r.bias_out[one, part * sz.hidden : (part + 1) * sz.hidden] = total[
                    layer * 4 + part : layer * 4 + part + 1, : sz.hidden
                ]
            row = slice(layer * 4 + 3, layer * 4 + 4)
            r.mix_out[one, :] = total[row, : sz.width]
            r.mlp_out[one, :] = total[row, sz.width : 2 * sz.width]
            lanes = total[layer * 4 : layer * 4 + 1, sz.hidden : sz.hidden + LANES]
            r.forget_out[one, :] = jnp.sum(lanes, axis=1, keepdims=True) * scale + jnp.zeros(
                (1, LANES), F32
            )
        pairs = (
            (r.bias_out, r.gate_bias_grad),
            (r.mix_out, r.mix_gain_grad),
            (r.mlp_out, r.mlp_gain_grad),
            (r.forget_out, r.forget_mean),
        )
        for k, (src, dst) in enumerate(pairs):
            copy = pltpu.make_async_copy(src, dst, r.small_out_sems.at[k])
            copy.start()
            units.leaving.append(copy)

    units.small_done = small_done
    units.small_start()
    for copy in out_copies:
        copy.wait()
    out_copies = from_steps(gx, r.input_grad, r.out_sems)
    units.passed(1)
    units.drain()
    for copy in out_copies:
        copy.wait()
    for part in range(2):
        sends_settled(part)


def run_whole_step(sz, layers, named):
    lengths = named["lengths"]
    rows, d, h, f = sz.rows, sz.width, sz.hidden, sz.inner
    vm = lambda *dims, kind=F32: pltpu.VMEM(dims, kind)
    sems = pltpu.SemaphoreType
    spec = dict(gate_bias=VMEM, mix_gain=VMEM, mlp_gain=VMEM)
    outputs = dict(
        layer_out=(shape(rows, d), ANY),
        input_grad=(shape(rows, d), ANY),
        gate_weight_grad=(shape(layers, 128, 384), ANY),
        gate_bias_grad=(shape(layers, 3 * h), ANY),
        out_weight_grad=(shape(layers, 64, 256), ANY),
        up_weight_grad=(shape(layers, 128, 256), ANY),
        down_weight_grad=(shape(layers, 64, 512), ANY),
        mix_gain_grad=(shape(layers, d), ANY),
        mlp_gain_grad=(shape(layers, d), ANY),
        forget_mean=(shape(layers, LANES), ANY),
    )
    results = len(outputs)
    kept = dict(
        u=((rows, d), BF16),
        a=((rows, h), F32),
        b=((rows, h), F32),
        zc=((rows, h), F32),
        states=((rows + sz.group, h), F32),
        y1=((rows, d), F32),
        v=((rows, d), BF16),
        p=((rows, f), F32),
        gb=((rows, f), BF16),
        stream=((rows, d), F32),
    )
    scratch = {}
    for name, (dims, kind) in kept.items():
        outputs[name + "_save"] = (shape(layers - 1, *dims, kind=kind), ANY)
        scratch[name] = vm(*dims, kind=kind)
    scratch.update(
        gate_w=vm(d, 3 * h, kind=BF16),
        out_w=vm(h, d, kind=BF16),
        up_w=vm(d, f, kind=BF16),
        down_w=vm(f, d, kind=BF16),
        valid=vm(rows, LANES),
        keep=vm(rows, LANES),
        gx=vm(rows, d),
        low=vm(rows, d, kind=BF16),
        low_t=vm(d, rows, kind=BF16),
        wide_t=vm(d, rows, kind=BF16),
        u_t=vm(d, rows, kind=BF16),
        go_t=vm(d, rows, kind=BF16),
        hb=vm(rows, h, kind=BF16),
        z1=vm(rows, 768),
        drive=vm(rows, h),
        forget=vm(8, LANES),
        ga=vm(rows, h),
        gz=vm(rows, 3 * h, kind=BF16),
        grad=vm(rows, d),
        gy1=vm(rows, d),
        decay=vm(rows, h),
        chunk_p=vm(sz.group, h),
        chunk_t=vm(sz.group, h),
        prefix=vm(2, sz.group, h),
        enter=vm(sz.group, h),
        mine=vm(8, h),
        slots=vm(2, layers, sz.sections, 8, h),
        mlp_sum=vm(8, d),
        mix_sum=vm(8, d),
        held=vm(HELD, 2, 2, 16, BLOCK, LANES),
        small=vm(STAGES + 1, 8, SMALL),
        small_arrived=vm(STAGES, 8, SMALL),
        in_sems=sems.DMA((3,)),
        bias_out=vm(layers, 3 * h),
        mix_out=vm(layers, d),
        mlp_out=vm(layers, d),
        forget_out=vm(layers, LANES),
        small_out_sems=sems.DMA((4,)),
        result_sems=sems.DMA((8 * layers, 2)),
        lens=pltpu.SMEM(lengths.shape, jnp.int32),
        out_sems=sems.DMA((d // LANES,)),
        natural=vm(d // LANES, rows, LANES),
        load_sems=sems.DMA((len(kept) + 4,)),
        save_sems=sems.DMA((len(kept) + 4,)),
        pair_send=sems.DMA((2, layers, 2, sz.sections - 1)),
        pair_recv=sems.DMA((2, layers, 2, sz.sections - 1)),
        send_sems=sems.DMA((SENDS, 2 * STAGES - 1)),
        recv_sems=sems.DMA((max(RINGS), 2 * STAGES - 1)),
        credits=sems.REGULAR((2 * STAGES - 1, 8 * layers)),
        small_send=sems.DMA((STAGES,)),
        small_recv=sems.DMA((STAGES,)),
    )
    for stage in range(STAGES):
        scratch[f"arrived{stage}"] = vm(RINGS[stage], 2, 16 >> stage, BLOCK, LANES)
    names = list(named) + list(outputs) + list(scratch)
    out = pl.pallas_call(
        functools.partial(whole_step, sz, layers, names),
        out_shape=tuple(value for value, _ in outputs.values()),
        in_specs=[spec.get(name, ANY) for name in named],
        out_specs=[place_of for _, place_of in outputs.values()],
        scratch_shapes=list(scratch.values()),
        compiler_params=pltpu.CompilerParams(
            collective_id=4, has_side_effects=True, vmem_limit_bytes=LIMIT
        ),
        name="whole_step",
    )(*named.values())
    return out[:results]


def deliver_kernel(count, *refs):
    sources, targets, held = refs[:count], refs[count : 2 * count], refs[2 * count : 3 * count - 1]
    sems = refs[3 * count - 1]
    arrivals = [
        pltpu.make_async_copy(sources[i], held[i], sems.at[0, i]) for i in range(count - 1)
    ]
    departures = [
        pltpu.make_async_copy(held[i], targets[i], sems.at[1, i]) for i in range(count - 1)
    ]
    for copy in arrivals:
        copy.start()
    for layer in range(targets[-1].shape[0]):
        targets[-1][layer] = sources[-1][layer, 0]
    for arrival, departure in zip(arrivals, departures):
        arrival.wait()
        departure.start()
    for copy in departures:
        copy.wait()


def deliver(values):
    count = len(values)
    scalars = pl.BlockSpec(memory_space=pltpu.SMEM)
    shapes = [shape(*value.shape) for value in values[:-1]] + [shape(values[-1].shape[0])]
    return pl.pallas_call(
        functools.partial(deliver_kernel, count),
        out_shape=tuple(shapes),
        in_specs=[ANY] * (count - 1) + [scalars],
        out_specs=[ANY] * (count - 1) + [scalars],
        scratch_shapes=[pltpu.VMEM(value.shape, F32) for value in values[:-1]]
        + [pltpu.SemaphoreType.DMA((2, count - 1))],
        compiler_params=pltpu.CompilerParams(vmem_limit_bytes=LIMIT),
        name="deliver",
    )(*values)


def mask_kernel(sizes, lens, valid, keep):
    fill_masks(lens, valid, keep, sizes)


def body(
    activations,
    cotangent,
    lengths,
    gate_weight,
    gate_bias,
    out_weight,
    up_weight,
    down_weight,
    mix_gain,
    mlp_gain,
):
    micro, span, width = activations.shape
    layers = gate_weight.shape[0]
    sz = Sizes(
        micro, span, width, out_weight.shape[1], up_weight.shape[2], lax.axis_size("section")
    )

    blocks = (width // 4, 3 * sz.hidden // 8, width // 8, sz.inner // 4, sz.hidden // 4)
    axes = (lax.axis_size("section"), lax.axis_size("batch"))
    if axes == (4, 8) and blocks == (128, 384, 64, 512, 256):
        out = run_whole_step(
            sz,
            layers,
            dict(
                activations=activations.reshape(sz.rows, width),
                cotangent=cotangent.reshape(sz.rows, width),
                lengths=lengths.T,
                gate_bias=gate_bias,
                mix_gain=mix_gain,
                mlp_gain=mlp_gain,
                gate_hbm=gate_weight,
                out_hbm=out_weight,
                up_hbm=up_weight,
                down_hbm=down_weight,
            ),
        )
        stream_out, input_grad, gate_g, bias_g, out_g, up_g, down_g, *rest = deliver(out)
        return (
            stream_out.reshape(activations.shape),
            input_grad.reshape(activations.shape),
            gate_g,
            bias_g,
            out_g.transpose(0, 2, 1),
            up_g,
            down_g.transpose(0, 2, 1),
            *rest,
        )

    def arranged(value):
        value = value.astype(F32).reshape(micro, CHUNKS, sz.steps, width)
        return value.transpose(2, 0, 1, 3).reshape(sz.rows, width)

    def restored(value):
        value = value.reshape(sz.steps, micro, CHUNKS, width).transpose(1, 2, 0, 3)
        return value.reshape(micro, span, width)

    masks = pl.pallas_call(
        functools.partial(mask_kernel, sz),
        out_shape=(shape(sz.rows, LANES), shape(sz.rows, LANES)),
        in_specs=[pl.BlockSpec(memory_space=pltpu.SMEM)],
        out_specs=[VMEM] * 2,
        name="masks",
    )(lengths)
    weights = (gate_weight, out_weight, up_weight, down_weight)
    stream = arranged(activations)
    streams, saved, forgets = [], [], []
    for layer in range(layers):
        streams.append(stream)
        stream, *kept, forget, pairs = run_forward(
            sz,
            layer,
            stream,
            masks,
            gate_bias[layer : layer + 1],
            mix_gain[layer : layer + 1],
            mlp_gain[layer : layer + 1],
            weights,
        )
        saved.append((*kept, pairs))
        forgets.append(forget)
    layer_out = restored(stream)
    gx = arranged(cotangent)
    true_count = jnp.sum(lengths).astype(F32)
    forgets = [jnp.sum(forget) for forget in forgets]
    sums, small = [None] * layers, [None] * layers
    for layer in reversed(range(layers)):
        gx, gate_g, out_g, up_g, down_g, bias_g, mix_g, mlp_g = run_backward(
            sz,
            layer,
            gx,
            streams[layer],
            masks,
            mix_gain[layer : layer + 1],
            mlp_gain[layer : layer + 1],
            saved[layer],
            weights,
        )
        sums[layer] = (gate_g, out_g.T, up_g, down_g.T)
        small[layer] = tuple(jnp.sum(part, axis=0) for part in (bias_g, mix_g, mlp_g))
    input_grad = restored(gx)
    stacked = tuple(jnp.stack(parts) for parts in zip(*sums))
    partial_sums = lax.psum_scatter(stacked, "section", scatter_dimension=1, tiled=True)
    large = lax.psum_scatter(partial_sums, "batch", scatter_dimension=2, tiled=True)
    bias_grad, mix_grad, mlp_grad = (jnp.stack(parts) for parts in zip(*small))
    bias_grad, mix_grad, mlp_grad, forget = lax.psum(
        (bias_grad, mix_grad, mlp_grad, jnp.stack(forgets)), ("section", "batch")
    )
    forget_mean = forget / (true_count * sz.hidden)
    return (
        layer_out,
        input_grad,
        large[0],
        bias_grad,
        large[1],
        large[2],
        large[3],
        mix_grad,
        mlp_grad,
        forget_mean,
    )


def solution(mesh):
    stream = P("batch", "section", None)
    block = P(None, "section", "batch")
    return jax.shard_map(
        body,
        mesh=mesh,
        in_specs=(stream, stream) + (P(),) * 8,
        out_specs=(stream, stream, block, P(), block, block, block, P(), P(), P()),
        check_vma=False,
    )
```

```python
import functools
import types

import jax
import jax.numpy as jnp
from jax import lax
from jax.experimental import pallas as pl
from jax.experimental.pallas import tpu as pltpu
from jax.sharding import PartitionSpec as P

epsilon = 1e-06
MESH = pl.DeviceIdType.MESH
F32, BF16 = jnp.float32, jnp.bfloat16
CHUNKS = 8
LANES = 128
ROOT_HALF = 0.7071067811865476
ROOT_TAU = 0.3989422804014327


def tile(index, size):
    return pl.ds(pl.multiple_of(index * size, size), size)


def inverse(value):
    r = pltpu.reciprocal(value, approx=True)
    return r * (2.0 - value * r)


def normal_below(p):
    return 0.5 + 0.5 * lax.erf(p * ROOT_HALF)


def steps_of(count, unroll, one, start, reverse=False):
    def turn(i, carry):
        for k in range(unroll):
            at = i * unroll + k
            carry = one(count - 1 - at if reverse else at, carry)
        return carry

    return lax.fori_loop(0, count // unroll, turn, start)


def odds(zf, zi):
    return jnp.exp(jnp.minimum(-zf, 86.0)), jnp.exp(jnp.minimum(-zi, 86.0))


def gate_weights(a, b):
    inv = inverse(2.0 + a + b)
    return (1.0 + b) * inv, (1.0 + a) * inv, inv


def greet_section(sections):
    me = lax.axis_index("section")
    barrier = pltpu.get_barrier_semaphore()
    for hop in range(1, sections):
        pl.semaphore_signal(
            barrier, inc=1, device_id={"section": lax.rem(me + hop, sections)}, device_id_type=MESH
        )
    pl.semaphore_wait(barrier, sections - 1)


def exchange(mine, slots, send_sems, recv_sems, sections):
    me = lax.axis_index("section")
    copies = []
    for hop in range(1, sections):
        copies.append(
            pltpu.make_async_remote_copy(
                src_ref=mine,
                dst_ref=slots.at[me],
                send_sem=send_sems.at[hop - 1],
                recv_sem=recv_sems.at[hop - 1],
                device_id={"section": lax.rem(me + hop, sections)},
                device_id_type=MESH,
            )
        )
    for copy in copies:
        copy.start()
    slots[me] = mine[...]
    for copy in copies:
        copy.wait()


def norm_rows(stream, gain, low, rows, step):
    def one(i, carry):
        at = tile(i, step)
        x = stream[at, :]
        r = lax.rsqrt(jnp.mean(x * x, axis=-1, keepdims=True) + epsilon)
        low[at, :] = (x * r * gain[...]).astype(BF16)
        return carry

    lax.fori_loop(0, rows // step, one, 0)


def norm_back(stream, gain, grad, through, out, gain_sum, rows, step, low=None):
    width = stream.shape[1]

    def one(i, total):
        at = tile(i, step)
        x = stream[at, :]
        r = lax.rsqrt(jnp.mean(x * x, axis=-1, keepdims=True) + epsilon)
        n = x * r
        g = grad[at, :]
        a = g * gain[...]
        value = through[at, :] + r * (a - n * jnp.mean(a * n, axis=-1, keepdims=True))
        out[at, :] = value
        if low is not None:
            low[at, :] = value.astype(BF16)
        return total + jnp.sum((g * n).reshape(step // 8, 8, width), axis=0)

    gain_sum[...] = lax.fori_loop(0, rows // step, one, jnp.zeros((8, width), F32))


def fill_masks(lens, valid, keep, sizes, turned=False):
    section = lax.axis_index("section")
    group = lax.axis_index("batch")
    starts, totals = [], []
    for s in range(sizes.micro):
        total, begin = 0, []
        for d in range(lens.shape[0 if turned else 1]):
            row = group * sizes.micro + s
            length = lens[d, row] if turned else lens[row, d]
            begin.append(jnp.where(length > 0, total, -1))
            total = total + length
        starts.append(begin)
        totals.append(total)
    chunk_place = lax.broadcasted_iota(jnp.int32, (8, LANES), 0) * sizes.steps

    def one(j, carry):
        for s in range(sizes.micro):
            place = section * sizes.span + j + chunk_place
            true = place < totals[s]
            first = place == starts[s][0]
            for begin in starts[s][1:]:
                first = first | (place == begin)
            at = pl.ds(pl.multiple_of(j * sizes.group + s * 8, 8), 8)
            valid[at, :] = jnp.where(true, 1.0, 0.0)
            keep[at, :] = jnp.where(true & jnp.logical_not(first), 1.0, 0.0)
        return carry

    lax.fori_loop(0, sizes.steps, one, 0)


def scan_totals(first, second, sizes, reverse, prefix, chunk, mine):
    for s in range(sizes.micro):
        p = jnp.ones((1, sizes.hidden), F32)
        t = jnp.zeros((1, sizes.hidden), F32)
        for c in reversed(range(CHUNKS)) if reverse else range(CHUNKS):
            at = s * 8 + c
            prefix[0, at : at + 1, :] = p
            prefix[1, at : at + 1, :] = t
            pc = first[at : at + 1, :]
            t = pc * t + second[at : at + 1, :]
            p = p * pc
        mine[s : s + 1, :] = p
        mine[sizes.micro + s : sizes.micro + s + 1, :] = t


def scan_enter(slots, prefix, enter, sizes, reverse):
    me = lax.axis_index("section")
    for s in range(sizes.micro):
        a = jnp.zeros((1, sizes.hidden), F32)
        order = range(sizes.sections - 1, 0, -1) if reverse else range(sizes.sections - 1)
        for k in order:
            reached = k > me if reverse else k < me
            pk = slots[k, s : s + 1, :]
            tk = slots[k, sizes.micro + s : sizes.micro + s + 1, :]
            a = jnp.where(reached, pk * a + tk, a)
        at = slice(s * 8, s * 8 + 8)
        enter[at, :] = prefix[0, at, :] * a + prefix[1, at, :]


def part_totals(first, second, sizes, reverse, prefix, mine, lanes):
    for s in range(sizes.micro):
        p = jnp.ones((1, lanes.stop - lanes.start), F32)
        t = jnp.zeros_like(p)
        for c in reversed(range(CHUNKS)) if reverse else range(CHUNKS):
            at = s * 8 + c
            prefix[0, at : at + 1, lanes] = p
            prefix[1, at : at + 1, lanes] = t
            pc = first[at : at + 1, lanes]
            t = pc * t + second[at : at + 1, lanes]
            p = p * pc
        mine[s : s + 1, lanes] = p
        mine[sizes.micro + s : sizes.micro + s + 1, lanes] = t


def part_enter(slots, prefix, enter, sizes, reverse, lanes):
    me = lax.axis_index("section")
    for s in range(sizes.micro):
        a = jnp.zeros((1, lanes.stop - lanes.start), F32)
        order = range(sizes.sections - 1, 0, -1) if reverse else range(sizes.sections - 1)
        for k in order:
            reached = k > me if reverse else k < me
            pk = slots[k, s : s + 1, lanes]
            tk = slots[k, sizes.micro + s : sizes.micro + s + 1, lanes]
            a = jnp.where(reached, pk * a + tk, a)
        at = slice(s * 8, s * 8 + 8)
        enter[at, lanes] = prefix[0, at, lanes] * a + prefix[1, at, lanes]


class Sizes:
    def __init__(self, micro, span, width, hidden, inner, sections):
        self.micro, self.span, self.width = micro, span, width
        self.hidden, self.inner, self.sections = hidden, inner, sections
        self.rows = micro * span
        self.steps = span // CHUNKS
        self.group = micro * CHUNKS


def forward_kernel(
    sizes,
    layer,
    stream,
    valid,
    keep,
    bias,
    mix_gain,
    mlp_gain,
    gate_hbm,
    out_hbm,
    up_hbm,
    down_hbm,
    next_stream,
    u,
    sf_out,
    si_out,
    zc_out,
    states,
    y1,
    v,
    p_out,
    gb,
    forget,
    pair_slots,
    gate_w,
    out_w,
    up_w,
    down_w,
    z,
    decay,
    drive,
    hb,
    chunk_p,
    chunk_t,
    prefix,
    enter,
    mine,
    weight_sems,
    send_sems,
    recv_sems,
):
    sz = sizes
    loads = [
        pltpu.make_async_copy(src.at[layer], dst, weight_sems.at[i])
        for i, (src, dst) in enumerate(
            ((gate_hbm, gate_w), (out_hbm, out_w), (up_hbm, up_w), (down_hbm, down_w))
        )
    ]
    for load in loads:
        load.start()
    greet_section(sz.sections)
    mine[...] = jnp.zeros_like(mine)
    norm_rows(stream, mix_gain, u, sz.rows, 64)
    loads[0].wait()
    forget[...] = jnp.zeros_like(forget)
    hw = 256

    def gate_tile(n, carry):
        for part in range(3):
            cols = pl.ds(pl.multiple_of(part * sz.hidden + n * hw, hw), hw)
            z[:, part * hw : (part + 1) * hw] = (
                jnp.dot(u[...], gate_w[:, cols], preferred_element_type=F32) + bias[:, cols]
            )

        def one(i, inner):
            at = tile(i, 64)
            for lane in range(hw // LANES):
                src = lambda part: z[
                    at, part * hw + lane * LANES : part * hw + (lane + 1) * LANES
                ]
                dst = pl.ds(pl.multiple_of(n * hw + lane * LANES, LANES), LANES)
                a = jnp.exp(jnp.minimum(-src(0), 86.0))
                b = jnp.exp(jnp.minimum(-src(1), 86.0))
                zc = src(2)
                fp, ip, _ = gate_weights(a, b)
                vm = valid[at, :]
                decay[at, dst] = fp * keep[at, :]
                drive[at, dst] = ip * zc * vm
                sf_out[at, dst] = a
                si_out[at, dst] = b
                zc_out[at, dst] = zc
                forget[...] += jnp.sum((fp * vm).reshape(8, 8, LANES), axis=0)
            return inner

        lax.fori_loop(0, sz.rows // 64, one, 0)
        return carry

    lax.fori_loop(0, sz.hidden // hw, gate_tile, 0)
    half = sz.hidden // 2
    for part in range(2):
        lanes = slice(part * half, (part + 1) * half)

        def totals(j, pair):
            at = tile(j, sz.group)
            d = decay[at, lanes]
            return pair[0] * d, pair[1] * d + drive[at, lanes]

        one = jnp.ones((sz.group, half), F32)
        pair = steps_of(sz.steps, 4, totals, (one, jnp.zeros_like(one)))
        chunk_p[:, lanes] = pair[0]
        chunk_t[:, lanes] = pair[1]
    scan_totals(chunk_p, chunk_t, sz, False, prefix, None, mine)
    exchange(mine, pair_slots, send_sems, recv_sems, sz.sections)
    scan_enter(pair_slots, prefix, enter, sz, False)
    states[0 : sz.group, :] = enter[...]
    for part in range(2):
        lanes = slice(part * half, (part + 1) * half)

        def walk(j, h):
            at = tile(j, sz.group)
            h = decay[at, lanes] * h + drive[at, lanes]
            states[tile(j + 1, sz.group), lanes] = h
            hb[at, lanes] = h.astype(BF16)
            return h

        steps_of(sz.steps, 4, walk, enter[:, lanes])
    loads[1].wait()

    def out_tile(n, carry):
        cols = tile(n, 256)
        y1[:, cols] = stream[:, cols] + jnp.dot(
            hb[...], out_w[:, cols], preferred_element_type=F32
        )
        return carry

    lax.fori_loop(0, sz.width // 256, out_tile, 0)
    norm_rows(y1, mlp_gain, v, sz.rows, 64)
    loads[2].wait()

    def up_tile(n, carry):
        cols = tile(n, 256)
        p_out[:, cols] = jnp.dot(v[...], up_w[:, cols], preferred_element_type=F32)

        def one(i, inner):
            at = tile(i, 64)
            p = p_out[at, cols]
            gb[at, cols] = (p * normal_below(p)).astype(BF16)
            return inner

        lax.fori_loop(0, sz.rows // 64, one, 0)
        return carry

    lax.fori_loop(0, sz.inner // 256, up_tile, 0)
    loads[3].wait()

    def down_tile(n, carry):
        cols = tile(n, 256)
        next_stream[:, cols] = y1[:, cols] + jnp.dot(
            gb[...], down_w[:, cols], preferred_element_type=F32
        )
        return carry

    lax.fori_loop(0, sz.width // 256, down_tile, 0)


def backward_kernel(
    sizes,
    layer,
    gx,
    stream,
    valid,
    keep,
    mix_gain,
    mlp_gain,
    u,
    sf_in,
    si_in,
    zc_in,
    states,
    y1,
    v,
    p_in,
    gb,
    pair_slots,
    gate_hbm,
    out_hbm,
    up_hbm,
    down_hbm,
    next_gx,
    gate_grad,
    out_grad,
    up_grad,
    down_grad,
    bias_sum,
    mix_sum,
    mlp_sum,
    gate_w,
    out_w,
    up_w,
    down_w,
    low,
    low_t,
    wide_t,
    hb,
    ga,
    gp,
    gz,
    grad,
    gy1,
    decay,
    chunk_p,
    chunk_t,
    prefix,
    enter,
    mine,
    slots,
    weight_sems,
    send_sems,
    recv_sems,
):
    sz = sizes
    loads = [
        pltpu.make_async_copy(src.at[layer], dst, weight_sems.at[i])
        for i, (src, dst) in enumerate(
            ((gate_hbm, gate_w), (out_hbm, out_w), (up_hbm, up_w), (down_hbm, down_w))
        )
    ]
    for load in reversed(loads):
        load.start()
    greet_section(sz.sections)
    mine[...] = jnp.zeros_like(mine)

    def cast(i, carry):
        at = tile(i, 64)
        low[at, :] = gx[at, :].astype(BF16)
        return carry

    lax.fori_loop(0, sz.rows // 64, cast, 0)
    low_t[...] = low[...].T

    def weight_grad(left_t, right, dst, step):
        def one(n, carry):
            cols = tile(n, step)
            dst[:, cols] = jnp.dot(left_t[...], right[:, cols], preferred_element_type=F32)
            return carry

        lax.fori_loop(0, right.shape[1] // step, one, 0)

    weight_grad(low_t, gb, down_grad, 256)
    loads[3].wait()

    def act_tile(n, carry):
        cols = tile(n, 256)
        ga[:, :256] = lax.dot_general(
            low[...], down_w[cols, :], (((1,), (1,)), ((), ())), preferred_element_type=F32
        )

        def one(i, inner):
            at = tile(i, 64)
            p = p_in[at, cols]
            slope = normal_below(p) + ROOT_TAU * p * jnp.exp(-0.5 * p * p)
            gp[at, cols] = (ga[at, :256] * slope).astype(BF16)
            return inner

        lax.fori_loop(0, sz.rows // 64, one, 0)
        return carry

    lax.fori_loop(0, sz.inner // 256, act_tile, 0)
    wide_t[...] = v[...].T
    weight_grad(wide_t, gp, up_grad, 256)
    loads[2].wait()

    def contract(left, weight, dst, step):
        def one(n, carry):
            cols = tile(n, step)
            dst[:, cols] = lax.dot_general(
                left[...], weight[cols, :], (((1,), (1,)), ((), ())), preferred_element_type=F32
            )
            return carry

        lax.fori_loop(0, weight.shape[0] // step, one, 0)

    contract(gp, up_w, grad, 256)
    norm_back(y1, mlp_gain, grad, gx, gy1, mlp_sum, sz.rows, 64)

    def cast_more(i, carry):
        at = tile(i, 64)
        low[at, :] = gy1[at, :].astype(BF16)
        return carry

    lax.fori_loop(0, sz.rows // 64, cast_more, 0)

    def cast_state(i, carry):
        hb[tile(i, sz.group), :] = states[tile(i + 1, sz.group), :].astype(BF16)
        return carry

    lax.fori_loop(0, sz.steps, cast_state, 0)
    low_t[...] = low[...].T
    weight_grad(low_t, hb, out_grad, 256)
    loads[1].wait()
    contract(low, out_w, ga, 256)
    half = sz.hidden // 2
    for part in range(2):
        lanes = slice(part * half, (part + 1) * half)

        def totals(i, pair):
            at = tile(sz.steps - 1 - i, sz.group)
            mask = jnp.concatenate([keep[at, :]] * (half // LANES), axis=1)
            d = gate_weights(sf_in[at, lanes], si_in[at, lanes])[0] * mask
            decay[at, lanes] = d
            return pair[0] * d, d * (ga[at, lanes] + pair[1])

        pair = lax.fori_loop(
            0,
            sz.steps,
            totals,
            (jnp.ones((sz.group, half), F32), jnp.zeros((sz.group, half), F32)),
        )
        chunk_p[:, lanes] = pair[0]
        chunk_t[:, lanes] = pair[1]
    scan_totals(chunk_p, chunk_t, sz, True, prefix, None, mine)
    exchange(mine, slots, send_sems, recv_sems, sz.sections)
    scan_enter(slots, prefix, enter, sz, True)

    def gate_lane(n, carry):
        lanes = tile(n, LANES)

        def walk(i, kept):
            m, bf, bi, bc = kept
            j = sz.steps - 1 - i
            at = tile(j, sz.group)
            d = decay[at, lanes]
            q = ga[at, lanes] + m
            a = sf_in[at, lanes]
            b = si_in[at, lanes]
            zc = zc_in[at, lanes]
            vm = valid[at, :]
            fp, ip, inv = gate_weights(a, b)
            gf = q * (states[at, lanes] * keep[at, :] - zc * vm)
            gzf = (gf * (a * inv) * fp).astype(BF16)
            gzi = (-gf * (b * inv) * ip).astype(BF16)
            gzc = (q * vm * ip).astype(BF16)
            gz[at, lanes] = gzf
            gz[at, pl.ds(pl.multiple_of(sz.hidden + n * LANES, LANES), LANES)] = gzi
            gz[at, pl.ds(pl.multiple_of(2 * sz.hidden + n * LANES, LANES), LANES)] = gzc
            return (
                d * q,
                bf + gzf.astype(F32),
                bi + gzi.astype(F32),
                bc + gzc.astype(F32),
            )

        zero = jnp.zeros((sz.group, LANES), F32)
        _, bf, bi, bc = lax.fori_loop(0, sz.steps, walk, (enter[:, lanes], zero, zero, zero))
        for part, total in enumerate((bf, bi, bc)):
            where = pl.ds(pl.multiple_of(part * sz.hidden + n * LANES, LANES), LANES)
            bias_sum[:, where] = jnp.sum(total.reshape(sz.group // 8, 8, LANES), axis=0)
        return carry

    lax.fori_loop(0, sz.hidden // LANES, gate_lane, 0)
    wide_t[...] = u[...].T
    weight_grad(wide_t, gz, gate_grad, 256)
    loads[0].wait()
    contract(gz, gate_w, grad, 256)
    norm_back(stream, mix_gain, grad, gy1, next_gx, mix_sum, sz.rows, 64)


VMEM = pl.BlockSpec(memory_space=pltpu.VMEM)
ANY = pl.BlockSpec(memory_space=pl.ANY)
LIMIT = 63 * 2**20


def shape(*dims, kind=F32):
    return jax.ShapeDtypeStruct(dims, kind)


def exchange_scratch(sz):
    return [
        pltpu.SemaphoreType.DMA((4,)),
        pltpu.SemaphoreType.DMA((sz.sections - 1,)),
        pltpu.SemaphoreType.DMA((sz.sections - 1,)),
    ]


def weight_scratch(sz):
    return [
        pltpu.VMEM((sz.width, 3 * sz.hidden), BF16),
        pltpu.VMEM((sz.hidden, sz.width), BF16),
        pltpu.VMEM((sz.width, sz.inner), BF16),
        pltpu.VMEM((sz.inner, sz.width), BF16),
    ]


def scan_scratch(sz):
    return [
        pltpu.VMEM((sz.group, sz.hidden), F32),
        pltpu.VMEM((sz.group, sz.hidden), F32),
        pltpu.VMEM((2, sz.group, sz.hidden), F32),
        pltpu.VMEM((sz.group, sz.hidden), F32),
        pltpu.VMEM((8, sz.hidden), F32),
    ]


def run_forward(sz, layer, stream, masks, bias, mix_gain, mlp_gain, weights):
    r, d, h, f = sz.rows, sz.width, sz.hidden, sz.inner
    return pl.pallas_call(
        functools.partial(forward_kernel, sz, layer),
        out_shape=(
            shape(r, d),
            shape(r, d, kind=BF16),
            shape(r, h),
            shape(r, h),
            shape(r, h),
            shape(r + sz.group, h),
            shape(r, d),
            shape(r, d, kind=BF16),
            shape(r, f),
            shape(r, f, kind=BF16),
            shape(8, LANES),
            shape(sz.sections, 8, h),
        ),
        in_specs=[VMEM] * 6 + [ANY] * 4,
        out_specs=[VMEM] * 12,
        scratch_shapes=weight_scratch(sz)
        + [
            pltpu.VMEM((r, 3 * 256), F32),
            pltpu.VMEM((r, h), F32),
            pltpu.VMEM((r, h), F32),
            pltpu.VMEM((r, h), BF16),
        ]
        + scan_scratch(sz)
        + exchange_scratch(sz),
        compiler_params=pltpu.CompilerParams(
            collective_id=layer, has_side_effects=True, vmem_limit_bytes=LIMIT
        ),
        name=f"forward_{layer}",
    )(stream, *masks, bias, mix_gain, mlp_gain, *weights)


def run_backward(sz, layer, gx, stream, masks, mix_gain, mlp_gain, saved, weights):
    r, d, h, f = sz.rows, sz.width, sz.hidden, sz.inner
    return pl.pallas_call(
        functools.partial(backward_kernel, sz, layer),
        out_shape=(
            shape(r, d),
            shape(d, 3 * h),
            shape(d, h),
            shape(d, f),
            shape(d, f),
            shape(8, 3 * h),
            shape(8, d),
            shape(8, d),
        ),
        in_specs=[VMEM] * 16 + [ANY] * 4,
        out_specs=[VMEM] * 8,
        scratch_shapes=weight_scratch(sz)
        + [
            pltpu.VMEM((r, d), BF16),
            pltpu.VMEM((d, r), BF16),
            pltpu.VMEM((d, r), BF16),
            pltpu.VMEM((r, h), BF16),
            pltpu.VMEM((r, h), F32),
            pltpu.VMEM((r, f), BF16),
            pltpu.VMEM((r, 3 * h), BF16),
            pltpu.VMEM((r, d), F32),
            pltpu.VMEM((r, d), F32),
            pltpu.VMEM((r, h), F32),
        ]
        + scan_scratch(sz)
        + [pltpu.VMEM((sz.sections, 8, h), F32)]
        + exchange_scratch(sz),
        compiler_params=pltpu.CompilerParams(
            collective_id=2 + layer, has_side_effects=True, vmem_limit_bytes=LIMIT
        ),
        name=f"backward_{layer}",
    )(gx, stream, *masks, mix_gain, mlp_gain, *saved, *weights)


BLOCK = 64
HELD = 3
RINGS = (4, 5, 5, 16, 16)
SENDS = 16
STAGES = 5
WINDOW = 4
DELAY = 1.5
SMALL = 1280


EVEN = ((0, 2, 1, 3), (1, 2, 0, 3))
ORDERS = [EVEN] * 16


class Units:
    def __init__(self, count, refs):
        self.count = count
        self.__dict__.update(vars(refs))
        self.arrived = [getattr(refs, f"arrived{stage}") for stage in range(STAGES)]
        section, batch = lax.axis_index("section"), lax.axis_index("batch")
        core, x = section % 2, section // 2
        y, za, zb = batch % 2, (batch // 2) % 2, batch // 4
        self.core = core
        self.where = (x, y, za, zb)
        self.partner = {
            "core": {"section": section + 1 - 2 * core},
            "x": {"section": section + 2 - 4 * x},
            "y": {"batch": batch + 1 - 2 * y},
            "za": {"batch": batch + 2 - 4 * za},
            "zb": {"batch": batch + 4 - 8 * zb},
        }
        self.now = 0.0
        self.links = ("core", "x", "y", "z")
        self.free_at = dict.fromkeys(self.links, 0.0)
        self.flying = dict.fromkeys(self.links, 0)
        self.queues = {link: [] for link in self.links}
        self.ready = {}
        self.summed = set()
        self.copies = {}
        self.small_left = None
        self.leaving = []

    def greet(self):
        section = lax.axis_index("section")
        others = [self.partner["y"], self.partner["za"], self.partner["zb"]]
        others += [{"section": lax.rem(section + hop, 4)} for hop in range(1, 4)]
        for other in others:
            pl.semaphore_signal(
                pltpu.get_barrier_semaphore(), inc=1, device_id=other, device_id_type=MESH
            )

    def greeted(self):
        pl.semaphore_wait(pltpu.get_barrier_semaphore(), 6)

    def name(self, unit, stage, half):
        return "core" if stage == 0 else ("x", "y", "za", "zb")[ORDERS[unit][half][stage - 1]]

    def link(self, unit, stage, half):
        name = self.name(unit, stage, half)
        return "z" if name[0] == "z" else name

    def bit(self, unit, stage, half):
        return self.where[ORDERS[unit][half][stage - 1]]

    def arrival(self, unit, stage, half):
        ref = self.arrived[stage].at[unit % RINGS[stage]]
        return ref if stage == 0 else ref.at[half]

    def copy(self, unit, stage, half):
        at = 0 if stage == 0 else 2 * stage - 1 + half
        if stage == 0:
            src = self.held.at[unit % HELD, 1 - self.core]
        else:
            count = 16 >> stage
            src = self.arrived[stage - 1].at[unit % RINGS[stage - 1], half]
            src = src.at[pl.ds((1 - self.bit(unit, stage, half)) * count, count)]
        return pltpu.make_async_remote_copy(
            src_ref=src,
            dst_ref=self.arrival(unit, stage, half),
            send_sem=self.send_sems.at[unit % SENDS, at],
            recv_sem=self.recv_sems.at[unit % RINGS[stage], at],
            device_id=self.partner[self.name(unit, stage, half)],
            device_id_type=MESH,
        )

    def has_place(self, unit, stage, half):
        before = unit - RINGS[stage]
        if before < 0:
            return True
        if stage == 0:
            return (before, 1, 0) in self.summed and (before, 1, 1) in self.summed
        return (before, min(stage + 1, STAGES - 1), half) in self.summed

    def credit(self, unit, stage, half):
        after = unit + RINGS[stage]
        if after < self.count:
            pl.semaphore_signal(
                self.credits.at[0 if stage == 0 else 2 * stage - 1 + half, after],
                inc=1,
                device_id=self.partner[self.name(after, stage, half)],
                device_id_type=MESH,
            )

    def pump(self):
        for link, queue in self.queues.items():
            while self.flying[link] < WINDOW:
                key = next((key for key in queue if self.has_place(*key)), None)
                if key is None:
                    break
                queue.remove(key)
                self.flying[link] += 1
                unit, stage, half = key
                if unit >= RINGS[stage]:
                    at = 0 if stage == 0 else 2 * stage - 1 + half
                    pl.semaphore_wait(self.credits.at[at, unit], 1)
                self.copies[key] = self.copy(*key)
                self.copies[key].start()
                blocks = 32 if stage == 0 else 16 >> stage
                self.ready[key] = self.expect(link, blocks * BLOCK * LANES * 4)

    def expect(self, link, size):
        rate = 250e3 if link == "core" else 45e3
        self.free_at[link] = max(self.now, self.free_at[link]) + size / rate
        return self.free_at[link] + DELAY

    def push(self, unit, stage, half):
        self.queues[self.link(unit, stage, half)].append((unit, stage, half))
        self.pump()

    def produced(self, us, *which):
        self.now += us
        for unit in which:
            self.push(unit, 0, 0)
        self.passed(0)

    def add(self, dst, src, count):
        turn = min(count, 4)

        def one(i, carry):
            for k in range(turn):
                dst[i * turn + k] += src[i * turn + k]
            return carry

        if count == turn:
            one(0, 0)
        else:
            lax.fori_loop(0, count // turn, one, 0)

    def step(self, unit, stage, half):
        key = (unit, stage, half)
        del self.ready[key]
        self.copies[key].wait_recv()
        here = self.arrival(unit, stage, half)
        if stage == 0:
            for h in range(2):
                self.add(here.at[h], self.held.at[unit % HELD, self.core, h], 16)
        else:
            count = 16 >> stage
            before = self.arrived[stage - 1].at[unit % RINGS[stage - 1], half]
            self.add(here, before.at[pl.ds(self.bit(unit, stage, half) * count, count)], count)
            self.copies.pop(key).wait_send()
        self.summed.add(key)
        self.flying[self.link(unit, stage, half)] -= 1
        self.now += 0.25
        if stage > 1 or (unit, 1, 1 - half) in self.summed:
            if stage > 0:
                self.credit(unit, stage - 1, half if stage > 1 else 0)
        if stage == 0:
            for h in range(2):
                self.push(unit, 1, h)
        elif stage < STAGES - 1:
            self.push(unit, stage + 1, half)
        else:
            self.finish(unit, half, here.at[0])
            self.credit(unit, stage, half)
        self.pump()

    def finish(self, unit, half, block):
        layer, k = self.count // 8 - 1 - unit // 8, unit % 8
        if k < 2 or k == 4:
            ref, at = (self.down_weight_grad, k) if k < 2 else (self.out_weight_grad, 0)
            to = ref.at[layer, :, at * 256 + half * 128 : at * 256 + half * 128 + 128]
        else:
            ref, at = (self.up_weight_grad, k - 2) if k < 4 else (self.gate_weight_grad, k - 5)
            rows = slice(half * BLOCK, half * BLOCK + BLOCK)
            to = ref.at[layer, rows, at * LANES : at * LANES + LANES]
        copy = pltpu.make_async_copy(block, to, self.result_sems.at[unit, half])
        copy.start()
        self.leaving.append(copy)

    def small_copy(self, stage):
        name = ("core", "x", "y", "za", "zb")[stage]
        return pltpu.make_async_remote_copy(
            src_ref=self.small.at[stage],
            dst_ref=self.small_arrived.at[stage],
            send_sem=self.small_send.at[stage],
            recv_sem=self.small_recv.at[stage],
            device_id=self.partner[name],
            device_id_type=MESH,
        )

    def small_start(self):
        self.small_left = 0
        self.small_copies = [self.small_copy(0)]
        self.small_copies[0].start()
        self.small_ready = self.now + 3.0

    def small_step(self):
        stage = self.small_left
        self.small_copies[stage].wait_recv()
        self.small[stage + 1] = self.small[stage] + self.small_arrived[stage]
        self.small_left += 1
        if self.small_left < STAGES:
            self.small_copies.append(self.small_copy(self.small_left))
            self.small_copies[-1].start()
            self.small_ready = self.now + 3.0
        else:
            for copy in self.small_copies:
                copy.wait_send()
            self.small_done()

    def open(self, unit, stage, half):
        halves = range(2) if stage == 0 else (half,)
        before = unit - RING
        return (
            before < 0
            or stage == STAGES - 1
            or all((before, stage + 1, h) in self.consumed for h in halves)
        )

    def next(self):
        best = min(self.ready.items(), key=lambda item: (item[1], item[0]), default=None)
        small = self.small_left is not None and self.small_left < STAGES
        if small and (best is None or self.small_ready <= best[1]):
            return self.small_ready, None
        return (best[1], best[0]) if best else None

    def take(self, item):
        self.now = max(self.now, item[0])
        if item[1] is None:
            self.small_step()
        else:
            self.step(*item[1])

    def passed(self, us):
        self.now += us
        while (item := self.next()) and item[0] <= self.now:
            self.take(item)

    def room(self, unit):
        before = (unit - HELD, 0, 0)
        while unit >= HELD and before not in self.summed:
            self.take(self.next())
        if before in self.copies:
            self.copies.pop(before).wait_send()

    def drain(self):
        while item := self.next():
            self.take(item)
        for key in list(self.copies):
            self.copies.pop(key).wait_send()
        for copy in self.leaving:
            copy.wait()


def place(unit, half, x, y, z):
    return spot(unit, half, (x, y, z % 2, z // 2))


def spot(unit, half, where):
    order = ORDERS[unit][half]
    return where[order[0]] * 8 + where[order[1]] * 4 + where[order[2]] * 2 + where[order[3]]


def strided(start, steps):
    return pl.ds(start, CHUNKS, stride=steps)


def whole_step(sz, layers, names, *args):
    r = types.SimpleNamespace(**dict(zip(names, args)))
    units = Units(8 * layers, r)
    valid, keep, low, low_t, wide_t = r.valid, r.keep, r.low, r.low_t, r.wide_t
    hb, ga, gz, grad, gy1, gx = r.hb, r.ga, r.gz, r.grad, r.gy1, r.gx
    gp = gz.at[:, : sz.inner]
    decay, enter, prefix, mine = r.decay, r.enter, r.prefix, r.mine
    small, held = r.small, r.held
    natural = r.natural
    last = layers - 1
    half = sz.hidden // 2
    zs = (ga.at[:, :768], r.z1)
    drive = r.drive
    homes = dict(gate_w=r.gate_hbm, out_w=r.out_hbm, up_w=r.up_hbm, down_w=r.down_hbm)
    homes.update(u=r.u_save, a=r.a_save, b=r.b_save, zc=r.zc_save, states=r.states_save)
    homes.update(y1=r.y1_save, v=r.v_save, p=r.p_save, gb=r.gb_save, stream=r.stream_save)
    keys = types.SimpleNamespace(**{name: name for name in homes})
    index_of = {name: i for i, name in enumerate(homes)}
    loads, saves = {}, {}

    def load(layer, name):
        copy = pltpu.make_async_copy(
            homes[name].at[layer], getattr(r, name), r.load_sems.at[index_of[name]]
        )
        copy.start()
        loads[name] = copy

    def need(*wanted):
        for name in wanted:
            if name in loads:
                loads.pop(name).wait()

    def save(layer, name, ref=None):
        if layer < last:
            src = getattr(r, name) if ref is None else ref
            copy = pltpu.make_async_copy(
                src, homes[name].at[layer], r.save_sems.at[index_of[name]]
            )
            copy.start()
            saves[name] = copy

    def settled(*which):
        for name in which:
            if name in saves:
                saves.pop(name).wait()

    def over(count, one):
        def each(i, carry):
            one(i)
            return carry

        lax.fori_loop(0, count, each, 0)

    act_load = pltpu.make_async_copy(r.activations, hb.at[:, : sz.width], r.in_sems.at[0])
    cot_load = pltpu.make_async_copy(r.cotangent, wide_t, r.in_sems.at[1])
    len_load = pltpu.make_async_copy(r.lengths, r.lens, r.in_sems.at[2])
    len_load.start()
    act_load.start()
    load(0, keys.gate_w)
    units.greet()
    mine[...] = jnp.zeros_like(mine)
    small[0] = jnp.zeros((8, SMALL), F32)
    len_load.wait()
    fill_masks(r.lens, valid, keep, sz, True)

    def norm_straight(stream, gain, low):
        for i in range(sz.rows // 64):
            at = slice(i * 64, i * 64 + 64)
            x = stream[at, :]
            scale = lax.rsqrt(jnp.mean(x * x, axis=-1, keepdims=True) + epsilon)
            low[at, :] = (x * scale * gain[...]).astype(BF16)

    def to_steps(src, put):
        def cast(i):
            at = tile(i, 64)
            for k in range(sz.width // LANES):
                natural[k, at, :] = src[at, k * LANES : (k + 1) * LANES].astype(F32)

        over(sz.rows // 64, cast)

        def gather(j):
            for k in range(sz.width // LANES):
                parts = [
                    natural[k, strided(s * sz.span + j, sz.steps), :] for s in range(sz.micro)
                ]
                put(tile(j, sz.group), slice(k * LANES, (k + 1) * LANES), jnp.concatenate(parts, axis=0))

        def gather_four(i):
            for k in range(4):
                gather(i * 4 + k)

        over(sz.steps // 4, gather_four)

    def from_steps(src, dst, sem):
        def scatter(j):
            for k in range(sz.width // LANES):
                value = src[tile(j, sz.group), k * LANES : (k + 1) * LANES]
                for s in range(sz.micro):
                    natural[k, strided(s * sz.span + j, sz.steps), :] = value[s * 8 : s * 8 + 8]

        over(sz.steps, scatter)
        copies = []
        for k in range(sz.width // LANES):
            lanes = slice(k * LANES, (k + 1) * LANES)
            copies.append(pltpu.make_async_copy(natural.at[k], dst.at[:, lanes], sem.at[k]))
            copies[-1].start()
        return copies

    act_load.wait()

    def put_gx(at, lanes, value):
        gx[at, lanes] = value

    to_steps(hb.at[:, : sz.width], put_gx)

    parts = [slice(part * half, (part + 1) * half) for part in range(2)]

    def exchange_start(way, layer, part):
        lanes = parts[part]
        slots = r.slots.at[way, layer]
        me = lax.axis_index("section")
        copies = []
        for hop in range(1, sz.sections):
            copies.append(
                pltpu.make_async_remote_copy(
                    src_ref=mine.at[:, lanes],
                    dst_ref=slots.at[me, :, lanes],
                    send_sem=r.pair_send.at[way, layer, part, hop - 1],
                    recv_sem=r.pair_recv.at[way, layer, part, hop - 1],
                    device_id={"section": lax.rem(me + hop, sz.sections)},
                    device_id_type=MESH,
                )
            )
        for copy in copies:
            copy.start()
        slots[me, :, lanes] = mine[:, lanes]
        return slots, copies

    sent = {}

    def sends_settled(part):
        for copy in sent.pop(part, ()):
            copy.wait_send()

    def exchange_end(slots, copies, reverse, part):
        for copy in copies:
            copy.wait_recv()
        sent[part] = copies
        part_enter(slots, prefix, enter, sz, reverse, parts[part])

    def in_turn(count, dots, rest, after=None, third=None):
        dots(0)
        for n in range(count):
            if n + 1 < count:
                dots(n + 1)
            if third is not None and n > 0:
                third(n - 1)
            rest(n)
            if after is not None:
                after(n)

    def keep_cotangent():
        cot_load.wait()

        def put_low(at, lanes, value):
            low[at, lanes] = value.astype(BF16)

        to_steps(wide_t, put_low)
        low_t[...] = low[...].T

    def forward(layer):
        stream = r.stream if layer > 0 else gx
        settled(keys.u)
        norm_straight(stream, r.mix_gain.at[layer : layer + 1], r.u)
        save(layer, keys.u)
        if layer == 0:
            save(layer, keys.stream, gx)
        need(keys.gate_w)
        if layer == 0:
            for name in (keys.out_w, keys.up_w, keys.down_w):
                load(0, name)
            cot_load.start()
        settled(keys.a, keys.b, keys.zc)
        hw = 256
        bias = r.gate_bias

        def gate_dots(n):
            for part in range(3):
                cols = slice(part * sz.hidden + n * hw, part * sz.hidden + (n + 1) * hw)
                zs[n % 2][:, part * hw : (part + 1) * hw] = (
                    jnp.dot(r.u[...], r.gate_w[:, cols], preferred_element_type=F32)
                    + bias[layer : layer + 1, cols]
                )

        def gate_rest(n):
            for chunk in range(sz.rows // 64):
                at = slice(chunk * 64, chunk * 64 + 64)
                vm, km = valid[at, :], keep[at, :]
                for lane in range(hw // LANES):
                    zf, zi, zc = (
                        zs[n % 2][at, part * hw + lane * LANES : part * hw + (lane + 1) * LANES]
                        for part in range(3)
                    )
                    cols = slice(n * hw + lane * LANES, n * hw + (lane + 1) * LANES)
                    a, b = odds(zf, zi)
                    fp, ip, _ = gate_weights(a, b)
                    decay[at, cols] = fp * km
                    drive[at, cols] = ip * zc * vm
                    r.a[at, cols] = a
                    r.b[at, cols] = b
                    r.zc[at, cols] = zc
                    r.forget[...] += jnp.sum((fp * vm).reshape(8, 8, LANES), axis=0)

        flights = []

        def gate_after(n):
            if n % 2 == 0:
                return
            lanes = parts[n // 2]

            def totals(j, pair):
                at = tile(j, sz.group)
                d = decay[at, lanes]
                return pair[0] * d, pair[1] * d + drive[at, lanes]

            one = jnp.ones((sz.group, half), F32)
            pair = steps_of(sz.steps, 8, totals, (one, jnp.zeros_like(one)))
            r.chunk_p[:, lanes] = pair[0]
            r.chunk_t[:, lanes] = pair[1]
            sends_settled(n // 2)
            part_totals(r.chunk_p, r.chunk_t, sz, False, prefix, mine, lanes)
            if layer == 0 and n == 1:
                units.greeted()
            flights.append(exchange_start(0, layer, n // 2))

        r.forget[...] = jnp.zeros_like(r.forget)
        in_turn(sz.hidden // hw, gate_dots, gate_rest, gate_after)
        small[0, layer * 4 : layer * 4 + 1, sz.hidden : sz.hidden + LANES] = jnp.sum(
            r.forget[...], axis=0, keepdims=True
        )
        for name in (keys.a, keys.b, keys.zc):
            save(layer, name)
        if layer < last:
            load(layer + 1, keys.gate_w)
        settled(keys.states, keys.y1, keys.v, keys.p, keys.gb, keys.stream)
        states = r.states
        for part, lanes in enumerate(parts):
            exchange_end(*flights[part], False, part)
            states[0 : sz.group, lanes] = enter[:, lanes]

            def walk(j, h):
                at = tile(j, sz.group)
                h = decay[at, lanes] * h + drive[at, lanes]
                states[tile(j + 1, sz.group), lanes] = h
                hb[at, lanes] = h.astype(BF16)
                return h

            steps_of(sz.steps, 8, walk, enter[:, lanes])
            if (layer, part) == (0, 0):
                keep_cotangent()
        save(layer, keys.states)
        need(keys.out_w)

        r.y1[...] = stream[...] + jnp.dot(hb[...], r.out_w[...], preferred_element_type=F32)
        save(layer, keys.y1)
        if layer < last:
            load(layer + 1, keys.out_w)
        norm_straight(r.y1, r.mlp_gain.at[layer : layer + 1], r.v)
        save(layer, keys.v)
        need(keys.up_w)

        tiles = range(8) if layer < last else (0, 2, 4, 6, 1, 3, 5, 7)

        def up_dots(n):
            cols = slice(tiles[n] * 256, (tiles[n] + 1) * 256)
            zs[n % 2][:, :256] = jnp.dot(
                r.v[...], r.up_w[:, cols], preferred_element_type=F32
            )

        def up_rest(n):
            cols = slice(tiles[n] * 256, (tiles[n] + 1) * 256)
            for chunk in range(sz.rows // 64):
                at = slice(chunk * 64, chunk * 64 + 64)
                p = zs[n % 2][at, :256]
                r.p[at, cols] = p
                r.gb[at, cols] = (p * normal_below(p)).astype(BF16)

        def down_part(n):
            s, unit = tiles[n] // 2, tiles[n] % 2
            value = jnp.dot(
                low_t[...],
                r.gb[:, tiles[n] * 256 : (tiles[n] + 1) * 256],
                preferred_element_type=F32,
            )
            for k in range(8):
                for h in range(2):
                    at = place(unit, h, s // 2, k % 2, k // 2)
                    held[unit, s % 2, h, at] = value[
                        k * 64 : k * 64 + 64, h * 128 : h * 128 + 128
                    ]

        def up_after(n):
            units.passed(0.3)
            if n == 4:
                units.produced(0, 0)

        if layer < last:
            in_turn(8, up_dots, up_rest)
        else:
            in_turn(8, up_dots, up_rest, up_after, down_part)
            down_part(7)
            units.produced(0.2, 1)
        save(layer, keys.p)
        save(layer, keys.gb)
        if layer < last:
            load(layer + 1, keys.up_w)
        need(keys.down_w)
        out = r.stream if layer < last else gy1

        out[...] = r.y1[...] + jnp.dot(r.gb[...], r.down_w[...], preferred_element_type=F32)
        if layer < last:
            load(layer + 1, keys.down_w)

    def down_grad(layer, unit):
        for k in range(2):
            units.room(unit + k)

        def one(n):
            s, t = n // 2, n % 2
            value = jnp.dot(low_t[...], r.gb[:, tile(n, 256)], preferred_element_type=F32)
            for b in range(8):
                for h in range(2):
                    at = [place(unit + k, h, s // 2, b % 2, b // 2) for k in range(2)]
                    held[(unit + t) % HELD, s % 2, h, jnp.where(t == 0, *at)] = value[
                        b * 64 : b * 64 + 64, h * 128 : h * 128 + 128
                    ]

        over(8, one)
        units.produced(2, unit, unit + 1)

    def cast(src, dst):
        def one(i):
            at = tile(i, 64)
            dst[at, :] = src[at, :].astype(dst.dtype)

        over(sz.rows // 64, one)

    def turn_rows(src, dst, n):
        at = tile(n, 128)
        dst[:, at] = src[at, :].T

    def contract(left, weight, dst, count, beside=None):
        def one(n):
            if beside is not None:
                beside(n)
            cols = tile(n, 256)
            dst[:, cols] = lax.dot_general(
                left[...], weight[cols, :], (((1,), (1,)), ((), ())), preferred_element_type=F32
            )

        over(count // 256, one)

    def up_grad(layer, unit):
        for k in range(2):
            units.room(unit + k)

        def one(b):
            value = jnp.dot(wide_t[...], gp[:, tile(b, 256)], preferred_element_type=F32)
            for s in range(4):
                for h in range(2):
                    for t in range(2):
                        at = place(unit + t, h, s // 2, b % 2, b // 2)
                        held[(unit + t) % HELD, s % 2, h, at] = value[
                            s * 128 + h * 64 : s * 128 + h * 64 + 64, t * 128 : t * 128 + 128
                        ]

        over(8, one)
        units.produced(2.5, unit, unit + 1)

    def out_grad(layer, unit):
        def cast_state(i):
            hb[tile(i, sz.group), :] = r.states[tile(i + 1, sz.group), :].astype(BF16)

        if layer < last:
            over(sz.steps, cast_state)
        units.room(unit)

        def one(s):
            value = jnp.dot(r.go_t[...], hb[:, tile(s, 256)], preferred_element_type=F32)
            for b in range(8):
                for h in range(2):
                    at = place(unit, h, s // 2, b % 2, b // 2)
                    held[unit % HELD, s % 2, h, at] = value[
                        b * 64 : b * 64 + 64, h * 128 : h * 128 + 128
                    ]

        over(4, one)
        units.produced(1.2, unit)

    def backward(layer, unit):
        late = layer < last

        def freed(*which):
            if layer > 0:
                for name in which:
                    load(layer - 1, name)

        if not late:
            freed(keys.gb)
        need(keys.down_w, keys.p, keys.v)

        def act_dots(n):
            zs[n % 2][:, :256] = lax.dot_general(
                low[...],
                r.down_w[n * 256 : (n + 1) * 256, :],
                (((1,), (1,)), ((), ())),
                preferred_element_type=F32,
            )

        def act_rest(n):
            if n < 4:
                turn_rows(r.v, wide_t, n)
            elif late:
                turn_rows(low, low_t, n - 4)
            cols = slice(n * 256, (n + 1) * 256)
            for chunk in range(sz.rows // 64):
                at = slice(chunk * 64, chunk * 64 + 64)
                p = r.p[at, cols]
                slope = normal_below(p) + ROOT_TAU * p * jnp.exp(-0.5 * p * p)
                gp[at, cols] = (zs[n % 2][at, :256] * slope).astype(BF16)

        in_turn(sz.inner // 256, act_dots, act_rest, lambda n: units.passed(0.6))
        freed(keys.down_w, keys.p, keys.v)
        if not late:
            up_grad(layer, unit + 2)
        need(keys.up_w, keys.y1, keys.u)

        def turn_u(n):
            for k in range(2):
                turn_rows(r.u, r.u_t, 2 * n + k)

        contract(gp, r.up_w, grad, sz.width, turn_u)
        freed(keys.u)
        freed(keys.up_w)
        units.passed(1.5)
        norm_back(r.y1, r.mlp_gain.at[layer : layer + 1], grad, gx, gy1, r.mlp_sum, sz.rows, 64, low)
        freed(keys.y1)
        need(keys.states)
        units.passed(2)
        need(keys.out_w, keys.a, keys.b)
        contract(low, r.out_w, ga, sz.hidden, lambda n: turn_rows(low, r.go_t, n))
        freed(keys.out_w)
        units.passed(1)
        if not late:
            out_grad(layer, unit + 4)
        flights = []
        for part, lanes in enumerate(parts):

            def totals(j, pair):
                at = tile(j, sz.group)
                if layer < last:
                    mask = jnp.concatenate([keep[at, :]] * (half // LANES), axis=1)
                    d = gate_weights(r.a[at, lanes], r.b[at, lanes])[0] * mask
                    decay[at, lanes] = d
                else:
                    d = decay[at, lanes]
                return pair[0] * d, d * (ga[at, lanes] + pair[1])

            one = jnp.ones((sz.group, half), F32)
            pair = steps_of(sz.steps, 2, totals, (one, jnp.zeros_like(one)), reverse=True)
            r.chunk_p[:, lanes] = pair[0]
            r.chunk_t[:, lanes] = pair[1]
            sends_settled(part)
            part_totals(r.chunk_p, r.chunk_t, sz, True, prefix, mine, lanes)
            flights.append(exchange_start(1, layer, part))
            carried = [units.expect(link, 16384) for link in ("core", "x", "x")]
            units.passed(0.8)
        need(keys.zc)
        if late:
            need(keys.gb)
            down_grad(layer, unit)
            up_grad(layer, unit + 2)
            out_grad(layer, unit + 4)
        unit += 5
        units.now = max(units.now, *carried)

        def gate_lanes(n):
            wide = 2 * LANES
            lanes = tile(n, wide)

            def walk(j, kept):
                m, bf, bi, bc = kept
                at = tile(j, sz.group)
                d = decay[at, lanes]
                q = ga[at, lanes] + m
                a, b, zc = r.a[at, lanes], r.b[at, lanes], r.zc[at, lanes]
                vm = jnp.concatenate([valid[at, :]] * 2, axis=1)
                km = jnp.concatenate([keep[at, :]] * 2, axis=1)
                fp, ip, inv = gate_weights(a, b)
                gf = q * (r.states[at, lanes] * km - zc * vm)
                parts = (
                    (gf * (a * inv) * fp).astype(BF16),
                    (-gf * (b * inv) * ip).astype(BF16),
                    (q * vm * ip).astype(BF16),
                )
                for part, value in enumerate(parts):
                    gz[at, pl.ds(pl.multiple_of(part * sz.hidden + n * wide, wide), wide)] = value
                return (d * q,) + tuple(
                    a + value.astype(F32) for a, value in zip((bf, bi, bc), parts)
                )

            zero = jnp.zeros((sz.group, wide), F32)
            _, *sums = steps_of(
                sz.steps, 4, walk, (enter[:, lanes], zero, zero, zero), reverse=True
            )
            for part, total in enumerate(sums):
                small[0, layer * 4 + part : layer * 4 + part + 1, lanes] = jnp.sum(
                    total, axis=0, keepdims=True
                )

        turns = sz.hidden // LANES // 4
        for part in range(2):
            exchange_end(*flights[part], True, part)
            over(turns, lambda n: gate_lanes(n + part * turns))
            units.passed(1.8)
        freed(keys.a, keys.b, keys.zc, keys.states)
        for k in range(2):
            units.room(unit + k)

        def gate_grad(b):
            cols = pl.ds(pl.multiple_of(b * 384, 128), 256)
            value = jnp.dot(r.u_t[...], gz[:, cols], preferred_element_type=F32)
            for s in range(4):
                for h in range(2):
                    for t in range(2):
                        at = place(unit + t, h, s // 2, b % 2, b // 2)
                        held[(unit + t) % HELD, s % 2, h, at] = value[
                            s * 128 + h * 64 : s * 128 + h * 64 + 64, t * 128 : t * 128 + 128
                        ]

        over(8, gate_grad)
        units.produced(3, unit, unit + 1)
        unit += 2
        units.room(unit)

        def gate_rest(z):
            right = jnp.concatenate(
                [
                    gz[:, pl.ds(pl.multiple_of((2 * z + y) * 384 + 256, 128), 128)]
                    for y in range(2)
                ],
                axis=1,
            )
            value = jnp.dot(r.u_t[...], right, preferred_element_type=F32)
            for s in range(4):
                for h in range(2):
                    for y in range(2):
                        at = place(unit, h, s // 2, y, z)
                        held[unit % HELD, s % 2, h, at] = value[
                            s * 128 + h * 64 : s * 128 + h * 64 + 64, y * 128 : y * 128 + 128
                        ]

        over(4, gate_rest)
        units.produced(1.5, unit)
        unit += 1
        need(keys.gate_w, keys.stream)
        contract(gz, r.gate_w, grad, sz.width)
        freed(keys.gate_w)
        units.passed(2.5)
        norm_back(r.stream, r.mix_gain.at[layer : layer + 1], grad, gy1, gx, r.mix_sum, sz.rows, 64, low)
        freed(keys.stream)
        row = slice(layer * 4 + 3, layer * 4 + 4)
        small[0, row, : sz.width] = jnp.sum(r.mix_sum[...], axis=0, keepdims=True)
        small[0, row, sz.width : 2 * sz.width] = jnp.sum(r.mlp_sum[...], axis=0, keepdims=True)
        units.passed(1.5)

    forward(0)
    for layer in range(1, layers):
        forward(layer)
    out_copies = from_steps(gy1, r.layer_out, r.out_sems)
    cast(low, gx)
    units.passed(2)
    for index, layer in enumerate(reversed(range(layers))):
        backward(layer, 8 * index)
    def small_done():
        total = small[STAGES]
        count = jnp.int32(0)
        for s in range(r.lens.shape[0]):
            for d in range(r.lens.shape[1]):
                count = count + r.lens[s, d]
        scale = 1.0 / (count.astype(F32) * sz.hidden)
        for layer in range(layers):
            one = slice(layer, layer + 1)
            for part in range(3):
                r.bias_out[one, part * sz.hidden : (part + 1) * sz.hidden] = total[
                    layer * 4 + part : layer * 4 + part + 1, : sz.hidden
                ]
            row = slice(layer * 4 + 3, layer * 4 + 4)
            r.mix_out[one, :] = total[row, : sz.width]
            r.mlp_out[one, :] = total[row, sz.width : 2 * sz.width]
            lanes = total[layer * 4 : layer * 4 + 1, sz.hidden : sz.hidden + LANES]
            r.forget_out[one, :] = jnp.sum(lanes, axis=1, keepdims=True) * scale + jnp.zeros(
                (1, LANES), F32
            )
        pairs = (
            (r.bias_out, r.gate_bias_grad),
            (r.mix_out, r.mix_gain_grad),
            (r.mlp_out, r.mlp_gain_grad),
            (r.forget_out, r.forget_mean),
        )
        for k, (src, dst) in enumerate(pairs):
            copy = pltpu.make_async_copy(src, dst, r.small_out_sems.at[k])
            copy.start()
            units.leaving.append(copy)

    units.small_done = small_done
    units.small_start()
    for copy in out_copies:
        copy.wait()
    out_copies = from_steps(gx, r.input_grad, r.out_sems)
    units.passed(1)
    units.drain()
    for copy in out_copies:
        copy.wait()
    for part in range(2):
        sends_settled(part)


def run_whole_step(sz, layers, named):
    lengths = named["lengths"]
    rows, d, h, f = sz.rows, sz.width, sz.hidden, sz.inner
    vm = lambda *dims, kind=F32: pltpu.VMEM(dims, kind)
    sems = pltpu.SemaphoreType
    spec = dict(gate_bias=VMEM, mix_gain=VMEM, mlp_gain=VMEM)
    outputs = dict(
        layer_out=(shape(rows, d), ANY),
        input_grad=(shape(rows, d), ANY),
        gate_weight_grad=(shape(layers, 128, 384), ANY),
        gate_bias_grad=(shape(layers, 3 * h), ANY),
        out_weight_grad=(shape(layers, 64, 256), ANY),
        up_weight_grad=(shape(layers, 128, 256), ANY),
        down_weight_grad=(shape(layers, 64, 512), ANY),
        mix_gain_grad=(shape(layers, d), ANY),
        mlp_gain_grad=(shape(layers, d), ANY),
        forget_mean=(shape(layers, LANES), ANY),
    )
    results = len(outputs)
    kept = dict(
        u=((rows, d), BF16),
        a=((rows, h), F32),
        b=((rows, h), F32),
        zc=((rows, h), F32),
        states=((rows + sz.group, h), F32),
        y1=((rows, d), F32),
        v=((rows, d), BF16),
        p=((rows, f), F32),
        gb=((rows, f), BF16),
        stream=((rows, d), F32),
    )
    scratch = {}
    for name, (dims, kind) in kept.items():
        outputs[name + "_save"] = (shape(layers - 1, *dims, kind=kind), ANY)
        scratch[name] = vm(*dims, kind=kind)
    scratch.update(
        gate_w=vm(d, 3 * h, kind=BF16),
        out_w=vm(h, d, kind=BF16),
        up_w=vm(d, f, kind=BF16),
        down_w=vm(f, d, kind=BF16),
        valid=vm(rows, LANES),
        keep=vm(rows, LANES),
        gx=vm(rows, d),
        low=vm(rows, d, kind=BF16),
        low_t=vm(d, rows, kind=BF16),
        wide_t=vm(d, rows, kind=BF16),
        u_t=vm(d, rows, kind=BF16),
        go_t=vm(d, rows, kind=BF16),
        hb=vm(rows, h, kind=BF16),
        z1=vm(rows, 768),
        drive=vm(rows, h),
        forget=vm(8, LANES),
        ga=vm(rows, h),
        gz=vm(rows, 3 * h, kind=BF16),
        grad=vm(rows, d),
        gy1=vm(rows, d),
        decay=vm(rows, h),
        chunk_p=vm(sz.group, h),
        chunk_t=vm(sz.group, h),
        prefix=vm(2, sz.group, h),
        enter=vm(sz.group, h),
        mine=vm(8, h),
        slots=vm(2, layers, sz.sections, 8, h),
        mlp_sum=vm(8, d),
        mix_sum=vm(8, d),
        held=vm(HELD, 2, 2, 16, BLOCK, LANES),
        small=vm(STAGES + 1, 8, SMALL),
        small_arrived=vm(STAGES, 8, SMALL),
        in_sems=sems.DMA((3,)),
        bias_out=vm(layers, 3 * h),
        mix_out=vm(layers, d),
        mlp_out=vm(layers, d),
        forget_out=vm(layers, LANES),
        small_out_sems=sems.DMA((4,)),
        result_sems=sems.DMA((8 * layers, 2)),
        lens=pltpu.SMEM(lengths.shape, jnp.int32),
        out_sems=sems.DMA((d // LANES,)),
        natural=vm(d // LANES, rows, LANES),
        load_sems=sems.DMA((len(kept) + 4,)),
        save_sems=sems.DMA((len(kept) + 4,)),
        pair_send=sems.DMA((2, layers, 2, sz.sections - 1)),
        pair_recv=sems.DMA((2, layers, 2, sz.sections - 1)),
        send_sems=sems.DMA((SENDS, 2 * STAGES - 1)),
        recv_sems=sems.DMA((max(RINGS), 2 * STAGES - 1)),
        credits=sems.REGULAR((2 * STAGES - 1, 8 * layers)),
        small_send=sems.DMA((STAGES,)),
        small_recv=sems.DMA((STAGES,)),
    )
    for stage in range(STAGES):
        scratch[f"arrived{stage}"] = vm(RINGS[stage], 2, 16 >> stage, BLOCK, LANES)
    names = list(named) + list(outputs) + list(scratch)
    out = pl.pallas_call(
        functools.partial(whole_step, sz, layers, names),
        out_shape=tuple(value for value, _ in outputs.values()),
        in_specs=[spec.get(name, ANY) for name in named],
        out_specs=[place_of for _, place_of in outputs.values()],
        scratch_shapes=list(scratch.values()),
        compiler_params=pltpu.CompilerParams(
            collective_id=4, has_side_effects=True, vmem_limit_bytes=LIMIT
        ),
        name="whole_step",
    )(*named.values())
    return out[:results]


def deliver_kernel(count, *refs):
    sources, targets, held = refs[:count], refs[count : 2 * count], refs[2 * count : 3 * count - 1]
    sems = refs[3 * count - 1]
    arrivals = [
        pltpu.make_async_copy(sources[i], held[i], sems.at[0, i]) for i in range(count - 1)
    ]
    departures = [
        pltpu.make_async_copy(held[i], targets[i], sems.at[1, i]) for i in range(count - 1)
    ]
    for copy in arrivals:
        copy.start()
    for layer in range(targets[-1].shape[0]):
        targets[-1][layer] = sources[-1][layer, 0]
    for arrival, departure in zip(arrivals, departures):
        arrival.wait()
        departure.start()
    for copy in departures:
        copy.wait()


def deliver(values):
    count = len(values)
    scalars = pl.BlockSpec(memory_space=pltpu.SMEM)
    shapes = [shape(*value.shape) for value in values[:-1]] + [shape(values[-1].shape[0])]
    return pl.pallas_call(
        functools.partial(deliver_kernel, count),
        out_shape=tuple(shapes),
        in_specs=[ANY] * (count - 1) + [scalars],
        out_specs=[ANY] * (count - 1) + [scalars],
        scratch_shapes=[pltpu.VMEM(value.shape, F32) for value in values[:-1]]
        + [pltpu.SemaphoreType.DMA((2, count - 1))],
        compiler_params=pltpu.CompilerParams(vmem_limit_bytes=LIMIT),
        name="deliver",
    )(*values)


def mask_kernel(sizes, lens, valid, keep):
    fill_masks(lens, valid, keep, sizes)


def body(
    activations,
    cotangent,
    lengths,
    gate_weight,
    gate_bias,
    out_weight,
    up_weight,
    down_weight,
    mix_gain,
    mlp_gain,
):
    micro, span, width = activations.shape
    layers = gate_weight.shape[0]
    sz = Sizes(
        micro, span, width, out_weight.shape[1], up_weight.shape[2], lax.axis_size("section")
    )

    blocks = (width // 4, 3 * sz.hidden // 8, width // 8, sz.inner // 4, sz.hidden // 4)
    axes = (lax.axis_size("section"), lax.axis_size("batch"))
    if axes == (4, 8) and blocks == (128, 384, 64, 512, 256):
        out = run_whole_step(
            sz,
            layers,
            dict(
                activations=activations.reshape(sz.rows, width),
                cotangent=cotangent.reshape(sz.rows, width),
                lengths=lengths.T,
                gate_bias=gate_bias,
                mix_gain=mix_gain,
                mlp_gain=mlp_gain,
                gate_hbm=gate_weight,
                out_hbm=out_weight,
                up_hbm=up_weight,
                down_hbm=down_weight,
            ),
        )
        stream_out, input_grad, gate_g, bias_g, out_g, up_g, down_g, *rest = deliver(out)
        return (
            stream_out.reshape(activations.shape),
            input_grad.reshape(activations.shape),
            gate_g,
            bias_g,
            out_g.transpose(0, 2, 1),
            up_g,
            down_g.transpose(0, 2, 1),
            *rest,
        )

    def arranged(value):
        value = value.astype(F32).reshape(micro, CHUNKS, sz.steps, width)
        return value.transpose(2, 0, 1, 3).reshape(sz.rows, width)

    def restored(value):
        value = value.reshape(sz.steps, micro, CHUNKS, width).transpose(1, 2, 0, 3)
        return value.reshape(micro, span, width)

    masks = pl.pallas_call(
        functools.partial(mask_kernel, sz),
        out_shape=(shape(sz.rows, LANES), shape(sz.rows, LANES)),
        in_specs=[pl.BlockSpec(memory_space=pltpu.SMEM)],
        out_specs=[VMEM] * 2,
        name="masks",
    )(lengths)
    weights = (gate_weight, out_weight, up_weight, down_weight)
    stream = arranged(activations)
    streams, saved, forgets = [], [], []
    for layer in range(layers):
        streams.append(stream)
        stream, *kept, forget, pairs = run_forward(
            sz,
            layer,
            stream,
            masks,
            gate_bias[layer : layer + 1],
            mix_gain[layer : layer + 1],
            mlp_gain[layer : layer + 1],
            weights,
        )
        saved.append((*kept, pairs))
        forgets.append(forget)
    layer_out = restored(stream)
    gx = arranged(cotangent)
    true_count = jnp.sum(lengths).astype(F32)
    forgets = [jnp.sum(forget) for forget in forgets]
    sums, small = [None] * layers, [None] * layers
    for layer in reversed(range(layers)):
        gx, gate_g, out_g, up_g, down_g, bias_g, mix_g, mlp_g = run_backward(
            sz,
            layer,
            gx,
            streams[layer],
            masks,
            mix_gain[layer : layer + 1],
            mlp_gain[layer : layer + 1],
            saved[layer],
            weights,
        )
        sums[layer] = (gate_g, out_g.T, up_g, down_g.T)
        small[layer] = tuple(jnp.sum(part, axis=0) for part in (bias_g, mix_g, mlp_g))
    input_grad = restored(gx)
    stacked = tuple(jnp.stack(parts) for parts in zip(*sums))
    partial_sums = lax.psum_scatter(stacked, "section", scatter_dimension=1, tiled=True)
    large = lax.psum_scatter(partial_sums, "batch", scatter_dimension=2, tiled=True)
    bias_grad, mix_grad, mlp_grad = (jnp.stack(parts) for parts in zip(*small))
    bias_grad, mix_grad, mlp_grad, forget = lax.psum(
        (bias_grad, mix_grad, mlp_grad, jnp.stack(forgets)), ("section", "batch")
    )
    forget_mean = forget / (true_count * sz.hidden)
    return (
        layer_out,
        input_grad,
        large[0],
        bias_grad,
        large[1],
        large[2],
        large[3],
        mix_grad,
        mlp_grad,
        forget_mean,
    )


def solution(mesh):
    stream = P("batch", "section", None)
    block = P(None, "section", "batch")
    return jax.shard_map(
        body,
        mesh=mesh,
        in_specs=(stream, stream) + (P(),) * 8,
        out_specs=(stream, stream, block, P(), block, block, block, P(), P(), P()),
        check_vma=False,
    )
```
